32 devices in a mesh: cam: 4 (over y, core), ex: 2 (over x), ey: 4 (over z).
Axes of the slice: x: 2, y: 2, z: 4, core: 2. Of those that a mesh axis runs over, the one named last changes fastest.
Arguments:
- scalar: float32 [8, 8, 32, 8, 512], P('ex', None, 'ey', None, 'cam'), may hold values from -3 to 3
- velocity: float32 [3, 8, 8, 32, 8, 512], P(None, 'ex', None, 'ey', None, 'cam'), may hold values from -6 to 6
- lumped_mass: float32 [8, 8, 32, 8, 512], P('ex', None, 'ey', None, 'cam'), may hold values from 0.3 to 3
- pixel_weights: bfloat16 [8, 512, 128], replicated, may hold values from -0.25 to 0.25
- cut_element: int32 [8, 4096], P(None, ('cam', 'ex', 'ey')), may hold values from 0 to 511
- pixel_block: int32 [8, 4096], P(None, ('cam', 'ex', 'ey')), may hold values from 0 to 1024, as said below
Outputs:
- advected: float32 [8, 8, 32, 8, 512], P('ex', None, 'ey', None, 'cam')
- images: float32 [8, 8192, 128], P('cam', ('ex', 'ey'))
The draws below stay inside these ranges and needn't reach their ends.
Inputs may be any that keep to these rules, and one draw needn't show every extreme that they name: `pixel_block`: A value of 1024 marks an empty slot; in each device's 128 slots of one camera the filled ones come first. `cut_element`: A local element number of the owning device, with the radial index fastest, then the azimuthal, then the axial.
All inputs are finite; a program needn't handle non-finite values.
Results may differ from the reference program's by a relative error of at most 0.0028.
Values may be sent and summed in bfloat16 or wider, within the bound.
No kernel may reach another device: no remote copies, remote signals or barrier semaphores. Data moves between devices by JAX's collectives and lax.ppermute only.
A program may use at most 64 MiB of HBM per device.

```python
import math
import jax
import jax.numpy as jnp
import numpy as np
from jax import lax

EA = 4
EB = 8
EC = 16
SLOTS = 128
NBLK = 1024
PIX = 128
NA = 8
NB = 32
NC = 64
CAMS = 8
N_CAM = 4
N_EX = 2
N_EY = 4


def node_parity_sign():
    nodes = jnp.arange(8, dtype=jnp.int32)
    depth = jnp.arange(NC * 8, dtype=jnp.int32) % 8
    parity = nodes[None, :, None, None, None] + nodes[None, None, None, :, None] + depth[None, None, None, None, :]
    return (1 - 2 * (parity % 2)).astype(jnp.float32)


def draw_scalar(key, part):
    size_key, noise_key = jax.random.split(jax.random.fold_in(key, 11))
    shape = (NA, 8, NB, 8, NC * 8)
    sign = node_parity_sign()
    magnitude = jax.random.uniform(size_key, shape, jnp.float32, 0.4, 1.2)
    noise = 0.6 * jnp.clip(jax.random.normal(noise_key, shape, jnp.float32), -3.0, 3.0)
    return (sign * magnitude + noise).astype(jnp.float32)


def draw_velocity(key, part):
    size_key, sign_key = jax.random.split(jax.random.fold_in(key, 23))
    shape = (3, NA, 8, NB, 8, NC * 8)
    magnitude = jax.random.uniform(size_key, shape, jnp.float32, 3.0, 6.0)
    sign = (2 * jax.random.randint(sign_key, shape, 0, 2) - 1).astype(jnp.float32)
    return (sign * magnitude).astype(jnp.float32)


def draw_pixel_block(key, part):
    count_key, block_key = jax.random.split(key)
    devices_all = N_CAM * N_EX * N_EY
    counts = jax.random.randint(count_key, (CAMS, devices_all), SLOTS // 4, SLOTS + 1)
    blocks = jax.random.randint(block_key, (CAMS, SLOTS * devices_all), 0, NBLK)
    position = jnp.arange(SLOTS * devices_all) % SLOTS
    owner_dev = jnp.arange(SLOTS * devices_all) // SLOTS
    is_live = position[None, :] < counts[:, owner_dev]
    return jnp.where(is_live, blocks, NBLK).astype(jnp.int32)


def with_ends(entries, rng, low, top_value):
    longest = entries.shape.index(max(entries.shape))
    spots = []
    for shift in (0, 1):
        where = [jax.random.randint(jax.random.fold_in(rng, axis), (), 0, length) for axis, length in enumerate(entries.shape)]
        where[longest] = (where[longest] + shift) % entries.shape[longest]
        spots.append(tuple(where))
    return entries.at[spots[0]].set(low).at[spots[1]].set(top_value)


def shard_levels(rng, dims, pieces, smallest, high):
    def one(dim, parts):
        heights = jax.random.uniform(jax.random.fold_in(jax.random.fold_in(rng, 6), dim), (parts,), jnp.float32, smallest / len(pieces), high / len(pieces))
        return jnp.repeat(jnp.exp(heights), dims[dim] // parts).reshape((-1,) + (1,) * (len(dims) - dim - 1))

    factor_of = one(*pieces[0])
    for cut in pieces[1:]:
        factor_of = factor_of * one(*cut)
    return factor_of


def bell_draw(stream_key, shape, scale, most, kind=jnp.bfloat16):
    values = jax.random.normal(stream_key, shape, jnp.float32) * scale
    return jnp.minimum(jnp.maximum(values, -most), most).astype(kind)


def setup_inputs(seed: int = 0) -> dict:
    key_list = jax.random.split(jax.random.key(seed), 7)
    return {
        "scalar": draw_scalar(jax.random.fold_in(key_list[6], 71), 0),
        "velocity": draw_velocity(jax.random.fold_in(key_list[6], 71), 0),
        "lumped_mass": jnp.clip(jnp.exp(math.log(3.0) - 2.3025851 * jax.random.uniform(key_list[2], (NA, 8, NB, 8, NC * 8), jnp.float32) ** shard_levels(key_list[2], (NA, 8, NB, 8, NC * 8), ((0, 2), (2, 4), (4, 4)), -0.2, 0.2)), 0.3, 3.0),
        "pixel_weights": bell_draw(key_list[3], (CAMS, 512, PIX), 512 ** -0.5, 0.25),
        "cut_element": with_ends(jax.random.randint(key_list[4], (CAMS, SLOTS * N_CAM * N_EX * N_EY), 0, EA * EB * EC), jax.random.fold_in(key_list[4], 1), 0, (EA * EB * EC) - 1).astype(jnp.int32),
        "pixel_block": draw_pixel_block(jax.random.fold_in(key_list[6], 71), 0),
    }


time_step = 0.01


def legendre_seven(points):
    previous = points * 0.0 + 1.0
    current = points * 1.0
    for order in range(1, 7):
        following = ((2 * order + 1) * points * current - order * previous) / (order + 1)
        previous = current
        current = following
    return current


def gll_derivative():
    degree = 7
    gll_nodes = np.array([-1.0, -0.8717401485096066, -0.5917001814331423, -0.2092992179024789, 0.2092992179024789, 0.5917001814331423, 0.8717401485096066, 1.0])
    values = legendre_seven(gll_nodes)
    derivative = np.zeros((degree + 1, degree + 1))
    for target in range(degree + 1):
        for source in range(degree + 1):
            if target != source:
                derivative[target, source] = values[target] / (values[source] * (gll_nodes[target] - gll_nodes[source]))
    derivative[0, 0] = -degree * (degree + 1) / 4.0
    derivative[degree, degree] = degree * (degree + 1) / 4.0
    return derivative


def pair_sum(extended, dim):
    length = extended.shape[dim] - 2
    middle = lax.slice_in_dim(extended, 1, length + 1, 1, dim)
    following = lax.slice_in_dim(extended, 2, length + 2, 1, dim)
    preceding = lax.slice_in_dim(extended, 0, length, 1, dim)
    shape = [1] * extended.ndim
    shape[dim] = length
    node = (jnp.arange(length, dtype=jnp.int32) % 8).reshape(shape)
    is_last = (node == 7).astype(jnp.float32)
    is_first = (node == 0).astype(jnp.float32)
    return middle + is_last * following + is_first * preceding


def wrap_pad(stack, dim):
    length = stack.shape[dim]
    return jnp.concatenate([lax.slice_in_dim(stack, length - 1, length, 1, dim), stack, lax.slice_in_dim(stack, 0, 1, 1, dim)], axis=dim)


def assemble(stack):
    summed = pair_sum(wrap_pad(stack, 1), 1)
    summed = pair_sum(wrap_pad(summed, 2), 2)
    zero_plane = jnp.zeros(summed.shape[:3] + (1,), jnp.float32)
    return pair_sum(jnp.concatenate([zero_plane, summed, zero_plane], axis=3), 3)


def convect(field, velocity, derivative):
    along_axial = jnp.einsum("pi,aibjz->apbjz", derivative, field, precision=lax.Precision.HIGHEST)
    along_azimuth = jnp.einsum("qj,aibjz->aibqz", derivative, field, precision=lax.Precision.HIGHEST)
    shape = field.shape
    split = field.reshape(shape[:4] + (shape[4] // 8, 8))
    along_radius = jnp.einsum("rk,aibjck->aibjcr", derivative, split, precision=lax.Precision.HIGHEST).reshape(shape)
    return velocity[0] * along_axial + velocity[1] * along_azimuth + velocity[2] * along_radius


def reference(scalar, velocity, lumped_mass, pixel_weights, cut_element, pixel_block):
    derivative = jnp.asarray(gll_derivative(), jnp.float32)
    shape = scalar.shape
    flat = (shape[0] * 8, shape[2] * 8, shape[4])
    first_stack = jnp.stack([(lumped_mass * convect(scalar, velocity, derivative)).reshape(flat), lumped_mass.reshape(flat)])
    first_sums = assemble(first_stack)
    assembled_mass = first_sums[1]
    rate_first = (first_sums[0] / assembled_mass).reshape(shape)
    first = scalar - time_step * rate_first
    second_stack = (lumped_mass * convect(first, velocity, derivative)).reshape((1,) + flat)
    rate_second = (assemble(second_stack)[0] / assembled_mass).reshape(shape)
    second = first - time_step * rate_second
    advected = 0.5 * (scalar + second)

    elements = advected.astype(jnp.bfloat16).reshape(NA, 8, NB, 8, NC, 8).transpose(0, 2, 4, 1, 3, 5).reshape(NA * NB * NC, 512)
    total = SLOTS * N_CAM * N_EX * N_EY
    owner_dev = jnp.arange(total, dtype=jnp.int32) // SLOTS
    cam_index = owner_dev // (N_EX * N_EY)
    ex_index = (owner_dev // N_EY) % N_EX
    ey_index = owner_dev % N_EY
    axial = ex_index[None, :] * EA + cut_element // (EB * EC)
    azimuth = ey_index[None, :] * EB + (cut_element // EC) % EB
    radial = cam_index[None, :] * EC + cut_element % EC
    flat_index = ((axial * NB + azimuth) * NC + radial).astype(jnp.int32)
    column = ex_index[None, :] * N_EY + ey_index[None, :]
    columns_all = N_EX * N_EY * NBLK
    target = jnp.where(pixel_block < NBLK, column * NBLK + pixel_block, columns_all).astype(jnp.int32)

    def render(packed):
        indices, targets, weight_rows = packed
        picked_rows = jnp.take(elements, indices, axis=0)
        values = jnp.dot(picked_rows, weight_rows, preferred_element_type=jnp.float32)
        return jnp.zeros((columns_all, PIX), jnp.float32).at[targets].add(values, mode="drop")

    images = lax.map(render, (flat_index, target, pixel_weights))
    return advected, images
```

```python
import functools

import jax
import jax.numpy as jnp
import numpy as np
from jax import lax
from jax.experimental import pallas as pl
from jax.experimental.pallas import tpu as pltpu
from jax.sharding import PartitionSpec as P

NBLK = 1024
F32 = jnp.float32
BF16 = jnp.bfloat16
VMEM = pl.BlockSpec(memory_space=pltpu.VMEM)
time_step = 0.01


def legendre_seven(points):
    previous = points * 0.0 + 1.0
    current = points * 1.0
    for order in range(1, 7):
        following = ((2 * order + 1) * points * current - order * previous) / (order + 1)
        previous = current
        current = following
    return current


def gll_derivative():
    degree = 7
    gll_nodes = np.array(
        [
            -1.0,
            -0.8717401485096066,
            -0.5917001814331423,
            -0.2092992179024789,
            0.2092992179024789,
            0.5917001814331423,
            0.8717401485096066,
            1.0,
        ]
    )
    values = legendre_seven(gll_nodes)
    derivative = np.zeros((degree + 1, degree + 1))
    for target in range(degree + 1):
        for source in range(degree + 1):
            if target != source:
                derivative[target, source] = values[target] / (
                    values[source] * (gll_nodes[target] - gll_nodes[source])
                )
    derivative[0, 0] = -degree * (degree + 1) / 4.0
    derivative[degree, degree] = degree * (degree + 1) / 4.0
    return derivative


def split_two(table):
    high = table.astype(np.float32).astype(BF16)
    low = (table - high.astype(np.float64)).astype(np.float32).astype(BF16)
    return high, low


def derivative_tables():
    derivative = gll_derivative()
    eye = np.eye(8)
    rows = np.concatenate([np.kron(derivative, eye), np.kron(eye, derivative)], axis=0)
    high, low = split_two(rows)
    row_table = np.concatenate([high, high, low], axis=1)
    lanes = np.kron(np.eye(16), derivative.T)
    high, low = split_two(lanes)
    lane_table = np.concatenate(
        [
            np.concatenate([high, low], axis=1),
            np.concatenate([high, np.zeros_like(high)], axis=1),
        ],
        axis=0,
    )
    return jnp.asarray(row_table), jnp.asarray(lane_table)


def lane_ids(shape):
    return lax.broadcasted_iota(jnp.int32, shape, len(shape) - 1)


def convect_pair(fields, row_table, lane_table):
    highs = [f.astype(BF16) for f in fields]
    lows = [(f - h.astype(F32)).astype(BF16) for f, h in zip(fields, highs)]
    high = jnp.concatenate(highs, axis=1)
    low = jnp.concatenate(lows, axis=1)
    stacked = jnp.concatenate([high, low, high], axis=0)
    by_rows = jnp.dot(row_table, stacked, preferred_element_type=F32)
    out = []
    for n in range(2):
        both = jnp.concatenate([highs[n], lows[n]], axis=1)
        by_lanes = jnp.dot(both, lane_table, preferred_element_type=F32)
        out.append(
            (
                by_rows[:64, 128 * n : 128 * n + 128],
                by_rows[64:, 128 * n : 128 * n + 128],
                by_lanes[:, :128] + by_lanes[:, 128:],
            )
        )
    return out


def join_lanes(g):
    lane = lane_ids(g.shape)
    node = lane & 7
    last = (node == 7) & (lane != 127)
    first = (node == 0) & (lane != 0)
    other = jnp.where(
        last, pltpu.roll(g, 127, 1), jnp.where(first, pltpu.roll(g, 1, 1), 0.0)
    )
    return g + other


def join_local(s_ref, count):
    for b in range(7):
        total = s_ref[:, 8 * b + 7, :] + s_ref[:, 8 * b + 8, :]
        s_ref[:, 8 * b + 7, :] = total
        s_ref[:, 8 * b + 8, :] = total
    for f in range(count):
        for a in range(3):
            at = 32 * f + 8 * a + 7
            total = s_ref[at] + s_ref[at + 1]
            s_ref[at] = total
            s_ref[at + 1] = total


def axial_faces(s_ref, x_ref, count):
    for f in range(count):
        x_ref[0, f] = s_ref[32 * f + 31]
        x_ref[1, f] = s_ref[32 * f]


def first_kernel(scalar_ref, velocity_ref, mass_ref, row_ref, lane_ref, s_ref, x_ref):
    row_table = row_ref[...]
    lane_table = lane_ref[...]

    def body(a, carry):
        at = pl.ds(pl.multiple_of(a * 8, 8), 8)
        for pair in range(4):
            spans = [slice(16 * pair + 8 * n, 16 * pair + 8 * n + 8) for n in range(2)]
            fields = [scalar_ref[at, s, :].reshape(64, 128) for s in spans]
            slopes = convect_pair(fields, row_table, lane_table)
            for s, (axial, azimuth, radius) in zip(spans, slopes):
                v = [velocity_ref[n, at, s, :].reshape(64, 128) for n in range(3)]
                mass = mass_ref[at, s, :].reshape(64, 128)
                g = mass * (v[0] * axial + v[1] * azimuth + v[2] * radius)
                s_ref[at, s, :] = join_lanes(g).reshape(8, 8, 128)
                s_ref[pl.ds(pl.multiple_of(a * 8 + 32, 8), 8), s, :] = join_lanes(mass).reshape(
                    8, 8, 128
                )
        return carry

    lax.fori_loop(0, 4, body, 0)
    join_local(s_ref, 2)
    axial_faces(s_ref, x_ref, 2)


def axial_kernel(count, s_in, x_ref, s_ref, up_ref, down_ref):
    for f in range(count):
        s_ref[32 * f] = s_in[32 * f] + x_ref[0, f]
        s_ref[32 * f + 31] = s_in[32 * f + 31] + x_ref[1, f]
    up_ref[...] = s_ref[:, 63, :]
    down_ref[...] = s_ref[:, 0, :]


def azimuth_kernel(count, s_in, first_ref, last_ref, s_ref, z_ref):
    s_ref[:, 0, :] = s_in[:, 0, :] + first_ref[...]
    s_ref[:, 63, :] = s_in[:, 63, :] + last_ref[...]
    slot = ((lane_ids((8, 128)) + 1) >> 1) & 63

    def body(q, carry):
        packed = jnp.zeros((8, 128), F32)
        for i in range(8):
            for b in range(8):
                u = 8 * i + b
                block = s_ref[8 * q + i, 8 * b : 8 * b + 8, :]
                if u:
                    block = pltpu.roll(block, 2 * u, 1)
                packed = jnp.where(slot == u, block, packed)
        z_ref[q] = packed
        return carry

    lax.fori_loop(0, 4 * count, body, 0)


def merged(left, right):
    lane = lane_ids(left.shape)
    return jnp.where((lane & 1) == 0, pltpu.roll(left, 1, 1), pltpu.roll(right, 127, 1))


def unpacked(packed, b):
    lane = lane_ids((8, 128))
    ends = (lane == 0) | (lane == 127)
    rows = []
    for i in range(8):
        u = 8 * i + b
        moved = pltpu.roll(packed, (128 - 2 * u) % 128, 1) if u else packed
        rows.append(jnp.where(ends, moved, 0.0))
    return jnp.concatenate(rows, axis=0)


def second_kernel(
    s_ref, left_ref, right_ref, scalar_ref, velocity_ref, mass_ref, row_ref, lane_ref,
    g_ref, x_ref, base_ref, half_ref,
):
    row_table = row_ref[...]
    lane_table = lane_ref[...]

    def body(a, carry):
        at = pl.ds(pl.multiple_of(a * 8, 8), 8)
        at_mass = pl.ds(pl.multiple_of(a * 8 + 32, 8), 8)
        radial_g = merged(left_ref[a], right_ref[a])
        radial_m = merged(left_ref[a + 4], right_ref[a + 4])
        for pair in range(4):
            spans = [slice(16 * pair + 8 * n, 16 * pair + 8 * n + 8) for n in range(2)]
            fields = []
            for n, s in enumerate(spans):
                b = 2 * pair + n
                g = s_ref[at, s, :].reshape(64, 128) + unpacked(radial_g, b)
                m = s_ref[at_mass, s, :].reshape(64, 128) + unpacked(radial_m, b)
                scale = time_step / m
                scalar = scalar_ref[at, s, :].reshape(64, 128)
                first = scalar - scale * g
                base_ref[at, s, :] = (0.5 * (scalar + first)).reshape(8, 8, 128)
                half_ref[at, s, :] = (0.5 * scale).reshape(8, 8, 128)
                fields.append(first)
            slopes = convect_pair(fields, row_table, lane_table)
            for s, (axial, azimuth, radius) in zip(spans, slopes):
                v = [velocity_ref[n, at, s, :].reshape(64, 128) for n in range(3)]
                mass = mass_ref[at, s, :].reshape(64, 128)
                g = mass * (v[0] * axial + v[1] * azimuth + v[2] * radius)
                g_ref[at, s, :] = join_lanes(g).reshape(8, 8, 128)
        return carry

    lax.fori_loop(0, 4, body, 0)
    join_local(g_ref, 1)
    axial_faces(g_ref, x_ref, 1)


def weight_kernel(weight_ref, out_ref):
    row = lax.broadcasted_iota(jnp.int32, (512, 512), 0)
    col = lax.broadcasted_iota(jnp.int32, (512, 512), 1)
    source = (row & 63) * 8 + (row >> 6)
    order = jnp.where(col == source, 1.0, 0.0).astype(BF16)
    for m in range(8):
        out_ref[m] = jnp.dot(order, weight_ref[m], preferred_element_type=F32).astype(BF16)


def render_kernel(
    g_ref, left_ref, right_ref, base_ref, half_ref, weight_ref, cut_ref, block_ref,
    advected_ref, payload_ref, turned_ref, element_ref,
):
    def body(a, carry):
        at = pl.ds(pl.multiple_of(a * 8, 8), 8)
        radial = merged(left_ref[a], right_ref[a])
        for pair in range(4):
            blocks = []
            for n in range(2):
                b = 2 * pair + n
                s = slice(8 * b, 8 * b + 8)
                g = g_ref[at, s, :].reshape(64, 128) + unpacked(radial, b)
                advected = base_ref[at, s, :].reshape(64, 128) - half_ref[at, s, :].reshape(
                    64, 128
                ) * g
                advected_ref[at, s, :] = advected.reshape(8, 8, 128)
                blocks.append(advected.astype(BF16).astype(F32))
            p = 4 * a + pair
            turned_ref[p] = jnp.concatenate(blocks, axis=0).T
            low_half = lane_ids((16, 128)) < 64
            top = pl.ds(pl.multiple_of(p * 32, 32), 16)
            bottom = pl.ds(pl.multiple_of(p * 32 + 16, 16), 16)
            for k in range(0, 8, 2):
                even = turned_ref[p, pl.ds(k, 16, stride=8), :]
                odd = turned_ref[p, pl.ds(k + 1, 16, stride=8), :]
                columns = slice(64 * k, 64 * k + 128)
                element_ref[top, columns] = jnp.where(
                    low_half, even, pltpu.roll(odd, 64, 1)
                ).astype(BF16)
                element_ref[bottom, columns] = jnp.where(
                    low_half, pltpu.roll(even, 64, 1), odd
                ).astype(BF16)
        return carry

    lax.fori_loop(0, 4, body, 0)
    cut = cut_ref[...].astype(F32).T
    lane = lane_ids((128, 512))
    blocks = block_ref[...]
    sub = lax.broadcasted_iota(jnp.int32, (16, 128), 0)
    for m in range(8):
        onehot = jnp.where(lane == cut[:, m : m + 1].astype(jnp.int32), 1.0, 0.0).astype(BF16)
        picked = jnp.dot(onehot, element_ref[...], preferred_element_type=F32).astype(BF16)
        values = jnp.dot(picked, weight_ref[m], preferred_element_type=F32)
        payload_ref[m // 2, m % 2, :128, :] = values.astype(BF16)
        ids = blocks[m : m + 1, :]
        tail = jnp.where(sub == 0, ids >> 5, jnp.where(sub == 1, ids & 31, 0))
        payload_ref[m // 2, m % 2, 128:, :] = tail.astype(F32).astype(BF16)


def image_kernel(payload_ref, image_ref):
    sources = payload_ref.shape[0]
    for m in range(2):
        ids, values = [], []
        for d in range(sources):
            tail = payload_ref[d, m, 128:, :].astype(F32).astype(jnp.int32)
            ids.append(tail[0:1, :] * 32 + tail[1:2, :])
            values.append(payload_ref[d, m, :128, :])
        ids = jnp.concatenate(ids, axis=1)
        values = jnp.concatenate(values, axis=0)
        for chunk in range(4):
            row = lax.broadcasted_iota(jnp.int32, (256, 128 * sources), 0) + 256 * chunk
            onehot = jnp.where(row == ids, 1.0, 0.0).astype(BF16)
            image_ref[m, 256 * chunk : 256 * chunk + 256, :] = jnp.dot(
                onehot, values, preferred_element_type=F32
            )


def call(kernel, out_shape, flops=10**7, size=10**6, **options):
    return pl.pallas_call(
        kernel,
        out_shape=out_shape,
        compiler_params=pltpu.CompilerParams(vmem_limit_bytes=24 * 2**20),
        cost_estimate=pl.CostEstimate(flops=flops, bytes_accessed=size, transcendentals=0),
        **options,
    )


def shape_of(*shape, dtype=F32):
    return jax.ShapeDtypeStruct(shape, dtype)


def ring(axis, wrap):
    count = lax.axis_size(axis)
    up = [(i, (i + 1) % count) for i in range(count if wrap else count - 1)]
    return up, [(j, i) for i, j in up]


def exchange(s, x, count):
    up, down = ring("ex", True)
    if lax.axis_size("ex") == 2:
        received = lax.ppermute(x, "ex", up)
    else:
        received = jnp.stack([lax.ppermute(x[0], "ex", up), lax.ppermute(x[1], "ex", down)])
    rows = 32 * count
    s, to_up, to_down = call(
        functools.partial(axial_kernel, count),
        (shape_of(*s.shape), shape_of(rows, 128), shape_of(rows, 128)),
        input_output_aliases={0: 0},
    )(s, received)
    up, down = ring("ey", True)
    first = lax.ppermute(to_up, "ey", up)
    last = lax.ppermute(to_down, "ey", down)
    s, z = call(
        functools.partial(azimuth_kernel, count),
        (shape_of(*s.shape), shape_of(4 * count, 8, 128)),
        input_output_aliases={0: 0},
    )(s, first, last)
    up, down = ring("cam", False)
    return s, lax.ppermute(z, "cam", up), lax.ppermute(z, "cam", down)


def per_device(scalar, velocity, lumped_mass, pixel_weights, cut_element, pixel_block):
    shape = scalar.shape
    flat = (32, 64, 128)
    scalar = scalar.reshape(flat)
    velocity = velocity.reshape((3,) + flat)
    mass = lumped_mass.reshape(flat)
    row_table, lane_table = derivative_tables()
    n_cam = lax.axis_size("cam")

    weights = call(weight_kernel, shape_of(8, 512, 128, dtype=BF16))(pixel_weights)
    s, x = call(first_kernel, (shape_of(64, 64, 128), shape_of(2, 2, 64, 128)))(
        scalar, velocity, mass, row_table, lane_table
    )
    s, left, right = exchange(s, x, 2)
    g, x, base, half = call(
        second_kernel,
        (shape_of(*flat), shape_of(2, 1, 64, 128), shape_of(*flat), shape_of(*flat)),
    )(s, left, right, scalar, velocity, mass, row_table, lane_table)
    g, left, right = exchange(g, x, 1)
    advected, payload = call(
        render_kernel,
        (shape_of(*flat), shape_of(n_cam, 2, 144, 128, dtype=BF16)),
        scratch_shapes=[pltpu.VMEM((16, 128, 128), F32), pltpu.VMEM((512, 512), BF16)],
    )(g, left, right, base, half, weights, cut_element, pixel_block)
    payload = lax.all_to_all(payload, "cam", 0, 0)
    images = call(image_kernel, shape_of(2, NBLK, 128))(payload)
    return (advected.reshape(shape), images)


def solution(mesh):
    placed = (
        P("ex", None, "ey", None, "cam"),
        P(None, "ex", None, "ey", None, "cam"),
        P("ex", None, "ey", None, "cam"),
        P(),
        P(None, ("cam", "ex", "ey")),
        P(None, ("cam", "ex", "ey")),
    )
    return jax.shard_map(
        per_device,
        mesh=mesh,
        in_specs=placed,
        out_specs=(P("ex", None, "ey", None, "cam"), P("cam", ("ex", "ey"), None)),
        check_vma=False,
    )
```

```python
import functools

import jax
import jax.numpy as jnp
import numpy as np
from jax import lax
from jax.experimental import pallas as pl
from jax.experimental.pallas import tpu as pltpu
from jax.sharding import PartitionSpec as P

NBLK = 1024
F32 = jnp.float32
BF16 = jnp.bfloat16
VMEM = pl.BlockSpec(memory_space=pltpu.VMEM)
HBM = pl.BlockSpec(memory_space=pltpu.HBM)
time_step = 0.01


def legendre_seven(points):
    previous = points * 0.0 + 1.0
    current = points * 1.0
    for order in range(1, 7):
        following = ((2 * order + 1) * points * current - order * previous) / (order + 1)
        previous = current
        current = following
    return current


def gll_derivative():
    degree = 7
    gll_nodes = np.array(
        [
            -1.0,
            -0.8717401485096066,
            -0.5917001814331423,
            -0.2092992179024789,
            0.2092992179024789,
            0.5917001814331423,
            0.8717401485096066,
            1.0,
        ]
    )
    values = legendre_seven(gll_nodes)
    derivative = np.zeros((degree + 1, degree + 1))
    for target in range(degree + 1):
        for source in range(degree + 1):
            if target != source:
                derivative[target, source] = values[target] / (
                    values[source] * (gll_nodes[target] - gll_nodes[source])
                )
    derivative[0, 0] = -degree * (degree + 1) / 4.0
    derivative[degree, degree] = degree * (degree + 1) / 4.0
    return derivative


def split_two(table):
    high = table.astype(np.float32).astype(BF16)
    low = (table - high.astype(np.float64)).astype(np.float32).astype(BF16)
    return high, low


def derivative_tables():
    derivative = gll_derivative()
    eye = np.eye(8)
    rows = np.concatenate([np.kron(derivative, eye), np.kron(eye, derivative)], axis=0)
    high, low = split_two(rows)
    row_table = np.concatenate([high, high, low, np.zeros_like(high)], axis=1)
    high, low = split_two(np.kron(np.eye(16), derivative.T))
    lane_table = np.concatenate(
        [
            np.concatenate([high, low], axis=1),
            np.concatenate([high, np.zeros_like(high)], axis=1),
        ],
        axis=0,
    )
    swap = np.zeros((128, 128))
    for c in range(15):
        swap[8 * c + 7, 8 * c + 8] = 1.0
        swap[8 * c + 8, 8 * c + 7] = 1.0
    join_table = np.concatenate([swap, swap], axis=0).astype(np.float32).astype(BF16)
    split = [row_table[:, :128], row_table[:, 128:], lane_table[:, :128], lane_table[:, 128:]]
    return jnp.asarray(np.concatenate(split + [join_table], axis=0))


def row_table(table_ref, first=0):
    high, low = table_ref[first:128], table_ref[128 + first : 256]
    return jnp.concatenate([high, low[:, :64]], axis=1)


def lane_table(table_ref):
    return jnp.concatenate([table_ref[256:512], table_ref[512:768]], axis=1)


def join_table(table_ref):
    return table_ref[768:1024]


def lane_ids(shape):
    return lax.broadcasted_iota(jnp.int32, shape, len(shape) - 1)


def row_ids(shape):
    return lax.broadcasted_iota(jnp.int32, shape, len(shape) - 2)


def halves(value):
    high = value.astype(BF16)
    return high, (value - high.astype(F32)).astype(BF16)


def dot(a, b):
    return jnp.dot(a, b, preferred_element_type=F32)


def by_lanes(pairs, table_ref):
    rows = jnp.concatenate([jnp.concatenate(p, axis=1) for p in pairs], axis=0)
    both = dot(rows, lane_table(table_ref))
    return both[:, :128] + both[:, 128:]


def join_lanes(values, table_ref):
    rows = jnp.concatenate([jnp.concatenate(halves(v), axis=1) for v in values], axis=0)
    other = dot(rows, join_table(table_ref))
    out, at = [], 0
    for v in values:
        out.append(v + other[at : at + v.shape[0]])
        at += v.shape[0]
    return out


def join_rows(value):
    row = row_ids(value.shape)
    last = ((row & 7) == 7) & (row != 63)
    first = ((row & 7) == 0) & (row != 0)
    other = jnp.where(
        last, pltpu.roll(value, 63, 0), jnp.where(first, pltpu.roll(value, 1, 0), 0.0)
    )
    return value + other


def convect_pair(fields, velocities, masses, table_ref):
    pairs = [halves(f) for f in fields]
    high = jnp.concatenate([p[0] for p in pairs], axis=1)
    low = jnp.concatenate([p[1] for p in pairs], axis=1)
    stacked = jnp.concatenate([high, low, high], axis=0)
    rows = dot(row_table(table_ref), stacked)
    radius = by_lanes(pairs, table_ref)
    out = []
    for n in range(2):
        lanes = slice(128 * n, 128 * n + 128)
        v = velocities[n]
        slope = v[0] * rows[:64, lanes] + v[1] * rows[64:, lanes]
        out.append(masses[n] * (slope + v[2] * radius[64 * n : 64 * n + 64]))
    return out


def face_kernel(
    scalar_hbm, velocity_hbm, mass_hbm, table_hbm, x_ref, table_ref, f_ref, v_ref, m_ref, sems,
):
    copies = []

    def start(source, target):
        copy = pltpu.make_async_copy(source, target, sems.at[len(copies)])
        copy.start()
        copies.append(copy)

    last = scalar_hbm.shape[0] - 1
    start(scalar_hbm.at[pl.ds(last - 7, 8)], f_ref.at[0])
    start(scalar_hbm.at[pl.ds(0, 8)], f_ref.at[1])
    start(velocity_hbm.at[:, last], v_ref.at[0])
    start(velocity_hbm.at[:, 0], v_ref.at[1])
    start(mass_hbm.at[last], m_ref.at[0])
    start(mass_hbm.at[0], m_ref.at[1])
    start(table_hbm, table_ref)
    for copy in copies:
        copy.wait()
    derivative = gll_derivative()
    fields = [f_ref[0, 7], f_ref[1, 0]]
    pairs = [halves(f) for f in fields]
    high = jnp.concatenate([p[0] for p in pairs], axis=1)
    low = jnp.concatenate([p[1] for p in pairs], axis=1)
    azimuth = dot(row_table(table_ref, 64), jnp.concatenate([high, low, high], axis=0))
    radius = by_lanes(pairs, table_ref)
    values = []
    for n, node in enumerate((7, 0)):
        axial = f_ref[n, 0] * float(derivative[node, 0])
        for p in range(1, 8):
            axial = axial + f_ref[n, p] * float(derivative[node, p])
        slope = v_ref[n, 0] * axial + v_ref[n, 1] * azimuth[:, 128 * n : 128 * n + 128]
        values.append(m_ref[n] * (slope + v_ref[n, 2] * radius[64 * n : 64 * n + 64]))
        values.append(m_ref[n])
    for n, value in enumerate(join_lanes(values, table_ref)):
        x_ref[n // 2, n % 2] = join_rows(value)


def join_block(s_ref):
    for b in range(s_ref.shape[1] // 8 - 1):
        total = s_ref[:, 8 * b + 7, :] + s_ref[:, 8 * b + 8, :]
        s_ref[:, 8 * b + 7, :] = total
        s_ref[:, 8 * b + 8, :] = total
    join_axial(s_ref)


def join_axial(s_ref):
    for f in range(s_ref.shape[0] // 32):
        for a in range(3):
            at = 32 * f + 8 * a + 7
            total = s_ref[at] + s_ref[at + 1]
            s_ref[at] = total
            s_ref[at + 1] = total


def pack_blocks(blocks):
    slot = ((lane_ids((8, 128)) + 1) >> 1) & 63
    parts = [jnp.zeros((8, 128), F32) for _ in range(4)]
    for n, (u, block) in enumerate(blocks):
        if u:
            block = pltpu.roll(block, 2 * u, 1)
        parts[n % 4] = jnp.where(slot == u, block, parts[n % 4])
    return (parts[0] + parts[1]) + (parts[2] + parts[3])


def pack_all(s_ref, z_ref):
    def body(q, carry):
        z_ref[q] = pack_blocks(
            [
                (56 - 8 * i + b, s_ref[8 * q + i, 8 * b : 8 * b + 8, :])
                for i in range(8)
                for b in range(8)
            ]
        )
        return carry

    lax.fori_loop(0, z_ref.shape[0], body, 0)


def first_kernel(
    scalar_hbm, velocity_hbm, mass_hbm, table_ref,
    s_ref, z_ref, scalar_ref, velocity_ref, mass_ref, sems,
):
    def copies(a):
        at = pl.ds(pl.multiple_of(a * 8, 8), 8)
        return [
            pltpu.make_async_copy(scalar_hbm.at[at], scalar_ref.at[at], sems.at[0, a]),
            pltpu.make_async_copy(velocity_hbm.at[:, at], velocity_ref.at[:, at], sems.at[1, a]),
            pltpu.make_async_copy(mass_hbm.at[at], mass_ref.at[at], sems.at[2, a]),
        ]

    for a in range(4):
        for copy in copies(a):
            copy.start()

    def body(a, carry):
        for copy in copies(a):
            copy.wait()
        at = pl.ds(pl.multiple_of(a * 8, 8), 8)
        at_mass = pl.ds(pl.multiple_of(a * 8 + 32, 8), 8)
        for pair in range(4):
            spans = [slice(16 * pair + 8 * n, 16 * pair + 8 * n + 8) for n in range(2)]
            fields = [scalar_ref[at, s, :].reshape(64, 128) for s in spans]
            velocities = [
                [velocity_ref[d, at, s, :].reshape(64, 128) for d in range(3)] for s in spans
            ]
            masses = [mass_ref[at, s, :].reshape(64, 128) for s in spans]
            values = convect_pair(fields, velocities, masses, table_ref)
            joined = join_lanes(values + masses, table_ref)
            for n, s in enumerate(spans):
                s_ref[at, s, :] = joined[n].reshape(8, 8, 128)
                s_ref[at_mass, s, :] = joined[n + 2].reshape(8, 8, 128)
        return carry

    lax.fori_loop(0, 4, body, 0)
    join_block(s_ref)
    pack_all(s_ref, z_ref)


def pack_kernel(s_ref, z_ref):
    pack_all(s_ref, z_ref)


def radial_kernel(count, z_in, x_ref, z_ref):
    for f in range(count):
        spans = [slice(8 * b, 8 * b + 8) for b in range(8)]
        z_ref[4 * f] = z_in[4 * f] + pack_blocks(
            [(56 + b, x_ref[0, f, s, :]) for b, s in enumerate(spans)]
        )
        z_ref[4 * f + 1] = z_in[4 * f + 1]
        z_ref[4 * f + 2] = z_in[4 * f + 2]
        z_ref[4 * f + 3] = z_in[4 * f + 3] + pack_blocks(
            [(b, x_ref[1, f, s, :]) for b, s in enumerate(spans)]
        )


def merged(one, two, cam_count):
    me = lax.axis_index("cam")
    even = (me & 1) == 0
    left = jnp.where(even, two, one)
    right = jnp.where(even, one, two)
    left = jnp.where(me == 0, 0.0, left)
    right = jnp.where(me == cam_count - 1, 0.0, right)
    lane = lane_ids((8, 128))
    return jnp.where((lane & 1) == 0, pltpu.roll(left, 1, 1), pltpu.roll(right, 127, 1))


def end_lanes(shape):
    lane = lane_ids(shape)
    return (lane == 0) | (lane == 127)


def azimuth_kernel(cam_count, s_ref, x_ref, one_ref, two_ref, even_ref, odd_ref):
    ends = end_lanes((8, 128))
    row = row_ids((8, 128))
    even = (lax.axis_index("ey") & 1) == 0
    for q in range(one_ref.shape[0]):
        packed = merged(one_ref[q], two_ref[q], cam_count)
        f, a = q // 4, q % 4
        at = slice(8 * q, 8 * q + 8)
        faces = []
        for line, shift in ((0, 16), (63, 2)):
            j = line & 7
            spread = jnp.broadcast_to(packed[j : j + 1, :], (8, 128))
            moved = pltpu.roll(spread, shift, 1, stride=16, stride_axis=0)
            face = s_ref[at, line, :] + jnp.where(ends, moved, 0.0)
            if a == 0:
                face = face + jnp.where(row == 0, x_ref[0, f, line : line + 1, :], 0.0)
            if a == 3:
                face = face + jnp.where(row == 7, x_ref[1, f, line : line + 1, :], 0.0)
            faces.append(face)
        even_ref[at, :] = jnp.where(even, faces[1], faces[0])
        odd_ref[at, :] = jnp.where(even, faces[0], faces[1])


def unpacked(packed, b):
    ends = end_lanes((8, 128))
    rows = []
    for i in range(8):
        u = 56 - 8 * i + b
        moved = pltpu.roll(packed, (128 - 2 * u) % 128, 1) if u else packed
        rows.append(jnp.where(ends, moved, 0.0))
    return rows


def assembled(s_ref, x_ref, packed, f, a, b, y_refs=None):
    span = slice(8 * b, 8 * b + 8)
    rows = unpacked(packed, b)
    rows[0] = rows[0] + jnp.where(a == 0, x_ref[0, f, span, :], 0.0)
    rows[7] = rows[7] + jnp.where(a == 3, x_ref[1, f, span, :], 0.0)
    block = s_ref[pl.ds(pl.multiple_of(a * 8 + 32 * f, 8), 8), span, :]
    if y_refs is not None:
        one_ref, two_ref = y_refs
        at = pl.ds(pl.multiple_of(a * 8 + 32 * f, 8), 8)
        even = (lax.axis_index("ey") & 1) == 0
        if b == 0:
            line, sublane = jnp.where(even, two_ref[at, :], one_ref[at, :]), 0
        else:
            line, sublane = jnp.where(even, one_ref[at, :], two_ref[at, :]), 7
        node = lax.broadcasted_iota(jnp.int32, (8, 8, 128), 1)
        block = block + jnp.where(node == sublane, line[:, None, :], 0.0)
    return block.reshape(64, 128) + jnp.concatenate(rows, axis=0)


def second_pairs(
    cam_count, pairs, s_ref, x_ref, one_ref, two_ref, y_refs, scalar_ref, velocity_ref, mass_ref,
    table_ref, g_ref, base_ref, half_ref,
):
    def body(a, carry):
        at = pl.ds(pl.multiple_of(a * 8, 8), 8)
        radial_g = merged(one_ref[a], two_ref[a], cam_count)
        radial_m = merged(one_ref[a + 4], two_ref[a + 4], cam_count)
        for n, pair in enumerate(pairs):
            fields, velocities, masses = [], [], []
            for h, b in enumerate(pair):
                s = slice(8 * b, 8 * b + 8)
                out = slice(16 * n + 8 * h, 16 * n + 8 * h + 8)
                g = assembled(s_ref, x_ref, radial_g, 0, a, b, y_refs)
                m = assembled(s_ref, x_ref, radial_m, 1, a, b, y_refs)
                scale = time_step / m
                scalar = scalar_ref[at, s, :].reshape(64, 128)
                first = scalar - scale * g
                base_ref[at, out, :] = (0.5 * (scalar + first)).reshape(8, 8, 128)
                half_ref[at, out, :] = (0.5 * scale).reshape(8, 8, 128)
                fields.append(first)
                velocities.append(
                    [velocity_ref[d, at, s, :].reshape(64, 128) for d in range(3)]
                )
                masses.append(mass_ref[at, s, :].reshape(64, 128))
            values = convect_pair(fields, velocities, masses, table_ref)
            joined = join_lanes(values, table_ref)
            for h in range(2):
                out = slice(16 * n + 8 * h, 16 * n + 8 * h + 8)
                g_ref[at, out, :] = joined[h].reshape(8, 8, 128)
        return carry

    lax.fori_loop(0, 4, body, 0)


def second_inner_kernel(
    cam_count, s_ref, x_ref, one_ref, two_ref, scalar_ref, velocity_ref, mass_ref,
    table_ref, g_ref, base_ref, half_ref,
):
    second_pairs(
        cam_count, ((1, 2), (3, 4), (5, 6)), s_ref, x_ref, one_ref, two_ref, None,
        scalar_ref, velocity_ref, mass_ref, table_ref, g_ref, base_ref, half_ref,
    )
    join_block(g_ref)


def second_outer_kernel(
    cam_count, s_ref, x_ref, one_ref, two_ref, y_one_ref, y_two_ref, scalar_ref, velocity_ref,
    mass_ref, table_ref, inner_ref, g_ref, x_out_ref, base_ref, half_ref, edge_ref,
):
    second_pairs(
        cam_count, ((0, 7),), s_ref, x_ref, one_ref, two_ref, (y_one_ref, y_two_ref),
        scalar_ref, velocity_ref, mass_ref, table_ref, edge_ref, base_ref, half_ref,
    )
    join_axial(edge_ref)
    g_ref[:, 0:8, :] = edge_ref[:, 0:8, :]
    g_ref[:, 8:56, :] = inner_ref[...]
    g_ref[:, 56:64, :] = edge_ref[:, 8:16, :]
    for low in (7, 55):
        total = g_ref[:, low, :] + g_ref[:, low + 1, :]
        g_ref[:, low, :] = total
        g_ref[:, low + 1, :] = total
    x_out_ref[0, 0] = g_ref[31]
    x_out_ref[1, 0] = g_ref[0]


def weight_kernel(weight_ref, out_ref):
    row = row_ids((512, 512))
    source = (row & 63) * 8 + (row >> 6)
    order = jnp.where(lane_ids((512, 512)) == source, 1.0, 0.0).astype(BF16)
    for m in range(8):
        out_ref[:, 128 * m : 128 * m + 128] = dot(order, weight_ref[m]).astype(BF16)


def pick_kernel(cut_ref, pick_ref):
    cut = cut_ref[...]
    a, b, c = cut >> 7, (cut >> 4) & 7, cut & 15
    inner = 96 * a + 16 * (b - 1) + c
    outer = 384 + 32 * a + jnp.where(b == 7, 16, 0) + c
    place = jnp.where((b == 0) | (b == 7), outer, inner)
    turned = place.astype(F32).T.astype(jnp.int32)
    lane = lane_ids((128, 512))
    for m in range(8):
        pick_ref[m] = jnp.where(lane == turned[:, m : m + 1], 1.0, 0.0).astype(BF16)


def advance(
    cam_count, pairs, g_ref, x_ref, one_ref, two_ref, y_refs, base_ref, half_ref,
    advected_ref, turned_ref, element_ref,
):
    def body(a, carry):
        at = pl.ds(pl.multiple_of(a * 8, 8), 8)
        radial = merged(one_ref[a], two_ref[a], cam_count)
        for n, pair in enumerate(pairs):
            blocks = []
            for h, b in enumerate(pair):
                g = assembled(g_ref, x_ref, radial, 0, a, b, y_refs)
                out = slice(16 * n + 8 * h, 16 * n + 8 * h + 8)
                base = base_ref[at, out, :].reshape(64, 128)
                half = half_ref[at, out, :].reshape(64, 128)
                advected = base - half * g
                advected_ref[at, out, :] = advected.reshape(8, 8, 128)
                blocks.append(advected.astype(BF16).astype(F32))
            p = len(pairs) * a + n
            turned_ref[p] = jnp.concatenate(blocks, axis=0).T
            low_half = lane_ids((16, 128)) < 64
            top = pl.ds(pl.multiple_of(p * 32, 32), 16)
            bottom = pl.ds(pl.multiple_of(p * 32 + 16, 16), 16)
            for k in range(0, 8, 2):
                even = turned_ref[p, pl.ds(k, 16, stride=8), :]
                odd = turned_ref[p, pl.ds(k + 1, 16, stride=8), :]
                columns = slice(64 * k, 64 * k + 128)
                element_ref[top, columns] = jnp.where(
                    low_half, even, pltpu.roll(odd, 64, 1)
                ).astype(BF16)
                element_ref[bottom, columns] = jnp.where(
                    low_half, pltpu.roll(even, 64, 1), odd
                ).astype(BF16)
        return carry

    lax.fori_loop(0, 4, body, 0)


def render_inner_kernel(
    cam_count, g_ref, x_ref, one_ref, two_ref, base_ref, half_ref, weight_ref, pick_ref,
    out_hbm, pixel_ref, advected_ref, turned_ref, element_ref, sem,
):
    advance(
        cam_count, ((1, 2), (3, 4), (5, 6)), g_ref, x_ref, one_ref, two_ref, None,
        base_ref, half_ref, advected_ref, turned_ref, element_ref,
    )
    copy = pltpu.make_async_copy(advected_ref, out_hbm.at[:, pl.ds(8, 48)], sem)
    copy.start()
    for m in range(8):
        values = dot(element_ref[...], weight_ref[:, 128 * m : 128 * m + 128]).astype(BF16)
        pixel_ref[m] = dot(pick_ref[m, :, :384], values)
    copy.wait()


def render_outer_kernel(
    cam_count, g_ref, x_ref, one_ref, two_ref, y_one_ref, y_two_ref, base_ref, half_ref,
    weight_ref, pick_ref, pixel_ref, block_ref, out_in,
    out_hbm, *rest,
):
    payload_refs = rest[:cam_count]
    advected_ref, turned_ref, element_ref, value_ref, sems = rest[cam_count:]
    advance(
        cam_count, ((0, 7),), g_ref, x_ref, one_ref, two_ref, (y_one_ref, y_two_ref),
        base_ref, half_ref, advected_ref, turned_ref, element_ref,
    )
    copies = [
        pltpu.make_async_copy(
            advected_ref.at[:, pl.ds(8 * n, 8)], out_hbm.at[:, pl.ds(56 * n, 8)], sems.at[n]
        )
        for n in range(2)
    ]
    for copy in copies:
        copy.start()
    cameras = pixel_ref.shape[0]
    for m in range(cameras):
        value_ref[m] = dot(element_ref[...], weight_ref[:, 128 * m : 128 * m + 128]).astype(BF16)
    me = lax.axis_index("cam")
    share = cameras // cam_count
    sub = row_ids((16, 128))
    for d in range(cam_count):
        for n in range(share):
            m = share * (me ^ d) + n
            values = dot(pick_ref[m, :, 384:], value_ref[m]) + pixel_ref[m]
            payload_refs[d][n, :128, :] = values.astype(BF16)
            ids = block_ref[pl.ds(m, 1), :]
            tail = jnp.where(sub == 0, ids >> 5, jnp.where(sub == 1, ids & 31, 0))
            payload_refs[d][n, 128:, :] = tail.astype(F32).astype(BF16)
    for copy in copies:
        copy.wait()


def image_kernel(*refs):
    payload_refs, (image_hbm, image_ref, sems) = refs[:-3], refs[-3:]
    copies = []
    for m in range(image_ref.shape[0]):
        ids, values = [], []
        for payload_ref in payload_refs:
            tail = payload_ref[m, 128:, :].astype(F32).astype(jnp.int32)
            ids.append(tail[0:1, :] * 32 + tail[1:2, :])
            values.append(payload_ref[m, :128, :])
        ids = jnp.concatenate(ids, axis=1)
        values = jnp.concatenate(values, axis=0)
        for chunk in range(4):
            at = slice(256 * chunk, 256 * chunk + 256)
            row = row_ids((256, ids.shape[1])) + 256 * chunk
            onehot = jnp.where(row == ids, 1.0, 0.0).astype(BF16)
            image_ref[m, at, :] = dot(onehot, values)
            copy = pltpu.make_async_copy(
                image_ref.at[m, at], image_hbm.at[m, at], sems.at[4 * m + chunk]
            )
            copy.start()
            copies.append(copy)
    for copy in copies:
        copy.wait()


def call(kernel, out_shape, flops=10**8, size=10**7, **options):
    return pl.pallas_call(
        kernel,
        out_shape=out_shape,
        compiler_params=pltpu.CompilerParams(vmem_limit_bytes=24 * 2**20),
        cost_estimate=pl.CostEstimate(flops=flops, bytes_accessed=size, transcendentals=0),
        **options,
    )


def shape_of(*shape, dtype=F32):
    return jax.ShapeDtypeStruct(shape, dtype)


def stay(*arrays):
    return [pltpu.with_memory_space_constraint(x, pltpu.HBM) for x in arrays]


def swaps(axis):
    count = lax.axis_size(axis)
    even = [(i, i ^ 1) for i in range(count)]
    odd = [(i, (i + 1) % count if i & 1 else (i - 1) % count) for i in range(count)]
    return even, odd


def swap_axial(x):
    count = lax.axis_size("ex")
    up = [(i, (i + 1) % count) for i in range(count)]
    if count == 2:
        return lax.ppermute(x, "ex", up)
    down = [(j, i) for i, j in up]
    return jnp.stack([lax.ppermute(x[0], "ex", up), lax.ppermute(x[1], "ex", down)])


def swap_both(one, two, axis):
    even, odd = swaps(axis)
    return lax.ppermute(one, axis, even), lax.ppermute(two, axis, odd)


def per_device(scalar, velocity, lumped_mass, pixel_weights, cut_element, pixel_block):
    shape = scalar.shape
    flat = (32, 64, 128)
    inner, outer = (32, 48, 128), (32, 16, 128)
    scalar = scalar.reshape(flat)
    velocity = velocity.reshape((3,) + flat)
    mass = lumped_mass.reshape(flat)
    tables = derivative_tables()
    n_cam = lax.axis_size("cam")
    cameras = pixel_weights.shape[0]
    share = cameras // n_cam
    part = functools.partial

    x, near = call(
        face_kernel,
        (shape_of(2, 2, 64, 128), shape_of(*tables.shape, dtype=BF16)),
        in_specs=[HBM] * 4,
        scratch_shapes=[
            pltpu.VMEM((2, 8, 64, 128), F32),
            pltpu.VMEM((2, 3, 64, 128), F32),
            pltpu.VMEM((2, 64, 128), F32),
            pltpu.SemaphoreType.DMA((7,)),
        ],
    )(*stay(scalar, velocity, mass, tables))
    x_got = swap_axial(x)
    s, z, scalar, velocity, mass = call(
        first_kernel,
        (shape_of(64, 64, 128), shape_of(8, 8, 128))
        + (shape_of(*flat), shape_of(3, *flat), shape_of(*flat)),
        in_specs=[HBM] * 3 + [VMEM],
        scratch_shapes=[pltpu.SemaphoreType.DMA((3, 4))],
    )(*stay(scalar, velocity, mass), near)
    weights = call(weight_kernel, shape_of(512, 128 * cameras, dtype=BF16))(pixel_weights)
    picks = call(pick_kernel, shape_of(cameras, 128, 512, dtype=BF16))(cut_element)

    z = call(part(radial_kernel, 2), shape_of(8, 8, 128))(z, x_got)
    z_got = swap_both(z, z, "cam")
    y = call(part(azimuth_kernel, n_cam), (shape_of(64, 128), shape_of(64, 128)))(s, x_got, *z_got)
    y_got = swap_both(*y, "ey")
    g_inner, *inner_terms = call(
        part(second_inner_kernel, n_cam), (shape_of(*inner),) * 3
    )(s, x_got, *z_got, scalar, velocity, mass, near)
    g, x, *outer_terms = call(
        part(second_outer_kernel, n_cam),
        (shape_of(*flat), shape_of(2, 1, 64, 128), shape_of(*outer), shape_of(*outer)),
        scratch_shapes=[pltpu.VMEM(outer, F32)],
    )(s, x_got, *z_got, *y_got, scalar, velocity, mass, near, g_inner)

    x_got = swap_axial(x)
    z = call(pack_kernel, shape_of(4, 8, 128))(g)
    z = call(part(radial_kernel, 1), shape_of(4, 8, 128))(z, x_got)
    z_got = swap_both(z, z, "cam")
    y = call(part(azimuth_kernel, n_cam), (shape_of(32, 128), shape_of(32, 128)))(g, x_got, *z_got)
    y_got = swap_both(*y, "ey")
    advected, pixels = call(
        part(render_inner_kernel, n_cam),
        (shape_of(*flat), shape_of(cameras, 128, 128)),
        out_specs=(HBM, VMEM),
        scratch_shapes=[
            pltpu.VMEM(inner, F32),
            pltpu.VMEM((12, 128, 128), F32),
            pltpu.VMEM((384, 512), BF16),
            pltpu.SemaphoreType.DMA,
        ],
    )(g, x_got, *z_got, *inner_terms, weights, picks)
    payload_shape = shape_of(share, 144, 128, dtype=BF16)
    advected, *payloads = call(
        part(render_outer_kernel, n_cam),
        (shape_of(*flat),) + (payload_shape,) * n_cam,
        in_specs=[VMEM] * 12 + [HBM],
        out_specs=(HBM,) + (VMEM,) * n_cam,
        input_output_aliases={12: 0},
        scratch_shapes=[
            pltpu.VMEM(outer, F32),
            pltpu.VMEM((4, 128, 128), F32),
            pltpu.VMEM((128, 512), BF16),
            pltpu.VMEM((cameras, 128, 128), BF16),
            pltpu.SemaphoreType.DMA((2,)),
        ],
    )(g, x_got, *z_got, *y_got, *outer_terms, weights, picks, pixels, pixel_block, advected)
    received = [payloads[0]]
    for d in range(1, n_cam):
        received.append(lax.ppermute(payloads[d], "cam", [(i, i ^ d) for i in range(n_cam)]))
    images = call(
        image_kernel,
        shape_of(share, NBLK, 128),
        out_specs=HBM,
        scratch_shapes=[
            pltpu.VMEM((share, NBLK, 128), F32),
            pltpu.SemaphoreType.DMA((4 * share,)),
        ],
    )(*received)
    return (advected.reshape(shape), images)


def solution(mesh):
    placed = (
        P("ex", None, "ey", None, "cam"),
        P(None, "ex", None, "ey", None, "cam"),
        P("ex", None, "ey", None, "cam"),
        P(),
        P(None, ("cam", "ex", "ey")),
        P(None, ("cam", "ex", "ey")),
    )
    return jax.shard_map(
        per_device,
        mesh=mesh,
        in_specs=placed,
        out_specs=(P("ex", None, "ey", None, "cam"), P("cam", ("ex", "ey"), None)),
        check_vma=False,
    )
```

```python
import functools

import jax
import jax.numpy as jnp
import numpy as np
from jax import lax
from jax.experimental import pallas as pl
from jax.experimental.pallas import tpu as pltpu
from jax.sharding import PartitionSpec as P

NBLK = 1024
F32 = jnp.float32
BF16 = jnp.bfloat16
VMEM = pl.BlockSpec(memory_space=pltpu.VMEM)
HBM = pl.BlockSpec(memory_space=pltpu.HBM)
time_step = 0.01


def legendre_seven(points):
    previous = points * 0.0 + 1.0
    current = points * 1.0
    for order in range(1, 7):
        following = ((2 * order + 1) * points * current - order * previous) / (order + 1)
        previous = current
        current = following
    return current


def gll_derivative():
    degree = 7
    gll_nodes = np.array(
        [
            -1.0,
            -0.8717401485096066,
            -0.5917001814331423,
            -0.2092992179024789,
            0.2092992179024789,
            0.5917001814331423,
            0.8717401485096066,
            1.0,
        ]
    )
    values = legendre_seven(gll_nodes)
    derivative = np.zeros((degree + 1, degree + 1))
    for target in range(degree + 1):
        for source in range(degree + 1):
            if target != source:
                derivative[target, source] = values[target] / (
                    values[source] * (gll_nodes[target] - gll_nodes[source])
                )
    derivative[0, 0] = -degree * (degree + 1) / 4.0
    derivative[degree, degree] = degree * (degree + 1) / 4.0
    return derivative


def split_two(table):
    high = table.astype(np.float32).astype(BF16)
    low = (table - high.astype(np.float64)).astype(np.float32).astype(BF16)
    return high, low


def derivative_tables():
    derivative = gll_derivative()
    eye = np.eye(8)
    rows = np.concatenate([np.kron(derivative, eye), np.kron(eye, derivative)], axis=0)
    high, low = split_two(rows)
    row_table = np.concatenate([high, high, low, np.zeros_like(high)], axis=1)
    high, low = split_two(np.kron(np.eye(16), derivative.T))
    lane_table = np.concatenate(
        [
            np.concatenate([high, low], axis=1),
            np.concatenate([high, np.zeros_like(high)], axis=1),
        ],
        axis=0,
    )
    swap = np.zeros((128, 128))
    for c in range(15):
        swap[8 * c + 7, 8 * c + 8] = 1.0
        swap[8 * c + 8, 8 * c + 7] = 1.0
    join_table = np.concatenate([swap, swap], axis=0).astype(np.float32).astype(BF16)
    spread = np.zeros((128, 128))
    spread[0, 0::2] = 1.0
    spread[127, 1::2] = 1.0
    turn = np.zeros((64, 256))
    for k in range(4):
        for c in range(16):
            turn[16 * k + c, 8 * c + 2 * k] = 1.0
            turn[16 * k + c, 128 + 8 * c + 2 * k + 1] = 1.0
    exact = np.concatenate([spread, spread, turn[:, :128], turn[:, 128:]], axis=0)
    split = [row_table[:, :128], row_table[:, 128:], lane_table[:, :128], lane_table[:, 128:]]
    split += [join_table, exact.astype(np.float32).astype(BF16)]
    return jnp.asarray(np.concatenate(split, axis=0))


def row_table(table_ref, first=0):
    high, low = table_ref[first:128], table_ref[128 + first : 256]
    return jnp.concatenate([high, low[:, :64]], axis=1)


def lane_table(table_ref):
    return jnp.concatenate([table_ref[256:512], table_ref[512:768]], axis=1)


def join_table(table_ref):
    return jnp.concatenate([table_ref[768:1024], table_ref[1024:1280]], axis=1)


def turn_table(table_ref):
    return jnp.concatenate([table_ref[1280:1344], table_ref[1344:1408]], axis=1)


def span_of(a, offset=0):
    if isinstance(a, int):
        return slice(8 * a + offset, 8 * a + offset + 8)
    return pl.ds(pl.multiple_of(a * 8 + offset, 8), 8)


def sweep(body, together):
    if together == 4:
        for a in range(4):
            body(a)
        return

    def step(n, carry):
        for m in range(together):
            body(n * together + m)
        return carry

    lax.fori_loop(0, 4 // together, step, 0)


def lane_ids(shape):
    return lax.broadcasted_iota(jnp.int32, shape, len(shape) - 1)


def row_ids(shape):
    return lax.broadcasted_iota(jnp.int32, shape, len(shape) - 2)


def halves(value):
    high = value.astype(BF16)
    return high, (value - high.astype(F32)).astype(BF16)


def dot(a, b):
    return jnp.dot(a, b, preferred_element_type=F32)


def by_lanes(pairs, table_ref):
    rows = jnp.concatenate([jnp.concatenate(p, axis=1) for p in pairs], axis=0)
    both = dot(rows, lane_table(table_ref))
    return both[:, :128] + both[:, 128:]


def join_lanes(values, table_ref):
    rows = jnp.concatenate([jnp.concatenate(halves(v), axis=1) for v in values], axis=0)
    other = dot(rows, join_table(table_ref))
    joined, spread, at = [], [], 0
    for v in values:
        span = slice(at, at + v.shape[0])
        joined.append(v + other[span, :128])
        spread.append(other[span, 128:])
        at += v.shape[0]
    return joined, spread


def join_rows(value):
    row = row_ids(value.shape)
    last = ((row & 7) == 7) & (row != 63)
    first = ((row & 7) == 0) & (row != 0)
    other = jnp.where(
        last, pltpu.roll(value, 63, 0), jnp.where(first, pltpu.roll(value, 1, 0), 0.0)
    )
    return value + other


def convect_pair(fields, velocities, masses, table_ref):
    pairs = [halves(f) for f in fields]
    high = jnp.concatenate([p[0] for p in pairs], axis=1)
    low = jnp.concatenate([p[1] for p in pairs], axis=1)
    stacked = jnp.concatenate([high, low, high], axis=0)
    rows = dot(row_table(table_ref), stacked)
    radius = by_lanes(pairs, table_ref)
    out = []
    for n in range(2):
        lanes = slice(128 * n, 128 * n + 128)
        v = velocities[n]
        slope = v[0] * rows[:64, lanes] + v[1] * rows[64:, lanes]
        out.append(masses[n] * (slope + v[2] * radius[64 * n : 64 * n + 64]))
    return out


def face_kernel(
    scalar_hbm, velocity_hbm, mass_hbm, table_hbm, x_ref, table_ref, f_ref, v_ref, m_ref, sems,
):
    copies = []

    def start(source, target):
        copy = pltpu.make_async_copy(source, target, sems.at[len(copies)])
        copy.start()
        copies.append(copy)

    last = scalar_hbm.shape[0] - 1
    start(scalar_hbm.at[pl.ds(last - 7, 8)], f_ref.at[0])
    start(scalar_hbm.at[pl.ds(0, 8)], f_ref.at[1])
    start(velocity_hbm.at[:, last], v_ref.at[0])
    start(velocity_hbm.at[:, 0], v_ref.at[1])
    start(mass_hbm.at[last], m_ref.at[0])
    start(mass_hbm.at[0], m_ref.at[1])
    start(table_hbm, table_ref)
    for copy in copies:
        copy.wait()
    derivative = gll_derivative()
    fields = [f_ref[0, 7], f_ref[1, 0]]
    pairs = [halves(f) for f in fields]
    high = jnp.concatenate([p[0] for p in pairs], axis=1)
    low = jnp.concatenate([p[1] for p in pairs], axis=1)
    azimuth = dot(row_table(table_ref, 64), jnp.concatenate([high, low, high], axis=0))
    radius = by_lanes(pairs, table_ref)
    values = []
    for n, node in enumerate((7, 0)):
        axial = f_ref[n, 0] * float(derivative[node, 0])
        for p in range(1, 8):
            axial = axial + f_ref[n, p] * float(derivative[node, p])
        slope = v_ref[n, 0] * axial + v_ref[n, 1] * azimuth[:, 128 * n : 128 * n + 128]
        values.append(m_ref[n] * (slope + v_ref[n, 2] * radius[64 * n : 64 * n + 64]))
        values.append(m_ref[n])
    for n, value in enumerate(join_lanes(values, table_ref)[0]):
        x_ref[n // 2, n % 2] = join_rows(value)


def join_block(s_ref):
    for b in range(s_ref.shape[1] // 8 - 1):
        total = s_ref[:, 8 * b + 7, :] + s_ref[:, 8 * b + 8, :]
        s_ref[:, 8 * b + 7, :] = total
        s_ref[:, 8 * b + 8, :] = total
    join_axial(s_ref)


def join_axial(s_ref):
    for f in range(s_ref.shape[0] // 32):
        for a in range(3):
            at = 32 * f + 8 * a + 7
            total = s_ref[at] + s_ref[at + 1]
            s_ref[at] = total
            s_ref[at + 1] = total


def pack_blocks(blocks):
    slot = ((lane_ids((8, 128)) + 1) >> 1) & 63
    parts = [jnp.zeros((8, 128), F32) for _ in range(4)]
    for n, (u, block) in enumerate(blocks):
        if u:
            block = pltpu.roll(block, 2 * u, 1)
        parts[n % 4] = jnp.where(slot == u, block, parts[n % 4])
    return (parts[0] + parts[1]) + (parts[2] + parts[3])


def pick_spread(spreads):
    slot = ((lane_ids((8, 128)) + 1) >> 1) & 63
    parts = [jnp.zeros((8, 128), F32) for _ in range(2)]
    for b, spread in spreads:
        for i in range(8):
            block = spread[8 * i : 8 * i + 8]
            parts[i % 2] = jnp.where(slot == 56 - 8 * i + b, block, parts[i % 2])
    return parts[0] + parts[1]


def join_packed(packed):
    lane, row = lane_ids((8, 128)), row_ids((8, 128))
    slot = ((lane + 1) >> 1) & 63
    b = slot & 7
    rows = []
    for value in packed:
        after = pltpu.roll(pltpu.roll(value, 126, 1), 7, 0)
        before = pltpu.roll(pltpu.roll(value, 2, 1), 1, 0)
        value = value + jnp.where((row == 7) & (b < 7), after, 0.0)
        rows.append(value + jnp.where((row == 0) & (b > 0), before, 0.0))
    out = list(rows)
    for a in range(3):
        out[a] = out[a] + jnp.where(slot < 8, pltpu.roll(rows[a + 1], 16, 1), 0.0)
        out[a + 1] = out[a + 1] + jnp.where(slot >= 56, pltpu.roll(rows[a], 112, 1), 0.0)
    return out


def first_kernel(scalar_ref, velocity_ref, mass_ref, table_ref, s_ref, z_ref):
    def body(a):
        at = span_of(a)
        spreads = [[], []]
        for pair in range(4):
            spans = [slice(16 * pair + 8 * n, 16 * pair + 8 * n + 8) for n in range(2)]
            fields = [scalar_ref[at, s, :].reshape(64, 128) for s in spans]
            velocities = [
                [velocity_ref[d, at, s, :].reshape(64, 128) for d in range(3)] for s in spans
            ]
            masses = [mass_ref[at, s, :].reshape(64, 128) for s in spans]
            values = convect_pair(fields, velocities, masses, table_ref)
            joined, spread = join_lanes(values + masses, table_ref)
            for n, s in enumerate(spans):
                for f in range(2):
                    s_ref[span_of(a, 32 * f), s, :] = joined[n + 2 * f].reshape(8, 8, 128)
                    spreads[f].append((2 * pair + n, spread[n + 2 * f]))
        for f in range(2):
            z_ref[a + 4 * f] = pick_spread(spreads[f])

    sweep(body, 2)
    join_block(s_ref)
    for f in range(2):
        for n, value in enumerate(join_packed([z_ref[4 * f + a] for a in range(4)])):
            z_ref[4 * f + n] = value


def radial_kernel(count, z_in, x_ref, z_ref):
    for f in range(count):
        spans = [slice(8 * b, 8 * b + 8) for b in range(8)]
        z_ref[4 * f] = z_in[4 * f] + pack_blocks(
            [(56 + b, x_ref[0, f, s, :]) for b, s in enumerate(spans)]
        )
        z_ref[4 * f + 1] = z_in[4 * f + 1]
        z_ref[4 * f + 2] = z_in[4 * f + 2]
        z_ref[4 * f + 3] = z_in[4 * f + 3] + pack_blocks(
            [(b, x_ref[1, f, s, :]) for b, s in enumerate(spans)]
        )


def merged(one, two, cam_count):
    me = lax.axis_index("cam")
    even = (me & 1) == 0
    left = jnp.where(even, two, one)
    right = jnp.where(even, one, two)
    left = jnp.where(me == 0, 0.0, left)
    right = jnp.where(me == cam_count - 1, 0.0, right)
    lane = lane_ids((8, 128))
    return jnp.where((lane & 1) == 0, pltpu.roll(left, 1, 1), pltpu.roll(right, 127, 1))


def end_lanes(shape):
    lane = lane_ids(shape)
    return (lane == 0) | (lane == 127)


def azimuth_kernel(cam_count, s_ref, x_ref, one_ref, two_ref, even_ref, odd_ref):
    ends = end_lanes((8, 128))
    row = row_ids((8, 128))
    even = (lax.axis_index("ey") & 1) == 0
    for q in range(one_ref.shape[0]):
        packed = merged(one_ref[q], two_ref[q], cam_count)
        f, a = q // 4, q % 4
        at = slice(8 * q, 8 * q + 8)
        faces = []
        for line, shift in ((0, 16), (63, 2)):
            j = line & 7
            spread = jnp.broadcast_to(packed[j : j + 1, :], (8, 128))
            moved = pltpu.roll(spread, shift, 1, stride=16, stride_axis=0)
            face = s_ref[at, line, :] + jnp.where(ends, moved, 0.0)
            if a == 0:
                face = face + jnp.where(row == 0, x_ref[0, f, line : line + 1, :], 0.0)
            if a == 3:
                face = face + jnp.where(row == 7, x_ref[1, f, line : line + 1, :], 0.0)
            faces.append(face)
        even_ref[at, :] = jnp.where(even, faces[1], faces[0])
        odd_ref[at, :] = jnp.where(even, faces[0], faces[1])


def unpacked(packed, b):
    ends = end_lanes((8, 128))
    rows = []
    for i in range(8):
        u = 56 - 8 * i + b
        moved = pltpu.roll(packed, (128 - 2 * u) % 128, 1) if u else packed
        rows.append(jnp.where(ends, moved, 0.0))
    return rows


def assembled(s_ref, x_ref, packed, f, a, b, y_refs=None):
    span = slice(8 * b, 8 * b + 8)
    rows = unpacked(packed, b)
    if not isinstance(a, int):
        rows[0] = rows[0] + jnp.where(a == 0, x_ref[0, f, span, :], 0.0)
        rows[7] = rows[7] + jnp.where(a == 3, x_ref[1, f, span, :], 0.0)
    elif a == 0:
        rows[0] = rows[0] + x_ref[0, f, span, :]
    elif a == 3:
        rows[7] = rows[7] + x_ref[1, f, span, :]
    at = span_of(a, 32 * f)
    block = s_ref[at, span, :]
    if y_refs is not None:
        one_ref, two_ref = y_refs
        even = (lax.axis_index("ey") & 1) == 0
        if b == 0:
            line, sublane = jnp.where(even, two_ref[at, :], one_ref[at, :]), 0
        else:
            line, sublane = jnp.where(even, one_ref[at, :], two_ref[at, :]), 7
        node = lax.broadcasted_iota(jnp.int32, (8, 8, 128), 1)
        block = block + jnp.where(node == sublane, line[:, None, :], 0.0)
    return block.reshape(64, 128) + jnp.concatenate(rows, axis=0)


def second_pairs(
    cam_count, pairs, together, s_ref, x_ref, one_ref, two_ref, y_refs, scalar_ref, velocity_ref,
    mass_ref, table_ref, g_ref, base_ref, half_ref, z_ref,
):
    def body(a):
        at = span_of(a)
        radial_g = merged(one_ref[a], two_ref[a], cam_count)
        radial_m = merged(one_ref[a + 4], two_ref[a + 4], cam_count)
        spreads = []
        for n, pair in enumerate(pairs):
            fields, velocities, masses = [], [], []
            for h, b in enumerate(pair):
                s = slice(8 * b, 8 * b + 8)
                out = slice(16 * n + 8 * h, 16 * n + 8 * h + 8)
                g = assembled(s_ref, x_ref, radial_g, 0, a, b, y_refs)
                m = assembled(s_ref, x_ref, radial_m, 1, a, b, y_refs)
                scale = time_step / m
                scalar = scalar_ref[at, s, :].reshape(64, 128)
                first = scalar - scale * g
                base_ref[at, out, :] = (0.5 * (scalar + first)).reshape(8, 8, 128)
                half_ref[at, out, :] = (0.5 * scale).reshape(8, 8, 128)
                fields.append(first)
                velocities.append(
                    [velocity_ref[d, at, s, :].reshape(64, 128) for d in range(3)]
                )
                masses.append(mass_ref[at, s, :].reshape(64, 128))
            values = convect_pair(fields, velocities, masses, table_ref)
            joined, spread = join_lanes(values, table_ref)
            for h, b in enumerate(pair):
                out = slice(16 * n + 8 * h, 16 * n + 8 * h + 8)
                g_ref[at, out, :] = joined[h].reshape(8, 8, 128)
                spreads.append((b, spread[h]))
        z_ref[a] = pick_spread(spreads)

    sweep(body, together)


def second_inner_kernel(
    cam_count, s_ref, x_ref, one_ref, two_ref, scalar_ref, velocity_ref, mass_ref,
    table_ref, g_ref, base_ref, half_ref, z_ref,
):
    second_pairs(
        cam_count, ((1, 2), (3, 4), (5, 6)), 2, s_ref, x_ref, one_ref, two_ref, None,
        scalar_ref, velocity_ref, mass_ref, table_ref, g_ref, base_ref, half_ref, z_ref,
    )
    join_block(g_ref)


def second_outer_kernel(
    cam_count, s_ref, x_ref, one_ref, two_ref, y_one_ref, y_two_ref, scalar_ref, velocity_ref,
    mass_ref, table_ref, inner_ref, z_in, g_ref, x_out_ref, base_ref, half_ref, z_ref, edge_ref,
):
    second_pairs(
        cam_count, ((0, 7),), 4, s_ref, x_ref, one_ref, two_ref, (y_one_ref, y_two_ref),
        scalar_ref, velocity_ref, mass_ref, table_ref, edge_ref, base_ref, half_ref, z_ref,
    )
    join_axial(edge_ref)
    g_ref[:, 0:8, :] = edge_ref[:, 0:8, :]
    g_ref[:, 8:56, :] = inner_ref[...]
    g_ref[:, 56:64, :] = edge_ref[:, 8:16, :]
    for low in (7, 55):
        total = g_ref[:, low, :] + g_ref[:, low + 1, :]
        g_ref[:, low, :] = total
        g_ref[:, low + 1, :] = total
    x_out_ref[0, 0] = g_ref[31]
    x_out_ref[1, 0] = g_ref[0]
    for n, value in enumerate(join_packed([z_ref[a] + z_in[a] for a in range(4)])):
        z_ref[n] = value


def weight_kernel(weight_ref, out_ref):
    row = row_ids((512, 512))
    source = (row & 63) * 8 + (row >> 6)
    order = jnp.where(lane_ids((512, 512)) == source, 1.0, 0.0).astype(BF16)
    for m in range(8):
        out_ref[:, 128 * m : 128 * m + 128] = dot(order, weight_ref[m]).astype(BF16)


def pick_kernel(cut_ref, pick_ref):
    cut = cut_ref[...]
    a, b, c = cut >> 7, (cut >> 4) & 7, cut & 15
    inner = 96 * a + 16 * (b - 1) + c
    outer = 384 + 32 * a + jnp.where(b == 7, 16, 0) + c
    place = jnp.where((b == 0) | (b == 7), outer, inner)
    turned = place.astype(F32).T.astype(jnp.int32)
    lane = lane_ids((128, 512))
    for m in range(8):
        pick_ref[m] = jnp.where(lane == turned[:, m : m + 1], 1.0, 0.0).astype(BF16)


def advance(
    cam_count, pairs, together, g_ref, x_ref, one_ref, two_ref, y_refs, base_ref, half_ref,
    table_ref, advected_ref, element_ref,
):
    def body(a):
        at = span_of(a)
        radial = merged(one_ref[a], two_ref[a], cam_count)
        for n, pair in enumerate(pairs):
            blocks = []
            for h, b in enumerate(pair):
                g = assembled(g_ref, x_ref, radial, 0, a, b, y_refs)
                out = slice(16 * n + 8 * h, 16 * n + 8 * h + 8)
                base = base_ref[at, out, :].reshape(64, 128)
                half = half_ref[at, out, :].reshape(64, 128)
                advected = base - half * g
                advected_ref[at, out, :] = advected.reshape(8, 8, 128)
                value = advected.astype(BF16)
                zero = jnp.zeros_like(value)
                blocks.append(jnp.concatenate([value, zero], axis=1))
                blocks.append(jnp.concatenate([zero, value], axis=1))
            turned = lax.dot_general(
                turn_table(table_ref),
                jnp.concatenate(blocks, axis=0),
                (((1,), (1,)), ((), ())),
                preferred_element_type=F32,
            ).astype(BF16)
            for h in range(2):
                place = 32 * (len(pairs) * a + n) + 16 * h
                if not isinstance(a, int):
                    place = pl.multiple_of(place, 16)
                for k in range(4):
                    element_ref[pl.ds(place, 16), 128 * k : 128 * k + 128] = turned[
                        16 * k : 16 * k + 16, 128 * h : 128 * h + 128
                    ]

    sweep(body, together)


def render_inner_kernel(
    cam_count, g_ref, x_ref, one_ref, two_ref, base_ref, half_ref, table_ref, weight_ref, pick_ref,
    out_hbm, pixel_ref, advected_ref, element_ref, sem,
):
    advance(
        cam_count, ((1, 2), (3, 4), (5, 6)), 2, g_ref, x_ref, one_ref, two_ref, None,
        base_ref, half_ref, table_ref, advected_ref, element_ref,
    )
    copy = pltpu.make_async_copy(advected_ref, out_hbm.at[:, pl.ds(8, 48)], sem)
    copy.start()
    for m in range(8):
        values = dot(element_ref[...], weight_ref[:, 128 * m : 128 * m + 128]).astype(BF16)
        pixel_ref[m] = dot(pick_ref[m, :, :384], values)
    copy.wait()


def render_outer_kernel(
    cam_count, g_ref, x_ref, one_ref, two_ref, y_one_ref, y_two_ref, base_ref, half_ref,
    table_ref, weight_ref, pick_ref, pixel_ref, block_ref, out_in,
    out_hbm, *rest,
):
    payload_refs = rest[:cam_count]
    advected_ref, element_ref, value_ref, sems = rest[cam_count:]
    advance(
        cam_count, ((0, 7),), 4, g_ref, x_ref, one_ref, two_ref, (y_one_ref, y_two_ref),
        base_ref, half_ref, table_ref, advected_ref, element_ref,
    )
    copies = [
        pltpu.make_async_copy(
            advected_ref.at[:, pl.ds(8 * n, 8)], out_hbm.at[:, pl.ds(56 * n, 8)], sems.at[n]
        )
        for n in range(2)
    ]
    for copy in copies:
        copy.start()
    cameras = pixel_ref.shape[0]
    for m in range(cameras):
        value_ref[m] = dot(element_ref[...], weight_ref[:, 128 * m : 128 * m + 128]).astype(BF16)
    me = lax.axis_index("cam")
    share = cameras // cam_count
    sub = row_ids((16, 128))
    for d in range(cam_count):
        for n in range(share):
            m = share * (me ^ d) + n
            values = dot(pick_ref[m, :, 384:], value_ref[m]) + pixel_ref[m]
            payload_refs[d][n, :128, :] = values.astype(BF16)
            ids = block_ref[pl.ds(m, 1), :]
            tail = jnp.where(sub == 0, ids >> 5, jnp.where(sub == 1, ids & 31, 0))
            payload_refs[d][n, 128:, :] = tail.astype(F32).astype(BF16)
    for copy in copies:
        copy.wait()


def scatter(payload_refs, m, chunk):
    ids, values = [], []
    for payload_ref in payload_refs:
        tail = payload_ref[m, 128:, :].astype(F32).astype(jnp.int32)
        ids.append(tail[0:1, :] * 32 + tail[1:2, :])
        values.append(payload_ref[m, :128, :])
    ids = jnp.concatenate(ids, axis=1)
    row = row_ids((256, ids.shape[1])) + 256 * chunk
    onehot = jnp.where(row == ids, 1.0, 0.0).astype(BF16)
    return dot(onehot, jnp.concatenate(values, axis=0))


def near_image_kernel(*refs):
    payload_refs, image_ref = refs[:-1], refs[-1]
    for m in range(image_ref.shape[0]):
        for chunk in range(4):
            at = slice(256 * chunk, 256 * chunk + 256)
            image_ref[m, at, :] = scatter(payload_refs, m, chunk)


def far_image_kernel(near_ref, *refs):
    payload_refs, (image_hbm, image_ref, sems) = refs[:-3], refs[-3:]
    copies = []
    for m in range(image_ref.shape[0]):
        for chunk in range(4):
            at = slice(256 * chunk, 256 * chunk + 256)
            image_ref[m, at, :] = near_ref[m, at, :] + scatter(payload_refs, m, chunk)
            copy = pltpu.make_async_copy(
                image_ref.at[m, at], image_hbm.at[m, at], sems.at[4 * m + chunk]
            )
            copy.start()
            copies.append(copy)
    for copy in copies:
        copy.wait()


def call(kernel, out_shape, flops=10**8, size=10**7, **options):
    return pl.pallas_call(
        kernel,
        out_shape=out_shape,
        compiler_params=pltpu.CompilerParams(vmem_limit_bytes=24 * 2**20),
        cost_estimate=pl.CostEstimate(flops=flops, bytes_accessed=size, transcendentals=0),
        **options,
    )


def shape_of(*shape, dtype=F32):
    return jax.ShapeDtypeStruct(shape, dtype)


def stay(*arrays):
    return [pltpu.with_memory_space_constraint(x, pltpu.HBM) for x in arrays]


def swaps(axis):
    count = lax.axis_size(axis)
    even = [(i, i ^ 1) for i in range(count)]
    odd = [(i, (i + 1) % count if i & 1 else (i - 1) % count) for i in range(count)]
    return even, odd


def swap_axial(x):
    count = lax.axis_size("ex")
    up = [(i, (i + 1) % count) for i in range(count)]
    if count == 2:
        return lax.ppermute(x, "ex", up)
    down = [(j, i) for i, j in up]
    return jnp.stack([lax.ppermute(x[0], "ex", up), lax.ppermute(x[1], "ex", down)])


def swap_both(one, two, axis):
    even, odd = swaps(axis)
    return lax.ppermute(one, axis, even), lax.ppermute(two, axis, odd)


def per_device(scalar, velocity, lumped_mass, pixel_weights, cut_element, pixel_block):
    shape = scalar.shape
    flat = (32, 64, 128)
    inner, outer = (32, 48, 128), (32, 16, 128)
    scalar = scalar.reshape(flat)
    velocity = velocity.reshape((3,) + flat)
    mass = lumped_mass.reshape(flat)
    tables = derivative_tables()
    n_cam = lax.axis_size("cam")
    cameras = pixel_weights.shape[0]
    share = cameras // n_cam
    part = functools.partial

    x, near = call(
        face_kernel,
        (shape_of(2, 2, 64, 128), shape_of(*tables.shape, dtype=BF16)),
        in_specs=[HBM] * 4,
        scratch_shapes=[
            pltpu.VMEM((2, 8, 64, 128), F32),
            pltpu.VMEM((2, 3, 64, 128), F32),
            pltpu.VMEM((2, 64, 128), F32),
            pltpu.SemaphoreType.DMA((7,)),
        ],
    )(*stay(scalar, velocity, mass, tables))
    x_got = swap_axial(x)
    s, z = call(first_kernel, (shape_of(64, 64, 128), shape_of(8, 8, 128)))(
        scalar, velocity, mass, near
    )
    weights = call(weight_kernel, shape_of(512, 128 * cameras, dtype=BF16))(pixel_weights)
    picks = call(pick_kernel, shape_of(cameras, 128, 512, dtype=BF16))(cut_element)

    z = call(part(radial_kernel, 2), shape_of(8, 8, 128))(z, x_got)
    z_got = swap_both(z, z, "cam")
    y = call(part(azimuth_kernel, n_cam), (shape_of(64, 128), shape_of(64, 128)))(s, x_got, *z_got)
    y_got = swap_both(*y, "ey")
    g_inner, *inner_terms, z_inner = call(
        part(second_inner_kernel, n_cam), (shape_of(*inner),) * 3 + (shape_of(4, 8, 128),)
    )(s, x_got, *z_got, scalar, velocity, mass, near)
    g, x, *outer_terms, z = call(
        part(second_outer_kernel, n_cam),
        (shape_of(*flat), shape_of(2, 1, 64, 128), shape_of(*outer), shape_of(*outer))
        + (shape_of(4, 8, 128),),
        scratch_shapes=[pltpu.VMEM(outer, F32)],
    )(s, x_got, *z_got, *y_got, scalar, velocity, mass, near, g_inner, z_inner)

    x_got = swap_axial(x)
    z = call(part(radial_kernel, 1), shape_of(4, 8, 128))(z, x_got)
    z_got = swap_both(z, z, "cam")
    y = call(part(azimuth_kernel, n_cam), (shape_of(32, 128), shape_of(32, 128)))(g, x_got, *z_got)
    y_got = swap_both(*y, "ey")
    advected, pixels = call(
        part(render_inner_kernel, n_cam),
        (shape_of(*flat), shape_of(cameras, 128, 128)),
        out_specs=(HBM, VMEM),
        scratch_shapes=[
            pltpu.VMEM(inner, F32),
            pltpu.VMEM((384, 512), BF16),
            pltpu.SemaphoreType.DMA,
        ],
    )(g, x_got, *z_got, *inner_terms, near, weights, picks)
    payload_shape = shape_of(share, 144, 128, dtype=BF16)
    advected, *payloads = call(
        part(render_outer_kernel, n_cam),
        (shape_of(*flat),) + (payload_shape,) * n_cam,
        in_specs=[VMEM] * 13 + [HBM],
        out_specs=(HBM,) + (VMEM,) * n_cam,
        input_output_aliases={13: 0},
        scratch_shapes=[
            pltpu.VMEM(outer, F32),
            pltpu.VMEM((128, 512), BF16),
            pltpu.VMEM((cameras, 128, 128), BF16),
            pltpu.SemaphoreType.DMA((2,)),
        ],
    )(g, x_got, *z_got, *y_got, *outer_terms, near, weights, picks, pixels, pixel_block, advected)
    received = {0: payloads[0]}
    for d in reversed(range(1, n_cam)):
        received[d] = lax.ppermute(payloads[d], "cam", [(i, i ^ d) for i in range(n_cam)])
    image_shape = shape_of(share, NBLK, 128)
    images = call(near_image_kernel, image_shape)(received[0], received[1])
    images = call(
        far_image_kernel,
        image_shape,
        out_specs=HBM,
        scratch_shapes=[
            pltpu.VMEM((share, NBLK, 128), F32),
            pltpu.SemaphoreType.DMA((4 * share,)),
        ],
    )(images, *[received[d] for d in range(2, n_cam)])
    return (advected.reshape(shape), images)


def solution(mesh):
    placed = (
        P("ex", None, "ey", None, "cam"),
        P(None, "ex", None, "ey", None, "cam"),
        P("ex", None, "ey", None, "cam"),
        P(),
        P(None, ("cam", "ex", "ey")),
        P(None, ("cam", "ex", "ey")),
    )
    return jax.shard_map(
        per_device,
        mesh=mesh,
        in_specs=placed,
        out_specs=(P("ex", None, "ey", None, "cam"), P("cam", ("ex", "ey"), None)),
        check_vma=False,
    )
```

```python
import functools

import jax
import jax.numpy as jnp
import numpy as np
from jax import lax
from jax.experimental import pallas as pl
from jax.experimental.pallas import tpu as pltpu
from jax.sharding import PartitionSpec as P

NBLK = 1024
F32 = jnp.float32
BF16 = jnp.bfloat16
VMEM = pl.BlockSpec(memory_space=pltpu.VMEM)
HBM = pl.BlockSpec(memory_space=pltpu.HBM)
time_step = 0.01


def legendre_seven(points):
    previous = points * 0.0 + 1.0
    current = points * 1.0
    for order in range(1, 7):
        following = ((2 * order + 1) * points * current - order * previous) / (order + 1)
        previous = current
        current = following
    return current


def gll_derivative():
    degree = 7
    gll_nodes = np.array(
        [
            -1.0,
            -0.8717401485096066,
            -0.5917001814331423,
            -0.2092992179024789,
            0.2092992179024789,
            0.5917001814331423,
            0.8717401485096066,
            1.0,
        ]
    )
    values = legendre_seven(gll_nodes)
    derivative = np.zeros((degree + 1, degree + 1))
    for target in range(degree + 1):
        for source in range(degree + 1):
            if target != source:
                derivative[target, source] = values[target] / (
                    values[source] * (gll_nodes[target] - gll_nodes[source])
                )
    derivative[0, 0] = -degree * (degree + 1) / 4.0
    derivative[degree, degree] = degree * (degree + 1) / 4.0
    return derivative


def split_two(table):
    high = table.astype(np.float32).astype(BF16)
    low = (table - high.astype(np.float64)).astype(np.float32).astype(BF16)
    return high, low


def derivative_tables():
    derivative = gll_derivative()
    eye = np.eye(8)
    rows = np.concatenate([np.kron(derivative, eye), np.kron(eye, derivative)], axis=0)
    high, low = split_two(rows)
    row_table = np.concatenate([high, high, low, np.zeros_like(high)], axis=1)
    high, low = split_two(np.kron(np.eye(16), derivative.T))
    lane_table = np.concatenate(
        [
            np.concatenate([high, low], axis=1),
            np.concatenate([high, np.zeros_like(high)], axis=1),
        ],
        axis=0,
    )
    swap = np.zeros((128, 128))
    for c in range(15):
        swap[8 * c + 7, 8 * c + 8] = 1.0
        swap[8 * c + 8, 8 * c + 7] = 1.0
    join_table = np.concatenate([swap, swap], axis=0).astype(np.float32).astype(BF16)
    spread = np.zeros((128, 128))
    spread[0, 0::2] = 1.0
    spread[127, 1::2] = 1.0
    turn = np.zeros((64, 256))
    for k in range(4):
        for c in range(16):
            turn[16 * k + c, 8 * c + 2 * k] = 1.0
            turn[16 * k + c, 128 + 8 * c + 2 * k + 1] = 1.0
    ends = turn.reshape(4, 16, 256)[:, ::15].reshape(8, 256)
    ends = np.concatenate([ends, np.zeros_like(ends)], axis=0)
    exact = [spread, spread, turn[:, :128], turn[:, 128:], ends[:, :128], ends[:, 128:]]
    exact = np.concatenate(exact, axis=0)
    split = [row_table[:, :128], row_table[:, 128:], lane_table[:, :128], lane_table[:, 128:]]
    split += [join_table, exact.astype(np.float32).astype(BF16)]
    return jnp.asarray(np.concatenate(split, axis=0))


def row_table(table_ref, first=0):
    high, low = table_ref[first:128], table_ref[128 + first : 256]
    return jnp.concatenate([high, low[:, :64]], axis=1)


def lane_table(table_ref):
    return jnp.concatenate([table_ref[256:512], table_ref[512:768]], axis=1)


def join_table(table_ref):
    return jnp.concatenate([table_ref[768:1024], table_ref[1024:1280]], axis=1)


def turn_table(table_ref):
    return jnp.concatenate([table_ref[1280:1344], table_ref[1344:1408]], axis=1)


def end_table(table_ref):
    return jnp.concatenate([table_ref[1408:1424], table_ref[1424:1440]], axis=1)


def span_of(a, offset=0):
    if isinstance(a, int):
        return slice(8 * a + offset, 8 * a + offset + 8)
    return pl.ds(pl.multiple_of(a * 8 + offset, 8), 8)


def sweep(body, together):
    if together == 4:
        for a in range(4):
            body(a)
        return

    def step(n, carry):
        for m in range(together):
            body(n * together + m)
        return carry

    lax.fori_loop(0, 4 // together, step, 0)


def lane_ids(shape):
    return lax.broadcasted_iota(jnp.int32, shape, len(shape) - 1)


def row_ids(shape):
    return lax.broadcasted_iota(jnp.int32, shape, len(shape) - 2)


def halves(value):
    high = value.astype(BF16)
    return high, (value - high.astype(F32)).astype(BF16)


def dot(a, b):
    return jnp.dot(a, b, preferred_element_type=F32)


def by_lanes(pairs, table_ref):
    rows = jnp.concatenate([jnp.concatenate(p, axis=1) for p in pairs], axis=0)
    both = dot(rows, lane_table(table_ref))
    return both[:, :128] + both[:, 128:]


def join_lanes(values, table_ref):
    rows = jnp.concatenate([jnp.concatenate(halves(v), axis=1) for v in values], axis=0)
    other = dot(rows, join_table(table_ref))
    joined, spread, at = [], [], 0
    for v in values:
        span = slice(at, at + v.shape[0])
        joined.append(v + other[span, :128])
        spread.append(other[span, 128:])
        at += v.shape[0]
    return joined, spread


def join_rows(value):
    row = row_ids(value.shape)
    last = ((row & 7) == 7) & (row != 63)
    first = ((row & 7) == 0) & (row != 0)
    other = jnp.where(
        last, pltpu.roll(value, 63, 0), jnp.where(first, pltpu.roll(value, 1, 0), 0.0)
    )
    return value + other


def convect_pair(fields, velocities, masses, table_ref):
    pairs = [halves(f) for f in fields]
    high = jnp.concatenate([p[0] for p in pairs], axis=1)
    low = jnp.concatenate([p[1] for p in pairs], axis=1)
    stacked = jnp.concatenate([high, low, high], axis=0)
    rows = dot(row_table(table_ref), stacked)
    radius = by_lanes(pairs, table_ref)
    out = []
    for n in range(2):
        lanes = slice(128 * n, 128 * n + 128)
        v = velocities[n]
        slope = v[0] * rows[:64, lanes] + v[1] * rows[64:, lanes]
        out.append(masses[n] * (slope + v[2] * radius[64 * n : 64 * n + 64]))
    return out


def face_kernel(
    scalar_hbm, velocity_hbm, mass_hbm, table_hbm, x_ref, table_ref, f_ref, v_ref, m_ref, sems,
):
    copies = []

    def start(source, target):
        copy = pltpu.make_async_copy(source, target, sems.at[len(copies)])
        copy.start()
        copies.append(copy)

    last = scalar_hbm.shape[0] - 1
    start(scalar_hbm.at[pl.ds(last - 7, 8)], f_ref.at[0])
    start(scalar_hbm.at[pl.ds(0, 8)], f_ref.at[1])
    start(velocity_hbm.at[:, last], v_ref.at[0])
    start(velocity_hbm.at[:, 0], v_ref.at[1])
    start(mass_hbm.at[last], m_ref.at[0])
    start(mass_hbm.at[0], m_ref.at[1])
    start(table_hbm, table_ref)
    for copy in copies:
        copy.wait()
    derivative = gll_derivative()
    fields = [f_ref[0, 7], f_ref[1, 0]]
    pairs = [halves(f) for f in fields]
    high = jnp.concatenate([p[0] for p in pairs], axis=1)
    low = jnp.concatenate([p[1] for p in pairs], axis=1)
    azimuth = dot(row_table(table_ref, 64), jnp.concatenate([high, low, high], axis=0))
    radius = by_lanes(pairs, table_ref)
    values = []
    for n, node in enumerate((7, 0)):
        axial = f_ref[n, 0] * float(derivative[node, 0])
        for p in range(1, 8):
            axial = axial + f_ref[n, p] * float(derivative[node, p])
        slope = v_ref[n, 0] * axial + v_ref[n, 1] * azimuth[:, 128 * n : 128 * n + 128]
        values.append(m_ref[n] * (slope + v_ref[n, 2] * radius[64 * n : 64 * n + 64]))
        values.append(m_ref[n])
    for n, value in enumerate(join_lanes(values, table_ref)[0]):
        x_ref[n // 2, n % 2] = join_rows(value).astype(BF16)


def join_block(s_ref):
    for b in range(s_ref.shape[1] // 8 - 1):
        total = s_ref[:, 8 * b + 7, :] + s_ref[:, 8 * b + 8, :]
        s_ref[:, 8 * b + 7, :] = total
        s_ref[:, 8 * b + 8, :] = total
    join_axial(s_ref)


def join_axial(s_ref):
    for f in range(s_ref.shape[0] // 32):
        for a in range(3):
            at = 32 * f + 8 * a + 7
            total = s_ref[at] + s_ref[at + 1]
            s_ref[at] = total
            s_ref[at + 1] = total


def pack_blocks(blocks):
    slot = ((lane_ids((8, 128)) + 1) >> 1) & 63
    parts = [jnp.zeros((8, 128), F32) for _ in range(4)]
    for n, (u, block) in enumerate(blocks):
        if u:
            block = pltpu.roll(block, 2 * u, 1)
        parts[n % 4] = jnp.where(slot == u, block, parts[n % 4])
    return (parts[0] + parts[1]) + (parts[2] + parts[3])


def pick_spread(spreads):
    slot = ((lane_ids((8, 128)) + 1) >> 1) & 63
    parts = [jnp.zeros((8, 128), F32) for _ in range(2)]
    for b, spread in spreads:
        for i in range(8):
            block = spread[8 * i : 8 * i + 8]
            parts[i % 2] = jnp.where(slot == 56 - 8 * i + b, block, parts[i % 2])
    return parts[0] + parts[1]


def join_packed(packed):
    lane, row = lane_ids((8, 128)), row_ids((8, 128))
    slot = ((lane + 1) >> 1) & 63
    b = slot & 7
    rows = []
    for value in packed:
        after = pltpu.roll(pltpu.roll(value, 126, 1), 7, 0)
        before = pltpu.roll(pltpu.roll(value, 2, 1), 1, 0)
        value = value + jnp.where((row == 7) & (b < 7), after, 0.0)
        rows.append(value + jnp.where((row == 0) & (b > 0), before, 0.0))
    out = list(rows)
    for a in range(3):
        out[a] = out[a] + jnp.where(slot < 8, pltpu.roll(rows[a + 1], 16, 1), 0.0)
        out[a + 1] = out[a + 1] + jnp.where(slot >= 56, pltpu.roll(rows[a], 112, 1), 0.0)
    return out


def first_kernel(scalar_ref, velocity_ref, mass_ref, table_ref, s_ref, z_ref):
    def body(a):
        at = span_of(a)
        spreads = [[], []]
        for pair in range(4):
            spans = [slice(16 * pair + 8 * n, 16 * pair + 8 * n + 8) for n in range(2)]
            fields = [scalar_ref[at, s, :].reshape(64, 128) for s in spans]
            velocities = [
                [velocity_ref[d, at, s, :].reshape(64, 128) for d in range(3)] for s in spans
            ]
            masses = [mass_ref[at, s, :].reshape(64, 128) for s in spans]
            values = convect_pair(fields, velocities, masses, table_ref)
            joined, spread = join_lanes(values + masses, table_ref)
            for n, s in enumerate(spans):
                for f in range(2):
                    s_ref[span_of(a, 32 * f), s, :] = joined[n + 2 * f].reshape(8, 8, 128)
                    spreads[f].append((2 * pair + n, spread[n + 2 * f]))
        for f in range(2):
            z_ref[a + 4 * f] = pick_spread(spreads[f])

    sweep(body, 2)
    join_block(s_ref)
    for f in range(2):
        for n, value in enumerate(join_packed([z_ref[4 * f + a] for a in range(4)])):
            z_ref[4 * f + n] = value


def radial_kernel(count, z_in, x_in, z_ref, x_ref):
    x_ref[...] = x_in[...].astype(F32)
    for f in range(count):
        spans = [slice(8 * b, 8 * b + 8) for b in range(8)]
        z_ref[4 * f] = z_in[4 * f] + pack_blocks(
            [(56 + b, x_ref[0, f, s, :]) for b, s in enumerate(spans)]
        )
        z_ref[4 * f + 1] = z_in[4 * f + 1]
        z_ref[4 * f + 2] = z_in[4 * f + 2]
        z_ref[4 * f + 3] = z_in[4 * f + 3] + pack_blocks(
            [(b, x_ref[1, f, s, :]) for b, s in enumerate(spans)]
        )


def merged(one, two, cam_count):
    me = lax.axis_index("cam")
    even = (me & 1) == 0
    left = jnp.where(even, two, one)
    right = jnp.where(even, one, two)
    left = jnp.where(me == 0, 0.0, left)
    right = jnp.where(me == cam_count - 1, 0.0, right)
    lane = lane_ids((8, 128))
    return jnp.where((lane & 1) == 0, pltpu.roll(left, 1, 1), pltpu.roll(right, 127, 1))


def end_lanes(shape):
    lane = lane_ids(shape)
    return (lane == 0) | (lane == 127)


def azimuth_kernel(cam_count, s_ref, x_ref, one_ref, two_ref, even_ref, odd_ref):
    ends = end_lanes((8, 128))
    row = row_ids((8, 128))
    even = (lax.axis_index("ey") & 1) == 0
    for q in range(one_ref.shape[0]):
        packed = merged(one_ref[q], two_ref[q], cam_count)
        f, a = q // 4, q % 4
        at = slice(8 * q, 8 * q + 8)
        faces = []
        for line, shift in ((0, 16), (63, 2)):
            j = line & 7
            spread = jnp.broadcast_to(packed[j : j + 1, :], (8, 128))
            moved = pltpu.roll(spread, shift, 1, stride=16, stride_axis=0)
            face = s_ref[at, line, :] + jnp.where(ends, moved, 0.0)
            if a == 0:
                face = face + jnp.where(row == 0, x_ref[0, f, line : line + 1, :], 0.0)
            if a == 3:
                face = face + jnp.where(row == 7, x_ref[1, f, line : line + 1, :], 0.0)
            faces.append(face)
        even_ref[at, :] = jnp.where(even, faces[1], faces[0])
        odd_ref[at, :] = jnp.where(even, faces[0], faces[1])


def unpacked(packed, b):
    ends = end_lanes((8, 128))
    rows = []
    for i in range(8):
        u = 56 - 8 * i + b
        moved = pltpu.roll(packed, (128 - 2 * u) % 128, 1) if u else packed
        rows.append(jnp.where(ends, moved, 0.0))
    return rows


def assembled(s_ref, x_ref, packed, f, a, b, y_refs=None):
    span = slice(8 * b, 8 * b + 8)
    at = span_of(a, 32 * f)
    block = s_ref[at, span, :]
    if packed is None:
        rows = [jnp.zeros((8, 128), F32) for _ in range(8)]
    else:
        rows = unpacked(packed, b)
    if not isinstance(a, int):
        rows[0] = rows[0] + jnp.where(a == 0, x_ref[0, f, span, :], 0.0)
        rows[7] = rows[7] + jnp.where(a == 3, x_ref[1, f, span, :], 0.0)
    elif a == 0:
        rows[0] = rows[0] + x_ref[0, f, span, :]
    elif a == 3:
        rows[7] = rows[7] + x_ref[1, f, span, :]
    if y_refs is not None:
        one_ref, two_ref = y_refs
        even = (lax.axis_index("ey") & 1) == 0
        if b == 0:
            line, sublane = jnp.where(even, two_ref[at, :], one_ref[at, :]), 0
        else:
            line, sublane = jnp.where(even, one_ref[at, :], two_ref[at, :]), 7
        node = lax.broadcasted_iota(jnp.int32, (8, 8, 128), 1)
        block = block + jnp.where(node == sublane, line[:, None, :], 0.0)
    return block.reshape(64, 128) + jnp.concatenate(rows, axis=0)


def second_pairs(
    cam_count, pairs, together, s_ref, x_ref, one_ref, two_ref, y_refs, scalar_ref, velocity_ref,
    mass_ref, table_ref, g_ref, base_ref, half_ref, z_ref,
):
    def body(a):
        at = span_of(a)
        radial_g = merged(one_ref[a], two_ref[a], cam_count)
        radial_m = merged(one_ref[a + 4], two_ref[a + 4], cam_count)
        spreads = []
        for n, pair in enumerate(pairs):
            fields, velocities, masses = [], [], []
            for h, b in enumerate(pair):
                s = slice(8 * b, 8 * b + 8)
                out = slice(16 * n + 8 * h, 16 * n + 8 * h + 8)
                g = assembled(s_ref, x_ref, radial_g, 0, a, b, y_refs)
                m = assembled(s_ref, x_ref, radial_m, 1, a, b, y_refs)
                scale = time_step / m
                scalar = scalar_ref[at, s, :].reshape(64, 128)
                first = scalar - scale * g
                base_ref[at, out, :] = (0.5 * (scalar + first)).reshape(8, 8, 128)
                half_ref[at, out, :] = (0.5 * scale).reshape(8, 8, 128)
                fields.append(first)
                velocities.append(
                    [velocity_ref[d, at, s, :].reshape(64, 128) for d in range(3)]
                )
                masses.append(mass_ref[at, s, :].reshape(64, 128))
            values = convect_pair(fields, velocities, masses, table_ref)
            joined, spread = join_lanes(values, table_ref)
            for h, b in enumerate(pair):
                out = slice(16 * n + 8 * h, 16 * n + 8 * h + 8)
                g_ref[at, out, :] = joined[h].reshape(8, 8, 128)
                spreads.append((b, spread[h]))
        z_ref[a] = pick_spread(spreads)

    sweep(body, together)


def second_inner_kernel(
    cam_count, s_ref, x_ref, one_ref, two_ref, scalar_ref, velocity_ref, mass_ref,
    table_ref, g_ref, base_ref, half_ref, z_ref,
):
    second_pairs(
        cam_count, ((1, 2), (3, 4), (5, 6)), 2, s_ref, x_ref, one_ref, two_ref, None,
        scalar_ref, velocity_ref, mass_ref, table_ref, g_ref, base_ref, half_ref, z_ref,
    )
    join_block(g_ref)


def second_outer_kernel(
    cam_count, s_ref, x_ref, one_ref, two_ref, y_one_ref, y_two_ref, scalar_ref, velocity_ref,
    mass_ref, table_ref, inner_ref, z_in, g_ref, x_out_ref, base_ref, half_ref, z_ref, edge_ref,
):
    second_pairs(
        cam_count, ((0, 7),), 4, s_ref, x_ref, one_ref, two_ref, (y_one_ref, y_two_ref),
        scalar_ref, velocity_ref, mass_ref, table_ref, edge_ref, base_ref, half_ref, z_ref,
    )
    join_axial(edge_ref)
    g_ref[:, 0:8, :] = edge_ref[:, 0:8, :]
    g_ref[:, 8:56, :] = inner_ref[...]
    g_ref[:, 56:64, :] = edge_ref[:, 8:16, :]
    for low in (7, 55):
        total = g_ref[:, low, :] + g_ref[:, low + 1, :]
        g_ref[:, low, :] = total
        g_ref[:, low + 1, :] = total
    x_out_ref[0, 0] = g_ref[31].astype(BF16)
    x_out_ref[1, 0] = g_ref[0].astype(BF16)
    for n, value in enumerate(join_packed([z_ref[a] + z_in[a] for a in range(4)])):
        z_ref[n] = value


def weight_kernel(weight_ref, out_ref):
    row = row_ids((512, 512))
    source = (row & 63) * 8 + (row >> 6)
    order = jnp.where(lane_ids((512, 512)) == source, 1.0, 0.0).astype(BF16)
    for m in range(8):
        out_ref[:, 128 * m : 128 * m + 128] = dot(order, weight_ref[m]).astype(BF16)


def pick_kernel(cut_ref, pick_ref):
    cut = cut_ref[...]
    a, b, c = cut >> 7, (cut >> 4) & 7, cut & 15
    order = jnp.where(a == 0, 2, jnp.where(a == 3, 3, a - 1))
    inner = 96 * order + 16 * (b - 1) + c
    ends = 512 + 12 * a + 2 * (b - 1) + (c >> 3)
    outer = 384 + 32 * a + jnp.where(b == 7, 16, 0) + c
    place = jnp.where((c == 0) | (c == 15), ends, inner)
    place = jnp.where((b == 0) | (b == 7), outer, place)
    turned = place.astype(F32).T.astype(jnp.int32)
    lane = lane_ids((128, 640))
    for m in range(8):
        pick_ref[m] = jnp.where(lane == turned[:, m : m + 1], 1.0, 0.0).astype(BF16)


def turn(blocks, table):
    rows = []
    for block in blocks:
        value = block.astype(BF16)
        zero = jnp.zeros_like(value)
        rows.append(jnp.concatenate([value, zero], axis=1))
        rows.append(jnp.concatenate([zero, value], axis=1))
    return lax.dot_general(
        table,
        jnp.concatenate(rows, axis=0),
        (((1,), (1,)), ((), ())),
        preferred_element_type=F32,
    )


def advanced(g_ref, x_ref, packed, y_refs, base_ref, half_ref, a, pair, place):
    blocks = []
    for h, b in enumerate(pair):
        g = assembled(g_ref, x_ref, packed, 0, a, b, y_refs)
        out = slice(place + 8 * h, place + 8 * h + 8)
        base = base_ref[span_of(a), out, :].reshape(64, 128)
        half = half_ref[span_of(a), out, :].reshape(64, 128)
        blocks.append(base - half * g)
    return blocks


def store_elements(element_ref, blocks, table_ref, place):
    turned = turn(blocks, turn_table(table_ref)).astype(BF16)
    for h in range(2):
        for k in range(4):
            element_ref[place + 16 * h : place + 16 * h + 16, 128 * k : 128 * k + 128] = turned[
                16 * k : 16 * k + 16, 128 * h : 128 * h + 128
            ]


def pixel_values(element_ref, weight_ref, m):
    return dot(element_ref[...], weight_ref[:, 256 * m : 256 * m + 256]).astype(BF16)


INNER = ((1, 2), (3, 4), (5, 6))


def inner_elements(layers, g_ref, x_ref, base_ref, half_ref, table_ref, element_ref):
    place = 0
    for a in layers:
        for n, pair in enumerate(INNER):
            blocks = advanced(g_ref, x_ref, None, None, base_ref, half_ref, a, pair, 16 * n)
            store_elements(element_ref, blocks, table_ref, place)
            place += 32


def early_kernel(g_ref, base_ref, half_ref, table_ref, weight_ref, value_ref, element_ref):
    inner_elements((1, 2), g_ref, None, base_ref, half_ref, table_ref, element_ref)
    for m in range(4):
        value_ref[:, 256 * m : 256 * m + 256] = pixel_values(element_ref, weight_ref, m)


def middle_kernel(
    g_ref, x_ref, base_ref, half_ref, table_ref, weight_ref, pick_ref, early_ref,
    pixel_ref, element_ref,
):
    inner_elements((0, 3), g_ref, x_ref, base_ref, half_ref, table_ref, element_ref)
    for m in range(4):
        late = pixel_values(element_ref, weight_ref, m)
        both = jnp.concatenate([early_ref[:, 256 * m : 256 * m + 256], late], axis=0)
        for n in range(2):
            pixel_ref[2 * m + n] = dot(
                pick_ref[2 * m + n, :, :384], both[:, 128 * n : 128 * n + 128]
            )


def render_inner_kernel(
    cam_count, g_ref, x_ref, one_ref, two_ref, base_ref, half_ref, table_ref, weight_ref, pick_ref,
    pixel_in, out_hbm, pixel_ref, advected_ref, end_ref, sem,
):
    end_ref[48:, :] = jnp.zeros((16, 512), F32)

    def body(a):
        packed = merged(one_ref[a], two_ref[a], cam_count)
        for n, pair in enumerate(INNER):
            blocks = advanced(g_ref, x_ref, packed, None, base_ref, half_ref, a, pair, 16 * n)
            for h in range(2):
                out = slice(16 * n + 8 * h, 16 * n + 8 * h + 8)
                advected_ref[span_of(a), out, :] = blocks[h].reshape(8, 8, 128)
            turned = turn(blocks, end_table(table_ref))
            for h in range(2):
                place = 12 * a + 4 * n + 2 * h
                for k in range(4):
                    end_ref[place : place + 2, 128 * k : 128 * k + 128] = turned[
                        2 * k : 2 * k + 2, 128 * h : 128 * h + 128
                    ]

    sweep(body, 4)
    copy = pltpu.make_async_copy(advected_ref, out_hbm.at[:, pl.ds(8, 48)], sem)
    copy.start()
    ends = end_ref[...].astype(BF16)
    for m in range(4):
        values = dot(ends, weight_ref[:, 256 * m : 256 * m + 256]).astype(BF16)
        for n in range(2):
            pixel_ref[2 * m + n] = pixel_in[2 * m + n] + dot(
                pick_ref[2 * m + n, :, 512:576], values[:, 128 * n : 128 * n + 128]
            )
    copy.wait()


def render_outer_kernel(
    cam_count, g_ref, x_ref, one_ref, two_ref, y_one_ref, y_two_ref, base_ref, half_ref,
    table_ref, weight_ref, pick_ref, pixel_ref, block_ref, out_in,
    out_hbm, *rest,
):
    payload_refs = rest[:cam_count]
    advected_ref, element_ref, value_ref, sems = rest[cam_count:]
    for a in range(4):
        packed = merged(one_ref[a], two_ref[a], cam_count)
        blocks = advanced(
            g_ref, x_ref, packed, (y_one_ref, y_two_ref), base_ref, half_ref, a, (0, 7), 0
        )
        for h in range(2):
            advected_ref[span_of(a), 8 * h : 8 * h + 8, :] = blocks[h].reshape(8, 8, 128)
        store_elements(element_ref, blocks, table_ref, 32 * a)
    copies = [
        pltpu.make_async_copy(
            advected_ref.at[:, pl.ds(8 * n, 8)], out_hbm.at[:, pl.ds(56 * n, 8)], sems.at[n]
        )
        for n in range(2)
    ]
    for copy in copies:
        copy.start()
    cameras = pixel_ref.shape[0]
    for m in range(cameras // 2):
        values = pixel_values(element_ref, weight_ref, m)
        value_ref[2 * m] = values[:, :128]
        value_ref[2 * m + 1] = values[:, 128:]
    me = lax.axis_index("cam")
    share = cameras // cam_count
    sub = row_ids((16, 128))
    for d in range(cam_count):
        for n in range(share):
            m = share * (me ^ d) + n
            values = dot(pick_ref[m, :, 384:512], value_ref[m]) + pixel_ref[m]
            payload_refs[d][n, :128, :] = values.astype(BF16)
            ids = block_ref[pl.ds(m, 1), :]
            tail = jnp.where(sub == 0, ids >> 5, jnp.where(sub == 1, ids & 31, 0))
            payload_refs[d][n, 128:, :] = tail.astype(F32).astype(BF16)
    for copy in copies:
        copy.wait()


def scatter(payload_refs, m, chunk):
    ids, values = [], []
    for payload_ref in payload_refs:
        tail = payload_ref[m, 128:, :].astype(F32).astype(jnp.int32)
        ids.append(tail[0:1, :] * 32 + tail[1:2, :])
        values.append(payload_ref[m, :128, :])
    ids = jnp.concatenate(ids, axis=1)
    row = row_ids((256, ids.shape[1])) + 256 * chunk
    onehot = jnp.where(row == ids, 1.0, 0.0).astype(BF16)
    return dot(onehot, jnp.concatenate(values, axis=0))


def near_image_kernel(*refs):
    payload_refs, image_ref = refs[:-1], refs[-1]
    for m in range(image_ref.shape[0]):
        for chunk in range(4):
            at = slice(256 * chunk, 256 * chunk + 256)
            image_ref[m, at, :] = scatter(payload_refs, m, chunk)


def far_image_kernel(near_ref, *refs):
    payload_refs, (image_hbm, image_ref, sems) = refs[:-3], refs[-3:]
    copies = []
    for m in range(image_ref.shape[0]):
        for chunk in range(4):
            at = slice(256 * chunk, 256 * chunk + 256)
            image_ref[m, at, :] = near_ref[m, at, :] + scatter(payload_refs, m, chunk)
            copy = pltpu.make_async_copy(
                image_ref.at[m, at], image_hbm.at[m, at], sems.at[4 * m + chunk]
            )
            copy.start()
            copies.append(copy)
    for copy in copies:
        copy.wait()


def call(kernel, out_shape, flops=10**8, size=10**7, **options):
    return pl.pallas_call(
        kernel,
        out_shape=out_shape,
        compiler_params=pltpu.CompilerParams(vmem_limit_bytes=24 * 2**20),
        cost_estimate=pl.CostEstimate(flops=flops, bytes_accessed=size, transcendentals=0),
        **options,
    )


def shape_of(*shape, dtype=F32):
    return jax.ShapeDtypeStruct(shape, dtype)


def stay(*arrays):
    return [pltpu.with_memory_space_constraint(x, pltpu.HBM) for x in arrays]


def swaps(axis):
    count = lax.axis_size(axis)
    even = [(i, i ^ 1) for i in range(count)]
    odd = [(i, (i + 1) % count if i & 1 else (i - 1) % count) for i in range(count)]
    return even, odd


def swap_axial(x):
    count = lax.axis_size("ex")
    up = [(i, (i + 1) % count) for i in range(count)]
    if count == 2:
        return lax.ppermute(x, "ex", up)
    down = [(j, i) for i, j in up]
    return jnp.stack([lax.ppermute(x[0], "ex", up), lax.ppermute(x[1], "ex", down)])


def swap_both(one, two, axis):
    even, odd = swaps(axis)
    return lax.ppermute(one, axis, even), lax.ppermute(two, axis, odd)


def per_device(scalar, velocity, lumped_mass, pixel_weights, cut_element, pixel_block):
    shape = scalar.shape
    flat = (32, 64, 128)
    inner, outer = (32, 48, 128), (32, 16, 128)
    scalar = scalar.reshape(flat)
    velocity = velocity.reshape((3,) + flat)
    mass = lumped_mass.reshape(flat)
    tables = derivative_tables()
    n_cam = lax.axis_size("cam")
    cameras = pixel_weights.shape[0]
    share = cameras // n_cam
    part = functools.partial

    x, near = call(
        face_kernel,
        (shape_of(2, 2, 64, 128, dtype=BF16), shape_of(*tables.shape, dtype=BF16)),
        in_specs=[HBM] * 4,
        scratch_shapes=[
            pltpu.VMEM((2, 8, 64, 128), F32),
            pltpu.VMEM((2, 3, 64, 128), F32),
            pltpu.VMEM((2, 64, 128), F32),
            pltpu.SemaphoreType.DMA((7,)),
        ],
    )(*stay(scalar, velocity, mass, tables))
    x_got = swap_axial(x)
    s, z = call(first_kernel, (shape_of(64, 64, 128), shape_of(8, 8, 128)))(
        scalar, velocity, mass, near
    )
    weights = call(weight_kernel, shape_of(512, 128 * cameras, dtype=BF16))(pixel_weights)
    picks = call(pick_kernel, shape_of(cameras, 128, 640, dtype=BF16))(cut_element)

    z, x_got = call(part(radial_kernel, 2), (shape_of(8, 8, 128), shape_of(2, 2, 64, 128)))(z, x_got)
    z_got = swap_both(z, z, "cam")
    z_got, weights, picks = lax.optimization_barrier((z_got, weights, picks))
    y = call(part(azimuth_kernel, n_cam), (shape_of(64, 128), shape_of(64, 128)))(s, x_got, *z_got)
    y_got = swap_both(*y, "ey")
    g_inner, *inner_terms, z_inner = call(
        part(second_inner_kernel, n_cam), (shape_of(*inner),) * 3 + (shape_of(4, 8, 128),)
    )(s, x_got, *z_got, scalar, velocity, mass, near)
    g, x, *outer_terms, z = call(
        part(second_outer_kernel, n_cam),
        (shape_of(*flat), shape_of(2, 1, 64, 128, dtype=BF16), shape_of(*outer), shape_of(*outer))
        + (shape_of(4, 8, 128),),
        scratch_shapes=[pltpu.VMEM(outer, F32)],
    )(s, x_got, *z_got, *y_got, scalar, velocity, mass, near, g_inner, z_inner)

    x_got = swap_axial(x)
    early = call(
        early_kernel,
        shape_of(192, 128 * cameras, dtype=BF16),
        scratch_shapes=[pltpu.VMEM((192, 512), BF16)],
    )(g, *inner_terms, near, weights)
    x_got, early = lax.optimization_barrier((x_got, early))
    z, x_got = call(part(radial_kernel, 1), (shape_of(4, 8, 128), shape_of(2, 1, 64, 128)))(z, x_got)
    z_got = swap_both(z, z, "cam")
    pixels = call(
        middle_kernel,
        shape_of(cameras, 128, 128),
        scratch_shapes=[pltpu.VMEM((192, 512), BF16)],
    )(g, x_got, *inner_terms, near, weights, picks, early)
    z_got, pixels = lax.optimization_barrier((z_got, pixels))
    y = call(part(azimuth_kernel, n_cam), (shape_of(32, 128), shape_of(32, 128)))(g, x_got, *z_got)
    y_got = swap_both(*y, "ey")
    advected, pixels = call(
        part(render_inner_kernel, n_cam),
        (shape_of(*flat), shape_of(cameras, 128, 128)),
        out_specs=(HBM, VMEM),
        scratch_shapes=[
            pltpu.VMEM(inner, F32),
            pltpu.VMEM((64, 512), F32),
            pltpu.SemaphoreType.DMA,
        ],
    )(g, x_got, *z_got, *inner_terms, near, weights, picks, pixels)
    payload_shape = shape_of(share, 144, 128, dtype=BF16)
    advected, *payloads = call(
        part(render_outer_kernel, n_cam),
        (shape_of(*flat),) + (payload_shape,) * n_cam,
        in_specs=[VMEM] * 13 + [HBM],
        out_specs=(HBM,) + (VMEM,) * n_cam,
        input_output_aliases={13: 0},
        scratch_shapes=[
            pltpu.VMEM(outer, F32),
            pltpu.VMEM((128, 512), BF16),
            pltpu.VMEM((cameras, 128, 128), BF16),
            pltpu.SemaphoreType.DMA((2,)),
        ],
    )(g, x_got, *z_got, *y_got, *outer_terms, near, weights, picks, pixels, pixel_block, advected)
    received = {0: payloads[0]}
    for d in reversed(range(1, n_cam)):
        received[d] = lax.ppermute(payloads[d], "cam", [(i, i ^ d) for i in range(n_cam)])
    image_shape = shape_of(share, NBLK, 128)
    images = call(near_image_kernel, image_shape)(received[0], received[1])
    images = call(
        far_image_kernel,
        image_shape,
        out_specs=HBM,
        scratch_shapes=[
            pltpu.VMEM((share, NBLK, 128), F32),
            pltpu.SemaphoreType.DMA((4 * share,)),
        ],
    )(images, *[received[d] for d in range(2, n_cam)])
    return (advected.reshape(shape), images)


def solution(mesh):
    placed = (
        P("ex", None, "ey", None, "cam"),
        P(None, "ex", None, "ey", None, "cam"),
        P("ex", None, "ey", None, "cam"),
        P(),
        P(None, ("cam", "ex", "ey")),
        P(None, ("cam", "ex", "ey")),
    )
    return jax.shard_map(
        per_device,
        mesh=mesh,
        in_specs=placed,
        out_specs=(P("ex", None, "ey", None, "cam"), P("cam", ("ex", "ey"), None)),
        check_vma=False,
    )
```

```python
import functools

import jax
import jax.numpy as jnp
import numpy as np
from jax import lax
from jax.experimental import pallas as pl
from jax.experimental.pallas import tpu as pltpu
from jax.sharding import PartitionSpec as P

NBLK = 1024
F32 = jnp.float32
BF16 = jnp.bfloat16
VMEM = pl.BlockSpec(memory_space=pltpu.VMEM)
HBM = pl.BlockSpec(memory_space=pltpu.HBM)
time_step = 0.01


def legendre_seven(points):
    previous = points * 0.0 + 1.0
    current = points * 1.0
    for order in range(1, 7):
        following = ((2 * order + 1) * points * current - order * previous) / (order + 1)
        previous = current
        current = following
    return current


def gll_derivative():
    degree = 7
    gll_nodes = np.array(
        [
            -1.0,
            -0.8717401485096066,
            -0.5917001814331423,
            -0.2092992179024789,
            0.2092992179024789,
            0.5917001814331423,
            0.8717401485096066,
            1.0,
        ]
    )
    values = legendre_seven(gll_nodes)
    derivative = np.zeros((degree + 1, degree + 1))
    for target in range(degree + 1):
        for source in range(degree + 1):
            if target != source:
                derivative[target, source] = values[target] / (
                    values[source] * (gll_nodes[target] - gll_nodes[source])
                )
    derivative[0, 0] = -degree * (degree + 1) / 4.0
    derivative[degree, degree] = degree * (degree + 1) / 4.0
    return derivative


def split_two(table):
    high = table.astype(np.float32).astype(BF16)
    low = (table - high.astype(np.float64)).astype(np.float32).astype(BF16)
    return high, low


def derivative_tables():
    derivative = gll_derivative()
    eye = np.eye(8)
    rows = np.concatenate([np.kron(derivative, eye), np.kron(eye, derivative)], axis=0)
    high, low = split_two(rows)
    row_table = np.concatenate([high, high, low, np.zeros_like(high)], axis=1)
    high, low = split_two(np.kron(np.eye(16), derivative.T))
    lane_table = np.concatenate(
        [
            np.concatenate([high, low], axis=1),
            np.concatenate([high, np.zeros_like(high)], axis=1),
        ],
        axis=0,
    )
    swap = np.zeros((128, 128))
    for c in range(15):
        swap[8 * c + 7, 8 * c + 8] = 1.0
        swap[8 * c + 8, 8 * c + 7] = 1.0
    join_table = np.concatenate([swap, swap], axis=0).astype(np.float32).astype(BF16)
    spread = np.zeros((128, 128))
    spread[0, 0::2] = 1.0
    spread[127, 1::2] = 1.0
    turn = np.zeros((64, 256))
    for k in range(4):
        for c in range(16):
            turn[16 * k + c, 8 * c + 2 * k] = 1.0
            turn[16 * k + c, 128 + 8 * c + 2 * k + 1] = 1.0
    ends = turn.reshape(4, 16, 256)[:, ::15].reshape(8, 256)
    ends = np.concatenate([ends, np.zeros_like(ends)], axis=0)
    exact = [spread, spread, turn[:, :128], turn[:, 128:], ends[:, :128], ends[:, 128:]]
    exact = np.concatenate(exact, axis=0)
    split = [row_table[:, :128], row_table[:, 128:], lane_table[:, :128], lane_table[:, 128:]]
    split += [join_table, exact.astype(np.float32).astype(BF16)]
    return jnp.asarray(np.concatenate(split, axis=0))


def row_table(table_ref, first=0):
    high, low = table_ref[first:128], table_ref[128 + first : 256]
    return jnp.concatenate([high, low[:, :64]], axis=1)


def lane_table(table_ref):
    return jnp.concatenate([table_ref[256:512], table_ref[512:768]], axis=1)


def join_table(table_ref):
    return jnp.concatenate([table_ref[768:1024], table_ref[1024:1280]], axis=1)


def turn_table(table_ref):
    return jnp.concatenate([table_ref[1280:1344], table_ref[1344:1408]], axis=1)


def end_table(table_ref):
    return jnp.concatenate([table_ref[1408:1424], table_ref[1424:1440]], axis=1)


def span_of(a, offset=0):
    if isinstance(a, int):
        return slice(8 * a + offset, 8 * a + offset + 8)
    return pl.ds(pl.multiple_of(a * 8 + offset, 8), 8)


def sweep(body, together):
    if together == 4:
        for a in range(4):
            body(a)
        return

    def step(n, carry):
        for m in range(together):
            body(n * together + m)
        return carry

    lax.fori_loop(0, 4 // together, step, 0)


def lane_ids(shape):
    return lax.broadcasted_iota(jnp.int32, shape, len(shape) - 1)


def row_ids(shape):
    return lax.broadcasted_iota(jnp.int32, shape, len(shape) - 2)


def halves(value):
    high = value.astype(BF16)
    return high, (value - high.astype(F32)).astype(BF16)


def dot(a, b):
    return jnp.dot(a, b, preferred_element_type=F32)


def by_lanes(pairs, table_ref):
    rows = jnp.concatenate([jnp.concatenate(p, axis=1) for p in pairs], axis=0)
    both = dot(rows, lane_table(table_ref))
    return both[:, :128] + both[:, 128:]


def join_lanes(values, table_ref):
    rows = jnp.concatenate([jnp.concatenate(halves(v), axis=1) for v in values], axis=0)
    other = dot(rows, join_table(table_ref))
    joined, spread, at = [], [], 0
    for v in values:
        span = slice(at, at + v.shape[0])
        joined.append(v + other[span, :128])
        spread.append(other[span, 128:])
        at += v.shape[0]
    return joined, spread


def join_rows(value):
    row = row_ids(value.shape)
    last = ((row & 7) == 7) & (row != 63)
    first = ((row & 7) == 0) & (row != 0)
    other = jnp.where(
        last, pltpu.roll(value, 63, 0), jnp.where(first, pltpu.roll(value, 1, 0), 0.0)
    )
    return value + other


def convect_pair(fields, velocities, masses, table_ref):
    pairs = [halves(f) for f in fields]
    high = jnp.concatenate([p[0] for p in pairs], axis=1)
    low = jnp.concatenate([p[1] for p in pairs], axis=1)
    stacked = jnp.concatenate([high, low, high], axis=0)
    rows = dot(row_table(table_ref), stacked)
    radius = by_lanes(pairs, table_ref)
    out = []
    for n in range(2):
        lanes = slice(128 * n, 128 * n + 128)
        v = velocities[n]
        slope = v[0] * rows[:64, lanes] + v[1] * rows[64:, lanes]
        out.append(masses[n] * (slope + v[2] * radius[64 * n : 64 * n + 64]))
    return out


def face_kernel(
    scalar_hbm, velocity_hbm, mass_hbm, table_hbm, x_ref, table_ref, f_ref, v_ref, m_ref, sems,
):
    copies = []

    def start(source, target):
        copy = pltpu.make_async_copy(source, target, sems.at[len(copies)])
        copy.start()
        copies.append(copy)

    last = scalar_hbm.shape[0] - 1
    start(scalar_hbm.at[pl.ds(last - 7, 8)], f_ref.at[0])
    start(scalar_hbm.at[pl.ds(0, 8)], f_ref.at[1])
    start(table_hbm, table_ref)
    start(velocity_hbm.at[:, last], v_ref.at[0])
    start(velocity_hbm.at[:, 0], v_ref.at[1])
    start(mass_hbm.at[last], m_ref.at[0])
    start(mass_hbm.at[0], m_ref.at[1])
    for copy in copies[:3]:
        copy.wait()
    derivative = gll_derivative()
    fields = [f_ref[0, 7], f_ref[1, 0]]
    pairs = [halves(f) for f in fields]
    high = jnp.concatenate([p[0] for p in pairs], axis=1)
    low = jnp.concatenate([p[1] for p in pairs], axis=1)
    azimuth = dot(row_table(table_ref, 64), jnp.concatenate([high, low, high], axis=0))
    radius = by_lanes(pairs, table_ref)
    for copy in copies[3:]:
        copy.wait()
    values = []
    for n, node in enumerate((7, 0)):
        axial = f_ref[n, 0] * float(derivative[node, 0])
        for p in range(1, 8):
            axial = axial + f_ref[n, p] * float(derivative[node, p])
        slope = v_ref[n, 0] * axial + v_ref[n, 1] * azimuth[:, 128 * n : 128 * n + 128]
        values.append(m_ref[n] * (slope + v_ref[n, 2] * radius[64 * n : 64 * n + 64]))
        values.append(m_ref[n])
    for n, value in enumerate(join_lanes(values, table_ref)[0]):
        x_ref[n // 2, n % 2] = join_rows(value).astype(BF16)


def join_block(s_ref):
    for b in range(s_ref.shape[1] // 8 - 1):
        total = s_ref[:, 8 * b + 7, :] + s_ref[:, 8 * b + 8, :]
        s_ref[:, 8 * b + 7, :] = total
        s_ref[:, 8 * b + 8, :] = total
    join_axial(s_ref)


def join_axial(s_ref):
    for f in range(s_ref.shape[0] // 32):
        for a in range(3):
            at = 32 * f + 8 * a + 7
            total = s_ref[at] + s_ref[at + 1]
            s_ref[at] = total
            s_ref[at + 1] = total


def pack_blocks(blocks):
    slot = ((lane_ids((8, 128)) + 1) >> 1) & 63
    parts = [jnp.zeros((8, 128), F32) for _ in range(4)]
    for n, (u, block) in enumerate(blocks):
        if u:
            block = pltpu.roll(block, 2 * u, 1)
        parts[n % 4] = jnp.where(slot == u, block, parts[n % 4])
    return (parts[0] + parts[1]) + (parts[2] + parts[3])


def pick_spread(spreads):
    slot = ((lane_ids((8, 128)) + 1) >> 1) & 63
    parts = [jnp.zeros((8, 128), F32) for _ in range(2)]
    for b, spread in spreads:
        for i in range(8):
            block = spread[8 * i : 8 * i + 8]
            parts[i % 2] = jnp.where(slot == 56 - 8 * i + b, block, parts[i % 2])
    return parts[0] + parts[1]


def join_packed(packed):
    lane, row = lane_ids((8, 128)), row_ids((8, 128))
    slot = ((lane + 1) >> 1) & 63
    b = slot & 7
    rows = []
    for value in packed:
        after = pltpu.roll(pltpu.roll(value, 126, 1), 7, 0)
        before = pltpu.roll(pltpu.roll(value, 2, 1), 1, 0)
        value = value + jnp.where((row == 7) & (b < 7), after, 0.0)
        rows.append(value + jnp.where((row == 0) & (b > 0), before, 0.0))
    out = list(rows)
    for a in range(3):
        out[a] = out[a] + jnp.where(slot < 8, pltpu.roll(rows[a + 1], 16, 1), 0.0)
        out[a + 1] = out[a + 1] + jnp.where(slot >= 56, pltpu.roll(rows[a], 112, 1), 0.0)
    return out


def first_kernel(scalar_ref, velocity_ref, mass_ref, table_ref, s_ref, z_ref):
    def body(a):
        at = span_of(a)
        spreads = [[], []]
        for pair in range(4):
            spans = [slice(16 * pair + 8 * n, 16 * pair + 8 * n + 8) for n in range(2)]
            fields = [scalar_ref[at, s, :].reshape(64, 128) for s in spans]
            velocities = [
                [velocity_ref[d, at, s, :].reshape(64, 128) for d in range(3)] for s in spans
            ]
            masses = [mass_ref[at, s, :].reshape(64, 128) for s in spans]
            values = convect_pair(fields, velocities, masses, table_ref)
            joined, spread = join_lanes(values + masses, table_ref)
            for n, s in enumerate(spans):
                for f in range(2):
                    s_ref[span_of(a, 32 * f), s, :] = joined[n + 2 * f].reshape(8, 8, 128)
                    spreads[f].append((2 * pair + n, spread[n + 2 * f]))
        for f in range(2):
            z_ref[a + 4 * f] = pick_spread(spreads[f])

    sweep(body, 2)
    join_block(s_ref)
    for f in range(2):
        for n, value in enumerate(join_packed([z_ref[4 * f + a] for a in range(4)])):
            z_ref[4 * f + n] = value


def radial_kernel(count, z_in, x_in, z_ref, x_ref):
    x_ref[...] = x_in[...].astype(F32)
    for f in range(count):
        spans = [slice(8 * b, 8 * b + 8) for b in range(8)]
        z_ref[4 * f] = z_in[4 * f] + pack_blocks(
            [(56 + b, x_ref[0, f, s, :]) for b, s in enumerate(spans)]
        )
        z_ref[4 * f + 1] = z_in[4 * f + 1]
        z_ref[4 * f + 2] = z_in[4 * f + 2]
        z_ref[4 * f + 3] = z_in[4 * f + 3] + pack_blocks(
            [(b, x_ref[1, f, s, :]) for b, s in enumerate(spans)]
        )


def merged(one, two, cam_count):
    me = lax.axis_index("cam")
    even = (me & 1) == 0
    left = jnp.where(even, two, one)
    right = jnp.where(even, one, two)
    left = jnp.where(me == 0, 0.0, left)
    right = jnp.where(me == cam_count - 1, 0.0, right)
    lane = lane_ids((8, 128))
    return jnp.where((lane & 1) == 0, pltpu.roll(left, 1, 1), pltpu.roll(right, 127, 1))


def end_lanes(shape):
    lane = lane_ids(shape)
    return (lane == 0) | (lane == 127)


def azimuth_kernel(cam_count, s_ref, x_ref, one_ref, two_ref, even_ref, odd_ref):
    ends = end_lanes((8, 128))
    row = row_ids((8, 128))
    even = (lax.axis_index("ey") & 1) == 0
    for q in range(one_ref.shape[0]):
        packed = merged(one_ref[q], two_ref[q], cam_count)
        f, a = q // 4, q % 4
        at = slice(8 * q, 8 * q + 8)
        faces = []
        for line, shift in ((0, 16), (63, 2)):
            j = line & 7
            spread = jnp.broadcast_to(packed[j : j + 1, :], (8, 128))
            moved = pltpu.roll(spread, shift, 1, stride=16, stride_axis=0)
            face = s_ref[at, line, :] + jnp.where(ends, moved, 0.0)
            if a == 0:
                face = face + jnp.where(row == 0, x_ref[0, f, line : line + 1, :], 0.0)
            if a == 3:
                face = face + jnp.where(row == 7, x_ref[1, f, line : line + 1, :], 0.0)
            faces.append(face)
        even_ref[at, :] = jnp.where(even, faces[1], faces[0])
        odd_ref[at, :] = jnp.where(even, faces[0], faces[1])


def unpacked(packed, b):
    ends = end_lanes((8, 128))
    rows = []
    for i in range(8):
        u = 56 - 8 * i + b
        moved = pltpu.roll(packed, (128 - 2 * u) % 128, 1) if u else packed
        rows.append(jnp.where(ends, moved, 0.0))
    return rows


def assembled(s_ref, x_ref, packed, f, a, b, y_refs=None):
    span = slice(8 * b, 8 * b + 8)
    at = span_of(a, 32 * f)
    block = s_ref[at, span, :]
    if packed is None:
        rows = [jnp.zeros((8, 128), F32) for _ in range(8)]
    else:
        rows = unpacked(packed, b)
    if not isinstance(a, int):
        rows[0] = rows[0] + jnp.where(a == 0, x_ref[0, f, span, :], 0.0)
        rows[7] = rows[7] + jnp.where(a == 3, x_ref[1, f, span, :], 0.0)
    elif a == 0:
        rows[0] = rows[0] + x_ref[0, f, span, :]
    elif a == 3:
        rows[7] = rows[7] + x_ref[1, f, span, :]
    if y_refs is not None:
        one_ref, two_ref = y_refs
        even = (lax.axis_index("ey") & 1) == 0
        if b == 0:
            line, sublane = jnp.where(even, two_ref[at, :], one_ref[at, :]), 0
        else:
            line, sublane = jnp.where(even, one_ref[at, :], two_ref[at, :]), 7
        node = lax.broadcasted_iota(jnp.int32, (8, 8, 128), 1)
        block = block + jnp.where(node == sublane, line[:, None, :], 0.0)
    return block.reshape(64, 128) + jnp.concatenate(rows, axis=0)


def second_pairs(
    cam_count, pairs, s_ref, x_ref, one_ref, two_ref, y_refs, scalar_ref, velocity_ref,
    mass_ref, table_ref, g_ref, base_ref, half_ref, z_ref,
):
    def body(a, layer=None):
        at = span_of(a)
        layer = a if layer is None else layer
        to = span_of(layer)
        radial_g = merged(one_ref[a], two_ref[a], cam_count)
        radial_m = merged(one_ref[a + 4], two_ref[a + 4], cam_count)
        spreads = []
        for n, pair in enumerate(pairs):
            fields, velocities, masses = [], [], []
            for h, b in enumerate(pair):
                s = slice(8 * b, 8 * b + 8)
                out = slice(16 * n + 8 * h, 16 * n + 8 * h + 8)
                g = assembled(s_ref, x_ref, radial_g, 0, a, b, y_refs)
                m = assembled(s_ref, x_ref, radial_m, 1, a, b, y_refs)
                scale = time_step / m
                scalar = scalar_ref[at, s, :].reshape(64, 128)
                first = scalar - scale * g
                base_ref[to, out, :] = (0.5 * (scalar + first)).reshape(8, 8, 128)
                half_ref[to, out, :] = (0.5 * scale).reshape(8, 8, 128)
                fields.append(first)
                velocities.append(
                    [velocity_ref[d, at, s, :].reshape(64, 128) for d in range(3)]
                )
                masses.append(mass_ref[at, s, :].reshape(64, 128))
            values = convect_pair(fields, velocities, masses, table_ref)
            joined, spread = join_lanes(values, table_ref)
            for h, b in enumerate(pair):
                out = slice(16 * n + 8 * h, 16 * n + 8 * h + 8)
                g_ref[to, out, :] = joined[h].reshape(8, 8, 128)
                spreads.append((b, spread[h]))
        z_ref[layer] = pick_spread(spreads)

    return body


def second_inner_kernel(
    cam_count, s_ref, x_ref, one_ref, two_ref, scalar_ref, velocity_ref, mass_ref,
    table_ref, g_ref, base_ref, half_ref, z_ref,
):
    body = second_pairs(
        cam_count, ((1, 2), (3, 4), (5, 6)), s_ref, x_ref, one_ref, two_ref, None,
        scalar_ref, velocity_ref, mass_ref, table_ref, g_ref, base_ref, half_ref, z_ref,
    )
    sweep(body, 2)
    join_block(g_ref)


def second_face_kernel(
    cam_count, s_ref, x_ref, one_ref, two_ref, y_one_ref, y_two_ref, scalar_ref, velocity_ref,
    mass_ref, table_ref, inner_ref, x_out_ref, edge_ref, base_ref, half_ref, z_ref,
):
    body = second_pairs(
        cam_count, ((0, 7),), s_ref, x_ref, one_ref, two_ref, (y_one_ref, y_two_ref),
        scalar_ref, velocity_ref, mass_ref, table_ref, edge_ref, base_ref, half_ref, z_ref,
    )
    body(0, 0)
    body(3, 1)
    row = row_ids((64, 128))
    for n, (layer, at) in enumerate(((15, 31), (0, 0))):
        face = jnp.concatenate(
            [edge_ref[layer, 0:8, :], inner_ref[at], edge_ref[layer, 8:16, :]], axis=0
        )
        after = jnp.where((row == 7) | (row == 55), pltpu.roll(face, 63, 0), 0.0)
        before = jnp.where((row == 8) | (row == 56), pltpu.roll(face, 1, 0), 0.0)
        x_out_ref[n, 0] = (face + (after + before)).astype(BF16)


def second_outer_kernel(
    cam_count, s_ref, x_ref, one_ref, two_ref, y_one_ref, y_two_ref, scalar_ref, velocity_ref,
    mass_ref, table_ref, inner_ref, z_in, edge_in, base_in, half_in, z_face,
    g_ref, base_ref, half_ref, z_ref, edge_ref,
):
    body = second_pairs(
        cam_count, ((0, 7),), s_ref, x_ref, one_ref, two_ref, (y_one_ref, y_two_ref),
        scalar_ref, velocity_ref, mass_ref, table_ref, edge_ref, base_ref, half_ref, z_ref,
    )
    body(1)
    body(2)
    for layer, a in ((0, 0), (1, 3)):
        for source, target in ((edge_in, edge_ref), (base_in, base_ref), (half_in, half_ref)):
            target[span_of(a)] = source[span_of(layer)]
        z_ref[a] = z_face[layer]
    join_axial(edge_ref)
    g_ref[:, 0:8, :] = edge_ref[:, 0:8, :]
    g_ref[:, 8:56, :] = inner_ref[...]
    g_ref[:, 56:64, :] = edge_ref[:, 8:16, :]
    for low in (7, 55):
        total = g_ref[:, low, :] + g_ref[:, low + 1, :]
        g_ref[:, low, :] = total
        g_ref[:, low + 1, :] = total
    for n, value in enumerate(join_packed([z_ref[a] + z_in[a] for a in range(4)])):
        z_ref[n] = value


def weight_kernel(weight_ref, out_ref):
    row = row_ids((512, 512))
    source = (row & 63) * 8 + (row >> 6)
    order = jnp.where(lane_ids((512, 512)) == source, 1.0, 0.0).astype(BF16)
    for m in range(8):
        out_ref[:, 128 * m : 128 * m + 128] = dot(order, weight_ref[m]).astype(BF16)


def pick_kernel(cut_ref, pick_ref):
    cut = cut_ref[...]
    a, b, c = cut >> 7, (cut >> 4) & 7, cut & 15
    order = jnp.where(a == 0, 2, jnp.where(a == 3, 3, a - 1))
    inner = 96 * order + 16 * (b - 1) + c
    ends = 512 + 12 * a + 2 * (b - 1) + (c >> 3)
    outer = 384 + 32 * a + jnp.where(b == 7, 16, 0) + c
    place = jnp.where((c == 0) | (c == 15), ends, inner)
    place = jnp.where((b == 0) | (b == 7), outer, place)
    turned = place.astype(F32).T.astype(jnp.int32)
    lane = lane_ids((128, 640))
    for m in range(8):
        pick_ref[m] = jnp.where(lane == turned[:, m : m + 1], 1.0, 0.0).astype(BF16)


def turn(blocks, table):
    rows = []
    for block in blocks:
        value = block.astype(BF16)
        zero = jnp.zeros_like(value)
        rows.append(jnp.concatenate([value, zero], axis=1))
        rows.append(jnp.concatenate([zero, value], axis=1))
    return lax.dot_general(
        table,
        jnp.concatenate(rows, axis=0),
        (((1,), (1,)), ((), ())),
        preferred_element_type=F32,
    )


def advanced(g_ref, x_ref, packed, y_refs, base_ref, half_ref, a, pair, place):
    blocks = []
    for h, b in enumerate(pair):
        g = assembled(g_ref, x_ref, packed, 0, a, b, y_refs)
        out = slice(place + 8 * h, place + 8 * h + 8)
        base = base_ref[span_of(a), out, :].reshape(64, 128)
        half = half_ref[span_of(a), out, :].reshape(64, 128)
        blocks.append(base - half * g)
    return blocks


def store_elements(element_ref, blocks, table_ref, place):
    turned = turn(blocks, turn_table(table_ref)).astype(BF16)
    for h in range(2):
        for k in range(4):
            element_ref[place + 16 * h : place + 16 * h + 16, 128 * k : 128 * k + 128] = turned[
                16 * k : 16 * k + 16, 128 * h : 128 * h + 128
            ]


def pixel_values(element_ref, weight_ref, m):
    return dot(element_ref[...], weight_ref[:, 256 * m : 256 * m + 256]).astype(BF16)


INNER = ((1, 2), (3, 4), (5, 6))


def inner_elements(layers, g_ref, x_ref, base_ref, half_ref, table_ref, element_ref):
    place = 0
    for a in layers:
        for n, pair in enumerate(INNER):
            blocks = advanced(g_ref, x_ref, None, None, base_ref, half_ref, a, pair, 16 * n)
            store_elements(element_ref, blocks, table_ref, place)
            place += 32


def early_kernel(g_ref, base_ref, half_ref, table_ref, weight_ref, value_ref, element_ref):
    inner_elements((1, 2), g_ref, None, base_ref, half_ref, table_ref, element_ref)
    for m in range(4):
        value_ref[:, 256 * m : 256 * m + 256] = pixel_values(element_ref, weight_ref, m)


def middle_kernel(
    g_ref, x_ref, base_ref, half_ref, table_ref, weight_ref, pick_ref, early_ref,
    pixel_ref, element_ref,
):
    inner_elements((0, 3), g_ref, x_ref, base_ref, half_ref, table_ref, element_ref)
    for m in range(4):
        late = pixel_values(element_ref, weight_ref, m)
        both = jnp.concatenate([early_ref[:, 256 * m : 256 * m + 256], late], axis=0)
        for n in range(2):
            pixel_ref[2 * m + n] = dot(
                pick_ref[2 * m + n, :, :384], both[:, 128 * n : 128 * n + 128]
            )


def render_inner_kernel(
    cam_count, g_ref, x_ref, one_ref, two_ref, base_ref, half_ref, table_ref, weight_ref, pick_ref,
    pixel_in, out_hbm, pixel_ref, advected_ref, end_ref, sem,
):
    end_ref[48:, :] = jnp.zeros((16, 512), F32)

    def body(a):
        packed = merged(one_ref[a], two_ref[a], cam_count)
        for n, pair in enumerate(INNER):
            blocks = advanced(g_ref, x_ref, packed, None, base_ref, half_ref, a, pair, 16 * n)
            for h in range(2):
                out = slice(16 * n + 8 * h, 16 * n + 8 * h + 8)
                advected_ref[span_of(a), out, :] = blocks[h].reshape(8, 8, 128)
            turned = turn(blocks, end_table(table_ref))
            for h in range(2):
                place = 12 * a + 4 * n + 2 * h
                for k in range(4):
                    end_ref[place : place + 2, 128 * k : 128 * k + 128] = turned[
                        2 * k : 2 * k + 2, 128 * h : 128 * h + 128
                    ]

    sweep(body, 4)
    copy = pltpu.make_async_copy(advected_ref, out_hbm.at[:, pl.ds(8, 48)], sem)
    copy.start()
    ends = end_ref[...].astype(BF16)
    for m in range(4):
        values = dot(ends, weight_ref[:, 256 * m : 256 * m + 256]).astype(BF16)
        for n in range(2):
            pixel_ref[2 * m + n] = pixel_in[2 * m + n] + dot(
                pick_ref[2 * m + n, :, 512:576], values[:, 128 * n : 128 * n + 128]
            )
    copy.wait()


def fill_payload(payload_ref, d, cameras, cam_count, pick_ref, value_ref, pixel_ref, block_ref):
    me = lax.axis_index("cam")
    share = cameras // cam_count
    sub = row_ids((16, 128))
    for n in range(share):
        m = share * (me ^ d) + n
        values = dot(pick_ref[m, :, 384:512], value_ref[m]) + pixel_ref[m]
        payload_ref[n, :128, :] = values.astype(BF16)
        ids = block_ref[pl.ds(m, 1), :]
        tail = jnp.where(sub == 0, ids >> 5, jnp.where(sub == 1, ids & 31, 0))
        payload_ref[n, 128:, :] = tail.astype(F32).astype(BF16)


def render_far_kernel(
    cam_count, g_ref, x_ref, one_ref, two_ref, y_one_ref, y_two_ref, base_ref, half_ref,
    table_ref, weight_ref, pick_ref, pixel_ref, block_ref, out_in,
    out_hbm, value_ref, *rest,
):
    payload_refs = rest[: cam_count - 2]
    advected_ref, element_ref, sems = rest[cam_count - 2 :]
    for a in range(4):
        packed = merged(one_ref[a], two_ref[a], cam_count)
        blocks = advanced(
            g_ref, x_ref, packed, (y_one_ref, y_two_ref), base_ref, half_ref, a, (0, 7), 0
        )
        for h in range(2):
            advected_ref[span_of(a), 8 * h : 8 * h + 8, :] = blocks[h].reshape(8, 8, 128)
        store_elements(element_ref, blocks, table_ref, 32 * a)
    copies = [
        pltpu.make_async_copy(
            advected_ref.at[:, pl.ds(8 * n, 8)], out_hbm.at[:, pl.ds(56 * n, 8)], sems.at[n]
        )
        for n in range(2)
    ]
    for copy in copies:
        copy.start()
    cameras = pixel_ref.shape[0]
    for m in range(cameras // 2):
        values = pixel_values(element_ref, weight_ref, m)
        value_ref[2 * m] = values[:, :128]
        value_ref[2 * m + 1] = values[:, 128:]
    for d in range(2, cam_count):
        fill_payload(
            payload_refs[d - 2], d, cameras, cam_count, pick_ref, value_ref, pixel_ref, block_ref
        )
    for copy in copies:
        copy.wait()


def render_near_kernel(
    cam_count, d, value_ref, pick_ref, pixel_ref, block_ref, payload_ref
):
    cameras = pixel_ref.shape[0]
    fill_payload(
        payload_ref, d, cameras, cam_count, pick_ref, value_ref, pixel_ref, block_ref
    )


def scatter(payload_refs, m, chunk):
    ids, values = [], []
    for payload_ref in payload_refs:
        tail = payload_ref[m, 128:, :].astype(F32).astype(jnp.int32)
        ids.append(tail[0:1, :] * 32 + tail[1:2, :])
        values.append(payload_ref[m, :128, :])
    ids = jnp.concatenate(ids, axis=1)
    row = row_ids((256, ids.shape[1])) + 256 * chunk
    onehot = jnp.where(row == ids, 1.0, 0.0).astype(BF16)
    return dot(onehot, jnp.concatenate(values, axis=0))


def own_image_kernel(cam_count, value_ref, pick_ref, pixel_ref, block_ref, image_ref, payload_ref):
    cameras = pixel_ref.shape[0]
    fill_payload(payload_ref, 0, cameras, cam_count, pick_ref, value_ref, pixel_ref, block_ref)
    for m in range(image_ref.shape[0]):
        for chunk in range(4):
            at = slice(256 * chunk, 256 * chunk + 256)
            image_ref[m, at, :] = scatter([payload_ref], m, chunk)


def image_kernel(own_ref, *refs):
    payload_refs, (image_hbm, image_ref, sems) = refs[:-3], refs[-3:]
    copies = []
    for m in range(image_ref.shape[0]):
        for chunk in range(4):
            at = slice(256 * chunk, 256 * chunk + 256)
            image_ref[m, at, :] = own_ref[m, at, :] + scatter(payload_refs, m, chunk)
            copy = pltpu.make_async_copy(
                image_ref.at[m, at], image_hbm.at[m, at], sems.at[4 * m + chunk]
            )
            copy.start()
            copies.append(copy)
    for copy in copies:
        copy.wait()


def call(kernel, out_shape, flops=10**8, size=10**7, **options):
    return pl.pallas_call(
        kernel,
        out_shape=out_shape,
        compiler_params=pltpu.CompilerParams(vmem_limit_bytes=24 * 2**20),
        cost_estimate=pl.CostEstimate(flops=flops, bytes_accessed=size, transcendentals=0),
        **options,
    )


def shape_of(*shape, dtype=F32):
    return jax.ShapeDtypeStruct(shape, dtype)


def stay(*arrays):
    return [pltpu.with_memory_space_constraint(x, pltpu.HBM) for x in arrays]


def swaps(axis):
    count = lax.axis_size(axis)
    even = [(i, i ^ 1) for i in range(count)]
    odd = [(i, (i + 1) % count if i & 1 else (i - 1) % count) for i in range(count)]
    return even, odd


def swap_axial(x):
    count = lax.axis_size("ex")
    up = [(i, (i + 1) % count) for i in range(count)]
    if count == 2:
        return lax.ppermute(x, "ex", up)
    down = [(j, i) for i, j in up]
    return jnp.stack([lax.ppermute(x[0], "ex", up), lax.ppermute(x[1], "ex", down)])


def swap_both(one, two, axis):
    even, odd = swaps(axis)
    return lax.ppermute(one, axis, even), lax.ppermute(two, axis, odd)


def per_device(scalar, velocity, lumped_mass, pixel_weights, cut_element, pixel_block):
    shape = scalar.shape
    flat = (32, 64, 128)
    inner, outer = (32, 48, 128), (32, 16, 128)
    scalar = scalar.reshape(flat)
    velocity = velocity.reshape((3,) + flat)
    mass = lumped_mass.reshape(flat)
    tables = derivative_tables()
    n_cam = lax.axis_size("cam")
    cameras = pixel_weights.shape[0]
    share = cameras // n_cam
    part = functools.partial

    x, near = call(
        face_kernel,
        (shape_of(2, 2, 64, 128, dtype=BF16), shape_of(*tables.shape, dtype=BF16)),
        in_specs=[HBM] * 4,
        scratch_shapes=[
            pltpu.VMEM((2, 8, 64, 128), F32),
            pltpu.VMEM((2, 3, 64, 128), F32),
            pltpu.VMEM((2, 64, 128), F32),
            pltpu.SemaphoreType.DMA((7,)),
        ],
    )(*stay(scalar, velocity, mass, tables))
    x_got = swap_axial(x)
    s, z = call(first_kernel, (shape_of(64, 64, 128), shape_of(8, 8, 128)))(
        scalar, velocity, mass, near
    )
    weights = call(weight_kernel, shape_of(512, 128 * cameras, dtype=BF16))(pixel_weights)
    picks = call(pick_kernel, shape_of(cameras, 128, 640, dtype=BF16))(cut_element)

    z, x_got = call(part(radial_kernel, 2), (shape_of(8, 8, 128), shape_of(2, 2, 64, 128)))(z, x_got)
    z_got = swap_both(z, z, "cam")
    z_got, weights, picks = lax.optimization_barrier((z_got, weights, picks))
    y = call(part(azimuth_kernel, n_cam), (shape_of(64, 128), shape_of(64, 128)))(s, x_got, *z_got)
    y_got = swap_both(*y, "ey")
    g_inner, *inner_terms, z_inner = call(
        part(second_inner_kernel, n_cam), (shape_of(*inner),) * 3 + (shape_of(4, 8, 128),)
    )(s, x_got, *z_got, scalar, velocity, mass, near)
    args = (s, x_got, *z_got, *y_got, scalar, velocity, mass, near, g_inner)
    some = (16, 16, 128)
    x, *faces = call(
        part(second_face_kernel, n_cam),
        (shape_of(2, 1, 64, 128, dtype=BF16),) + (shape_of(*some),) * 3 + (shape_of(2, 8, 128),),
    )(*args)
    g, *outer_terms, z = call(
        part(second_outer_kernel, n_cam),
        (shape_of(*flat), shape_of(*outer), shape_of(*outer), shape_of(4, 8, 128)),
        scratch_shapes=[pltpu.VMEM(outer, F32)],
    )(*args, z_inner, *faces)

    x_got = swap_axial(x)
    early = call(
        early_kernel,
        shape_of(192, 128 * cameras, dtype=BF16),
        scratch_shapes=[pltpu.VMEM((192, 512), BF16)],
    )(g, *inner_terms, near, weights)
    x_got, early = lax.optimization_barrier((x_got, early))
    z, x_got = call(part(radial_kernel, 1), (shape_of(4, 8, 128), shape_of(2, 1, 64, 128)))(z, x_got)
    z_got = swap_both(z, z, "cam")
    pixels = call(
        middle_kernel,
        shape_of(cameras, 128, 128),
        scratch_shapes=[pltpu.VMEM((192, 512), BF16)],
    )(g, x_got, *inner_terms, near, weights, picks, early)
    z_got, pixels = lax.optimization_barrier((z_got, pixels))
    y = call(part(azimuth_kernel, n_cam), (shape_of(32, 128), shape_of(32, 128)))(g, x_got, *z_got)
    y_got = swap_both(*y, "ey")
    advected, pixels = call(
        part(render_inner_kernel, n_cam),
        (shape_of(*flat), shape_of(cameras, 128, 128)),
        out_specs=(HBM, VMEM),
        scratch_shapes=[
            pltpu.VMEM(inner, F32),
            pltpu.VMEM((64, 512), F32),
            pltpu.SemaphoreType.DMA,
        ],
    )(g, x_got, *z_got, *inner_terms, near, weights, picks, pixels)
    payload_shape = shape_of(share, 144, 128, dtype=BF16)
    advected, values, *far = call(
        part(render_far_kernel, n_cam),
        (shape_of(*flat), shape_of(cameras, 128, 128, dtype=BF16)) + (payload_shape,) * (n_cam - 2),
        in_specs=[VMEM] * 13 + [HBM],
        out_specs=(HBM, VMEM) + (VMEM,) * (n_cam - 2),
        input_output_aliases={13: 0},
        scratch_shapes=[
            pltpu.VMEM(outer, F32),
            pltpu.VMEM((128, 512), BF16),
            pltpu.SemaphoreType.DMA((2,)),
        ],
    )(g, x_got, *z_got, *y_got, *outer_terms, near, weights, picks, pixels, pixel_block, advected)
    parts = (values, picks, pixels, pixel_block)
    image_shape = shape_of(share, NBLK, 128)
    images = call(
        part(own_image_kernel, n_cam),
        image_shape,
        scratch_shapes=[pltpu.VMEM(payload_shape.shape, BF16)],
    )(*parts)
    images, parts = lax.optimization_barrier((images, parts))
    beside = call(part(render_near_kernel, n_cam, 1), payload_shape)(*parts)
    received = []
    for d, payload in [(1, beside)] + [(n + 2, p) for n, p in enumerate(far)]:
        received.append(lax.ppermute(payload, "cam", [(i, i ^ d) for i in range(n_cam)]))
    images = call(
        image_kernel,
        image_shape,
        out_specs=HBM,
        scratch_shapes=[
            pltpu.VMEM((share, NBLK, 128), F32),
            pltpu.SemaphoreType.DMA((4 * share,)),
        ],
    )(images, *received)
    return (advected.reshape(shape), images)


def solution(mesh):
    placed = (
        P("ex", None, "ey", None, "cam"),
        P(None, "ex", None, "ey", None, "cam"),
        P("ex", None, "ey", None, "cam"),
        P(),
        P(None, ("cam", "ex", "ey")),
        P(None, ("cam", "ex", "ey")),
    )
    return jax.shard_map(
        per_device,
        mesh=mesh,
        in_specs=placed,
        out_specs=(P("ex", None, "ey", None, "cam"), P("cam", ("ex", "ey"), None)),
        check_vma=False,
    )
```

```python
import functools

import jax
import jax.numpy as jnp
import numpy as np
from jax import lax
from jax.experimental import pallas as pl
from jax.experimental.pallas import tpu as pltpu
from jax.sharding import PartitionSpec as P

NBLK = 1024
F32 = jnp.float32
BF16 = jnp.bfloat16
VMEM = pl.BlockSpec(memory_space=pltpu.VMEM)
HBM = pl.BlockSpec(memory_space=pltpu.HBM)
time_step = 0.01


def legendre_seven(points):
    previous = points * 0.0 + 1.0
    current = points * 1.0
    for order in range(1, 7):
        following = ((2 * order + 1) * points * current - order * previous) / (order + 1)
        previous = current
        current = following
    return current


def gll_derivative():
    degree = 7
    gll_nodes = np.array(
        [
            -1.0,
            -0.8717401485096066,
            -0.5917001814331423,
            -0.2092992179024789,
            0.2092992179024789,
            0.5917001814331423,
            0.8717401485096066,
            1.0,
        ]
    )
    values = legendre_seven(gll_nodes)
    derivative = np.zeros((degree + 1, degree + 1))
    for target in range(degree + 1):
        for source in range(degree + 1):
            if target != source:
                derivative[target, source] = values[target] / (
                    values[source] * (gll_nodes[target] - gll_nodes[source])
                )
    derivative[0, 0] = -degree * (degree + 1) / 4.0
    derivative[degree, degree] = degree * (degree + 1) / 4.0
    return derivative


def split_two(table):
    high = table.astype(np.float32).astype(BF16)
    low = (table - high.astype(np.float64)).astype(np.float32).astype(BF16)
    return high, low


def derivative_tables():
    derivative = gll_derivative()
    eye = np.eye(8)
    rows = np.concatenate([np.kron(derivative, eye), np.kron(eye, derivative)], axis=0)
    high, low = split_two(rows)
    row_table = np.concatenate([high, high, low, np.zeros_like(high)], axis=1)
    high, low = split_two(np.kron(np.eye(16), derivative.T))
    lane_table = np.concatenate(
        [
            np.concatenate([high, low], axis=1),
            np.concatenate([high, np.zeros_like(high)], axis=1),
        ],
        axis=0,
    )
    swap = np.zeros((128, 128))
    for c in range(15):
        swap[8 * c + 7, 8 * c + 8] = 1.0
        swap[8 * c + 8, 8 * c + 7] = 1.0
    join_table = np.concatenate([swap, swap], axis=0).astype(np.float32).astype(BF16)
    spread = np.zeros((128, 128))
    spread[0, 0::2] = 1.0
    spread[127, 1::2] = 1.0
    turn = np.zeros((64, 256))
    for k in range(4):
        for c in range(16):
            turn[16 * k + c, 8 * c + 2 * k] = 1.0
            turn[16 * k + c, 128 + 8 * c + 2 * k + 1] = 1.0
    ends = turn.reshape(4, 16, 256)[:, ::15].reshape(8, 256)
    ends = np.concatenate([ends, np.zeros_like(ends)], axis=0)
    exact = [spread, spread, turn[:, :128], turn[:, 128:], ends[:, :128], ends[:, 128:]]
    exact = np.concatenate(exact, axis=0)
    split = [row_table[:, :128], row_table[:, 128:], lane_table[:, :128], lane_table[:, 128:]]
    split += [join_table, exact.astype(np.float32).astype(BF16)]
    return jnp.asarray(np.concatenate(split, axis=0))


def row_table(table_ref, first=0):
    high, low = table_ref[first:128], table_ref[128 + first : 256]
    return jnp.concatenate([high, low[:, :64]], axis=1)


def lane_table(table_ref):
    return jnp.concatenate([table_ref[256:512], table_ref[512:768]], axis=1)


def join_table(table_ref):
    return jnp.concatenate([table_ref[768:1024], table_ref[1024:1280]], axis=1)


def turn_table(table_ref):
    return jnp.concatenate([table_ref[1280:1344], table_ref[1344:1408]], axis=1)


def end_table(table_ref):
    return jnp.concatenate([table_ref[1408:1424], table_ref[1424:1440]], axis=1)


def span_of(a, offset=0):
    if isinstance(a, int):
        return slice(8 * a + offset, 8 * a + offset + 8)
    return pl.ds(pl.multiple_of(a * 8 + offset, 8), 8)


def sweep(body, together):
    if together == 4:
        for a in range(4):
            body(a)
        return

    def step(n, carry):
        for m in range(together):
            body(n * together + m)
        return carry

    lax.fori_loop(0, 4 // together, step, 0)


def lane_ids(shape):
    return lax.broadcasted_iota(jnp.int32, shape, len(shape) - 1)


def row_ids(shape):
    return lax.broadcasted_iota(jnp.int32, shape, len(shape) - 2)


def halves(value):
    high = value.astype(BF16)
    return high, (value - high.astype(F32)).astype(BF16)


def dot(a, b):
    return jnp.dot(a, b, preferred_element_type=F32)


def by_lanes(pairs, table_ref):
    rows = jnp.concatenate([jnp.concatenate(p, axis=1) for p in pairs], axis=0)
    both = dot(rows, lane_table(table_ref))
    return both[:, :128] + both[:, 128:]


def join_lanes(values, table_ref):
    rows = jnp.concatenate([jnp.concatenate(halves(v), axis=1) for v in values], axis=0)
    other = dot(rows, join_table(table_ref))
    joined, spread, at = [], [], 0
    for v in values:
        span = slice(at, at + v.shape[0])
        joined.append(v + other[span, :128])
        spread.append(other[span, 128:])
        at += v.shape[0]
    return joined, spread


def join_rows(value):
    row = row_ids(value.shape)
    last = ((row & 7) == 7) & (row != 63)
    first = ((row & 7) == 0) & (row != 0)
    other = jnp.where(
        last, pltpu.roll(value, 63, 0), jnp.where(first, pltpu.roll(value, 1, 0), 0.0)
    )
    return value + other


def convect_pair(fields, velocities, masses, table_ref):
    pairs = [halves(f) for f in fields]
    high = jnp.concatenate([p[0] for p in pairs], axis=1)
    low = jnp.concatenate([p[1] for p in pairs], axis=1)
    stacked = jnp.concatenate([high, low, high], axis=0)
    rows = dot(row_table(table_ref), stacked)
    radius = by_lanes(pairs, table_ref)
    out = []
    for n in range(2):
        lanes = slice(128 * n, 128 * n + 128)
        v = velocities[n]
        slope = v[0] * rows[:64, lanes] + v[1] * rows[64:, lanes]
        out.append(masses[n] * (slope + v[2] * radius[64 * n : 64 * n + 64]))
    return out


def face_kernel(
    scalar_hbm, velocity_hbm, mass_hbm, table_hbm, x_ref, table_ref, f_ref, v_ref, m_ref, sems,
):
    copies = []

    def start(source, target):
        copy = pltpu.make_async_copy(source, target, sems.at[len(copies)])
        copy.start()
        copies.append(copy)

    last = scalar_hbm.shape[0] - 1
    start(scalar_hbm.at[pl.ds(last - 7, 8)], f_ref.at[0])
    start(scalar_hbm.at[pl.ds(0, 8)], f_ref.at[1])
    start(table_hbm, table_ref)
    start(velocity_hbm.at[:, last], v_ref.at[0])
    start(velocity_hbm.at[:, 0], v_ref.at[1])
    start(mass_hbm.at[last], m_ref.at[0])
    start(mass_hbm.at[0], m_ref.at[1])
    for copy in copies[:3]:
        copy.wait()
    derivative = gll_derivative()
    fields = [f_ref[0, 7], f_ref[1, 0]]
    pairs = [halves(f) for f in fields]
    high = jnp.concatenate([p[0] for p in pairs], axis=1)
    low = jnp.concatenate([p[1] for p in pairs], axis=1)
    azimuth = dot(row_table(table_ref, 64), jnp.concatenate([high, low, high], axis=0))
    radius = by_lanes(pairs, table_ref)
    for copy in copies[3:]:
        copy.wait()
    values = []
    for n, node in enumerate((7, 0)):
        axial = f_ref[n, 0] * float(derivative[node, 0])
        for p in range(1, 8):
            axial = axial + f_ref[n, p] * float(derivative[node, p])
        slope = v_ref[n, 0] * axial + v_ref[n, 1] * azimuth[:, 128 * n : 128 * n + 128]
        values.append(m_ref[n] * (slope + v_ref[n, 2] * radius[64 * n : 64 * n + 64]))
        values.append(m_ref[n])
    for n, value in enumerate(join_lanes(values, table_ref)[0]):
        x_ref[n // 2, n % 2] = join_rows(value).astype(BF16)


def join_block(s_ref):
    for b in range(s_ref.shape[1] // 8 - 1):
        total = s_ref[:, 8 * b + 7, :] + s_ref[:, 8 * b + 8, :]
        s_ref[:, 8 * b + 7, :] = total
        s_ref[:, 8 * b + 8, :] = total
    join_axial(s_ref)


def join_axial(s_ref):
    for f in range(s_ref.shape[0] // 32):
        for a in range(3):
            at = 32 * f + 8 * a + 7
            total = s_ref[at] + s_ref[at + 1]
            s_ref[at] = total
            s_ref[at + 1] = total


def pack_blocks(blocks):
    slot = ((lane_ids((8, 128)) + 1) >> 1) & 63
    parts = [jnp.zeros((8, 128), F32) for _ in range(4)]
    for n, (u, block) in enumerate(blocks):
        if u:
            block = pltpu.roll(block, 2 * u, 1)
        parts[n % 4] = jnp.where(slot == u, block, parts[n % 4])
    return (parts[0] + parts[1]) + (parts[2] + parts[3])


def pick_spread(spreads):
    slot = ((lane_ids((8, 128)) + 1) >> 1) & 63
    parts = [jnp.zeros((8, 128), F32) for _ in range(2)]
    for b, spread in spreads:
        for i in range(8):
            block = spread[8 * i : 8 * i + 8]
            parts[i % 2] = jnp.where(slot == 56 - 8 * i + b, block, parts[i % 2])
    return parts[0] + parts[1]


def join_packed(packed):
    lane, row = lane_ids((8, 128)), row_ids((8, 128))
    slot = ((lane + 1) >> 1) & 63
    b = slot & 7
    rows = []
    for value in packed:
        after = pltpu.roll(pltpu.roll(value, 126, 1), 7, 0)
        before = pltpu.roll(pltpu.roll(value, 2, 1), 1, 0)
        value = value + jnp.where((row == 7) & (b < 7), after, 0.0)
        rows.append(value + jnp.where((row == 0) & (b > 0), before, 0.0))
    out = list(rows)
    for a in range(3):
        out[a] = out[a] + jnp.where(slot < 8, pltpu.roll(rows[a + 1], 16, 1), 0.0)
        out[a + 1] = out[a + 1] + jnp.where(slot >= 56, pltpu.roll(rows[a], 112, 1), 0.0)
    return out


def first_kernel(scalar_ref, velocity_ref, mass_ref, table_ref, s_ref, z_ref):
    def body(a):
        at = span_of(a)
        spreads = [[], []]
        for pair in range(4):
            spans = [slice(16 * pair + 8 * n, 16 * pair + 8 * n + 8) for n in range(2)]
            fields = [scalar_ref[at, s, :].reshape(64, 128) for s in spans]
            velocities = [
                [velocity_ref[d, at, s, :].reshape(64, 128) for d in range(3)] for s in spans
            ]
            masses = [mass_ref[at, s, :].reshape(64, 128) for s in spans]
            values = convect_pair(fields, velocities, masses, table_ref)
            joined, spread = join_lanes(values + masses, table_ref)
            for n, s in enumerate(spans):
                for f in range(2):
                    s_ref[span_of(a, 32 * f), s, :] = joined[n + 2 * f].reshape(8, 8, 128)
                    spreads[f].append((2 * pair + n, spread[n + 2 * f]))
        for f in range(2):
            z_ref[a + 4 * f] = pick_spread(spreads[f])

    sweep(body, 2)
    join_block(s_ref)
    for f in range(2):
        for n, value in enumerate(join_packed([z_ref[4 * f + a] for a in range(4)])):
            z_ref[4 * f + n] = value


def radial_faces(count, z_in, x_in, x_ref):
    x_ref[...] = x_in[...].astype(F32)
    rows = []
    for f in range(count):
        spans = [slice(8 * b, 8 * b + 8) for b in range(8)]
        low = pack_blocks([(56 + b, x_ref[0, f, s, :]) for b, s in enumerate(spans)])
        high = pack_blocks([(b, x_ref[1, f, s, :]) for b, s in enumerate(spans)])
        rows += [z_in[4 * f] + low, z_in[4 * f + 1], z_in[4 * f + 2], z_in[4 * f + 3] + high]
    return jnp.concatenate(rows, axis=0).astype(BF16)


def id_tile(block_ref):
    ids = block_ref[...]
    return jnp.concatenate([ids >> 5, ids & 31], axis=0).astype(F32).astype(BF16)


def first_radial_kernel(z_in, x_in, block_ref, one_ref, two_ref, x_ref):
    faces = radial_faces(2, z_in, x_in, x_ref)
    one_ref[:64, :] = faces
    one_ref[64:, :] = id_tile(block_ref)
    two_ref[...] = faces


def second_radial_kernel(z_in, x_in, block_ref, got_ref, one_ref, two_ref, x_ref):
    faces = radial_faces(1, z_in, x_in, x_ref)
    one_ref[...] = faces
    two_ref[:32, :] = faces
    two_ref[32:48, :] = id_tile(block_ref)
    two_ref[48:, :] = got_ref[64:, :]


def merged(one, two, cam_count):
    me = lax.axis_index("cam")
    even = (me & 1) == 0
    left = jnp.where(even, two, one)
    right = jnp.where(even, one, two)
    left = jnp.where(me == 0, 0.0, left)
    right = jnp.where(me == cam_count - 1, 0.0, right)
    lane = lane_ids((8, 128))
    return jnp.where((lane & 1) == 0, pltpu.roll(left, 1, 1), pltpu.roll(right, 127, 1))


def end_lanes(shape):
    lane = lane_ids(shape)
    return (lane == 0) | (lane == 127)


def azimuth_kernel(cam_count, s_ref, x_ref, one_ref, two_ref, even_ref, odd_ref, packed_ref):
    ends = end_lanes((8, 128))
    row = row_ids((8, 128))
    even = (lax.axis_index("ey") & 1) == 0
    rows = s_ref.shape[0]
    one = one_ref[:rows, :].astype(F32)
    two = two_ref[:rows, :].astype(F32)
    ups, downs = [], []
    for q in range(rows // 8):
        at = slice(8 * q, 8 * q + 8)
        packed = merged(one[at], two[at], cam_count)
        packed_ref[q] = packed
        f, a = q // 4, q % 4
        faces = []
        for line, shift in ((0, 16), (63, 2)):
            j = line & 7
            spread = jnp.broadcast_to(packed[j : j + 1, :], (8, 128))
            moved = pltpu.roll(spread, shift, 1, stride=16, stride_axis=0)
            face = s_ref[at, line, :] + jnp.where(ends, moved, 0.0)
            if a == 0:
                face = face + jnp.where(row == 0, x_ref[0, f, line : line + 1, :], 0.0)
            if a == 3:
                face = face + jnp.where(row == 7, x_ref[1, f, line : line + 1, :], 0.0)
            faces.append(face)
        ups.append(jnp.where(even, faces[1], faces[0]))
        downs.append(jnp.where(even, faces[0], faces[1]))
    even_ref[...] = jnp.concatenate(ups, axis=0).astype(BF16)
    odd_ref[...] = jnp.concatenate(downs, axis=0).astype(BF16)


def unpacked(packed, b):
    ends = end_lanes((8, 128))
    rows = []
    for i in range(8):
        u = 56 - 8 * i + b
        moved = pltpu.roll(packed, (128 - 2 * u) % 128, 1) if u else packed
        rows.append(jnp.where(ends, moved, 0.0))
    return rows


def assembled(s_ref, x_ref, packed, f, a, b, y_refs=None):
    span = slice(8 * b, 8 * b + 8)
    at = span_of(a, 32 * f)
    block = s_ref[at, span, :]
    if packed is None:
        rows = [jnp.zeros((8, 128), F32) for _ in range(8)]
    else:
        rows = unpacked(packed, b)
    if not isinstance(a, int):
        rows[0] = rows[0] + jnp.where(a == 0, x_ref[0, f, span, :], 0.0)
        rows[7] = rows[7] + jnp.where(a == 3, x_ref[1, f, span, :], 0.0)
    elif a == 0:
        rows[0] = rows[0] + x_ref[0, f, span, :]
    elif a == 3:
        rows[7] = rows[7] + x_ref[1, f, span, :]
    if y_refs is not None:
        one_ref, two_ref = y_refs
        even = (lax.axis_index("ey") & 1) == 0
        at = slice(16 * (a // 2) + 32 * f, 16 * (a // 2) + 32 * f + 16)
        one, two = one_ref[at, :].astype(F32), two_ref[at, :].astype(F32)
        if b == 0:
            line, sublane = jnp.where(even, two, one), 0
        else:
            line, sublane = jnp.where(even, one, two), 7
        line = line[8 * (a % 2) : 8 * (a % 2) + 8]
        node = lax.broadcasted_iota(jnp.int32, (8, 8, 128), 1)
        block = block + jnp.where(node == sublane, line[:, None, :], 0.0)
    return block.reshape(64, 128) + jnp.concatenate(rows, axis=0)


def second_pairs(
    pairs, s_ref, x_ref, packed_ref, y_refs, scalar_ref, velocity_ref,
    mass_ref, table_ref, g_ref, base_ref, half_ref, z_ref,
):
    def body(a, layer=None):
        at = span_of(a)
        layer = a if layer is None else layer
        to = span_of(layer)
        radial_g = packed_ref[a]
        radial_m = packed_ref[a + 4]
        spreads = []
        for n, pair in enumerate(pairs):
            fields, velocities, masses = [], [], []
            for h, b in enumerate(pair):
                s = slice(8 * b, 8 * b + 8)
                out = slice(16 * n + 8 * h, 16 * n + 8 * h + 8)
                g = assembled(s_ref, x_ref, radial_g, 0, a, b, y_refs)
                m = assembled(s_ref, x_ref, radial_m, 1, a, b, y_refs)
                scale = time_step / m
                scalar = scalar_ref[at, s, :].reshape(64, 128)
                first = scalar - scale * g
                base_ref[to, out, :] = (0.5 * (scalar + first)).reshape(8, 8, 128)
                half_ref[to, out, :] = (0.5 * scale).reshape(8, 8, 128)
                fields.append(first)
                velocities.append(
                    [velocity_ref[d, at, s, :].reshape(64, 128) for d in range(3)]
                )
                masses.append(mass_ref[at, s, :].reshape(64, 128))
            values = convect_pair(fields, velocities, masses, table_ref)
            joined, spread = join_lanes(values, table_ref)
            for h, b in enumerate(pair):
                out = slice(16 * n + 8 * h, 16 * n + 8 * h + 8)
                g_ref[to, out, :] = joined[h].reshape(8, 8, 128)
                spreads.append((b, spread[h]))
        z_ref[layer] = pick_spread(spreads)

    return body


def second_inner_kernel(
    s_ref, x_ref, packed_ref, scalar_ref, velocity_ref, mass_ref,
    table_ref, g_ref, base_ref, half_ref, z_ref,
):
    body = second_pairs(
        ((1, 2), (3, 4), (5, 6)), s_ref, x_ref, packed_ref, None,
        scalar_ref, velocity_ref, mass_ref, table_ref, g_ref, base_ref, half_ref, z_ref,
    )
    sweep(body, 2)
    join_block(g_ref)


def second_face_kernel(
    s_ref, x_ref, packed_ref, y_one_ref, y_two_ref, scalar_ref, velocity_ref,
    mass_ref, table_ref, inner_ref, x_out_ref, edge_ref, base_ref, half_ref, z_ref,
):
    body = second_pairs(
        ((0, 7),), s_ref, x_ref, packed_ref, (y_one_ref, y_two_ref),
        scalar_ref, velocity_ref, mass_ref, table_ref, edge_ref, base_ref, half_ref, z_ref,
    )
    body(0, 0)
    body(3, 1)
    row = row_ids((64, 128))
    for n, (layer, at) in enumerate(((15, 31), (0, 0))):
        face = jnp.concatenate(
            [edge_ref[layer, 0:8, :], inner_ref[at], edge_ref[layer, 8:16, :]], axis=0
        )
        after = jnp.where((row == 7) | (row == 55), pltpu.roll(face, 63, 0), 0.0)
        before = jnp.where((row == 8) | (row == 56), pltpu.roll(face, 1, 0), 0.0)
        x_out_ref[n, 0] = (face + (after + before)).astype(BF16)


def second_outer_kernel(
    s_ref, x_ref, packed_ref, y_one_ref, y_two_ref, scalar_ref, velocity_ref,
    mass_ref, table_ref, inner_ref, z_in, edge_in, base_in, half_in, z_face,
    g_ref, base_ref, half_ref, z_ref, edge_ref,
):
    body = second_pairs(
        ((0, 7),), s_ref, x_ref, packed_ref, (y_one_ref, y_two_ref),
        scalar_ref, velocity_ref, mass_ref, table_ref, edge_ref, base_ref, half_ref, z_ref,
    )
    body(1)
    body(2)
    for layer, a in ((0, 0), (1, 3)):
        for source, target in ((edge_in, edge_ref), (base_in, base_ref), (half_in, half_ref)):
            target[span_of(a)] = source[span_of(layer)]
        z_ref[a] = z_face[layer]
    join_axial(edge_ref)
    g_ref[:, 0:8, :] = edge_ref[:, 0:8, :]
    g_ref[:, 8:56, :] = inner_ref[...]
    g_ref[:, 56:64, :] = edge_ref[:, 8:16, :]
    for low in (7, 55):
        total = g_ref[:, low, :] + g_ref[:, low + 1, :]
        g_ref[:, low, :] = total
        g_ref[:, low + 1, :] = total
    for n, value in enumerate(join_packed([z_ref[a] + z_in[a] for a in range(4)])):
        z_ref[n] = value


def weight_kernel(weight_ref, out_ref):
    row = row_ids((512, 512))
    source = (row & 63) * 8 + (row >> 6)
    order = jnp.where(lane_ids((512, 512)) == source, 1.0, 0.0).astype(BF16)
    for m in range(8):
        out_ref[:, 128 * m : 128 * m + 128] = dot(order, weight_ref[m]).astype(BF16)


def pick_kernel(cut_ref, pick_ref):
    cut = cut_ref[...]
    a, b, c = cut >> 7, (cut >> 4) & 7, cut & 15
    order = jnp.where(a == 0, 2, jnp.where(a == 3, 3, a - 1))
    inner = 96 * order + 16 * (b - 1) + c
    ends = 512 + 12 * a + 2 * (b - 1) + (c >> 3)
    outer = 384 + 32 * a + jnp.where(b == 7, 16, 0) + c
    place = jnp.where((c == 0) | (c == 15), ends, inner)
    place = jnp.where((b == 0) | (b == 7), outer, place)
    turned = place.astype(F32).T.astype(jnp.int32)
    lane = lane_ids((128, 640))
    for m in range(8):
        pick_ref[m] = jnp.where(lane == turned[:, m : m + 1], 1.0, 0.0).astype(BF16)


def turn(blocks, table):
    rows = []
    for block in blocks:
        value = block.astype(BF16)
        zero = jnp.zeros_like(value)
        rows.append(jnp.concatenate([value, zero], axis=1))
        rows.append(jnp.concatenate([zero, value], axis=1))
    return lax.dot_general(
        table,
        jnp.concatenate(rows, axis=0),
        (((1,), (1,)), ((), ())),
        preferred_element_type=F32,
    )


def advanced(g_ref, x_ref, packed, y_refs, base_ref, half_ref, a, pair, place):
    blocks = []
    for h, b in enumerate(pair):
        g = assembled(g_ref, x_ref, packed, 0, a, b, y_refs)
        out = slice(place + 8 * h, place + 8 * h + 8)
        base = base_ref[span_of(a), out, :].reshape(64, 128)
        half = half_ref[span_of(a), out, :].reshape(64, 128)
        blocks.append(base - half * g)
    return blocks


def store_elements(element_ref, blocks, table_ref, place):
    turned = turn(blocks, turn_table(table_ref)).astype(BF16)
    for h in range(2):
        for k in range(4):
            element_ref[place + 16 * h : place + 16 * h + 16, 128 * k : 128 * k + 128] = turned[
                16 * k : 16 * k + 16, 128 * h : 128 * h + 128
            ]


def pixel_values(element_ref, weight_ref, m):
    return dot(element_ref[...], weight_ref[:, 256 * m : 256 * m + 256]).astype(BF16)


INNER = ((1, 2), (3, 4), (5, 6))


def inner_elements(layers, g_ref, x_ref, base_ref, half_ref, table_ref, element_ref):
    place = 0
    for a in layers:
        for n, pair in enumerate(INNER):
            blocks = advanced(g_ref, x_ref, None, None, base_ref, half_ref, a, pair, 16 * n)
            store_elements(element_ref, blocks, table_ref, place)
            place += 32


def early_kernel(g_ref, base_ref, half_ref, table_ref, weight_ref, value_ref, element_ref):
    inner_elements((1, 2), g_ref, None, base_ref, half_ref, table_ref, element_ref)
    for m in range(4):
        value_ref[:, 256 * m : 256 * m + 256] = pixel_values(element_ref, weight_ref, m)


def middle_kernel(
    g_ref, x_ref, base_ref, half_ref, table_ref, weight_ref, pick_ref, early_ref,
    pixel_ref, element_ref,
):
    inner_elements((0, 3), g_ref, x_ref, base_ref, half_ref, table_ref, element_ref)
    for m in range(4):
        late = pixel_values(element_ref, weight_ref, m)
        both = jnp.concatenate([early_ref[:, 256 * m : 256 * m + 256], late], axis=0)
        for n in range(2):
            pixel_ref[2 * m + n] = dot(
                pick_ref[2 * m + n, :, :384], both[:, 128 * n : 128 * n + 128]
            )


def render_inner_kernel(
    g_ref, x_ref, packed_ref, base_ref, half_ref, table_ref, weight_ref, pick_ref,
    pixel_in, out_hbm, pixel_ref, advected_ref, end_ref, sem,
):
    end_ref[48:, :] = jnp.zeros((16, 512), F32)

    def body(a):
        packed = packed_ref[a]
        for n, pair in enumerate(INNER):
            blocks = advanced(g_ref, x_ref, packed, None, base_ref, half_ref, a, pair, 16 * n)
            for h in range(2):
                out = slice(16 * n + 8 * h, 16 * n + 8 * h + 8)
                advected_ref[span_of(a), out, :] = blocks[h].reshape(8, 8, 128)
            turned = turn(blocks, end_table(table_ref))
            for h in range(2):
                place = 12 * a + 4 * n + 2 * h
                for k in range(4):
                    end_ref[place : place + 2, 128 * k : 128 * k + 128] = turned[
                        2 * k : 2 * k + 2, 128 * h : 128 * h + 128
                    ]

    sweep(body, 4)
    copy = pltpu.make_async_copy(advected_ref, out_hbm.at[:, pl.ds(8, 48)], sem)
    copy.start()
    ends = end_ref[...].astype(BF16)
    for m in range(4):
        values = dot(ends, weight_ref[:, 256 * m : 256 * m + 256]).astype(BF16)
        for n in range(2):
            pixel_ref[2 * m + n] = pixel_in[2 * m + n] + dot(
                pick_ref[2 * m + n, :, 512:576], values[:, 128 * n : 128 * n + 128]
            )
    copy.wait()


def fill_payload(payload_ref, d, cam_count, pick_ref, value_ref, pixel_ref):
    me = lax.axis_index("cam")
    share = pixel_ref.shape[0] // cam_count
    for n in range(share):
        m = share * (me ^ d) + n
        values = dot(pick_ref[m, :, 384:512], value_ref[m]) + pixel_ref[m]
        payload_ref[n] = values.astype(BF16)


def render_far_kernel(
    cam_count, g_ref, x_ref, packed_ref, y_one_ref, y_two_ref, base_ref, half_ref,
    table_ref, weight_ref, pick_ref, pixel_ref, out_in,
    out_hbm, value_ref, *rest,
):
    payload_refs = rest[: cam_count - 2]
    advected_ref, element_ref, sems = rest[cam_count - 2 :]
    for a in range(4):
        packed = packed_ref[a]
        blocks = advanced(
            g_ref, x_ref, packed, (y_one_ref, y_two_ref), base_ref, half_ref, a, (0, 7), 0
        )
        for h in range(2):
            advected_ref[span_of(a), 8 * h : 8 * h + 8, :] = blocks[h].reshape(8, 8, 128)
        store_elements(element_ref, blocks, table_ref, 32 * a)
    copies = [
        pltpu.make_async_copy(
            advected_ref.at[:, pl.ds(8 * n, 8)], out_hbm.at[:, pl.ds(56 * n, 8)], sems.at[n]
        )
        for n in range(2)
    ]
    for copy in copies:
        copy.start()
    cameras = pixel_ref.shape[0]
    for m in range(cameras // 2):
        values = pixel_values(element_ref, weight_ref, m)
        value_ref[2 * m] = values[:, :128]
        value_ref[2 * m + 1] = values[:, 128:]
    for d in range(2, cam_count):
        fill_payload(payload_refs[d - 2], d, cam_count, pick_ref, value_ref, pixel_ref)
    for copy in copies:
        copy.wait()


def render_near_kernel(cam_count, d, value_ref, pick_ref, pixel_ref, payload_ref):
    fill_payload(payload_ref, d, cam_count, pick_ref, value_ref, pixel_ref)


def block_kernel(share, block_ref, first_ref, second_ref, onehot_ref, id_ref):
    me = lax.axis_index("cam")
    id_ref[0] = block_ref[...]
    tiles = ((1, first_ref[64:80, :]), (3, second_ref[32:48, :]), (2, second_ref[48:64, :]))
    for d, tile in tiles:
        ids = tile.astype(F32).astype(jnp.int32)
        id_ref[d] = ids[:8] * 32 + ids[8:]
    for m in range(share):
        ids = [id_ref[d, pl.ds(share * me + m, 1), :] for d in range(4)]
        ids = jnp.concatenate(ids, axis=1)
        for chunk in range(4):
            row = row_ids((256, ids.shape[1])) + 256 * chunk
            onehot_ref[m, 256 * chunk : 256 * chunk + 256, :] = jnp.where(
                row == ids, 1.0, 0.0
            ).astype(BF16)


def own_image_kernel(cam_count, value_ref, pick_ref, pixel_ref, onehot_ref, image_ref, payload_ref):
    fill_payload(payload_ref, 0, cam_count, pick_ref, value_ref, pixel_ref)
    for m in range(image_ref.shape[0]):
        image_ref[m] = dot(onehot_ref[m, :, :128], payload_ref[m])


def image_kernel(own_ref, onehot_ref, *refs):
    payload_refs, (image_hbm, image_ref, sems) = refs[:-3], refs[-3:]
    copies = []
    for m in range(image_ref.shape[0]):
        values = jnp.concatenate([payload_ref[m] for payload_ref in payload_refs], axis=0)
        for chunk in range(4):
            at = slice(256 * chunk, 256 * chunk + 256)
            image_ref[m, at, :] = own_ref[m, at, :] + dot(onehot_ref[m, at, 128:], values)
            copy = pltpu.make_async_copy(
                image_ref.at[m, at], image_hbm.at[m, at], sems.at[4 * m + chunk]
            )
            copy.start()
            copies.append(copy)
    for copy in copies:
        copy.wait()


def call(kernel, out_shape, flops=10**8, size=10**7, **options):
    return pl.pallas_call(
        kernel,
        out_shape=out_shape,
        compiler_params=pltpu.CompilerParams(vmem_limit_bytes=24 * 2**20),
        cost_estimate=pl.CostEstimate(flops=flops, bytes_accessed=size, transcendentals=0),
        **options,
    )


def shape_of(*shape, dtype=F32):
    return jax.ShapeDtypeStruct(shape, dtype)


def stay(*arrays):
    return [pltpu.with_memory_space_constraint(x, pltpu.HBM) for x in arrays]


def swaps(axis):
    count = lax.axis_size(axis)
    even = [(i, i ^ 1) for i in range(count)]
    odd = [(i, (i + 1) % count if i & 1 else (i - 1) % count) for i in range(count)]
    return even, odd


def swap_axial(x):
    count = lax.axis_size("ex")
    up = [(i, (i + 1) % count) for i in range(count)]
    if count == 2:
        return lax.ppermute(x, "ex", up)
    down = [(j, i) for i, j in up]
    return jnp.stack([lax.ppermute(x[0], "ex", up), lax.ppermute(x[1], "ex", down)])


def swap_both(one, two, axis):
    even, odd = swaps(axis)
    return lax.ppermute(one, axis, even), lax.ppermute(two, axis, odd)


def per_device(scalar, velocity, lumped_mass, pixel_weights, cut_element, pixel_block):
    shape = scalar.shape
    flat = (32, 64, 128)
    inner, outer = (32, 48, 128), (32, 16, 128)
    scalar = scalar.reshape(flat)
    velocity = velocity.reshape((3,) + flat)
    mass = lumped_mass.reshape(flat)
    tables = derivative_tables()
    n_cam = lax.axis_size("cam")
    cameras = pixel_weights.shape[0]
    share = cameras // n_cam
    part = functools.partial

    x, near = call(
        face_kernel,
        (shape_of(2, 2, 64, 128, dtype=BF16), shape_of(*tables.shape, dtype=BF16)),
        in_specs=[HBM] * 4,
        scratch_shapes=[
            pltpu.VMEM((2, 8, 64, 128), F32),
            pltpu.VMEM((2, 3, 64, 128), F32),
            pltpu.VMEM((2, 64, 128), F32),
            pltpu.SemaphoreType.DMA((7,)),
        ],
    )(*stay(scalar, velocity, mass, tables))
    x_got = swap_axial(x)
    s, z = call(first_kernel, (shape_of(64, 64, 128), shape_of(8, 8, 128)))(
        scalar, velocity, mass, near
    )
    weights = call(weight_kernel, shape_of(512, 128 * cameras, dtype=BF16))(pixel_weights)
    picks = call(pick_kernel, shape_of(cameras, 128, 640, dtype=BF16))(cut_element)

    half = functools.partial(shape_of, dtype=BF16)
    *z, x_got = call(
        first_radial_kernel, (half(80, 128), half(64, 128), shape_of(2, 2, 64, 128))
    )(z, x_got, pixel_block)
    z_got = swap_both(*z, "cam")
    z_got, weights, picks = lax.optimization_barrier((z_got, weights, picks))
    ids_got = z_got[0]
    *y, packed = call(
        part(azimuth_kernel, n_cam), (half(64, 128), half(64, 128), shape_of(8, 8, 128))
    )(s, x_got, *z_got)
    y_got = swap_both(*y, "ey")
    g_inner, *inner_terms, z_inner = call(
        second_inner_kernel, (shape_of(*inner),) * 3 + (shape_of(4, 8, 128),)
    )(s, x_got, packed, scalar, velocity, mass, near)
    args = (s, x_got, packed, *y_got, scalar, velocity, mass, near, g_inner)
    some = (16, 16, 128)
    x, *faces = call(
        second_face_kernel,
        (shape_of(2, 1, 64, 128, dtype=BF16),) + (shape_of(*some),) * 3 + (shape_of(2, 8, 128),),
    )(*args)
    g, *outer_terms, z = call(
        second_outer_kernel,
        (shape_of(*flat), shape_of(*outer), shape_of(*outer), shape_of(4, 8, 128)),
        scratch_shapes=[pltpu.VMEM(outer, F32)],
    )(*args, z_inner, *faces)

    x_got = swap_axial(x)
    early = call(
        early_kernel,
        shape_of(192, 128 * cameras, dtype=BF16),
        scratch_shapes=[pltpu.VMEM((192, 512), BF16)],
    )(g, *inner_terms, near, weights)
    x_got, early = lax.optimization_barrier((x_got, early))
    *z, x_got = call(
        second_radial_kernel, (half(32, 128), half(64, 128), shape_of(2, 1, 64, 128))
    )(z, x_got, pixel_block, ids_got)
    z_got = swap_both(*z, "cam")
    pixels = call(
        middle_kernel,
        shape_of(cameras, 128, 128),
        scratch_shapes=[pltpu.VMEM((192, 512), BF16)],
    )(g, x_got, *inner_terms, near, weights, picks, early)
    z_got, pixels = lax.optimization_barrier((z_got, pixels))
    *y, packed = call(
        part(azimuth_kernel, n_cam), (half(32, 128), half(32, 128), shape_of(4, 8, 128))
    )(g, x_got, *z_got)
    y_got = swap_both(*y, "ey")
    packed, ids = lax.optimization_barrier((packed, (ids_got, z_got[1])))
    onehot = call(
        part(block_kernel, share),
        half(share, NBLK, 128 * n_cam),
        scratch_shapes=[pltpu.VMEM((n_cam, cameras, 128), jnp.int32)],
    )(pixel_block, *ids)
    advected, pixels = call(
        render_inner_kernel,
        (shape_of(*flat), shape_of(cameras, 128, 128)),
        out_specs=(HBM, VMEM),
        scratch_shapes=[
            pltpu.VMEM(inner, F32),
            pltpu.VMEM((64, 512), F32),
            pltpu.SemaphoreType.DMA,
        ],
    )(g, x_got, packed, *inner_terms, near, weights, picks, pixels)
    y_got, onehot = lax.optimization_barrier((y_got, onehot))
    payload_shape = half(share, 128, 128)
    advected, values, *far = call(
        part(render_far_kernel, n_cam),
        (shape_of(*flat), shape_of(cameras, 128, 128, dtype=BF16)) + (payload_shape,) * (n_cam - 2),
        in_specs=[VMEM] * 11 + [HBM],
        out_specs=(HBM, VMEM) + (VMEM,) * (n_cam - 2),
        input_output_aliases={11: 0},
        scratch_shapes=[
            pltpu.VMEM(outer, F32),
            pltpu.VMEM((128, 512), BF16),
            pltpu.SemaphoreType.DMA((2,)),
        ],
    )(g, x_got, packed, *y_got, *outer_terms, near, weights, picks, pixels, advected)
    parts = (values, picks, pixels)
    image_shape = shape_of(share, NBLK, 128)
    images = call(
        part(own_image_kernel, n_cam),
        image_shape,
        scratch_shapes=[pltpu.VMEM(payload_shape.shape, BF16)],
    )(*parts, onehot)
    images, parts = lax.optimization_barrier((images, parts))
    beside = call(part(render_near_kernel, n_cam, 1), payload_shape)(*parts)
    received = []
    for d, payload in [(1, beside)] + [(n + 2, p) for n, p in enumerate(far)]:
        received.append(lax.ppermute(payload, "cam", [(i, i ^ d) for i in range(n_cam)]))
    images = call(
        image_kernel,
        image_shape,
        out_specs=HBM,
        scratch_shapes=[
            pltpu.VMEM((share, NBLK, 128), F32),
            pltpu.SemaphoreType.DMA((4 * share,)),
        ],
    )(images, onehot, *received)
    return (advected.reshape(shape), images)


def solution(mesh):
    placed = (
        P("ex", None, "ey", None, "cam"),
        P(None, "ex", None, "ey", None, "cam"),
        P("ex", None, "ey", None, "cam"),
        P(),
        P(None, ("cam", "ex", "ey")),
        P(None, ("cam", "ex", "ey")),
    )
    return jax.shard_map(
        per_device,
        mesh=mesh,
        in_specs=placed,
        out_specs=(P("ex", None, "ey", None, "cam"), P("cam", ("ex", "ey"), None)),
        check_vma=False,
    )
```

```python
import functools

import jax
import jax.numpy as jnp
import numpy as np
from jax import lax
from jax.experimental import pallas as pl
from jax.experimental.pallas import tpu as pltpu
from jax.sharding import PartitionSpec as P

NBLK = 1024
F32 = jnp.float32
BF16 = jnp.bfloat16
VMEM = pl.BlockSpec(memory_space=pltpu.VMEM)
HBM = pl.BlockSpec(memory_space=pltpu.HBM)
time_step = 0.01


def legendre_seven(points):
    previous = points * 0.0 + 1.0
    current = points * 1.0
    for order in range(1, 7):
        following = ((2 * order + 1) * points * current - order * previous) / (order + 1)
        previous = current
        current = following
    return current


def gll_derivative():
    degree = 7
    gll_nodes = np.array(
        [
            -1.0,
            -0.8717401485096066,
            -0.5917001814331423,
            -0.2092992179024789,
            0.2092992179024789,
            0.5917001814331423,
            0.8717401485096066,
            1.0,
        ]
    )
    values = legendre_seven(gll_nodes)
    derivative = np.zeros((degree + 1, degree + 1))
    for target in range(degree + 1):
        for source in range(degree + 1):
            if target != source:
                derivative[target, source] = values[target] / (
                    values[source] * (gll_nodes[target] - gll_nodes[source])
                )
    derivative[0, 0] = -degree * (degree + 1) / 4.0
    derivative[degree, degree] = degree * (degree + 1) / 4.0
    return derivative


def split_two(table):
    high = table.astype(np.float32).astype(BF16)
    low = (table - high.astype(np.float64)).astype(np.float32).astype(BF16)
    return high, low


def derivative_tables():
    derivative = gll_derivative()
    eye = np.eye(8)
    rows = np.concatenate([np.kron(derivative, eye), np.kron(eye, derivative)], axis=0)
    high, low = split_two(rows)
    row_table = np.concatenate([high, high, low, np.zeros_like(high)], axis=1)
    high, low = split_two(np.kron(np.eye(16), derivative.T))
    lane_table = np.concatenate(
        [
            np.concatenate([high, low], axis=1),
            np.concatenate([high, np.zeros_like(high)], axis=1),
        ],
        axis=0,
    )
    swap = np.zeros((128, 128))
    for c in range(15):
        swap[8 * c + 7, 8 * c + 8] = 1.0
        swap[8 * c + 8, 8 * c + 7] = 1.0
    join_table = np.concatenate([swap, swap], axis=0).astype(np.float32).astype(BF16)
    spread = np.zeros((128, 128))
    spread[0, 0::2] = 1.0
    spread[127, 1::2] = 1.0
    turn = np.zeros((64, 256))
    for k in range(4):
        for c in range(16):
            turn[16 * k + c, 8 * c + 2 * k] = 1.0
            turn[16 * k + c, 128 + 8 * c + 2 * k + 1] = 1.0
    ends = turn.reshape(4, 16, 256)[:, ::15].reshape(8, 256)
    ends = np.concatenate([ends, np.zeros_like(ends)], axis=0)
    partial = np.zeros((16, 64))
    for i in range(8):
        partial[i, 8 * i + 1 : 8 * i + 8] = derivative[0, 1:]
        partial[8 + i, 8 * i : 8 * i + 7] = derivative[7, :7]
    high, low = split_two(partial)
    partial = np.concatenate([high, high, low, np.zeros_like(high)], axis=1)
    exact = [spread, spread, turn[:, :128], turn[:, 128:], ends[:, :128], ends[:, 128:]]
    exact = np.concatenate(exact, axis=0)
    split = [row_table[:, :128], row_table[:, 128:], lane_table[:, :128], lane_table[:, 128:]]
    split += [join_table, exact.astype(np.float32).astype(BF16)]
    split += [partial[:, :128], partial[:, 128:]]
    return jnp.asarray(np.concatenate(split, axis=0))


def row_table(table_ref, first=0):
    high, low = table_ref[first:128], table_ref[128 + first : 256]
    return jnp.concatenate([high, low[:, :64]], axis=1)


def lane_table(table_ref):
    return jnp.concatenate([table_ref[256:512], table_ref[512:768]], axis=1)


def join_table(table_ref):
    return jnp.concatenate([table_ref[768:1024], table_ref[1024:1280]], axis=1)


def turn_table(table_ref):
    return jnp.concatenate([table_ref[1280:1344], table_ref[1344:1408]], axis=1)


def end_table(table_ref):
    return jnp.concatenate([table_ref[1408:1424], table_ref[1424:1440]], axis=1)


def partial_table(table_ref):
    return jnp.concatenate([table_ref[1440:1456], table_ref[1456:1472][:, :64]], axis=1)


def span_of(a, offset=0):
    if isinstance(a, int):
        return slice(8 * a + offset, 8 * a + offset + 8)
    return pl.ds(pl.multiple_of(a * 8 + offset, 8), 8)


def sweep(body, together):
    if together == 4:
        for a in range(4):
            body(a)
        return

    def step(n, carry):
        for m in range(together):
            body(n * together + m)
        return carry

    lax.fori_loop(0, 4 // together, step, 0)


def lane_ids(shape):
    return lax.broadcasted_iota(jnp.int32, shape, len(shape) - 1)


def row_ids(shape):
    return lax.broadcasted_iota(jnp.int32, shape, len(shape) - 2)


def halves(value):
    high = value.astype(BF16)
    return high, (value - high.astype(F32)).astype(BF16)


def dot(a, b):
    return jnp.dot(a, b, preferred_element_type=F32)


def by_lanes(pairs, table_ref):
    rows = jnp.concatenate([jnp.concatenate(p, axis=1) for p in pairs], axis=0)
    both = dot(rows, lane_table(table_ref))
    return both[:, :128] + both[:, 128:]


def join_lanes(values, table_ref):
    rows = jnp.concatenate([jnp.concatenate(halves(v), axis=1) for v in values], axis=0)
    other = dot(rows, join_table(table_ref))
    joined, spread, at = [], [], 0
    for v in values:
        span = slice(at, at + v.shape[0])
        joined.append(v + other[span, :128])
        spread.append(other[span, 128:])
        at += v.shape[0]
    return joined, spread


def join_rows(value):
    row = row_ids(value.shape)
    last = ((row & 7) == 7) & (row != 63)
    first = ((row & 7) == 0) & (row != 0)
    other = jnp.where(
        last, pltpu.roll(value, 63, 0), jnp.where(first, pltpu.roll(value, 1, 0), 0.0)
    )
    return value + other


def convect_pair(fields, velocities, masses, table_ref):
    pairs = [halves(f) for f in fields]
    high = jnp.concatenate([p[0] for p in pairs], axis=1)
    low = jnp.concatenate([p[1] for p in pairs], axis=1)
    stacked = jnp.concatenate([high, low, high], axis=0)
    rows = dot(row_table(table_ref), stacked)
    radius = by_lanes(pairs, table_ref)
    out = []
    for n in range(2):
        lanes = slice(128 * n, 128 * n + 128)
        v = velocities[n]
        slope = v[0] * rows[:64, lanes] + v[1] * rows[64:, lanes]
        out.append(masses[n] * (slope + v[2] * radius[64 * n : 64 * n + 64]))
    return out


def face_kernel(
    scalar_hbm, velocity_hbm, mass_hbm, table_hbm, x_ref, table_ref, f_ref, v_ref, m_ref, sems,
):
    copies = []

    def start(source, target):
        copy = pltpu.make_async_copy(source, target, sems.at[len(copies)])
        copy.start()
        copies.append(copy)

    last = scalar_hbm.shape[0] - 1
    start(scalar_hbm.at[pl.ds(last - 7, 8)], f_ref.at[0])
    start(scalar_hbm.at[pl.ds(0, 8)], f_ref.at[1])
    start(table_hbm, table_ref)
    start(velocity_hbm.at[:, last], v_ref.at[0])
    start(velocity_hbm.at[:, 0], v_ref.at[1])
    start(mass_hbm.at[last], m_ref.at[0])
    start(mass_hbm.at[0], m_ref.at[1])
    for copy in copies[:3]:
        copy.wait()
    derivative = gll_derivative()
    fields = [f_ref[0, 7], f_ref[1, 0]]
    pairs = [halves(f) for f in fields]
    high = jnp.concatenate([p[0] for p in pairs], axis=1)
    low = jnp.concatenate([p[1] for p in pairs], axis=1)
    azimuth = dot(row_table(table_ref, 64), jnp.concatenate([high, low, high], axis=0))
    radius = by_lanes(pairs, table_ref)
    for copy in copies[3:]:
        copy.wait()
    values = []
    for n, node in enumerate((7, 0)):
        axial = f_ref[n, 0] * float(derivative[node, 0])
        for p in range(1, 8):
            axial = axial + f_ref[n, p] * float(derivative[node, p])
        slope = v_ref[n, 0] * axial + v_ref[n, 1] * azimuth[:, 128 * n : 128 * n + 128]
        values.append(m_ref[n] * (slope + v_ref[n, 2] * radius[64 * n : 64 * n + 64]))
        values.append(m_ref[n])
    for n, value in enumerate(join_lanes(values, table_ref)[0]):
        x_ref[n // 2, n % 2] = join_rows(value).astype(BF16)


def join_block(s_ref):
    for b in range(s_ref.shape[1] // 8 - 1):
        total = s_ref[:, 8 * b + 7, :] + s_ref[:, 8 * b + 8, :]
        s_ref[:, 8 * b + 7, :] = total
        s_ref[:, 8 * b + 8, :] = total
    join_axial(s_ref)


def join_axial(s_ref):
    for f in range(s_ref.shape[0] // 32):
        for a in range(3):
            at = 32 * f + 8 * a + 7
            total = s_ref[at] + s_ref[at + 1]
            s_ref[at] = total
            s_ref[at + 1] = total


def pack_blocks(blocks):
    slot = ((lane_ids((8, 128)) + 1) >> 1) & 63
    parts = [jnp.zeros((8, 128), F32) for _ in range(4)]
    for n, (u, block) in enumerate(blocks):
        if u:
            block = pltpu.roll(block, 2 * u, 1)
        parts[n % 4] = jnp.where(slot == u, block, parts[n % 4])
    return (parts[0] + parts[1]) + (parts[2] + parts[3])


def pick_spread(spreads):
    slot = ((lane_ids((8, 128)) + 1) >> 1) & 63
    parts = [jnp.zeros((8, 128), F32) for _ in range(2)]
    for b, spread in spreads:
        for i in range(8):
            block = spread[8 * i : 8 * i + 8]
            parts[i % 2] = jnp.where(slot == 56 - 8 * i + b, block, parts[i % 2])
    return parts[0] + parts[1]


def join_packed(packed):
    lane, row = lane_ids((8, 128)), row_ids((8, 128))
    slot = ((lane + 1) >> 1) & 63
    b = slot & 7
    rows = []
    for value in packed:
        after = pltpu.roll(pltpu.roll(value, 126, 1), 7, 0)
        before = pltpu.roll(pltpu.roll(value, 2, 1), 1, 0)
        value = value + jnp.where((row == 7) & (b < 7), after, 0.0)
        rows.append(value + jnp.where((row == 0) & (b > 0), before, 0.0))
    out = list(rows)
    for a in range(3):
        out[a] = out[a] + jnp.where(slot < 8, pltpu.roll(rows[a + 1], 16, 1), 0.0)
        out[a + 1] = out[a + 1] + jnp.where(slot >= 56, pltpu.roll(rows[a], 112, 1), 0.0)
    return out


def first_kernel(scalar_ref, velocity_ref, mass_ref, table_ref, s_ref, z_ref):
    def body(a):
        at = span_of(a)
        spreads = [[], []]
        for pair in range(4):
            spans = [slice(16 * pair + 8 * n, 16 * pair + 8 * n + 8) for n in range(2)]
            fields = [scalar_ref[at, s, :].reshape(64, 128) for s in spans]
            velocities = [
                [velocity_ref[d, at, s, :].reshape(64, 128) for d in range(3)] for s in spans
            ]
            masses = [mass_ref[at, s, :].reshape(64, 128) for s in spans]
            values = convect_pair(fields, velocities, masses, table_ref)
            joined, spread = join_lanes(values + masses, table_ref)
            for n, s in enumerate(spans):
                for f in range(2):
                    s_ref[span_of(a, 32 * f), s, :] = joined[n + 2 * f].reshape(8, 8, 128)
                    spreads[f].append((2 * pair + n, spread[n + 2 * f]))
        for f in range(2):
            z_ref[a + 4 * f] = pick_spread(spreads[f])

    sweep(body, 2)
    join_block(s_ref)
    for f in range(2):
        for n, value in enumerate(join_packed([z_ref[4 * f + a] for a in range(4)])):
            z_ref[4 * f + n] = value


def radial_faces(count, z_in, x_in, x_ref):
    x_ref[...] = x_in[...].astype(F32)
    rows = []
    for f in range(count):
        spans = [slice(8 * b, 8 * b + 8) for b in range(8)]
        low = pack_blocks([(56 + b, x_ref[0, f, s, :]) for b, s in enumerate(spans)])
        high = pack_blocks([(b, x_ref[1, f, s, :]) for b, s in enumerate(spans)])
        rows += [z_in[4 * f] + low, z_in[4 * f + 1], z_in[4 * f + 2], z_in[4 * f + 3] + high]
    return jnp.concatenate(rows, axis=0).astype(BF16)


def id_tile(block_ref):
    ids = block_ref[...]
    return jnp.concatenate([ids >> 5, ids & 31], axis=0).astype(F32).astype(BF16)


def first_radial_kernel(z_in, x_in, block_ref, one_ref, two_ref, x_ref):
    faces = radial_faces(2, z_in, x_in, x_ref)
    one_ref[:64, :] = faces
    one_ref[64:, :] = id_tile(block_ref)
    two_ref[...] = faces


def second_radial_kernel(z_in, x_in, block_ref, got_ref, one_ref, two_ref, x_ref):
    faces = radial_faces(1, z_in, x_in, x_ref)
    one_ref[...] = faces
    two_ref[:32, :] = faces
    two_ref[32:48, :] = id_tile(block_ref)
    two_ref[48:, :] = got_ref[64:, :]


def merged(one, two, cam_count):
    me = lax.axis_index("cam")
    even = (me & 1) == 0
    left = jnp.where(even, two, one)
    right = jnp.where(even, one, two)
    left = jnp.where(me == 0, 0.0, left)
    right = jnp.where(me == cam_count - 1, 0.0, right)
    lane = lane_ids((8, 128))
    return jnp.where((lane & 1) == 0, pltpu.roll(left, 1, 1), pltpu.roll(right, 127, 1))


def end_lanes(shape):
    lane = lane_ids(shape)
    return (lane == 0) | (lane == 127)


def azimuth_kernel(
    cam_count, s_ref, x_ref, one_ref, two_ref, scalar_ref, velocity_ref, mass_ref, table_ref,
    even_ref, odd_ref, packed_ref,
):
    ends = end_lanes((8, 128))
    row = row_ids((8, 128))
    even = (lax.axis_index("ey") & 1) == 0
    count = s_ref.shape[0]
    one = one_ref[:count, :].astype(F32)
    two = two_ref[:count, :].astype(F32)
    low, high = [], []
    for q in range(count // 8):
        at = slice(8 * q, 8 * q + 8)
        packed = merged(one[at], two[at], cam_count)
        packed_ref[q] = packed
        f, a = q // 4, q % 4
        for line, shift, faces in ((0, 16, low), (63, 2, high)):
            j = line & 7
            spread = jnp.broadcast_to(packed[j : j + 1, :], (8, 128))
            moved = pltpu.roll(spread, shift, 1, stride=16, stride_axis=0)
            face = s_ref[at, line, :] + jnp.where(ends, moved, 0.0)
            if a == 0:
                face = face + jnp.where(row == 0, x_ref[0, f, line : line + 1, :], 0.0)
            if a == 3:
                face = face + jnp.where(row == 7, x_ref[1, f, line : line + 1, :], 0.0)
            faces.append(face)
    slopes = [[], []]
    for a in range(4):
        pairs = []
        for b in (0, 7):
            g = assembled(s_ref, x_ref, packed_ref[a], 0, a, b)
            m = assembled(s_ref, x_ref, packed_ref[a + 4], 1, a, b)
            scalar = scalar_ref[span_of(a), 8 * b : 8 * b + 8, :].reshape(64, 128)
            pairs.append(halves(scalar - (time_step / m) * g))
        tops = jnp.concatenate([p[0] for p in pairs], axis=1)
        rests = jnp.concatenate([p[1] for p in pairs], axis=1)
        both = dot(partial_table(table_ref), jnp.concatenate([tops, rests, tops], axis=0))
        slopes[0].append(both[:8, :128])
        slopes[1].append(both[8:, 128:])
    messages = []
    for faces, line, slope in ((low, 0, slopes[0]), (high, 63, slopes[1])):
        flow = [mass_ref[:, line, :] * velocity_ref[d, :, line, :] for d in range(3)]
        share = flow[1] * jnp.concatenate(slope, axis=0)
        rows = faces + [share] + flow + [scalar_ref[:, line, :]]
        messages.append(jnp.concatenate(rows, axis=0))
    even_ref[...] = jnp.where(even, messages[1], messages[0]).astype(BF16)
    odd_ref[...] = jnp.where(even, messages[0], messages[1]).astype(BF16)


def unpacked(packed, b):
    ends = end_lanes((8, 128))
    rows = []
    for i in range(8):
        u = 56 - 8 * i + b
        moved = pltpu.roll(packed, (128 - 2 * u) % 128, 1) if u else packed
        rows.append(jnp.where(ends, moved, 0.0))
    return rows


def assembled(s_ref, x_ref, packed, f, a, b, y_refs=None):
    span = slice(8 * b, 8 * b + 8)
    at = span_of(a, 32 * f)
    block = s_ref[at, span, :]
    if packed is None:
        rows = [jnp.zeros((8, 128), F32) for _ in range(8)]
    else:
        rows = unpacked(packed, b)
    if not isinstance(a, int):
        rows[0] = rows[0] + jnp.where(a == 0, x_ref[0, f, span, :], 0.0)
        rows[7] = rows[7] + jnp.where(a == 3, x_ref[1, f, span, :], 0.0)
    elif a == 0:
        rows[0] = rows[0] + x_ref[0, f, span, :]
    elif a == 3:
        rows[7] = rows[7] + x_ref[1, f, span, :]
    if y_refs is not None:
        one_ref, two_ref = y_refs
        even = (lax.axis_index("ey") & 1) == 0
        at = slice(16 * (a // 2) + 32 * f, 16 * (a // 2) + 32 * f + 16)
        one, two = one_ref[at, :].astype(F32), two_ref[at, :].astype(F32)
        if b == 0:
            line, sublane = jnp.where(even, two, one), 0
        else:
            line, sublane = jnp.where(even, one, two), 7
        line = line[8 * (a % 2) : 8 * (a % 2) + 8]
        node = lax.broadcasted_iota(jnp.int32, (8, 8, 128), 1)
        block = block + jnp.where(node == sublane, line[:, None, :], 0.0)
    return block.reshape(64, 128) + jnp.concatenate(rows, axis=0)


def second_pairs(
    pairs, s_ref, x_ref, packed_ref, y_refs, scalar_ref, velocity_ref,
    mass_ref, table_ref, g_ref, base_ref, half_ref, z_ref, first_ref=None,
):
    def body(a, layer=None):
        at = span_of(a)
        layer = a if layer is None else layer
        to = span_of(layer)
        radial_g = packed_ref[a]
        radial_m = packed_ref[a + 4]
        spreads = []
        for n, pair in enumerate(pairs):
            fields, velocities, masses = [], [], []
            for h, b in enumerate(pair):
                s = slice(8 * b, 8 * b + 8)
                out = slice(16 * n + 8 * h, 16 * n + 8 * h + 8)
                g = assembled(s_ref, x_ref, radial_g, 0, a, b, y_refs)
                m = assembled(s_ref, x_ref, radial_m, 1, a, b, y_refs)
                scale = time_step / m
                scalar = scalar_ref[at, s, :].reshape(64, 128)
                first = scalar - scale * g
                base_ref[to, out, :] = (0.5 * (scalar + first)).reshape(8, 8, 128)
                half_ref[to, out, :] = (0.5 * scale).reshape(8, 8, 128)
                fields.append(first)
                if first_ref is not None:
                    first_ref[to, out, :] = first.reshape(8, 8, 128)
                velocities.append(
                    [velocity_ref[d, at, s, :].reshape(64, 128) for d in range(3)]
                )
                masses.append(mass_ref[at, s, :].reshape(64, 128))
            values = convect_pair(fields, velocities, masses, table_ref)
            joined, spread = join_lanes(values, table_ref)
            for h, b in enumerate(pair):
                out = slice(16 * n + 8 * h, 16 * n + 8 * h + 8)
                g_ref[to, out, :] = joined[h].reshape(8, 8, 128)
                spreads.append((b, spread[h]))
        z_ref[layer] = pick_spread(spreads)

    return body


def second_inner_kernel(
    s_ref, x_ref, packed_ref, scalar_ref, velocity_ref, mass_ref,
    table_ref, g_ref, base_ref, half_ref, z_ref,
):
    body = second_pairs(
        ((1, 2), (3, 4), (5, 6)), s_ref, x_ref, packed_ref, None,
        scalar_ref, velocity_ref, mass_ref, table_ref, g_ref, base_ref, half_ref, z_ref,
    )
    sweep(body, 2)
    join_block(g_ref)


def add_beyond(layers, y_one_ref, y_two_ref, first_ref, scalar_ref, table_ref, g_ref, z_ref):
    even = (lax.axis_index("ey") & 1) == 0
    one, two = y_one_ref[64:, :].astype(F32), y_two_ref[64:, :].astype(F32)
    sides = (jnp.where(even, two, one), jnp.where(even, one, two))
    rows = []
    for h, (line, outer) in enumerate(((0, 0), (15, 63))):
        for a, n in layers:
            change = first_ref[span_of(n), line, :] - scalar_ref[span_of(a), outer, :]
            rows.append(sides[h][128 + 8 * a : 136 + 8 * a] + change)
    count = len(layers)
    field = jnp.concatenate(rows + [jnp.zeros((64 - 16 * count, 128), F32)], axis=0)
    high, low = halves(field)
    axial = dot(row_table(table_ref, 64), jnp.concatenate([high, low, high], axis=0))
    radius = by_lanes([(high, low)], table_ref)
    corner = float(gll_derivative()[7, 7])
    values = []
    for h, sign in ((0, corner), (1, -corner)):
        for k, (a, _) in enumerate(layers):
            at = slice(8 * (count * h + k), 8 * (count * h + k) + 8)
            share, *flow = [sides[h][32 * n + 8 * a : 32 * n + 8 * a + 8] for n in range(4)]
            azimuth = sign * field[at]
            values.append(share + flow[0] * axial[at] + flow[1] * azimuth + flow[2] * radius[at])
    (joined,), (spread,) = join_lanes([jnp.concatenate(values, axis=0)], table_ref)
    slot = ((lane_ids((8, 128)) + 1) >> 1) & 63
    row = row_ids((8, 128))
    for h, line in ((0, 0), (1, 15)):
        for k, (_, n) in enumerate(layers):
            at = slice(8 * (count * h + k), 8 * (count * h + k) + 8)
            g_ref[span_of(n), line, :] = g_ref[span_of(n), line, :] + joined[at]
            mine = jnp.where(slot == 56 - 8 * row + 7 * h, spread[at], 0.0)
            total = jnp.sum(mine, axis=0, keepdims=True)
            z_ref[n] = z_ref[n] + jnp.where(row == 7 * h, total, 0.0)


def second_face_kernel(
    s_ref, x_ref, packed_ref, y_one_ref, y_two_ref, scalar_ref, velocity_ref,
    mass_ref, table_ref, inner_ref, x_out_ref, edge_ref, base_ref, half_ref, z_ref, first_ref,
):
    body = second_pairs(
        ((0, 7),), s_ref, x_ref, packed_ref, (y_one_ref, y_two_ref), scalar_ref, velocity_ref,
        mass_ref, table_ref, edge_ref, base_ref, half_ref, z_ref, first_ref,
    )
    body(0, 0)
    body(3, 1)
    add_beyond(((0, 0), (3, 1)), y_one_ref, y_two_ref, first_ref, scalar_ref, table_ref, edge_ref, z_ref)
    row = row_ids((64, 128))
    for n, (layer, at) in enumerate(((15, 31), (0, 0))):
        face = jnp.concatenate(
            [edge_ref[layer, 0:8, :], inner_ref[at], edge_ref[layer, 8:16, :]], axis=0
        )
        after = jnp.where((row == 7) | (row == 55), pltpu.roll(face, 63, 0), 0.0)
        before = jnp.where((row == 8) | (row == 56), pltpu.roll(face, 1, 0), 0.0)
        x_out_ref[n, 0] = (face + (after + before)).astype(BF16)


def second_outer_kernel(
    s_ref, x_ref, packed_ref, y_one_ref, y_two_ref, scalar_ref, velocity_ref,
    mass_ref, table_ref, inner_ref, z_in, edge_in, base_in, half_in, z_face,
    g_ref, base_ref, half_ref, z_ref, edge_ref, first_ref,
):
    body = second_pairs(
        ((0, 7),), s_ref, x_ref, packed_ref, (y_one_ref, y_two_ref), scalar_ref, velocity_ref,
        mass_ref, table_ref, edge_ref, base_ref, half_ref, z_ref, first_ref,
    )
    body(1)
    body(2)
    add_beyond(((1, 1), (2, 2)), y_one_ref, y_two_ref, first_ref, scalar_ref, table_ref, edge_ref, z_ref)
    for layer, a in ((0, 0), (1, 3)):
        for source, target in ((edge_in, edge_ref), (base_in, base_ref), (half_in, half_ref)):
            target[span_of(a)] = source[span_of(layer)]
        z_ref[a] = z_face[layer]
    join_axial(edge_ref)
    g_ref[:, 0:8, :] = edge_ref[:, 0:8, :]
    g_ref[:, 8:56, :] = inner_ref[...]
    g_ref[:, 56:64, :] = edge_ref[:, 8:16, :]
    for low in (7, 55):
        total = g_ref[:, low, :] + g_ref[:, low + 1, :]
        g_ref[:, low, :] = total
        g_ref[:, low + 1, :] = total
    for n, value in enumerate(join_packed([z_ref[a] + z_in[a] for a in range(4)])):
        z_ref[n] = value


def weight_kernel(weight_ref, out_ref):
    row = row_ids((512, 512))
    source = (row & 63) * 8 + (row >> 6)
    order = jnp.where(lane_ids((512, 512)) == source, 1.0, 0.0).astype(BF16)
    for m in range(8):
        out_ref[:, 128 * m : 128 * m + 128] = dot(order, weight_ref[m]).astype(BF16)


def pick_kernel(cut_ref, pick_ref):
    cut = cut_ref[...]
    a, b, c = cut >> 7, (cut >> 4) & 7, cut & 15
    order = jnp.where(a == 0, 2, jnp.where(a == 3, 3, a - 1))
    inner = 128 * order + 16 * b + c
    ends = 512 + 16 * a + 2 * b + (c >> 3)
    place = jnp.where((c == 0) | (c == 15), ends, inner)
    turned = place.astype(F32).T.astype(jnp.int32)
    lane = lane_ids((128, 640))
    for m in range(8):
        pick_ref[m] = jnp.where(lane == turned[:, m : m + 1], 1.0, 0.0).astype(BF16)


def turn(blocks, table):
    rows = []
    for block in blocks:
        value = block.astype(BF16)
        zero = jnp.zeros_like(value)
        rows.append(jnp.concatenate([value, zero], axis=1))
        rows.append(jnp.concatenate([zero, value], axis=1))
    return lax.dot_general(
        table,
        jnp.concatenate(rows, axis=0),
        (((1,), (1,)), ((), ())),
        preferred_element_type=F32,
    )


PAIRS = ((0, 1), (2, 3), (4, 5), (6, 7))


def term(refs, a, b):
    inner_ref, outer_ref = refs
    at = span_of(a)
    if b in (0, 7):
        return outer_ref[at, 8 * (b // 7) : 8 * (b // 7) + 8, :].reshape(64, 128)
    return inner_ref[at, 8 * b - 8 : 8 * b, :].reshape(64, 128)


def advanced(g_ref, x_ref, packed, bases, halfs, a, pair):
    blocks = []
    for b in pair:
        g = assembled(g_ref, x_ref, packed, 0, a, b)
        blocks.append(term(bases, a, b) - term(halfs, a, b) * g)
    return blocks


def store_elements(element_ref, blocks, table_ref, place):
    turned = turn(blocks, turn_table(table_ref)).astype(BF16)
    for h in range(2):
        for k in range(4):
            element_ref[place + 16 * h : place + 16 * h + 16, 128 * k : 128 * k + 128] = turned[
                16 * k : 16 * k + 16, 128 * h : 128 * h + 128
            ]


def pixel_values(element_ref, weight_ref, m):
    return dot(element_ref[...], weight_ref[:, 256 * m : 256 * m + 256]).astype(BF16)


def layer_elements(layers, g_ref, x_ref, bases, halfs, table_ref, element_ref):
    place = 0
    for a in layers:
        for pair in PAIRS:
            blocks = advanced(g_ref, x_ref, None, bases, halfs, a, pair)
            store_elements(element_ref, blocks, table_ref, place)
            place += 32


def early_kernel(
    g_ref, base_one, half_one, base_two, half_two, table_ref, weight_ref, value_ref, element_ref
):
    bases, halfs = (base_one, base_two), (half_one, half_two)
    layer_elements((1, 2), g_ref, None, bases, halfs, table_ref, element_ref)
    for m in range(4):
        value_ref[:, 256 * m : 256 * m + 256] = pixel_values(element_ref, weight_ref, m)


def middle_kernel(
    g_ref, x_ref, base_one, half_one, base_two, half_two, table_ref, weight_ref, pick_ref,
    early_ref, pixel_ref, element_ref,
):
    bases, halfs = (base_one, base_two), (half_one, half_two)
    layer_elements((0, 3), g_ref, x_ref, bases, halfs, table_ref, element_ref)
    for m in range(4):
        late = pixel_values(element_ref, weight_ref, m)
        both = jnp.concatenate([early_ref[:, 256 * m : 256 * m + 256], late], axis=0)
        for n in range(2):
            pixel_ref[2 * m + n] = dot(
                pick_ref[2 * m + n, :, :512], both[:, 128 * n : 128 * n + 128]
            )


def fill_payload(payload_ref, d, cam_count, pick_ref, value_ref, pixel_ref):
    me = lax.axis_index("cam")
    share = pixel_ref.shape[0] // cam_count
    for n in range(share):
        m = share * (me ^ d) + n
        values = dot(pick_ref[m, :, 512:576], value_ref[m]) + pixel_ref[m]
        payload_ref[n] = values.astype(BF16)


def render_far_kernel(
    cam_count, g_ref, x_ref, one_ref, two_ref, base_one, half_one, base_two, half_two,
    table_ref, weight_ref, pick_ref, pixel_ref, out_hbm, value_ref, *rest,
):
    payload_refs = rest[: cam_count - 2]
    advected_ref, end_ref, sem = rest[cam_count - 2 :]
    bases, halfs = (base_one, base_two), (half_one, half_two)
    one, two = one_ref[:32, :].astype(F32), two_ref[:32, :].astype(F32)
    for a in range(4):
        packed = merged(one[8 * a : 8 * a + 8], two[8 * a : 8 * a + 8], cam_count)
        for n, pair in enumerate(PAIRS):
            blocks = advanced(g_ref, x_ref, packed, bases, halfs, a, pair)
            turned = turn(blocks, end_table(table_ref))
            for h, b in enumerate(pair):
                advected_ref[span_of(a), 8 * b : 8 * b + 8, :] = blocks[h].reshape(8, 8, 128)
                place = 16 * a + 2 * b
                for k in range(4):
                    end_ref[place : place + 2, 128 * k : 128 * k + 128] = turned[
                        2 * k : 2 * k + 2, 128 * h : 128 * h + 128
                    ]
    copy = pltpu.make_async_copy(advected_ref, out_hbm, sem)
    copy.start()
    ends = end_ref[...].astype(BF16)
    for m in range(pixel_ref.shape[0] // 2):
        values = dot(ends, weight_ref[:, 256 * m : 256 * m + 256]).astype(BF16)
        value_ref[2 * m] = values[:, :128]
        value_ref[2 * m + 1] = values[:, 128:]
    for d in range(2, cam_count):
        fill_payload(payload_refs[d - 2], d, cam_count, pick_ref, value_ref, pixel_ref)
    copy.wait()


def render_near_kernel(cam_count, d, value_ref, pick_ref, pixel_ref, payload_ref):
    fill_payload(payload_ref, d, cam_count, pick_ref, value_ref, pixel_ref)


def own_image_kernel(
    cam_count, value_ref, pick_ref, pixel_ref, block_ref, first_ref, second_ref,
    image_ref, onehot_ref, payload_ref, id_ref,
):
    me = lax.axis_index("cam")
    share = image_ref.shape[0]
    id_ref[0] = block_ref[...]
    tiles = ((1, first_ref[64:80, :]), (3, second_ref[32:48, :]), (2, second_ref[48:64, :]))
    for d, tile in tiles:
        ids = tile.astype(F32).astype(jnp.int32)
        id_ref[d] = ids[:8] * 32 + ids[8:]
    fill_payload(payload_ref, 0, cam_count, pick_ref, value_ref, pixel_ref)
    for m in range(share):
        ids = [id_ref[d, pl.ds(share * me + m, 1), :] for d in range(4)]
        ids = jnp.concatenate(ids, axis=1)
        for chunk in range(4):
            at = slice(256 * chunk, 256 * chunk + 256)
            row = row_ids((256, ids.shape[1])) + 256 * chunk
            onehot = jnp.where(row == ids, 1.0, 0.0).astype(BF16)
            onehot_ref[m, at, :] = onehot
            image_ref[m, at, :] = dot(onehot[:, :128], payload_ref[m])


def image_kernel(own_ref, onehot_ref, *refs):
    payload_refs, (image_hbm, image_ref, sems) = refs[:-3], refs[-3:]
    copies = []
    for m in range(image_ref.shape[0]):
        values = jnp.concatenate([payload_ref[m] for payload_ref in payload_refs], axis=0)
        for chunk in range(4):
            at = slice(256 * chunk, 256 * chunk + 256)
            image_ref[m, at, :] = own_ref[m, at, :] + dot(onehot_ref[m, at, 128:], values)
            copy = pltpu.make_async_copy(
                image_ref.at[m, at], image_hbm.at[m, at], sems.at[4 * m + chunk]
            )
            copy.start()
            copies.append(copy)
    for copy in copies:
        copy.wait()


def call(kernel, out_shape, flops=10**8, size=10**7, **options):
    return pl.pallas_call(
        kernel,
        out_shape=out_shape,
        compiler_params=pltpu.CompilerParams(vmem_limit_bytes=24 * 2**20),
        cost_estimate=pl.CostEstimate(flops=flops, bytes_accessed=size, transcendentals=0),
        **options,
    )


def shape_of(*shape, dtype=F32):
    return jax.ShapeDtypeStruct(shape, dtype)


def stay(*arrays):
    return [pltpu.with_memory_space_constraint(x, pltpu.HBM) for x in arrays]


def swaps(axis):
    count = lax.axis_size(axis)
    even = [(i, i ^ 1) for i in range(count)]
    odd = [(i, (i + 1) % count if i & 1 else (i - 1) % count) for i in range(count)]
    return even, odd


def swap_axial(x):
    count = lax.axis_size("ex")
    up = [(i, (i + 1) % count) for i in range(count)]
    if count == 2:
        return lax.ppermute(x, "ex", up)
    down = [(j, i) for i, j in up]
    return jnp.stack([lax.ppermute(x[0], "ex", up), lax.ppermute(x[1], "ex", down)])


def swap_both(one, two, axis):
    even, odd = swaps(axis)
    return lax.ppermute(one, axis, even), lax.ppermute(two, axis, odd)


def per_device(scalar, velocity, lumped_mass, pixel_weights, cut_element, pixel_block):
    shape = scalar.shape
    flat = (32, 64, 128)
    inner, outer = (32, 48, 128), (32, 16, 128)
    scalar = scalar.reshape(flat)
    velocity = velocity.reshape((3,) + flat)
    mass = lumped_mass.reshape(flat)
    tables = derivative_tables()
    n_cam = lax.axis_size("cam")
    cameras = pixel_weights.shape[0]
    share = cameras // n_cam
    part = functools.partial

    x, near = call(
        face_kernel,
        (shape_of(2, 2, 64, 128, dtype=BF16), shape_of(*tables.shape, dtype=BF16)),
        in_specs=[HBM] * 4,
        scratch_shapes=[
            pltpu.VMEM((2, 8, 64, 128), F32),
            pltpu.VMEM((2, 3, 64, 128), F32),
            pltpu.VMEM((2, 64, 128), F32),
            pltpu.SemaphoreType.DMA((7,)),
        ],
    )(*stay(scalar, velocity, mass, tables))
    x_got = swap_axial(x)
    s, z = call(first_kernel, (shape_of(64, 64, 128), shape_of(8, 8, 128)))(
        scalar, velocity, mass, near
    )
    weights = call(weight_kernel, shape_of(512, 128 * cameras, dtype=BF16))(pixel_weights)
    picks = call(pick_kernel, shape_of(cameras, 128, 640, dtype=BF16))(cut_element)

    half = functools.partial(shape_of, dtype=BF16)
    *z, x_got = call(
        first_radial_kernel, (half(80, 128), half(64, 128), shape_of(2, 2, 64, 128))
    )(z, x_got, pixel_block)
    z_got = swap_both(*z, "cam")
    z_got, weights, picks = lax.optimization_barrier((z_got, weights, picks))
    ids_got = z_got[0]
    *y, packed = call(
        part(azimuth_kernel, n_cam), (half(224, 128), half(224, 128), shape_of(8, 8, 128))
    )(s, x_got, *z_got, scalar, velocity, mass, near)
    y_got = swap_both(*y, "ey")
    g_inner, *inner_terms, z_inner = call(
        second_inner_kernel, (shape_of(*inner),) * 3 + (shape_of(4, 8, 128),)
    )(s, x_got, packed, scalar, velocity, mass, near)
    args = (s, x_got, packed, *y_got, scalar, velocity, mass, near, g_inner)
    some = (16, 16, 128)
    x, *faces = call(
        second_face_kernel,
        (shape_of(2, 1, 64, 128, dtype=BF16),) + (shape_of(*some),) * 3 + (shape_of(2, 8, 128),),
        scratch_shapes=[pltpu.VMEM(some, F32)],
    )(*args)
    g, *outer_terms, z = call(
        second_outer_kernel,
        (shape_of(*flat), shape_of(*outer), shape_of(*outer), shape_of(4, 8, 128)),
        scratch_shapes=[pltpu.VMEM(outer, F32), pltpu.VMEM(outer, F32)],
    )(*args, z_inner, *faces)

    terms = (*inner_terms, *outer_terms)
    x_got = swap_axial(x)
    early = call(
        early_kernel,
        shape_of(256, 128 * cameras, dtype=BF16),
        scratch_shapes=[pltpu.VMEM((256, 512), BF16)],
    )(g, *terms, near, weights)
    x_got, early = lax.optimization_barrier((x_got, early))
    *z, x_got = call(
        second_radial_kernel, (half(32, 128), half(64, 128), shape_of(2, 1, 64, 128))
    )(z, x_got, pixel_block, ids_got)
    z_got = swap_both(*z, "cam")
    pixels = call(
        middle_kernel,
        shape_of(cameras, 128, 128),
        scratch_shapes=[pltpu.VMEM((256, 512), BF16)],
    )(g, x_got, *terms, near, weights, picks, early)
    z_got, pixels = lax.optimization_barrier((z_got, pixels))
    payload_shape = half(share, 128, 128)
    advected, values, *far = call(
        part(render_far_kernel, n_cam),
        (shape_of(*flat), half(cameras, 64, 128)) + (payload_shape,) * (n_cam - 2),
        out_specs=(HBM, VMEM) + (VMEM,) * (n_cam - 2),
        scratch_shapes=[
            pltpu.VMEM(flat, F32),
            pltpu.VMEM((64, 512), F32),
            pltpu.SemaphoreType.DMA,
        ],
    )(g, x_got, *z_got, *terms, near, weights, picks, pixels)
    parts = (values, picks, pixels)
    image_shape = shape_of(share, NBLK, 128)
    images, onehot = call(
        part(own_image_kernel, n_cam),
        (image_shape, half(share, NBLK, 128 * n_cam)),
        scratch_shapes=[
            pltpu.VMEM(payload_shape.shape, BF16),
            pltpu.VMEM((n_cam, cameras, 128), jnp.int32),
        ],
    )(*parts, pixel_block, ids_got, z_got[1])
    images, parts = lax.optimization_barrier((images, parts))
    beside = call(part(render_near_kernel, n_cam, 1), payload_shape)(*parts)
    received = []
    for d, payload in [(1, beside)] + [(n + 2, p) for n, p in enumerate(far)]:
        received.append(lax.ppermute(payload, "cam", [(i, i ^ d) for i in range(n_cam)]))
    images = call(
        image_kernel,
        image_shape,
        out_specs=HBM,
        scratch_shapes=[
            pltpu.VMEM((share, NBLK, 128), F32),
            pltpu.SemaphoreType.DMA((4 * share,)),
        ],
    )(images, onehot, *received)
    return (advected.reshape(shape), images)


def solution(mesh):
    placed = (
        P("ex", None, "ey", None, "cam"),
        P(None, "ex", None, "ey", None, "cam"),
        P("ex", None, "ey", None, "cam"),
        P(),
        P(None, ("cam", "ex", "ey")),
        P(None, ("cam", "ex", "ey")),
    )
    return jax.shard_map(
        per_device,
        mesh=mesh,
        in_specs=placed,
        out_specs=(P("ex", None, "ey", None, "cam"), P("cam", ("ex", "ey"), None)),
        check_vma=False,
    )
```

```python
import functools

import jax
import jax.numpy as jnp
import numpy as np
from jax import lax
from jax.experimental import pallas as pl
from jax.experimental.pallas import tpu as pltpu
from jax.sharding import PartitionSpec as P

NBLK = 1024
F32 = jnp.float32
BF16 = jnp.bfloat16
VMEM = pl.BlockSpec(memory_space=pltpu.VMEM)
HBM = pl.BlockSpec(memory_space=pltpu.HBM)
time_step = 0.01


def legendre_seven(points):
    previous = points * 0.0 + 1.0
    current = points * 1.0
    for order in range(1, 7):
        following = ((2 * order + 1) * points * current - order * previous) / (order + 1)
        previous = current
        current = following
    return current


def gll_derivative():
    degree = 7
    gll_nodes = np.array(
        [
            -1.0,
            -0.8717401485096066,
            -0.5917001814331423,
            -0.2092992179024789,
            0.2092992179024789,
            0.5917001814331423,
            0.8717401485096066,
            1.0,
        ]
    )
    values = legendre_seven(gll_nodes)
    derivative = np.zeros((degree + 1, degree + 1))
    for target in range(degree + 1):
        for source in range(degree + 1):
            if target != source:
                derivative[target, source] = values[target] / (
                    values[source] * (gll_nodes[target] - gll_nodes[source])
                )
    derivative[0, 0] = -degree * (degree + 1) / 4.0
    derivative[degree, degree] = degree * (degree + 1) / 4.0
    return derivative


def split_two(table):
    high = table.astype(np.float32).astype(BF16)
    low = (table - high.astype(np.float64)).astype(np.float32).astype(BF16)
    return high, low


def derivative_tables():
    derivative = gll_derivative()
    eye = np.eye(8)
    rows = np.concatenate([np.kron(derivative, eye), np.kron(eye, derivative)], axis=0)
    high, low = split_two(rows)
    row_table = np.concatenate([high, high, low, np.zeros_like(high)], axis=1)
    high, low = split_two(np.kron(np.eye(16), derivative.T))
    lane_table = np.concatenate(
        [
            np.concatenate([high, low], axis=1),
            np.concatenate([high, np.zeros_like(high)], axis=1),
        ],
        axis=0,
    )
    swap = np.zeros((128, 128))
    for c in range(15):
        swap[8 * c + 7, 8 * c + 8] = 1.0
        swap[8 * c + 8, 8 * c + 7] = 1.0
    join_table = np.concatenate([swap, swap], axis=0).astype(np.float32).astype(BF16)
    spread = np.zeros((128, 128))
    spread[0, 0::2] = 1.0
    spread[127, 1::2] = 1.0
    turn = np.zeros((64, 256))
    for k in range(4):
        for c in range(16):
            turn[16 * k + c, 8 * c + 2 * k] = 1.0
            turn[16 * k + c, 128 + 8 * c + 2 * k + 1] = 1.0
    ends = turn.reshape(4, 16, 256)[:, ::15].reshape(8, 256)
    ends = np.concatenate([ends, np.zeros_like(ends)], axis=0)
    partial = np.zeros((16, 64))
    for i in range(8):
        partial[i, 8 * i + 1 : 8 * i + 8] = derivative[0, 1:]
        partial[8 + i, 8 * i : 8 * i + 7] = derivative[7, :7]
    high, low = split_two(partial)
    partial = np.concatenate([high, high, low, np.zeros_like(high)], axis=1)
    exact = [spread, spread, turn[:, :128], turn[:, 128:], ends[:, :128], ends[:, 128:]]
    exact = np.concatenate(exact, axis=0)
    split = [row_table[:, :128], row_table[:, 128:], lane_table[:, :128], lane_table[:, 128:]]
    split += [join_table, exact.astype(np.float32).astype(BF16)]
    split += [partial[:, :128], partial[:, 128:]]
    return jnp.asarray(np.concatenate(split, axis=0))


def row_table(table_ref, first=0):
    high, low = table_ref[first:128], table_ref[128 + first : 256]
    return jnp.concatenate([high, low[:, :64]], axis=1)


def lane_table(table_ref):
    return jnp.concatenate([table_ref[256:512], table_ref[512:768]], axis=1)


def join_table(table_ref):
    return jnp.concatenate([table_ref[768:1024], table_ref[1024:1280]], axis=1)


def turn_table(table_ref):
    return jnp.concatenate([table_ref[1280:1344], table_ref[1344:1408]], axis=1)


def end_table(table_ref):
    return jnp.concatenate([table_ref[1408:1424], table_ref[1424:1440]], axis=1)


def partial_table(table_ref):
    return jnp.concatenate([table_ref[1440:1456], table_ref[1456:1472][:, :64]], axis=1)


def span_of(a, offset=0):
    if isinstance(a, int):
        return slice(8 * a + offset, 8 * a + offset + 8)
    return pl.ds(pl.multiple_of(a * 8 + offset, 8), 8)


def sweep(body, together):
    if together == 4:
        for a in range(4):
            body(a)
        return

    def step(n, carry):
        for m in range(together):
            body(n * together + m)
        return carry

    lax.fori_loop(0, 4 // together, step, 0)


def lane_ids(shape):
    return lax.broadcasted_iota(jnp.int32, shape, len(shape) - 1)


def row_ids(shape):
    return lax.broadcasted_iota(jnp.int32, shape, len(shape) - 2)


def halves(value):
    high = value.astype(BF16)
    return high, (value - high.astype(F32)).astype(BF16)


def dot(a, b):
    return jnp.dot(a, b, preferred_element_type=F32)


def by_lanes(pairs, table_ref):
    rows = jnp.concatenate([jnp.concatenate(p, axis=1) for p in pairs], axis=0)
    both = dot(rows, lane_table(table_ref))
    return both[:, :128] + both[:, 128:]


def join_lanes(values, table_ref):
    rows = jnp.concatenate([jnp.concatenate(halves(v), axis=1) for v in values], axis=0)
    other = dot(rows, join_table(table_ref))
    joined, spread, at = [], [], 0
    for v in values:
        span = slice(at, at + v.shape[0])
        joined.append(v + other[span, :128])
        spread.append(other[span, 128:])
        at += v.shape[0]
    return joined, spread


def join_rows(value):
    row = row_ids(value.shape)
    last = ((row & 7) == 7) & (row != 63)
    first = ((row & 7) == 0) & (row != 0)
    other = jnp.where(
        last, pltpu.roll(value, 63, 0), jnp.where(first, pltpu.roll(value, 1, 0), 0.0)
    )
    return value + other


def convect_pair(fields, velocities, masses, table_ref):
    pairs = [halves(f) for f in fields]
    high = jnp.concatenate([p[0] for p in pairs], axis=1)
    low = jnp.concatenate([p[1] for p in pairs], axis=1)
    stacked = jnp.concatenate([high, low, high], axis=0)
    rows = dot(row_table(table_ref), stacked)
    radius = by_lanes(pairs, table_ref)
    out = []
    for n in range(2):
        lanes = slice(128 * n, 128 * n + 128)
        v = velocities[n]
        slope = v[0] * rows[:64, lanes] + v[1] * rows[64:, lanes]
        out.append(masses[n] * (slope + v[2] * radius[64 * n : 64 * n + 64]))
    return out


def face_kernel(
    scalar_hbm, velocity_hbm, mass_hbm, table_hbm, x_ref, table_ref, f_ref, v_ref, m_ref, sems,
):
    copies = []

    def start(source, target):
        copy = pltpu.make_async_copy(source, target, sems.at[len(copies)])
        copy.start()
        copies.append(copy)

    last = scalar_hbm.shape[0] - 1
    start(scalar_hbm.at[pl.ds(last - 7, 8)], f_ref.at[0])
    start(scalar_hbm.at[pl.ds(0, 8)], f_ref.at[1])
    start(table_hbm, table_ref)
    start(velocity_hbm.at[:, last], v_ref.at[0])
    start(velocity_hbm.at[:, 0], v_ref.at[1])
    start(mass_hbm.at[last], m_ref.at[0])
    start(mass_hbm.at[0], m_ref.at[1])
    for copy in copies[:3]:
        copy.wait()
    derivative = gll_derivative()
    fields = [f_ref[0, 7], f_ref[1, 0]]
    pairs = [halves(f) for f in fields]
    high = jnp.concatenate([p[0] for p in pairs], axis=1)
    low = jnp.concatenate([p[1] for p in pairs], axis=1)
    azimuth = dot(row_table(table_ref, 64), jnp.concatenate([high, low, high], axis=0))
    radius = by_lanes(pairs, table_ref)
    for copy in copies[3:]:
        copy.wait()
    values = []
    for n, node in enumerate((7, 0)):
        axial = f_ref[n, 0] * float(derivative[node, 0])
        for p in range(1, 8):
            axial = axial + f_ref[n, p] * float(derivative[node, p])
        slope = v_ref[n, 0] * axial + v_ref[n, 1] * azimuth[:, 128 * n : 128 * n + 128]
        values.append(m_ref[n] * (slope + v_ref[n, 2] * radius[64 * n : 64 * n + 64]))
        values.append(m_ref[n])
    for n, value in enumerate(join_lanes(values, table_ref)[0]):
        x_ref[n // 2, n % 2] = join_rows(value).astype(BF16)


def join_block(s_ref):
    for b in range(s_ref.shape[1] // 8 - 1):
        total = s_ref[:, 8 * b + 7, :] + s_ref[:, 8 * b + 8, :]
        s_ref[:, 8 * b + 7, :] = total
        s_ref[:, 8 * b + 8, :] = total
    join_axial(s_ref)


def join_axial(s_ref):
    for f in range(s_ref.shape[0] // 32):
        for a in range(3):
            at = 32 * f + 8 * a + 7
            total = s_ref[at] + s_ref[at + 1]
            s_ref[at] = total
            s_ref[at + 1] = total


def pack_blocks(blocks):
    slot = ((lane_ids((8, 128)) + 1) >> 1) & 63
    parts = [jnp.zeros((8, 128), F32) for _ in range(4)]
    for n, (u, block) in enumerate(blocks):
        if u:
            block = pltpu.roll(block, 2 * u, 1)
        parts[n % 4] = jnp.where(slot == u, block, parts[n % 4])
    return (parts[0] + parts[1]) + (parts[2] + parts[3])


def pick_spread(spreads):
    slot = ((lane_ids((8, 128)) + 1) >> 1) & 63
    parts = [jnp.zeros((8, 128), F32) for _ in range(2)]
    for b, spread in spreads:
        for i in range(8):
            block = spread[8 * i : 8 * i + 8]
            parts[i % 2] = jnp.where(slot == 56 - 8 * i + b, block, parts[i % 2])
    return parts[0] + parts[1]


def join_packed(packed):
    lane, row = lane_ids((8, 128)), row_ids((8, 128))
    slot = ((lane + 1) >> 1) & 63
    b = slot & 7
    rows = []
    for value in packed:
        after = pltpu.roll(pltpu.roll(value, 126, 1), 7, 0)
        before = pltpu.roll(pltpu.roll(value, 2, 1), 1, 0)
        value = value + jnp.where((row == 7) & (b < 7), after, 0.0)
        rows.append(value + jnp.where((row == 0) & (b > 0), before, 0.0))
    out = list(rows)
    for a in range(3):
        out[a] = out[a] + jnp.where(slot < 8, pltpu.roll(rows[a + 1], 16, 1), 0.0)
        out[a + 1] = out[a + 1] + jnp.where(slot >= 56, pltpu.roll(rows[a], 112, 1), 0.0)
    return out


def first_kernel(scalar_ref, velocity_ref, mass_ref, table_ref, s_ref, z_ref):
    def body(a):
        at = span_of(a)
        spreads = [[], []]
        for pair in range(4):
            spans = [slice(16 * pair + 8 * n, 16 * pair + 8 * n + 8) for n in range(2)]
            fields = [scalar_ref[at, s, :].reshape(64, 128) for s in spans]
            velocities = [
                [velocity_ref[d, at, s, :].reshape(64, 128) for d in range(3)] for s in spans
            ]
            masses = [mass_ref[at, s, :].reshape(64, 128) for s in spans]
            values = convect_pair(fields, velocities, masses, table_ref)
            joined, spread = join_lanes(values + masses, table_ref)
            for n, s in enumerate(spans):
                for f in range(2):
                    s_ref[span_of(a, 32 * f), s, :] = joined[n + 2 * f].reshape(8, 8, 128)
                    spreads[f].append((2 * pair + n, spread[n + 2 * f]))
        for f in range(2):
            z_ref[a + 4 * f] = pick_spread(spreads[f])

    sweep(body, 2)
    join_block(s_ref)
    for f in range(2):
        for n, value in enumerate(join_packed([z_ref[4 * f + a] for a in range(4)])):
            z_ref[4 * f + n] = value


def radial_faces(count, z_in, x_in, x_ref):
    x_ref[...] = x_in[...].astype(F32)
    rows = []
    for f in range(count):
        spans = [slice(8 * b, 8 * b + 8) for b in range(8)]
        low = pack_blocks([(56 + b, x_ref[0, f, s, :]) for b, s in enumerate(spans)])
        high = pack_blocks([(b, x_ref[1, f, s, :]) for b, s in enumerate(spans)])
        rows += [z_in[4 * f] + low, z_in[4 * f + 1], z_in[4 * f + 2], z_in[4 * f + 3] + high]
    return jnp.concatenate(rows, axis=0).astype(BF16)


def id_tile(block_ref):
    ids = block_ref[...]
    return jnp.concatenate([ids >> 5, ids & 31], axis=0).astype(F32).astype(BF16)


def first_radial_kernel(z_in, x_in, block_ref, one_ref, two_ref, x_ref):
    faces = radial_faces(2, z_in, x_in, x_ref)
    one_ref[:64, :] = faces
    one_ref[64:, :] = id_tile(block_ref)
    two_ref[...] = faces


def second_radial_kernel(z_in, x_in, block_ref, got_ref, one_ref, two_ref, x_ref):
    faces = radial_faces(1, z_in, x_in, x_ref)
    one_ref[...] = faces
    two_ref[:32, :] = faces
    two_ref[32:48, :] = id_tile(block_ref)
    two_ref[48:, :] = got_ref[64:, :]


def merged(one, two, cam_count):
    me = lax.axis_index("cam")
    even = (me & 1) == 0
    left = jnp.where(even, two, one)
    right = jnp.where(even, one, two)
    left = jnp.where(me == 0, 0.0, left)
    right = jnp.where(me == cam_count - 1, 0.0, right)
    lane = lane_ids((8, 128))
    return jnp.where((lane & 1) == 0, pltpu.roll(left, 1, 1), pltpu.roll(right, 127, 1))


def end_lanes(shape):
    lane = lane_ids(shape)
    return (lane == 0) | (lane == 127)


def azimuth_kernel(
    cam_count, s_ref, x_ref, one_ref, two_ref, scalar_ref, velocity_ref, mass_ref, table_ref,
    even_ref, odd_ref, packed_ref,
):
    ends = end_lanes((8, 128))
    row = row_ids((8, 128))
    even = (lax.axis_index("ey") & 1) == 0
    count = s_ref.shape[0]
    one = one_ref[:count, :].astype(F32)
    two = two_ref[:count, :].astype(F32)
    low, high = [], []
    for q in range(count // 8):
        at = slice(8 * q, 8 * q + 8)
        packed = merged(one[at], two[at], cam_count)
        packed_ref[q] = packed
        f, a = q // 4, q % 4
        for line, shift, faces in ((0, 16, low), (63, 2, high)):
            j = line & 7
            spread = jnp.broadcast_to(packed[j : j + 1, :], (8, 128))
            moved = pltpu.roll(spread, shift, 1, stride=16, stride_axis=0)
            face = s_ref[at, line, :] + jnp.where(ends, moved, 0.0)
            if a == 0:
                face = face + jnp.where(row == 0, x_ref[0, f, line : line + 1, :], 0.0)
            if a == 3:
                face = face + jnp.where(row == 7, x_ref[1, f, line : line + 1, :], 0.0)
            faces.append(face)
    slopes = [[], []]
    for a in range(4):
        pairs = []
        for b in (0, 7):
            g = assembled(s_ref, x_ref, packed_ref[a], 0, a, b)
            m = assembled(s_ref, x_ref, packed_ref[a + 4], 1, a, b)
            scalar = scalar_ref[span_of(a), 8 * b : 8 * b + 8, :].reshape(64, 128)
            pairs.append(halves(scalar - (time_step / m) * g))
        tops = jnp.concatenate([p[0] for p in pairs], axis=1)
        rests = jnp.concatenate([p[1] for p in pairs], axis=1)
        both = dot(partial_table(table_ref), jnp.concatenate([tops, rests, tops], axis=0))
        slopes[0].append(both[:8, :128])
        slopes[1].append(both[8:, 128:])
    messages = []
    for faces, line, slope in ((low, 0, slopes[0]), (high, 63, slopes[1])):
        flow = [mass_ref[:, line, :] * velocity_ref[d, :, line, :] for d in range(3)]
        share = flow[1] * jnp.concatenate(slope, axis=0)
        rows = faces + [share] + flow + [scalar_ref[:, line, :]]
        messages.append(jnp.concatenate(rows, axis=0))
    even_ref[...] = jnp.where(even, messages[1], messages[0]).astype(BF16)
    odd_ref[...] = jnp.where(even, messages[0], messages[1]).astype(BF16)


def unpacked(packed, b):
    ends = end_lanes((8, 128))
    rows = []
    for i in range(8):
        u = 56 - 8 * i + b
        moved = pltpu.roll(packed, (128 - 2 * u) % 128, 1) if u else packed
        rows.append(jnp.where(ends, moved, 0.0))
    return rows


def assembled(s_ref, x_ref, packed, f, a, b, y_refs=None):
    span = slice(8 * b, 8 * b + 8)
    at = span_of(a, 32 * f)
    block = s_ref[at, span, :]
    if packed is None:
        rows = [jnp.zeros((8, 128), F32) for _ in range(8)]
    else:
        rows = unpacked(packed, b)
    if not isinstance(a, int):
        rows[0] = rows[0] + jnp.where(a == 0, x_ref[0, f, span, :], 0.0)
        rows[7] = rows[7] + jnp.where(a == 3, x_ref[1, f, span, :], 0.0)
    elif a == 0:
        rows[0] = rows[0] + x_ref[0, f, span, :]
    elif a == 3:
        rows[7] = rows[7] + x_ref[1, f, span, :]
    if y_refs is not None:
        one_ref, two_ref = y_refs
        even = (lax.axis_index("ey") & 1) == 0
        at = slice(16 * (a // 2) + 32 * f, 16 * (a // 2) + 32 * f + 16)
        one, two = one_ref[at, :].astype(F32), two_ref[at, :].astype(F32)
        if b == 0:
            line, sublane = jnp.where(even, two, one), 0
        else:
            line, sublane = jnp.where(even, one, two), 7
        line = line[8 * (a % 2) : 8 * (a % 2) + 8]
        node = lax.broadcasted_iota(jnp.int32, (8, 8, 128), 1)
        block = block + jnp.where(node == sublane, line[:, None, :], 0.0)
    return block.reshape(64, 128) + jnp.concatenate(rows, axis=0)


def second_pairs(
    pairs, s_ref, x_ref, packed_ref, y_refs, scalar_ref, velocity_ref,
    mass_ref, table_ref, g_ref, base_ref, half_ref, z_ref, first_ref=None,
):
    def body(a, layer=None):
        at = span_of(a)
        layer = a if layer is None else layer
        to = span_of(layer)
        radial_g = packed_ref[a]
        radial_m = packed_ref[a + 4]
        spreads = []
        for n, pair in enumerate(pairs):
            fields, velocities, masses = [], [], []
            for h, b in enumerate(pair):
                s = slice(8 * b, 8 * b + 8)
                out = slice(16 * n + 8 * h, 16 * n + 8 * h + 8)
                g = assembled(s_ref, x_ref, radial_g, 0, a, b, y_refs)
                m = assembled(s_ref, x_ref, radial_m, 1, a, b, y_refs)
                scale = time_step / m
                scalar = scalar_ref[at, s, :].reshape(64, 128)
                first = scalar - scale * g
                base_ref[to, out, :] = (0.5 * (scalar + first)).reshape(8, 8, 128)
                half_ref[to, out, :] = (0.5 * scale).reshape(8, 8, 128)
                fields.append(first)
                if first_ref is not None:
                    first_ref[to, out, :] = first.reshape(8, 8, 128)
                velocities.append(
                    [velocity_ref[d, at, s, :].reshape(64, 128) for d in range(3)]
                )
                masses.append(mass_ref[at, s, :].reshape(64, 128))
            values = convect_pair(fields, velocities, masses, table_ref)
            joined, spread = join_lanes(values, table_ref)
            for h, b in enumerate(pair):
                out = slice(16 * n + 8 * h, 16 * n + 8 * h + 8)
                g_ref[to, out, :] = joined[h].reshape(8, 8, 128)
                spreads.append((b, spread[h]))
        z_ref[layer] = pick_spread(spreads)

    return body


def second_inner_kernel(
    s_ref, x_ref, packed_ref, scalar_ref, velocity_ref, mass_ref,
    table_ref, g_ref, base_ref, half_ref, z_ref,
):
    body = second_pairs(
        ((1, 2), (3, 4), (5, 6)), s_ref, x_ref, packed_ref, None,
        scalar_ref, velocity_ref, mass_ref, table_ref, g_ref, base_ref, half_ref, z_ref,
    )
    sweep(body, 2)
    join_block(g_ref)


def add_beyond(layers, y_one_ref, y_two_ref, first_ref, scalar_ref, table_ref, g_ref, z_ref):
    even = (lax.axis_index("ey") & 1) == 0
    one, two = y_one_ref[64:, :].astype(F32), y_two_ref[64:, :].astype(F32)
    sides = (jnp.where(even, two, one), jnp.where(even, one, two))
    rows = []
    for h, (line, outer) in enumerate(((0, 0), (15, 63))):
        for a, n in layers:
            change = first_ref[span_of(n), line, :] - scalar_ref[span_of(a), outer, :]
            rows.append(sides[h][128 + 8 * a : 136 + 8 * a] + change)
    count = len(layers)
    field = jnp.concatenate(rows + [jnp.zeros((64 - 16 * count, 128), F32)], axis=0)
    high, low = halves(field)
    axial = dot(row_table(table_ref, 64), jnp.concatenate([high, low, high], axis=0))
    radius = by_lanes([(high, low)], table_ref)
    corner = float(gll_derivative()[7, 7])
    values = []
    for h, sign in ((0, corner), (1, -corner)):
        for k, (a, _) in enumerate(layers):
            at = slice(8 * (count * h + k), 8 * (count * h + k) + 8)
            share, *flow = [sides[h][32 * n + 8 * a : 32 * n + 8 * a + 8] for n in range(4)]
            azimuth = sign * field[at]
            values.append(share + flow[0] * axial[at] + flow[1] * azimuth + flow[2] * radius[at])
    (joined,), (spread,) = join_lanes([jnp.concatenate(values, axis=0)], table_ref)
    slot = ((lane_ids((8, 128)) + 1) >> 1) & 63
    row = row_ids((8, 128))
    for h, line in ((0, 0), (1, 15)):
        for k, (_, n) in enumerate(layers):
            at = slice(8 * (count * h + k), 8 * (count * h + k) + 8)
            g_ref[span_of(n), line, :] = g_ref[span_of(n), line, :] + joined[at]
            mine = jnp.where(slot == 56 - 8 * row + 7 * h, spread[at], 0.0)
            total = jnp.sum(mine, axis=0, keepdims=True)
            z_ref[n] = z_ref[n] + jnp.where(row == 7 * h, total, 0.0)


def second_face_kernel(
    s_ref, x_ref, packed_ref, y_one_ref, y_two_ref, scalar_ref, velocity_ref,
    mass_ref, table_ref, inner_ref, x_out_ref, edge_ref, base_ref, half_ref, z_ref, first_ref,
):
    body = second_pairs(
        ((0, 7),), s_ref, x_ref, packed_ref, (y_one_ref, y_two_ref), scalar_ref, velocity_ref,
        mass_ref, table_ref, edge_ref, base_ref, half_ref, z_ref, first_ref,
    )
    body(0, 0)
    body(3, 1)
    add_beyond(((0, 0), (3, 1)), y_one_ref, y_two_ref, first_ref, scalar_ref, table_ref, edge_ref, z_ref)
    row = row_ids((64, 128))
    for n, (layer, at) in enumerate(((15, 31), (0, 0))):
        face = jnp.concatenate(
            [edge_ref[layer, 0:8, :], inner_ref[at], edge_ref[layer, 8:16, :]], axis=0
        )
        after = jnp.where((row == 7) | (row == 55), pltpu.roll(face, 63, 0), 0.0)
        before = jnp.where((row == 8) | (row == 56), pltpu.roll(face, 1, 0), 0.0)
        x_out_ref[n, 0] = (face + (after + before)).astype(BF16)


def second_outer_kernel(
    s_ref, x_ref, packed_ref, y_one_ref, y_two_ref, scalar_ref, velocity_ref,
    mass_ref, table_ref, inner_ref, z_in, edge_in, base_in, half_in, z_face,
    g_ref, base_ref, half_ref, z_ref, edge_ref, first_ref,
):
    body = second_pairs(
        ((0, 7),), s_ref, x_ref, packed_ref, (y_one_ref, y_two_ref), scalar_ref, velocity_ref,
        mass_ref, table_ref, edge_ref, base_ref, half_ref, z_ref, first_ref,
    )
    body(1)
    body(2)
    add_beyond(((1, 1), (2, 2)), y_one_ref, y_two_ref, first_ref, scalar_ref, table_ref, edge_ref, z_ref)
    for layer, a in ((0, 0), (1, 3)):
        for source, target in ((edge_in, edge_ref), (base_in, base_ref), (half_in, half_ref)):
            target[span_of(a)] = source[span_of(layer)]
        z_ref[a] = z_face[layer]
    join_axial(edge_ref)
    g_ref[:, 0:8, :] = edge_ref[:, 0:8, :]
    g_ref[:, 8:56, :] = inner_ref[...]
    g_ref[:, 56:64, :] = edge_ref[:, 8:16, :]
    for low in (7, 55):
        total = g_ref[:, low, :] + g_ref[:, low + 1, :]
        g_ref[:, low, :] = total
        g_ref[:, low + 1, :] = total
    for n, value in enumerate(join_packed([z_ref[a] + z_in[a] for a in range(4)])):
        z_ref[n] = value


def weight_kernel(weight_ref, out_ref):
    row = row_ids((512, 512))
    source = (row & 63) * 8 + (row >> 6)
    order = jnp.where(lane_ids((512, 512)) == source, 1.0, 0.0).astype(BF16)
    for m in range(8):
        out_ref[:, 128 * m : 128 * m + 128] = dot(order, weight_ref[m]).astype(BF16)


def pick_kernel(cut_ref, pick_ref):
    cut = cut_ref[...]
    a, b, c = cut >> 7, (cut >> 4) & 7, cut & 15
    order = jnp.where(a == 0, 2, jnp.where(a == 3, 3, a - 1))
    inner = 128 * order + 16 * b + c
    ends = 512 + 16 * a + 2 * b + (c >> 3)
    place = jnp.where((c == 0) | (c == 15), ends, inner)
    turned = place.astype(F32).T.astype(jnp.int32)
    lane = lane_ids((128, 640))
    for m in range(8):
        pick_ref[m] = jnp.where(lane == turned[:, m : m + 1], 1.0, 0.0).astype(BF16)


def turn(blocks, table):
    rows = []
    for block in blocks:
        value = block.astype(BF16)
        zero = jnp.zeros_like(value)
        rows.append(jnp.concatenate([value, zero], axis=1))
        rows.append(jnp.concatenate([zero, value], axis=1))
    return lax.dot_general(
        table,
        jnp.concatenate(rows, axis=0),
        (((1,), (1,)), ((), ())),
        preferred_element_type=F32,
    )


PAIRS = ((0, 1), (2, 3), (4, 5), (6, 7))


def term(refs, a, b):
    inner_ref, outer_ref = refs
    at = span_of(a)
    if b in (0, 7):
        return outer_ref[at, 8 * (b // 7) : 8 * (b // 7) + 8, :].reshape(64, 128)
    return inner_ref[at, 8 * b - 8 : 8 * b, :].reshape(64, 128)


def advanced(g_ref, x_ref, packed, bases, halfs, a, pair):
    blocks = []
    for b in pair:
        g = assembled(g_ref, x_ref, packed, 0, a, b)
        blocks.append(term(bases, a, b) - term(halfs, a, b) * g)
    return blocks


def store_elements(element_ref, blocks, table_ref, place):
    turned = turn(blocks, turn_table(table_ref)).astype(BF16)
    for h in range(2):
        for k in range(4):
            element_ref[place + 16 * h : place + 16 * h + 16, 128 * k : 128 * k + 128] = turned[
                16 * k : 16 * k + 16, 128 * h : 128 * h + 128
            ]


def pixel_values(element_ref, weight_ref, m):
    return dot(element_ref[...], weight_ref[:, 256 * m : 256 * m + 256]).astype(BF16)


def layer_elements(layers, g_ref, x_ref, bases, halfs, table_ref, element_ref):
    place = 0
    for a in layers:
        for pair in PAIRS:
            blocks = advanced(g_ref, x_ref, None, bases, halfs, a, pair)
            store_elements(element_ref, blocks, table_ref, place)
            place += 32


def early_kernel(
    g_ref, base_one, half_one, base_two, half_two, table_ref, weight_ref, value_ref, element_ref
):
    bases, halfs = (base_one, base_two), (half_one, half_two)
    layer_elements((1, 2), g_ref, None, bases, halfs, table_ref, element_ref)
    for m in range(4):
        value_ref[:, 256 * m : 256 * m + 256] = pixel_values(element_ref, weight_ref, m)


def middle_kernel(
    g_ref, x_ref, base_one, half_one, base_two, half_two, table_ref, weight_ref, pick_ref,
    early_ref, pixel_ref, element_ref,
):
    bases, halfs = (base_one, base_two), (half_one, half_two)
    layer_elements((0, 3), g_ref, x_ref, bases, halfs, table_ref, element_ref)
    for m in range(4):
        late = pixel_values(element_ref, weight_ref, m)
        both = jnp.concatenate([early_ref[:, 256 * m : 256 * m + 256], late], axis=0)
        for n in range(2):
            pixel_ref[2 * m + n] = dot(
                pick_ref[2 * m + n, :, :512], both[:, 128 * n : 128 * n + 128]
            )


def fill_payload(payload_ref, d, cam_count, pick_ref, value_ref, pixel_ref):
    me = lax.axis_index("cam")
    share = pixel_ref.shape[0] // cam_count
    for n in range(share):
        m = share * (me ^ d) + n
        values = dot(pick_ref[m, :, 512:576], value_ref[m]) + pixel_ref[m]
        payload_ref[n] = values.astype(BF16)


def final_layers(cam_count, g_ref, x_ref, one_ref, two_ref, terms, use):
    base_one, half_one, base_two, half_two = terms
    bases, halfs = (base_one, base_two), (half_one, half_two)
    one, two = one_ref[:32, :].astype(F32), two_ref[:32, :].astype(F32)
    for a in range(4):
        packed = merged(one[8 * a : 8 * a + 8], two[8 * a : 8 * a + 8], cam_count)
        for pair in PAIRS:
            use(a, pair, advanced(g_ref, x_ref, packed, bases, halfs, a, pair))


def render_far_kernel(
    cam_count, g_ref, x_ref, one_ref, two_ref, base_one, half_one, base_two, half_two,
    table_ref, weight_ref, pick_ref, pixel_ref, value_ref, *rest,
):
    payload_refs, end_ref = rest[:-1], rest[-1]

    def use(a, pair, blocks):
        turned = turn(blocks, end_table(table_ref))
        for h, b in enumerate(pair):
            place = 16 * a + 2 * b
            for k in range(4):
                end_ref[place : place + 2, 128 * k : 128 * k + 128] = turned[
                    2 * k : 2 * k + 2, 128 * h : 128 * h + 128
                ]

    terms = (base_one, half_one, base_two, half_two)
    final_layers(cam_count, g_ref, x_ref, one_ref, two_ref, terms, use)
    ends = end_ref[...].astype(BF16)
    for m in range(pixel_ref.shape[0] // 2):
        values = dot(ends, weight_ref[:, 256 * m : 256 * m + 256]).astype(BF16)
        value_ref[2 * m] = values[:, :128]
        value_ref[2 * m + 1] = values[:, 128:]
    for d in range(2, cam_count):
        fill_payload(payload_refs[d - 2], d, cam_count, pick_ref, value_ref, pixel_ref)


def advected_kernel(
    cam_count, g_ref, x_ref, one_ref, two_ref, base_one, half_one, base_two, half_two,
    out_hbm, advected_ref, sems,
):
    copies = []

    def use(a, pair, blocks):
        for h, b in enumerate(pair):
            advected_ref[span_of(a), 8 * b : 8 * b + 8, :] = blocks[h].reshape(8, 8, 128)
        if pair == PAIRS[-1]:
            at = span_of(a)
            copy = pltpu.make_async_copy(advected_ref.at[at], out_hbm.at[at], sems.at[a])
            copy.start()
            copies.append(copy)

    terms = (base_one, half_one, base_two, half_two)
    final_layers(cam_count, g_ref, x_ref, one_ref, two_ref, terms, use)
    for copy in copies:
        copy.wait()


def render_near_kernel(cam_count, d, value_ref, pick_ref, pixel_ref, payload_ref):
    fill_payload(payload_ref, d, cam_count, pick_ref, value_ref, pixel_ref)


def own_image_kernel(
    cam_count, value_ref, pick_ref, pixel_ref, block_ref, first_ref, second_ref,
    image_ref, onehot_ref, payload_ref, id_ref,
):
    me = lax.axis_index("cam")
    share = image_ref.shape[0]
    id_ref[0] = block_ref[...]
    tiles = ((1, first_ref[64:80, :]), (3, second_ref[32:48, :]), (2, second_ref[48:64, :]))
    for d, tile in tiles:
        ids = tile.astype(F32).astype(jnp.int32)
        id_ref[d] = ids[:8] * 32 + ids[8:]
    fill_payload(payload_ref, 0, cam_count, pick_ref, value_ref, pixel_ref)
    for m in range(share):
        ids = [id_ref[d, pl.ds(share * me + m, 1), :] for d in range(4)]
        ids = jnp.concatenate(ids, axis=1)
        for chunk in range(4):
            at = slice(256 * chunk, 256 * chunk + 256)
            row = row_ids((256, ids.shape[1])) + 256 * chunk
            onehot = jnp.where(row == ids, 1.0, 0.0).astype(BF16)
            onehot_ref[m, at, :] = onehot
            image_ref[m, at, :] = dot(onehot[:, :128], payload_ref[m])


def image_kernel(own_ref, onehot_ref, *refs):
    payload_refs, (image_hbm, image_ref, sems) = refs[:-3], refs[-3:]
    copies = []
    for m in range(image_ref.shape[0]):
        values = jnp.concatenate([payload_ref[m] for payload_ref in payload_refs], axis=0)
        for chunk in range(4):
            at = slice(256 * chunk, 256 * chunk + 256)
            image_ref[m, at, :] = own_ref[m, at, :] + dot(onehot_ref[m, at, 128:], values)
            copy = pltpu.make_async_copy(
                image_ref.at[m, at], image_hbm.at[m, at], sems.at[4 * m + chunk]
            )
            copy.start()
            copies.append(copy)
    for copy in copies:
        copy.wait()


def call(kernel, out_shape, flops=10**8, size=10**7, **options):
    return pl.pallas_call(
        kernel,
        out_shape=out_shape,
        compiler_params=pltpu.CompilerParams(vmem_limit_bytes=24 * 2**20),
        cost_estimate=pl.CostEstimate(flops=flops, bytes_accessed=size, transcendentals=0),
        **options,
    )


def shape_of(*shape, dtype=F32):
    return jax.ShapeDtypeStruct(shape, dtype)


def stay(*arrays):
    return [pltpu.with_memory_space_constraint(x, pltpu.HBM) for x in arrays]


def swaps(axis):
    count = lax.axis_size(axis)
    even = [(i, i ^ 1) for i in range(count)]
    odd = [(i, (i + 1) % count if i & 1 else (i - 1) % count) for i in range(count)]
    return even, odd


def swap_axial(x):
    count = lax.axis_size("ex")
    up = [(i, (i + 1) % count) for i in range(count)]
    if count == 2:
        return lax.ppermute(x, "ex", up)
    down = [(j, i) for i, j in up]
    return jnp.stack([lax.ppermute(x[0], "ex", up), lax.ppermute(x[1], "ex", down)])


def swap_both(one, two, axis):
    even, odd = swaps(axis)
    return lax.ppermute(one, axis, even), lax.ppermute(two, axis, odd)


def per_device(scalar, velocity, lumped_mass, pixel_weights, cut_element, pixel_block):
    shape = scalar.shape
    flat = (32, 64, 128)
    inner, outer = (32, 48, 128), (32, 16, 128)
    scalar = scalar.reshape(flat)
    velocity = velocity.reshape((3,) + flat)
    mass = lumped_mass.reshape(flat)
    tables = derivative_tables()
    n_cam = lax.axis_size("cam")
    cameras = pixel_weights.shape[0]
    share = cameras // n_cam
    part = functools.partial

    x, near = call(
        face_kernel,
        (shape_of(2, 2, 64, 128, dtype=BF16), shape_of(*tables.shape, dtype=BF16)),
        in_specs=[HBM] * 4,
        scratch_shapes=[
            pltpu.VMEM((2, 8, 64, 128), F32),
            pltpu.VMEM((2, 3, 64, 128), F32),
            pltpu.VMEM((2, 64, 128), F32),
            pltpu.SemaphoreType.DMA((7,)),
        ],
    )(*stay(scalar, velocity, mass, tables))
    x_got = swap_axial(x)
    s, z = call(first_kernel, (shape_of(64, 64, 128), shape_of(8, 8, 128)))(
        scalar, velocity, mass, near
    )
    weights = call(weight_kernel, shape_of(512, 128 * cameras, dtype=BF16))(pixel_weights)
    picks = call(pick_kernel, shape_of(cameras, 128, 640, dtype=BF16))(cut_element)

    half = functools.partial(shape_of, dtype=BF16)
    *z, x_got = call(
        first_radial_kernel, (half(80, 128), half(64, 128), shape_of(2, 2, 64, 128))
    )(z, x_got, pixel_block)
    z_got = swap_both(*z, "cam")
    z_got, weights, picks = lax.optimization_barrier((z_got, weights, picks))
    ids_got = z_got[0]
    *y, packed = call(
        part(azimuth_kernel, n_cam), (half(224, 128), half(224, 128), shape_of(8, 8, 128))
    )(s, x_got, *z_got, scalar, velocity, mass, near)
    y_got = swap_both(*y, "ey")
    g_inner, *inner_terms, z_inner = call(
        second_inner_kernel, (shape_of(*inner),) * 3 + (shape_of(4, 8, 128),)
    )(s, x_got, packed, scalar, velocity, mass, near)
    args = (s, x_got, packed, *y_got, scalar, velocity, mass, near, g_inner)
    some = (16, 16, 128)
    x, *faces = call(
        second_face_kernel,
        (shape_of(2, 1, 64, 128, dtype=BF16),) + (shape_of(*some),) * 3 + (shape_of(2, 8, 128),),
        scratch_shapes=[pltpu.VMEM(some, F32)],
    )(*args)
    g, *outer_terms, z = call(
        second_outer_kernel,
        (shape_of(*flat), shape_of(*outer), shape_of(*outer), shape_of(4, 8, 128)),
        scratch_shapes=[pltpu.VMEM(outer, F32), pltpu.VMEM(outer, F32)],
    )(*args, z_inner, *faces)

    terms = (*inner_terms, *outer_terms)
    x_got = swap_axial(x)
    early = call(
        early_kernel,
        shape_of(256, 128 * cameras, dtype=BF16),
        scratch_shapes=[pltpu.VMEM((256, 512), BF16)],
    )(g, *terms, near, weights)
    x_got, early = lax.optimization_barrier((x_got, early))
    *z, x_got = call(
        second_radial_kernel, (half(32, 128), half(64, 128), shape_of(2, 1, 64, 128))
    )(z, x_got, pixel_block, ids_got)
    z_got = swap_both(*z, "cam")
    pixels = call(
        middle_kernel,
        shape_of(cameras, 128, 128),
        scratch_shapes=[pltpu.VMEM((256, 512), BF16)],
    )(g, x_got, *terms, near, weights, picks, early)
    z_got, pixels = lax.optimization_barrier((z_got, pixels))
    payload_shape = half(share, 128, 128)
    values, *far = call(
        part(render_far_kernel, n_cam),
        (half(cameras, 64, 128),) + (payload_shape,) * (n_cam - 2),
        scratch_shapes=[pltpu.VMEM((64, 512), F32)],
    )(g, x_got, *z_got, *terms, near, weights, picks, pixels)
    parts = (values, picks, pixels)
    image_shape = shape_of(share, NBLK, 128)
    images, onehot = call(
        part(own_image_kernel, n_cam),
        (image_shape, half(share, NBLK, 128 * n_cam)),
        scratch_shapes=[
            pltpu.VMEM(payload_shape.shape, BF16),
            pltpu.VMEM((n_cam, cameras, 128), jnp.int32),
        ],
    )(*parts, pixel_block, ids_got, z_got[1])
    images, parts = lax.optimization_barrier((images, parts))
    beside = call(part(render_near_kernel, n_cam, 1), payload_shape)(*parts)
    final = (g, x_got, *z_got, *terms)
    final, beside = lax.optimization_barrier((final, beside))
    advected = call(
        part(advected_kernel, n_cam),
        shape_of(*flat),
        out_specs=HBM,
        scratch_shapes=[pltpu.VMEM(flat, F32), pltpu.SemaphoreType.DMA((4,))],
    )(*final)
    images, advected = lax.optimization_barrier((images, advected))
    received = []
    for d, payload in [(1, beside)] + [(n + 2, p) for n, p in enumerate(far)]:
        received.append(lax.ppermute(payload, "cam", [(i, i ^ d) for i in range(n_cam)]))
    images = call(
        image_kernel,
        image_shape,
        out_specs=HBM,
        scratch_shapes=[
            pltpu.VMEM((share, NBLK, 128), F32),
            pltpu.SemaphoreType.DMA((4 * share,)),
        ],
    )(images, onehot, *received)
    return (advected.reshape(shape), images)


def solution(mesh):
    placed = (
        P("ex", None, "ey", None, "cam"),
        P(None, "ex", None, "ey", None, "cam"),
        P("ex", None, "ey", None, "cam"),
        P(),
        P(None, ("cam", "ex", "ey")),
        P(None, ("cam", "ex", "ey")),
    )
    return jax.shard_map(
        per_device,
        mesh=mesh,
        in_specs=placed,
        out_specs=(P("ex", None, "ey", None, "cam"), P("cam", ("ex", "ey"), None)),
        check_vma=False,
    )
```

```python
import functools

import jax
import jax.numpy as jnp
import numpy as np
from jax import lax
from jax.experimental import pallas as pl
from jax.experimental.pallas import tpu as pltpu
from jax.sharding import PartitionSpec as P

NBLK = 1024
F32 = jnp.float32
BF16 = jnp.bfloat16
VMEM = pl.BlockSpec(memory_space=pltpu.VMEM)
HBM = pl.BlockSpec(memory_space=pltpu.HBM)
time_step = 0.01


def legendre_seven(points):
    previous = points * 0.0 + 1.0
    current = points * 1.0
    for order in range(1, 7):
        following = ((2 * order + 1) * points * current - order * previous) / (order + 1)
        previous = current
        current = following
    return current


def gll_derivative():
    degree = 7
    gll_nodes = np.array(
        [
            -1.0,
            -0.8717401485096066,
            -0.5917001814331423,
            -0.2092992179024789,
            0.2092992179024789,
            0.5917001814331423,
            0.8717401485096066,
            1.0,
        ]
    )
    values = legendre_seven(gll_nodes)
    derivative = np.zeros((degree + 1, degree + 1))
    for target in range(degree + 1):
        for source in range(degree + 1):
            if target != source:
                derivative[target, source] = values[target] / (
                    values[source] * (gll_nodes[target] - gll_nodes[source])
                )
    derivative[0, 0] = -degree * (degree + 1) / 4.0
    derivative[degree, degree] = degree * (degree + 1) / 4.0
    return derivative


def split_two(table):
    high = table.astype(np.float32).astype(BF16)
    low = (table - high.astype(np.float64)).astype(np.float32).astype(BF16)
    return high, low


def derivative_tables():
    derivative = gll_derivative()
    eye = np.eye(8)
    rows = np.concatenate([np.kron(derivative, eye), np.kron(eye, derivative)], axis=0)
    high, low = split_two(rows)
    row_table = np.concatenate([high, high, low, np.zeros_like(high)], axis=1)
    high, low = split_two(np.kron(np.eye(16), derivative.T))
    lane_table = np.concatenate(
        [
            np.concatenate([high, low], axis=1),
            np.concatenate([high, np.zeros_like(high)], axis=1),
        ],
        axis=0,
    )
    swap = np.zeros((128, 128))
    for c in range(15):
        swap[8 * c + 7, 8 * c + 8] = 1.0
        swap[8 * c + 8, 8 * c + 7] = 1.0
    join_table = np.concatenate([swap, swap], axis=0).astype(np.float32).astype(BF16)
    spread = np.zeros((128, 128))
    spread[0, 0::2] = 1.0
    spread[127, 1::2] = 1.0
    turn = np.zeros((64, 256))
    for k in range(4):
        for c in range(16):
            turn[16 * k + c, 8 * c + 2 * k] = 1.0
            turn[16 * k + c, 128 + 8 * c + 2 * k + 1] = 1.0
    ends = turn.reshape(4, 16, 256)[:, ::15].reshape(8, 256)
    ends = np.concatenate([ends, np.zeros_like(ends)], axis=0)
    partial = np.zeros((16, 64))
    for i in range(8):
        partial[i, 8 * i + 1 : 8 * i + 8] = derivative[0, 1:]
        partial[8 + i, 8 * i : 8 * i + 7] = derivative[7, :7]
    high, low = split_two(partial)
    partial = np.concatenate([high, high, low, np.zeros_like(high)], axis=1)
    exact = [spread, spread, turn[:, :128], turn[:, 128:], ends[:, :128], ends[:, 128:]]
    exact = np.concatenate(exact, axis=0)
    split = [row_table[:, :128], row_table[:, 128:], lane_table[:, :128], lane_table[:, 128:]]
    split += [join_table, exact.astype(np.float32).astype(BF16)]
    split += [partial[:, :128], partial[:, 128:]]
    return jnp.asarray(np.concatenate(split, axis=0))


def row_table(table_ref, first=0):
    high, low = table_ref[first:128], table_ref[128 + first : 256]
    return jnp.concatenate([high, low[:, :64]], axis=1)


def lane_table(table_ref):
    return jnp.concatenate([table_ref[256:512], table_ref[512:768]], axis=1)


def join_table(table_ref):
    return jnp.concatenate([table_ref[768:1024], table_ref[1024:1280]], axis=1)


def turn_table(table_ref):
    return jnp.concatenate([table_ref[1280:1344], table_ref[1344:1408]], axis=1)


def end_table(table_ref):
    return jnp.concatenate([table_ref[1408:1424], table_ref[1424:1440]], axis=1)


def partial_table(table_ref):
    return jnp.concatenate([table_ref[1440:1456], table_ref[1456:1472][:, :64]], axis=1)


def span_of(a, offset=0):
    if isinstance(a, int):
        return slice(8 * a + offset, 8 * a + offset + 8)
    return pl.ds(pl.multiple_of(a * 8 + offset, 8), 8)


def sweep(body, together):
    if together == 4:
        for a in range(4):
            body(a)
        return

    def step(n, carry):
        for m in range(together):
            body(n * together + m)
        return carry

    lax.fori_loop(0, 4 // together, step, 0)


def lane_ids(shape):
    return lax.broadcasted_iota(jnp.int32, shape, len(shape) - 1)


def row_ids(shape):
    return lax.broadcasted_iota(jnp.int32, shape, len(shape) - 2)


def halves(value):
    high = value.astype(BF16)
    return high, (value - high.astype(F32)).astype(BF16)


def dot(a, b):
    return jnp.dot(a, b, preferred_element_type=F32)


def by_lanes(pairs, table_ref):
    rows = jnp.concatenate([jnp.concatenate(p, axis=1) for p in pairs], axis=0)
    both = dot(rows, lane_table(table_ref))
    return both[:, :128] + both[:, 128:]


def join_lanes(values, table_ref):
    rows = jnp.concatenate([jnp.concatenate(halves(v), axis=1) for v in values], axis=0)
    other = dot(rows, join_table(table_ref))
    joined, spread, at = [], [], 0
    for v in values:
        span = slice(at, at + v.shape[0])
        joined.append(v + other[span, :128])
        spread.append(other[span, 128:])
        at += v.shape[0]
    return joined, spread


def join_rows(value):
    row = row_ids(value.shape)
    last = ((row & 7) == 7) & (row != 63)
    first = ((row & 7) == 0) & (row != 0)
    other = jnp.where(
        last, pltpu.roll(value, 63, 0), jnp.where(first, pltpu.roll(value, 1, 0), 0.0)
    )
    return value + other


def convect_pair(fields, velocities, masses, table_ref):
    pairs = [halves(f) for f in fields]
    high = jnp.concatenate([p[0] for p in pairs], axis=1)
    low = jnp.concatenate([p[1] for p in pairs], axis=1)
    stacked = jnp.concatenate([high, low, high], axis=0)
    rows = dot(row_table(table_ref), stacked)
    radius = by_lanes(pairs, table_ref)
    out = []
    for n in range(2):
        lanes = slice(128 * n, 128 * n + 128)
        v = velocities[n]
        slope = v[0] * rows[:64, lanes] + v[1] * rows[64:, lanes]
        out.append(masses[n] * (slope + v[2] * radius[64 * n : 64 * n + 64]))
    return out


def face_kernel(
    scalar_hbm, velocity_hbm, mass_hbm, table_hbm, x_ref, table_ref, f_ref, v_ref, m_ref, sems,
):
    copies = []

    def start(source, target):
        copy = pltpu.make_async_copy(source, target, sems.at[len(copies)])
        copy.start()
        copies.append(copy)

    last = scalar_hbm.shape[0] - 1
    start(scalar_hbm.at[pl.ds(last - 7, 8)], f_ref.at[0])
    start(scalar_hbm.at[pl.ds(0, 8)], f_ref.at[1])
    start(table_hbm, table_ref)
    start(velocity_hbm.at[:, last], v_ref.at[0])
    start(velocity_hbm.at[:, 0], v_ref.at[1])
    start(mass_hbm.at[last], m_ref.at[0])
    start(mass_hbm.at[0], m_ref.at[1])
    for copy in copies[:3]:
        copy.wait()
    derivative = gll_derivative()
    fields = [f_ref[0, 7], f_ref[1, 0]]
    pairs = [halves(f) for f in fields]
    high = jnp.concatenate([p[0] for p in pairs], axis=1)
    low = jnp.concatenate([p[1] for p in pairs], axis=1)
    azimuth = dot(row_table(table_ref, 64), jnp.concatenate([high, low, high], axis=0))
    radius = by_lanes(pairs, table_ref)
    for copy in copies[3:]:
        copy.wait()
    values = []
    for n, node in enumerate((7, 0)):
        axial = f_ref[n, 0] * float(derivative[node, 0])
        for p in range(1, 8):
            axial = axial + f_ref[n, p] * float(derivative[node, p])
        slope = v_ref[n, 0] * axial + v_ref[n, 1] * azimuth[:, 128 * n : 128 * n + 128]
        values.append(m_ref[n] * (slope + v_ref[n, 2] * radius[64 * n : 64 * n + 64]))
        values.append(m_ref[n])
    for n, value in enumerate(join_lanes(values, table_ref)[0]):
        x_ref[n // 2, n % 2] = join_rows(value).astype(BF16)


def join_block(s_ref):
    for b in range(s_ref.shape[1] // 8 - 1):
        total = s_ref[:, 8 * b + 7, :] + s_ref[:, 8 * b + 8, :]
        s_ref[:, 8 * b + 7, :] = total
        s_ref[:, 8 * b + 8, :] = total
    join_axial(s_ref)


def join_axial(s_ref):
    for f in range(s_ref.shape[0] // 32):
        for a in range(3):
            at = 32 * f + 8 * a + 7
            total = s_ref[at] + s_ref[at + 1]
            s_ref[at] = total
            s_ref[at + 1] = total


def pack_blocks(blocks):
    slot = ((lane_ids((8, 128)) + 1) >> 1) & 63
    parts = [jnp.zeros((8, 128), F32) for _ in range(4)]
    for n, (u, block) in enumerate(blocks):
        if u:
            block = pltpu.roll(block, 2 * u, 1)
        parts[n % 4] = jnp.where(slot == u, block, parts[n % 4])
    return (parts[0] + parts[1]) + (parts[2] + parts[3])


def pick_spread(spreads):
    slot = ((lane_ids((8, 128)) + 1) >> 1) & 63
    parts = [jnp.zeros((8, 128), F32) for _ in range(2)]
    for b, spread in spreads:
        for i in range(8):
            block = spread[8 * i : 8 * i + 8]
            parts[i % 2] = jnp.where(slot == 56 - 8 * i + b, block, parts[i % 2])
    return parts[0] + parts[1]


def join_packed(packed):
    lane, row = lane_ids((8, 128)), row_ids((8, 128))
    slot = ((lane + 1) >> 1) & 63
    b = slot & 7
    rows = []
    for value in packed:
        after = pltpu.roll(pltpu.roll(value, 126, 1), 7, 0)
        before = pltpu.roll(pltpu.roll(value, 2, 1), 1, 0)
        value = value + jnp.where((row == 7) & (b < 7), after, 0.0)
        rows.append(value + jnp.where((row == 0) & (b > 0), before, 0.0))
    out = list(rows)
    for a in range(3):
        out[a] = out[a] + jnp.where(slot < 8, pltpu.roll(rows[a + 1], 16, 1), 0.0)
        out[a + 1] = out[a + 1] + jnp.where(slot >= 56, pltpu.roll(rows[a], 112, 1), 0.0)
    return out


def first_kernel(scalar_ref, velocity_ref, mass_ref, table_ref, s_ref, z_ref):
    def body(a):
        at = span_of(a)
        spreads = [[], []]
        for pair in range(4):
            spans = [slice(16 * pair + 8 * n, 16 * pair + 8 * n + 8) for n in range(2)]
            fields = [scalar_ref[at, s, :].reshape(64, 128) for s in spans]
            velocities = [
                [velocity_ref[d, at, s, :].reshape(64, 128) for d in range(3)] for s in spans
            ]
            masses = [mass_ref[at, s, :].reshape(64, 128) for s in spans]
            values = convect_pair(fields, velocities, masses, table_ref)
            joined, spread = join_lanes(values + masses, table_ref)
            for n, s in enumerate(spans):
                for f in range(2):
                    s_ref[span_of(a, 32 * f), s, :] = joined[n + 2 * f].reshape(8, 8, 128)
                    spreads[f].append((2 * pair + n, spread[n + 2 * f]))
        for f in range(2):
            z_ref[a + 4 * f] = pick_spread(spreads[f])

    sweep(body, 2)
    join_block(s_ref)
    for f in range(2):
        for n, value in enumerate(join_packed([z_ref[4 * f + a] for a in range(4)])):
            z_ref[4 * f + n] = value


def radial_faces(count, z_in, x_in, x_ref):
    x_ref[...] = x_in[...].astype(F32)
    rows = []
    for f in range(count):
        spans = [slice(8 * b, 8 * b + 8) for b in range(8)]
        low = pack_blocks([(56 + b, x_ref[0, f, s, :]) for b, s in enumerate(spans)])
        high = pack_blocks([(b, x_ref[1, f, s, :]) for b, s in enumerate(spans)])
        rows += [z_in[4 * f] + low, z_in[4 * f + 1], z_in[4 * f + 2], z_in[4 * f + 3] + high]
    return jnp.concatenate(rows, axis=0).astype(BF16)


def id_tile(block_ref):
    ids = block_ref[...]
    return jnp.concatenate([ids >> 5, ids & 31], axis=0).astype(F32).astype(BF16)


def first_radial_kernel(z_in, x_in, block_ref, one_ref, two_ref, x_ref):
    faces = radial_faces(2, z_in, x_in, x_ref)
    one_ref[:64, :] = faces
    one_ref[64:, :] = id_tile(block_ref)
    two_ref[...] = faces


def second_radial_kernel(z_in, x_in, block_ref, got_ref, one_ref, two_ref, x_ref):
    faces = radial_faces(1, z_in, x_in, x_ref)
    one_ref[...] = faces
    two_ref[:32, :] = faces
    two_ref[32:48, :] = id_tile(block_ref)
    two_ref[48:, :] = got_ref[64:, :]


def merged(one, two, cam_count):
    me = lax.axis_index("cam")
    even = (me & 1) == 0
    left = jnp.where(even, two, one)
    right = jnp.where(even, one, two)
    left = jnp.where(me == 0, 0.0, left)
    right = jnp.where(me == cam_count - 1, 0.0, right)
    lane = lane_ids((8, 128))
    return jnp.where((lane & 1) == 0, pltpu.roll(left, 1, 1), pltpu.roll(right, 127, 1))


def end_lanes(shape):
    lane = lane_ids(shape)
    return (lane == 0) | (lane == 127)


def azimuth_kernel(
    cam_count, s_ref, x_ref, one_ref, two_ref, scalar_ref, velocity_ref, mass_ref, table_ref,
    even_ref, odd_ref, packed_ref,
):
    ends = end_lanes((8, 128))
    row = row_ids((8, 128))
    even = (lax.axis_index("ey") & 1) == 0
    count = s_ref.shape[0]
    one = one_ref[:count, :].astype(F32)
    two = two_ref[:count, :].astype(F32)
    low, high = [], []
    for q in range(count // 8):
        at = slice(8 * q, 8 * q + 8)
        packed = merged(one[at], two[at], cam_count)
        packed_ref[q] = packed
        f, a = q // 4, q % 4
        for line, shift, faces in ((0, 16, low), (63, 2, high)):
            j = line & 7
            spread = jnp.broadcast_to(packed[j : j + 1, :], (8, 128))
            moved = pltpu.roll(spread, shift, 1, stride=16, stride_axis=0)
            face = s_ref[at, line, :] + jnp.where(ends, moved, 0.0)
            if a == 0:
                face = face + jnp.where(row == 0, x_ref[0, f, line : line + 1, :], 0.0)
            if a == 3:
                face = face + jnp.where(row == 7, x_ref[1, f, line : line + 1, :], 0.0)
            faces.append(face)
    slopes = [[], []]
    for a in range(4):
        pairs = []
        for b in (0, 7):
            g = assembled(s_ref, x_ref, packed_ref[a], 0, a, b)
            m = assembled(s_ref, x_ref, packed_ref[a + 4], 1, a, b)
            scalar = scalar_ref[span_of(a), 8 * b : 8 * b + 8, :].reshape(64, 128)
            pairs.append(halves(scalar - (time_step / m) * g))
        tops = jnp.concatenate([p[0] for p in pairs], axis=1)
        rests = jnp.concatenate([p[1] for p in pairs], axis=1)
        both = dot(partial_table(table_ref), jnp.concatenate([tops, rests, tops], axis=0))
        slopes[0].append(both[:8, :128])
        slopes[1].append(both[8:, 128:])
    messages = []
    for faces, line, slope in ((low, 0, slopes[0]), (high, 63, slopes[1])):
        flow = [mass_ref[:, line, :] * velocity_ref[d, :, line, :] for d in range(3)]
        share = flow[1] * jnp.concatenate(slope, axis=0)
        rows = faces + [share] + flow + [scalar_ref[:, line, :]]
        messages.append(jnp.concatenate(rows, axis=0))
    even_ref[...] = jnp.where(even, messages[1], messages[0]).astype(BF16)
    odd_ref[...] = jnp.where(even, messages[0], messages[1]).astype(BF16)


def unpacked(packed, b):
    ends = end_lanes((8, 128))
    rows = []
    for i in range(8):
        u = 56 - 8 * i + b
        moved = pltpu.roll(packed, (128 - 2 * u) % 128, 1) if u else packed
        rows.append(jnp.where(ends, moved, 0.0))
    return rows


def assembled(s_ref, x_ref, packed, f, a, b, y_refs=None):
    span = slice(8 * b, 8 * b + 8)
    at = span_of(a, 32 * f)
    block = s_ref[at, span, :]
    if packed is None:
        rows = [jnp.zeros((8, 128), F32) for _ in range(8)]
    else:
        rows = unpacked(packed, b)
    if not isinstance(a, int):
        rows[0] = rows[0] + jnp.where(a == 0, x_ref[0, f, span, :], 0.0)
        rows[7] = rows[7] + jnp.where(a == 3, x_ref[1, f, span, :], 0.0)
    elif a == 0:
        rows[0] = rows[0] + x_ref[0, f, span, :]
    elif a == 3:
        rows[7] = rows[7] + x_ref[1, f, span, :]
    if y_refs is not None:
        one_ref, two_ref = y_refs
        even = (lax.axis_index("ey") & 1) == 0
        at = slice(16 * (a // 2) + 32 * f, 16 * (a // 2) + 32 * f + 16)
        one, two = one_ref[at, :].astype(F32), two_ref[at, :].astype(F32)
        if b == 0:
            line, sublane = jnp.where(even, two, one), 0
        else:
            line, sublane = jnp.where(even, one, two), 7
        line = line[8 * (a % 2) : 8 * (a % 2) + 8]
        node = lax.broadcasted_iota(jnp.int32, (8, 8, 128), 1)
        block = block + jnp.where(node == sublane, line[:, None, :], 0.0)
    return block.reshape(64, 128) + jnp.concatenate(rows, axis=0)


def second_pairs(
    pairs, s_ref, x_ref, packed_ref, y_refs, scalar_ref, velocity_ref,
    mass_ref, table_ref, g_ref, base_ref, half_ref, z_ref, first_ref=None,
):
    def body(a, layer=None):
        at = span_of(a)
        layer = a if layer is None else layer
        to = span_of(layer)
        radial_g = packed_ref[a]
        radial_m = packed_ref[a + 4]
        spreads = []
        for n, pair in enumerate(pairs):
            fields, velocities, masses = [], [], []
            for h, b in enumerate(pair):
                s = slice(8 * b, 8 * b + 8)
                out = slice(16 * n + 8 * h, 16 * n + 8 * h + 8)
                g = assembled(s_ref, x_ref, radial_g, 0, a, b, y_refs)
                m = assembled(s_ref, x_ref, radial_m, 1, a, b, y_refs)
                scale = time_step / m
                scalar = scalar_ref[at, s, :].reshape(64, 128)
                first = scalar - scale * g
                base_ref[to, out, :] = (0.5 * (scalar + first)).reshape(8, 8, 128)
                half_ref[to, out, :] = (0.5 * scale).reshape(8, 8, 128)
                fields.append(first)
                if first_ref is not None:
                    first_ref[to, out, :] = first.reshape(8, 8, 128)
                velocities.append(
                    [velocity_ref[d, at, s, :].reshape(64, 128) for d in range(3)]
                )
                masses.append(mass_ref[at, s, :].reshape(64, 128))
            values = convect_pair(fields, velocities, masses, table_ref)
            joined, spread = join_lanes(values, table_ref)
            for h, b in enumerate(pair):
                out = slice(16 * n + 8 * h, 16 * n + 8 * h + 8)
                g_ref[to, out, :] = joined[h].reshape(8, 8, 128)
                spreads.append((b, spread[h]))
        z_ref[layer] = pick_spread(spreads)

    return body


def second_inner_kernel(
    s_ref, x_ref, packed_ref, scalar_ref, velocity_ref, mass_ref,
    table_ref, g_ref, base_ref, half_ref, z_ref,
):
    body = second_pairs(
        ((1, 2), (3, 4), (5, 6)), s_ref, x_ref, packed_ref, None,
        scalar_ref, velocity_ref, mass_ref, table_ref, g_ref, base_ref, half_ref, z_ref,
    )
    sweep(body, 2)
    join_block(g_ref)


def add_beyond(layers, y_one_ref, y_two_ref, first_ref, scalar_ref, table_ref, g_ref, z_ref):
    even = (lax.axis_index("ey") & 1) == 0
    one, two = y_one_ref[64:, :].astype(F32), y_two_ref[64:, :].astype(F32)
    sides = (jnp.where(even, two, one), jnp.where(even, one, two))
    rows = []
    for h, (line, outer) in enumerate(((0, 0), (15, 63))):
        for a, n in layers:
            change = first_ref[span_of(n), line, :] - scalar_ref[span_of(a), outer, :]
            rows.append(sides[h][128 + 8 * a : 136 + 8 * a] + change)
    count = len(layers)
    field = jnp.concatenate(rows + [jnp.zeros((64 - 16 * count, 128), F32)], axis=0)
    high, low = halves(field)
    axial = dot(row_table(table_ref, 64), jnp.concatenate([high, low, high], axis=0))
    radius = by_lanes([(high, low)], table_ref)
    corner = float(gll_derivative()[7, 7])
    values = []
    for h, sign in ((0, corner), (1, -corner)):
        for k, (a, _) in enumerate(layers):
            at = slice(8 * (count * h + k), 8 * (count * h + k) + 8)
            share, *flow = [sides[h][32 * n + 8 * a : 32 * n + 8 * a + 8] for n in range(4)]
            azimuth = sign * field[at]
            values.append(share + flow[0] * axial[at] + flow[1] * azimuth + flow[2] * radius[at])
    (joined,), (spread,) = join_lanes([jnp.concatenate(values, axis=0)], table_ref)
    slot = ((lane_ids((8, 128)) + 1) >> 1) & 63
    row = row_ids((8, 128))
    for h, line in ((0, 0), (1, 15)):
        for k, (_, n) in enumerate(layers):
            at = slice(8 * (count * h + k), 8 * (count * h + k) + 8)
            g_ref[span_of(n), line, :] = g_ref[span_of(n), line, :] + joined[at]
            mine = jnp.where(slot == 56 - 8 * row + 7 * h, spread[at], 0.0)
            total = jnp.sum(mine, axis=0, keepdims=True)
            z_ref[n] = z_ref[n] + jnp.where(row == 7 * h, total, 0.0)


def second_face_kernel(
    s_ref, x_ref, packed_ref, y_one_ref, y_two_ref, scalar_ref, velocity_ref,
    mass_ref, table_ref, inner_ref, x_out_ref, edge_ref, base_ref, half_ref, z_ref, first_ref,
):
    body = second_pairs(
        ((0, 7),), s_ref, x_ref, packed_ref, (y_one_ref, y_two_ref), scalar_ref, velocity_ref,
        mass_ref, table_ref, edge_ref, base_ref, half_ref, z_ref, first_ref,
    )
    body(0, 0)
    body(3, 1)
    add_beyond(((0, 0), (3, 1)), y_one_ref, y_two_ref, first_ref, scalar_ref, table_ref, edge_ref, z_ref)
    row = row_ids((64, 128))
    for n, (layer, at) in enumerate(((15, 31), (0, 0))):
        face = jnp.concatenate(
            [edge_ref[layer, 0:8, :], inner_ref[at], edge_ref[layer, 8:16, :]], axis=0
        )
        after = jnp.where((row == 7) | (row == 55), pltpu.roll(face, 63, 0), 0.0)
        before = jnp.where((row == 8) | (row == 56), pltpu.roll(face, 1, 0), 0.0)
        x_out_ref[n, 0] = (face + (after + before)).astype(BF16)


def second_outer_kernel(
    s_ref, x_ref, packed_ref, y_one_ref, y_two_ref, scalar_ref, velocity_ref,
    mass_ref, table_ref, inner_ref, z_in, edge_in, base_in, half_in, z_face,
    g_ref, base_ref, half_ref, z_ref, edge_ref, first_ref,
):
    body = second_pairs(
        ((0, 7),), s_ref, x_ref, packed_ref, (y_one_ref, y_two_ref), scalar_ref, velocity_ref,
        mass_ref, table_ref, edge_ref, base_ref, half_ref, z_ref, first_ref,
    )
    body(1)
    body(2)
    add_beyond(((1, 1), (2, 2)), y_one_ref, y_two_ref, first_ref, scalar_ref, table_ref, edge_ref, z_ref)
    for layer, a in ((0, 0), (1, 3)):
        for source, target in ((edge_in, edge_ref), (base_in, base_ref), (half_in, half_ref)):
            target[span_of(a)] = source[span_of(layer)]
        z_ref[a] = z_face[layer]
    join_axial(edge_ref)
    g_ref[:, 0:8, :] = edge_ref[:, 0:8, :]
    g_ref[:, 8:56, :] = inner_ref[...]
    g_ref[:, 56:64, :] = edge_ref[:, 8:16, :]
    for low in (7, 55):
        total = g_ref[:, low, :] + g_ref[:, low + 1, :]
        g_ref[:, low, :] = total
        g_ref[:, low + 1, :] = total
    for n, value in enumerate(join_packed([z_ref[a] + z_in[a] for a in range(4)])):
        z_ref[n] = value


def weight_kernel(weight_ref, out_ref):
    row = row_ids((512, 512))
    source = (row & 63) * 8 + (row >> 6)
    order = jnp.where(lane_ids((512, 512)) == source, 1.0, 0.0).astype(BF16)
    for m in range(8):
        out_ref[:, 128 * m : 128 * m + 128] = dot(order, weight_ref[m]).astype(BF16)


def pick_kernel(cut_ref, pick_ref):
    cut = cut_ref[...]
    a, b, c = cut >> 7, (cut >> 4) & 7, cut & 15
    order = jnp.where(a == 0, 2, jnp.where(a == 3, 3, a - 1))
    inner = 128 * order + 16 * b + c
    ends = 512 + 16 * a + 2 * b + (c >> 3)
    place = jnp.where((c == 0) | (c == 15), ends, inner)
    turned = place.astype(F32).T.astype(jnp.int32)
    lane = lane_ids((128, 640))
    for m in range(8):
        pick_ref[m] = jnp.where(lane == turned[:, m : m + 1], 1.0, 0.0).astype(BF16)


def turn(blocks, table):
    rows = []
    for block in blocks:
        value = block.astype(BF16)
        zero = jnp.zeros_like(value)
        rows.append(jnp.concatenate([value, zero], axis=1))
        rows.append(jnp.concatenate([zero, value], axis=1))
    return lax.dot_general(
        table,
        jnp.concatenate(rows, axis=0),
        (((1,), (1,)), ((), ())),
        preferred_element_type=F32,
    )


PAIRS = ((0, 1), (2, 3), (4, 5), (6, 7))


def term(refs, a, b):
    inner_ref, outer_ref = refs
    at = span_of(a)
    if b in (0, 7):
        return outer_ref[at, 8 * (b // 7) : 8 * (b // 7) + 8, :].reshape(64, 128)
    return inner_ref[at, 8 * b - 8 : 8 * b, :].reshape(64, 128)


def advanced(g_ref, x_ref, packed, bases, halfs, a, pair):
    blocks = []
    for b in pair:
        g = assembled(g_ref, x_ref, packed, 0, a, b)
        blocks.append(term(bases, a, b) - term(halfs, a, b) * g)
    return blocks


def store_elements(element_ref, blocks, table_ref, place):
    turned = turn(blocks, turn_table(table_ref)).astype(BF16)
    for h in range(2):
        for k in range(4):
            element_ref[place + 16 * h : place + 16 * h + 16, 128 * k : 128 * k + 128] = turned[
                16 * k : 16 * k + 16, 128 * h : 128 * h + 128
            ]


def pixel_values(element_ref, weight_ref, m):
    return dot(element_ref[...], weight_ref[:, 256 * m : 256 * m + 256]).astype(BF16)


def layer_elements(layers, g_ref, x_ref, bases, halfs, table_ref, element_ref):
    place = 0
    for a in layers:
        for pair in PAIRS:
            blocks = advanced(g_ref, x_ref, None, bases, halfs, a, pair)
            store_elements(element_ref, blocks, table_ref, place)
            place += 32


def early_kernel(
    g_ref, base_one, half_one, base_two, half_two, table_ref, weight_ref, pick_ref,
    pixel_ref, element_ref,
):
    bases, halfs = (base_one, base_two), (half_one, half_two)
    layer_elements((1, 2), g_ref, None, bases, halfs, table_ref, element_ref)
    for m in range(4):
        values = pixel_values(element_ref, weight_ref, m)
        for n in range(2):
            pixel_ref[2 * m + n] = dot(
                pick_ref[2 * m + n, :, :256], values[:, 128 * n : 128 * n + 128]
            )


def middle_kernel(
    g_ref, x_ref, base_one, half_one, base_two, half_two, table_ref, weight_ref, pick_ref,
    early_ref, pixel_ref, element_ref,
):
    bases, halfs = (base_one, base_two), (half_one, half_two)
    layer_elements((0, 3), g_ref, x_ref, bases, halfs, table_ref, element_ref)
    for m in range(4):
        values = pixel_values(element_ref, weight_ref, m)
        for n in range(2):
            pixel_ref[2 * m + n] = early_ref[2 * m + n] + dot(
                pick_ref[2 * m + n, :, 256:512], values[:, 128 * n : 128 * n + 128]
            )


def fill_payload(payload_ref, d, cam_count, ends, weight_ref, pick_ref, pixel_ref):
    owner = lax.axis_index("cam") ^ d
    share = pixel_ref.shape[0] // cam_count
    width = 128 * share
    block = weight_ref[:, pl.ds(pl.multiple_of(owner * width, 128), width)]
    values = dot(ends, block).astype(BF16)
    for n in range(share):
        m = share * owner + n
        picked = dot(pick_ref[m, :, 512:576], values[:, 128 * n : 128 * n + 128])
        payload_ref[n] = (picked + pixel_ref[m]).astype(BF16)


def final_layers(cam_count, g_ref, x_ref, one_ref, two_ref, terms, use):
    base_one, half_one, base_two, half_two = terms
    bases, halfs = (base_one, base_two), (half_one, half_two)
    one, two = one_ref[:32, :].astype(F32), two_ref[:32, :].astype(F32)
    for a in range(4):
        packed = merged(one[8 * a : 8 * a + 8], two[8 * a : 8 * a + 8], cam_count)
        for pair in PAIRS:
            use(a, pair, advanced(g_ref, x_ref, packed, bases, halfs, a, pair))


def render_far_kernel(
    cam_count, g_ref, x_ref, one_ref, two_ref, base_one, half_one, base_two, half_two,
    table_ref, weight_ref, pick_ref, pixel_ref, out_ref, *rest,
):
    payload_refs, end_ref = rest[:-1], rest[-1]

    def use(a, pair, blocks):
        turned = turn(blocks, end_table(table_ref))
        for h, b in enumerate(pair):
            place = 16 * a + 2 * b
            for k in range(4):
                end_ref[place : place + 2, 128 * k : 128 * k + 128] = turned[
                    2 * k : 2 * k + 2, 128 * h : 128 * h + 128
                ]

    terms = (base_one, half_one, base_two, half_two)
    final_layers(cam_count, g_ref, x_ref, one_ref, two_ref, terms, use)
    ends = end_ref[...].astype(BF16)
    out_ref[...] = ends
    for d in range(2, cam_count):
        fill_payload(payload_refs[d - 2], d, cam_count, ends, weight_ref, pick_ref, pixel_ref)


def advected_kernel(
    cam_count, g_ref, x_ref, one_ref, two_ref, base_one, half_one, base_two, half_two,
    out_hbm, advected_ref, sems,
):
    copies = []

    def use(a, pair, blocks):
        for h, b in enumerate(pair):
            advected_ref[span_of(a), 8 * b : 8 * b + 8, :] = blocks[h].reshape(8, 8, 128)
        if pair == PAIRS[-1]:
            at = span_of(a)
            copy = pltpu.make_async_copy(advected_ref.at[at], out_hbm.at[at], sems.at[a])
            copy.start()
            copies.append(copy)

    terms = (base_one, half_one, base_two, half_two)
    final_layers(cam_count, g_ref, x_ref, one_ref, two_ref, terms, use)
    for copy in copies:
        copy.wait()


def render_near_kernel(cam_count, d, end_ref, weight_ref, pick_ref, pixel_ref, payload_ref):
    fill_payload(payload_ref, d, cam_count, end_ref[...], weight_ref, pick_ref, pixel_ref)


def own_image_kernel(
    cam_count, end_ref, weight_ref, pick_ref, pixel_ref, block_ref, first_ref, second_ref,
    image_ref, onehot_ref, payload_ref, id_ref,
):
    me = lax.axis_index("cam")
    share = image_ref.shape[0]
    id_ref[0] = block_ref[...]
    tiles = ((1, first_ref[64:80, :]), (3, second_ref[32:48, :]), (2, second_ref[48:64, :]))
    for d, tile in tiles:
        ids = tile.astype(F32).astype(jnp.int32)
        id_ref[d] = ids[:8] * 32 + ids[8:]
    fill_payload(payload_ref, 0, cam_count, end_ref[...], weight_ref, pick_ref, pixel_ref)
    for m in range(share):
        ids = [id_ref[d, pl.ds(share * me + m, 1), :] for d in range(4)]
        ids = jnp.concatenate(ids, axis=1)
        for chunk in range(4):
            at = slice(256 * chunk, 256 * chunk + 256)
            row = row_ids((256, ids.shape[1])) + 256 * chunk
            onehot = jnp.where(row == ids, 1.0, 0.0).astype(BF16)
            onehot_ref[m, at, :] = onehot
            image_ref[m, at, :] = dot(onehot[:, :128], payload_ref[m])


def image_kernel(own_ref, onehot_ref, *refs):
    payload_refs, (image_hbm, image_ref, sems) = refs[:-3], refs[-3:]
    copies = []
    for m in range(image_ref.shape[0]):
        values = jnp.concatenate([payload_ref[m] for payload_ref in payload_refs], axis=0)
        for chunk in range(4):
            at = slice(256 * chunk, 256 * chunk + 256)
            image_ref[m, at, :] = own_ref[m, at, :] + dot(onehot_ref[m, at, 128:], values)
            copy = pltpu.make_async_copy(
                image_ref.at[m, at], image_hbm.at[m, at], sems.at[4 * m + chunk]
            )
            copy.start()
            copies.append(copy)
    for copy in copies:
        copy.wait()


def call(kernel, out_shape, flops=10**8, size=10**7, **options):
    return pl.pallas_call(
        kernel,
        out_shape=out_shape,
        compiler_params=pltpu.CompilerParams(vmem_limit_bytes=24 * 2**20),
        cost_estimate=pl.CostEstimate(flops=flops, bytes_accessed=size, transcendentals=0),
        **options,
    )


def shape_of(*shape, dtype=F32):
    return jax.ShapeDtypeStruct(shape, dtype)


def stay(*arrays):
    return [pltpu.with_memory_space_constraint(x, pltpu.HBM) for x in arrays]


def swaps(axis):
    count = lax.axis_size(axis)
    even = [(i, i ^ 1) for i in range(count)]
    odd = [(i, (i + 1) % count if i & 1 else (i - 1) % count) for i in range(count)]
    return even, odd


def swap_axial(x):
    count = lax.axis_size("ex")
    up = [(i, (i + 1) % count) for i in range(count)]
    if count == 2:
        return lax.ppermute(x, "ex", up)
    down = [(j, i) for i, j in up]
    return jnp.stack([lax.ppermute(x[0], "ex", up), lax.ppermute(x[1], "ex", down)])


def swap_both(one, two, axis):
    even, odd = swaps(axis)
    return lax.ppermute(one, axis, even), lax.ppermute(two, axis, odd)


def per_device(scalar, velocity, lumped_mass, pixel_weights, cut_element, pixel_block):
    shape = scalar.shape
    flat = (32, 64, 128)
    inner, outer = (32, 48, 128), (32, 16, 128)
    scalar = scalar.reshape(flat)
    velocity = velocity.reshape((3,) + flat)
    mass = lumped_mass.reshape(flat)
    tables = derivative_tables()
    n_cam = lax.axis_size("cam")
    cameras = pixel_weights.shape[0]
    share = cameras // n_cam
    part = functools.partial

    x, near = call(
        face_kernel,
        (shape_of(2, 2, 64, 128, dtype=BF16), shape_of(*tables.shape, dtype=BF16)),
        in_specs=[HBM] * 4,
        scratch_shapes=[
            pltpu.VMEM((2, 8, 64, 128), F32),
            pltpu.VMEM((2, 3, 64, 128), F32),
            pltpu.VMEM((2, 64, 128), F32),
            pltpu.SemaphoreType.DMA((7,)),
        ],
    )(*stay(scalar, velocity, mass, tables))
    x_got = swap_axial(x)
    s, z = call(first_kernel, (shape_of(64, 64, 128), shape_of(8, 8, 128)))(
        scalar, velocity, mass, near
    )
    weights = call(weight_kernel, shape_of(512, 128 * cameras, dtype=BF16))(pixel_weights)
    picks = call(pick_kernel, shape_of(cameras, 128, 640, dtype=BF16))(cut_element)

    half = functools.partial(shape_of, dtype=BF16)
    *z, x_got = call(
        first_radial_kernel, (half(80, 128), half(64, 128), shape_of(2, 2, 64, 128))
    )(z, x_got, pixel_block)
    z_got = swap_both(*z, "cam")
    z_got, weights, picks = lax.optimization_barrier((z_got, weights, picks))
    ids_got = z_got[0]
    *y, packed = call(
        part(azimuth_kernel, n_cam), (half(224, 128), half(224, 128), shape_of(8, 8, 128))
    )(s, x_got, *z_got, scalar, velocity, mass, near)
    y_got = swap_both(*y, "ey")
    g_inner, *inner_terms, z_inner = call(
        second_inner_kernel, (shape_of(*inner),) * 3 + (shape_of(4, 8, 128),)
    )(s, x_got, packed, scalar, velocity, mass, near)
    args = (s, x_got, packed, *y_got, scalar, velocity, mass, near, g_inner)
    some = (16, 16, 128)
    x, *faces = call(
        second_face_kernel,
        (shape_of(2, 1, 64, 128, dtype=BF16),) + (shape_of(*some),) * 3 + (shape_of(2, 8, 128),),
        scratch_shapes=[pltpu.VMEM(some, F32)],
    )(*args)
    g, *outer_terms, z = call(
        second_outer_kernel,
        (shape_of(*flat), shape_of(*outer), shape_of(*outer), shape_of(4, 8, 128)),
        scratch_shapes=[pltpu.VMEM(outer, F32), pltpu.VMEM(outer, F32)],
    )(*args, z_inner, *faces)

    terms = (*inner_terms, *outer_terms)
    x_got = swap_axial(x)
    early = call(
        early_kernel,
        shape_of(cameras, 128, 128),
        scratch_shapes=[pltpu.VMEM((256, 512), BF16)],
    )(g, *terms, near, weights, picks)
    x_got, early = lax.optimization_barrier((x_got, early))
    *z, x_got = call(
        second_radial_kernel, (half(32, 128), half(64, 128), shape_of(2, 1, 64, 128))
    )(z, x_got, pixel_block, ids_got)
    z_got = swap_both(*z, "cam")
    pixels = call(
        middle_kernel,
        shape_of(cameras, 128, 128),
        scratch_shapes=[pltpu.VMEM((256, 512), BF16)],
    )(g, x_got, *terms, near, weights, picks, early)
    z_got, pixels = lax.optimization_barrier((z_got, pixels))
    payload_shape = half(share, 128, 128)
    ends, *far = call(
        part(render_far_kernel, n_cam),
        (half(64, 512),) + (payload_shape,) * (n_cam - 2),
        scratch_shapes=[pltpu.VMEM((64, 512), F32)],
    )(g, x_got, *z_got, *terms, near, weights, picks, pixels)
    parts = (ends, weights, picks, pixels)
    image_shape = shape_of(share, NBLK, 128)
    images, onehot = call(
        part(own_image_kernel, n_cam),
        (image_shape, half(share, NBLK, 128 * n_cam)),
        scratch_shapes=[
            pltpu.VMEM(payload_shape.shape, BF16),
            pltpu.VMEM((n_cam, cameras, 128), jnp.int32),
        ],
    )(*parts, pixel_block, ids_got, z_got[1])
    images, parts = lax.optimization_barrier((images, parts))
    beside = call(part(render_near_kernel, n_cam, 1), payload_shape)(*parts)
    final = (g, x_got, *z_got, *terms)
    final, beside = lax.optimization_barrier((final, beside))
    advected = call(
        part(advected_kernel, n_cam),
        shape_of(*flat),
        out_specs=HBM,
        scratch_shapes=[pltpu.VMEM(flat, F32), pltpu.SemaphoreType.DMA((4,))],
    )(*final)
    images, advected = lax.optimization_barrier((images, advected))
    received = []
    for d, payload in [(1, beside)] + [(n + 2, p) for n, p in enumerate(far)]:
        received.append(lax.ppermute(payload, "cam", [(i, i ^ d) for i in range(n_cam)]))
    images = call(
        image_kernel,
        image_shape,
        out_specs=HBM,
        scratch_shapes=[
            pltpu.VMEM((share, NBLK, 128), F32),
            pltpu.SemaphoreType.DMA((4 * share,)),
        ],
    )(images, onehot, *received)
    return (advected.reshape(shape), images)


def solution(mesh):
    placed = (
        P("ex", None, "ey", None, "cam"),
        P(None, "ex", None, "ey", None, "cam"),
        P("ex", None, "ey", None, "cam"),
        P(),
        P(None, ("cam", "ex", "ey")),
        P(None, ("cam", "ex", "ey")),
    )
    return jax.shard_map(
        per_device,
        mesh=mesh,
        in_specs=placed,
        out_specs=(P("ex", None, "ey", None, "cam"), P("cam", ("ex", "ey"), None)),
        check_vma=False,
    )
```

```python
import functools

import jax
import jax.numpy as jnp
import numpy as np
from jax import lax
from jax.experimental import pallas as pl
from jax.experimental.pallas import tpu as pltpu
from jax.sharding import PartitionSpec as P

NBLK = 1024
F32 = jnp.float32
BF16 = jnp.bfloat16
VMEM = pl.BlockSpec(memory_space=pltpu.VMEM)
HBM = pl.BlockSpec(memory_space=pltpu.HBM)
time_step = 0.01


def legendre_seven(points):
    previous = points * 0.0 + 1.0
    current = points * 1.0
    for order in range(1, 7):
        following = ((2 * order + 1) * points * current - order * previous) / (order + 1)
        previous = current
        current = following
    return current


def gll_derivative():
    degree = 7
    gll_nodes = np.array(
        [
            -1.0,
            -0.8717401485096066,
            -0.5917001814331423,
            -0.2092992179024789,
            0.2092992179024789,
            0.5917001814331423,
            0.8717401485096066,
            1.0,
        ]
    )
    values = legendre_seven(gll_nodes)
    derivative = np.zeros((degree + 1, degree + 1))
    for target in range(degree + 1):
        for source in range(degree + 1):
            if target != source:
                derivative[target, source] = values[target] / (
                    values[source] * (gll_nodes[target] - gll_nodes[source])
                )
    derivative[0, 0] = -degree * (degree + 1) / 4.0
    derivative[degree, degree] = degree * (degree + 1) / 4.0
    return derivative


def split_two(table):
    high = table.astype(np.float32).astype(BF16)
    low = (table - high.astype(np.float64)).astype(np.float32).astype(BF16)
    return high, low


def derivative_tables():
    derivative = gll_derivative()
    eye = np.eye(8)
    rows = np.concatenate([np.kron(derivative, eye), np.kron(eye, derivative)], axis=0)
    high, low = split_two(rows)
    row_table = np.concatenate([high, high, low, np.zeros_like(high)], axis=1)
    high, low = split_two(np.kron(np.eye(16), derivative.T))
    lane_table = np.concatenate(
        [
            np.concatenate([high, low], axis=1),
            np.concatenate([high, np.zeros_like(high)], axis=1),
        ],
        axis=0,
    )
    swap = np.zeros((128, 128))
    for c in range(15):
        swap[8 * c + 7, 8 * c + 8] = 1.0
        swap[8 * c + 8, 8 * c + 7] = 1.0
    join_table = np.concatenate([swap, swap], axis=0).astype(np.float32).astype(BF16)
    spread = np.zeros((128, 128))
    spread[0, 0::2] = 1.0
    spread[127, 1::2] = 1.0
    turn = np.zeros((64, 256))
    for k in range(4):
        for c in range(16):
            turn[16 * k + c, 8 * c + 2 * k] = 1.0
            turn[16 * k + c, 128 + 8 * c + 2 * k + 1] = 1.0
    ends = turn.reshape(4, 16, 256)[:, ::15].reshape(8, 256)
    ends = np.concatenate([ends, np.zeros_like(ends)], axis=0)
    partial = np.zeros((16, 64))
    for i in range(8):
        partial[i, 8 * i + 1 : 8 * i + 8] = derivative[0, 1:]
        partial[8 + i, 8 * i : 8 * i + 7] = derivative[7, :7]
    high, low = split_two(partial)
    partial = np.concatenate([high, high, low, np.zeros_like(high)], axis=1)
    exact = [spread, spread, turn[:, :128], turn[:, 128:], ends[:, :128], ends[:, 128:]]
    exact = np.concatenate(exact, axis=0)
    split = [row_table[:, :128], row_table[:, 128:], lane_table[:, :128], lane_table[:, 128:]]
    split += [join_table, exact.astype(np.float32).astype(BF16)]
    split += [partial[:, :128], partial[:, 128:]]
    return jnp.asarray(np.concatenate(split, axis=0))


def row_table(table_ref, first=0):
    high, low = table_ref[first:128], table_ref[128 + first : 256]
    return jnp.concatenate([high, low[:, :64]], axis=1)


def lane_table(table_ref):
    return jnp.concatenate([table_ref[256:512], table_ref[512:768]], axis=1)


def join_table(table_ref):
    return jnp.concatenate([table_ref[768:1024], table_ref[1024:1280]], axis=1)


def turn_table(table_ref):
    return jnp.concatenate([table_ref[1280:1344], table_ref[1344:1408]], axis=1)


def end_table(table_ref):
    return jnp.concatenate([table_ref[1408:1424], table_ref[1424:1440]], axis=1)


def partial_table(table_ref):
    return jnp.concatenate([table_ref[1440:1456], table_ref[1456:1472][:, :64]], axis=1)


def span_of(a, offset=0):
    if isinstance(a, int):
        return slice(8 * a + offset, 8 * a + offset + 8)
    return pl.ds(pl.multiple_of(a * 8 + offset, 8), 8)


def sweep(body, together):
    if together == 4:
        for a in range(4):
            body(a)
        return

    def step(n, carry):
        for m in range(together):
            body(n * together + m)
        return carry

    lax.fori_loop(0, 4 // together, step, 0)


def lane_ids(shape):
    return lax.broadcasted_iota(jnp.int32, shape, len(shape) - 1)


def row_ids(shape):
    return lax.broadcasted_iota(jnp.int32, shape, len(shape) - 2)


def halves(value):
    high = value.astype(BF16)
    return high, (value - high.astype(F32)).astype(BF16)


def dot(a, b):
    return jnp.dot(a, b, preferred_element_type=F32)


def by_lanes(pairs, table_ref):
    rows = jnp.concatenate([jnp.concatenate(p, axis=1) for p in pairs], axis=0)
    both = dot(rows, lane_table(table_ref))
    return both[:, :128] + both[:, 128:]


def join_lanes(values, table_ref):
    rows = jnp.concatenate([jnp.concatenate(halves(v), axis=1) for v in values], axis=0)
    other = dot(rows, join_table(table_ref))
    joined, spread, at = [], [], 0
    for v in values:
        span = slice(at, at + v.shape[0])
        joined.append(v + other[span, :128])
        spread.append(other[span, 128:])
        at += v.shape[0]
    return joined, spread


def join_rows(value):
    row = row_ids(value.shape)
    last = ((row & 7) == 7) & (row != 63)
    first = ((row & 7) == 0) & (row != 0)
    other = jnp.where(
        last, pltpu.roll(value, 63, 0), jnp.where(first, pltpu.roll(value, 1, 0), 0.0)
    )
    return value + other


def convect_pair(fields, velocities, masses, table_ref):
    pairs = [halves(f) for f in fields]
    high = jnp.concatenate([p[0] for p in pairs], axis=1)
    low = jnp.concatenate([p[1] for p in pairs], axis=1)
    stacked = jnp.concatenate([high, low, high], axis=0)
    rows = dot(row_table(table_ref), stacked)
    radius = by_lanes(pairs, table_ref)
    out = []
    for n in range(2):
        lanes = slice(128 * n, 128 * n + 128)
        v = velocities[n]
        slope = v[0] * rows[:64, lanes] + v[1] * rows[64:, lanes]
        out.append(masses[n] * (slope + v[2] * radius[64 * n : 64 * n + 64]))
    return out


def face_kernel(
    scalar_hbm, velocity_hbm, mass_hbm, table_hbm, x_ref, table_ref, f_ref, v_ref, m_ref, sems,
):
    copies = []

    def start(source, target):
        copy = pltpu.make_async_copy(source, target, sems.at[len(copies)])
        copy.start()
        copies.append(copy)

    last = scalar_hbm.shape[0] - 1
    start(scalar_hbm.at[pl.ds(last - 7, 8)], f_ref.at[0])
    start(scalar_hbm.at[pl.ds(0, 8)], f_ref.at[1])
    start(table_hbm, table_ref)
    start(velocity_hbm.at[:, last], v_ref.at[0])
    start(velocity_hbm.at[:, 0], v_ref.at[1])
    start(mass_hbm.at[last], m_ref.at[0])
    start(mass_hbm.at[0], m_ref.at[1])
    for copy in copies[:3]:
        copy.wait()
    derivative = gll_derivative()
    fields = [f_ref[0, 7], f_ref[1, 0]]
    pairs = [halves(f) for f in fields]
    high = jnp.concatenate([p[0] for p in pairs], axis=1)
    low = jnp.concatenate([p[1] for p in pairs], axis=1)
    azimuth = dot(row_table(table_ref, 64), jnp.concatenate([high, low, high], axis=0))
    radius = by_lanes(pairs, table_ref)
    for copy in copies[3:]:
        copy.wait()
    values = []
    for n, node in enumerate((7, 0)):
        axial = f_ref[n, 0] * float(derivative[node, 0])
        for p in range(1, 8):
            axial = axial + f_ref[n, p] * float(derivative[node, p])
        slope = v_ref[n, 0] * axial + v_ref[n, 1] * azimuth[:, 128 * n : 128 * n + 128]
        values.append(m_ref[n] * (slope + v_ref[n, 2] * radius[64 * n : 64 * n + 64]))
        values.append(m_ref[n])
    for n, value in enumerate(join_lanes(values, table_ref)[0]):
        x_ref[n // 2, n % 2] = join_rows(value).astype(BF16)


def join_block(s_ref):
    for b in range(s_ref.shape[1] // 8 - 1):
        total = s_ref[:, 8 * b + 7, :] + s_ref[:, 8 * b + 8, :]
        s_ref[:, 8 * b + 7, :] = total
        s_ref[:, 8 * b + 8, :] = total
    join_axial(s_ref)


def join_axial(s_ref):
    for f in range(s_ref.shape[0] // 32):
        for a in range(3):
            at = 32 * f + 8 * a + 7
            total = s_ref[at] + s_ref[at + 1]
            s_ref[at] = total
            s_ref[at + 1] = total


def pack_blocks(blocks):
    slot = ((lane_ids((8, 128)) + 1) >> 1) & 63
    parts = [jnp.zeros((8, 128), F32) for _ in range(4)]
    for n, (u, block) in enumerate(blocks):
        if u:
            block = pltpu.roll(block, 2 * u, 1)
        parts[n % 4] = jnp.where(slot == u, block, parts[n % 4])
    return (parts[0] + parts[1]) + (parts[2] + parts[3])


def pick_spread(spreads):
    slot = ((lane_ids((8, 128)) + 1) >> 1) & 63
    parts = [jnp.zeros((8, 128), F32) for _ in range(2)]
    for b, spread in spreads:
        for i in range(8):
            block = spread[8 * i : 8 * i + 8]
            parts[i % 2] = jnp.where(slot == 56 - 8 * i + b, block, parts[i % 2])
    return parts[0] + parts[1]


def join_packed(packed):
    lane, row = lane_ids((8, 128)), row_ids((8, 128))
    slot = ((lane + 1) >> 1) & 63
    b = slot & 7
    rows = []
    for value in packed:
        after = pltpu.roll(pltpu.roll(value, 126, 1), 7, 0)
        before = pltpu.roll(pltpu.roll(value, 2, 1), 1, 0)
        value = value + jnp.where((row == 7) & (b < 7), after, 0.0)
        rows.append(value + jnp.where((row == 0) & (b > 0), before, 0.0))
    out = list(rows)
    for a in range(3):
        out[a] = out[a] + jnp.where(slot < 8, pltpu.roll(rows[a + 1], 16, 1), 0.0)
        out[a + 1] = out[a + 1] + jnp.where(slot >= 56, pltpu.roll(rows[a], 112, 1), 0.0)
    return out


def first_kernel(scalar_ref, velocity_ref, mass_ref, table_ref, s_ref, z_ref):
    def body(a):
        at = span_of(a)
        spreads = [[], []]
        for pair in range(4):
            spans = [slice(16 * pair + 8 * n, 16 * pair + 8 * n + 8) for n in range(2)]
            fields = [scalar_ref[at, s, :].reshape(64, 128) for s in spans]
            velocities = [
                [velocity_ref[d, at, s, :].reshape(64, 128) for d in range(3)] for s in spans
            ]
            masses = [mass_ref[at, s, :].reshape(64, 128) for s in spans]
            values = convect_pair(fields, velocities, masses, table_ref)
            joined, spread = join_lanes(values + masses, table_ref)
            for n, s in enumerate(spans):
                for f in range(2):
                    s_ref[span_of(a, 32 * f), s, :] = joined[n + 2 * f].reshape(8, 8, 128)
                    spreads[f].append((2 * pair + n, spread[n + 2 * f]))
        for f in range(2):
            z_ref[a + 4 * f] = pick_spread(spreads[f])

    sweep(body, 2)
    join_block(s_ref)
    for f in range(2):
        for n, value in enumerate(join_packed([z_ref[4 * f + a] for a in range(4)])):
            z_ref[4 * f + n] = value


def radial_faces(count, z_in, x_in, x_ref):
    x_ref[...] = x_in[...].astype(F32)
    rows = []
    for f in range(count):
        spans = [slice(8 * b, 8 * b + 8) for b in range(8)]
        low = pack_blocks([(56 + b, x_ref[0, f, s, :]) for b, s in enumerate(spans)])
        high = pack_blocks([(b, x_ref[1, f, s, :]) for b, s in enumerate(spans)])
        rows += [z_in[4 * f] + low, z_in[4 * f + 1], z_in[4 * f + 2], z_in[4 * f + 3] + high]
    return jnp.concatenate(rows, axis=0).astype(BF16)


def id_tile(block_ref):
    ids = block_ref[...]
    return jnp.concatenate([ids >> 5, ids & 31], axis=0).astype(F32).astype(BF16)


def first_radial_kernel(z_in, x_in, block_ref, one_ref, two_ref, x_ref):
    faces = radial_faces(2, z_in, x_in, x_ref)
    one_ref[:64, :] = faces
    one_ref[64:, :] = id_tile(block_ref)
    two_ref[...] = faces


def second_radial_kernel(z_in, x_in, block_ref, got_ref, one_ref, two_ref, x_ref):
    faces = radial_faces(1, z_in, x_in, x_ref)
    one_ref[...] = faces
    two_ref[:32, :] = faces
    two_ref[32:48, :] = id_tile(block_ref)
    two_ref[48:, :] = got_ref[64:, :]


def merged(one, two, cam_count):
    me = lax.axis_index("cam")
    even = (me & 1) == 0
    left = jnp.where(even, two, one)
    right = jnp.where(even, one, two)
    left = jnp.where(me == 0, 0.0, left)
    right = jnp.where(me == cam_count - 1, 0.0, right)
    lane = lane_ids((8, 128))
    return jnp.where((lane & 1) == 0, pltpu.roll(left, 1, 1), pltpu.roll(right, 127, 1))


def end_lanes(shape):
    lane = lane_ids(shape)
    return (lane == 0) | (lane == 127)


def azimuth_kernel(
    cam_count, s_ref, x_ref, one_ref, two_ref, scalar_ref, velocity_ref, mass_ref, table_ref,
    odd_ref, even_ref, packed_ref,
):
    ends = end_lanes((8, 128))
    row = row_ids((8, 128))
    even = (lax.axis_index("ey") & 1) == 0
    count = s_ref.shape[0]
    one = one_ref[:count, :].astype(F32)
    two = two_ref[:count, :].astype(F32)
    low, high = [], []
    for q in range(count // 8):
        at = slice(8 * q, 8 * q + 8)
        packed = merged(one[at], two[at], cam_count)
        packed_ref[q] = packed
        f, a = q // 4, q % 4
        for line, shift, faces in ((0, 16, low), (63, 2, high)):
            j = line & 7
            spread = jnp.broadcast_to(packed[j : j + 1, :], (8, 128))
            moved = pltpu.roll(spread, shift, 1, stride=16, stride_axis=0)
            face = s_ref[at, line, :] + jnp.where(ends, moved, 0.0)
            if a == 0:
                face = face + jnp.where(row == 0, x_ref[0, f, line : line + 1, :], 0.0)
            if a == 3:
                face = face + jnp.where(row == 7, x_ref[1, f, line : line + 1, :], 0.0)
            faces.append(face)
    slopes = [[], []]
    for a in range(4):
        pairs = []
        for b in (0, 7):
            g = assembled(s_ref, x_ref, packed_ref[a], 0, a, b)
            m = assembled(s_ref, x_ref, packed_ref[a + 4], 1, a, b)
            scalar = scalar_ref[span_of(a), 8 * b : 8 * b + 8, :].reshape(64, 128)
            pairs.append(halves(scalar - (time_step / m) * g))
        tops = jnp.concatenate([p[0] for p in pairs], axis=1)
        rests = jnp.concatenate([p[1] for p in pairs], axis=1)
        both = dot(partial_table(table_ref), jnp.concatenate([tops, rests, tops], axis=0))
        slopes[0].append(both[:8, :128])
        slopes[1].append(both[8:, 128:])
    messages = []
    for faces, line, slope in ((low, 0, slopes[0]), (high, 63, slopes[1])):
        flow = [mass_ref[:, line, :] * velocity_ref[d, :, line, :] for d in range(3)]
        share = flow[1] * jnp.concatenate(slope, axis=0)
        rows = faces + [share] + flow + [scalar_ref[:, line, :]]
        messages.append(jnp.concatenate(rows, axis=0))
    even_ref[...] = jnp.where(even, messages[1], messages[0]).astype(BF16)
    odd_ref[...] = jnp.where(even, messages[0], messages[1]).astype(BF16)


def unpacked(packed, b):
    ends = end_lanes((8, 128))
    rows = []
    for i in range(8):
        u = 56 - 8 * i + b
        moved = pltpu.roll(packed, (128 - 2 * u) % 128, 1) if u else packed
        rows.append(jnp.where(ends, moved, 0.0))
    return rows


def assembled(s_ref, x_ref, packed, f, a, b, y_refs=None):
    span = slice(8 * b, 8 * b + 8)
    at = span_of(a, 32 * f)
    block = s_ref[at, span, :]
    if packed is None:
        rows = [jnp.zeros((8, 128), F32) for _ in range(8)]
    else:
        rows = unpacked(packed, b)
    if not isinstance(a, int):
        rows[0] = rows[0] + jnp.where(a == 0, x_ref[0, f, span, :], 0.0)
        rows[7] = rows[7] + jnp.where(a == 3, x_ref[1, f, span, :], 0.0)
    elif a == 0:
        rows[0] = rows[0] + x_ref[0, f, span, :]
    elif a == 3:
        rows[7] = rows[7] + x_ref[1, f, span, :]
    if y_refs is not None:
        one_ref, two_ref = y_refs
        even = (lax.axis_index("ey") & 1) == 0
        at = slice(16 * (a // 2) + 32 * f, 16 * (a // 2) + 32 * f + 16)
        one, two = one_ref[at, :].astype(F32), two_ref[at, :].astype(F32)
        if b == 0:
            line, sublane = jnp.where(even, one, two), 0
        else:
            line, sublane = jnp.where(even, two, one), 7
        line = line[8 * (a % 2) : 8 * (a % 2) + 8]
        node = lax.broadcasted_iota(jnp.int32, (8, 8, 128), 1)
        block = block + jnp.where(node == sublane, line[:, None, :], 0.0)
    return block.reshape(64, 128) + jnp.concatenate(rows, axis=0)


def second_pairs(
    pairs, s_ref, x_ref, packed_ref, y_refs, scalar_ref, velocity_ref,
    mass_ref, table_ref, g_ref, base_ref, half_ref, z_ref, first_ref=None,
):
    def body(a, layer=None):
        at = span_of(a)
        layer = a if layer is None else layer
        to = span_of(layer)
        radial_g = packed_ref[a]
        radial_m = packed_ref[a + 4]
        spreads = []
        for n, pair in enumerate(pairs):
            fields, velocities, masses = [], [], []
            for h, b in enumerate(pair):
                s = slice(8 * b, 8 * b + 8)
                out = slice(16 * n + 8 * h, 16 * n + 8 * h + 8)
                g = assembled(s_ref, x_ref, radial_g, 0, a, b, y_refs)
                m = assembled(s_ref, x_ref, radial_m, 1, a, b, y_refs)
                scale = time_step / m
                scalar = scalar_ref[at, s, :].reshape(64, 128)
                first = scalar - scale * g
                base_ref[to, out, :] = (0.5 * (scalar + first)).reshape(8, 8, 128)
                half_ref[to, out, :] = (0.5 * scale).reshape(8, 8, 128)
                fields.append(first)
                if first_ref is not None:
                    first_ref[to, out, :] = first.reshape(8, 8, 128)
                velocities.append(
                    [velocity_ref[d, at, s, :].reshape(64, 128) for d in range(3)]
                )
                masses.append(mass_ref[at, s, :].reshape(64, 128))
            values = convect_pair(fields, velocities, masses, table_ref)
            joined, spread = join_lanes(values, table_ref)
            for h, b in enumerate(pair):
                out = slice(16 * n + 8 * h, 16 * n + 8 * h + 8)
                g_ref[to, out, :] = joined[h].reshape(8, 8, 128)
                spreads.append((b, spread[h]))
        z_ref[layer] = pick_spread(spreads)

    return body


def second_inner_kernel(
    s_ref, x_ref, packed_ref, scalar_ref, velocity_ref, mass_ref,
    table_ref, g_ref, base_ref, half_ref, z_ref,
):
    body = second_pairs(
        ((1, 2), (3, 4), (5, 6)), s_ref, x_ref, packed_ref, None,
        scalar_ref, velocity_ref, mass_ref, table_ref, g_ref, base_ref, half_ref, z_ref,
    )
    sweep(body, 2)
    join_block(g_ref)


def add_beyond(layers, y_one_ref, y_two_ref, first_ref, scalar_ref, table_ref, g_ref, z_ref):
    even = (lax.axis_index("ey") & 1) == 0
    one, two = y_one_ref[64:, :].astype(F32), y_two_ref[64:, :].astype(F32)
    sides = (jnp.where(even, one, two), jnp.where(even, two, one))
    rows = []
    for h, (line, outer) in enumerate(((0, 0), (15, 63))):
        for a, n in layers:
            change = first_ref[span_of(n), line, :] - scalar_ref[span_of(a), outer, :]
            rows.append(sides[h][128 + 8 * a : 136 + 8 * a] + change)
    count = len(layers)
    field = jnp.concatenate(rows + [jnp.zeros((64 - 16 * count, 128), F32)], axis=0)
    high, low = halves(field)
    axial = dot(row_table(table_ref, 64), jnp.concatenate([high, low, high], axis=0))
    radius = by_lanes([(high, low)], table_ref)
    corner = float(gll_derivative()[7, 7])
    values = []
    for h, sign in ((0, corner), (1, -corner)):
        for k, (a, _) in enumerate(layers):
            at = slice(8 * (count * h + k), 8 * (count * h + k) + 8)
            share, *flow = [sides[h][32 * n + 8 * a : 32 * n + 8 * a + 8] for n in range(4)]
            azimuth = sign * field[at]
            values.append(share + flow[0] * axial[at] + flow[1] * azimuth + flow[2] * radius[at])
    (joined,), (spread,) = join_lanes([jnp.concatenate(values, axis=0)], table_ref)
    slot = ((lane_ids((8, 128)) + 1) >> 1) & 63
    row = row_ids((8, 128))
    for h, line in ((0, 0), (1, 15)):
        for k, (_, n) in enumerate(layers):
            at = slice(8 * (count * h + k), 8 * (count * h + k) + 8)
            g_ref[span_of(n), line, :] = g_ref[span_of(n), line, :] + joined[at]
            mine = jnp.where(slot == 56 - 8 * row + 7 * h, spread[at], 0.0)
            total = jnp.sum(mine, axis=0, keepdims=True)
            z_ref[n] = z_ref[n] + jnp.where(row == 7 * h, total, 0.0)


def second_face_kernel(
    s_ref, x_ref, packed_ref, y_one_ref, y_two_ref, scalar_ref, velocity_ref,
    mass_ref, table_ref, inner_ref, x_out_ref, edge_ref, base_ref, half_ref, z_ref, first_ref,
):
    body = second_pairs(
        ((0, 7),), s_ref, x_ref, packed_ref, (y_one_ref, y_two_ref), scalar_ref, velocity_ref,
        mass_ref, table_ref, edge_ref, base_ref, half_ref, z_ref, first_ref,
    )
    body(0, 0)
    body(3, 1)
    add_beyond(((0, 0), (3, 1)), y_one_ref, y_two_ref, first_ref, scalar_ref, table_ref, edge_ref, z_ref)
    row = row_ids((64, 128))
    for n, (layer, at) in enumerate(((15, 31), (0, 0))):
        face = jnp.concatenate(
            [edge_ref[layer, 0:8, :], inner_ref[at], edge_ref[layer, 8:16, :]], axis=0
        )
        after = jnp.where((row == 7) | (row == 55), pltpu.roll(face, 63, 0), 0.0)
        before = jnp.where((row == 8) | (row == 56), pltpu.roll(face, 1, 0), 0.0)
        x_out_ref[n, 0] = (face + (after + before)).astype(BF16)


def second_outer_kernel(
    s_ref, x_ref, packed_ref, y_one_ref, y_two_ref, scalar_ref, velocity_ref,
    mass_ref, table_ref, inner_ref, z_in, edge_in, base_in, half_in, z_face,
    g_ref, base_ref, half_ref, z_ref, edge_ref, first_ref,
):
    body = second_pairs(
        ((0, 7),), s_ref, x_ref, packed_ref, (y_one_ref, y_two_ref), scalar_ref, velocity_ref,
        mass_ref, table_ref, edge_ref, base_ref, half_ref, z_ref, first_ref,
    )
    body(1)
    body(2)
    add_beyond(((1, 1), (2, 2)), y_one_ref, y_two_ref, first_ref, scalar_ref, table_ref, edge_ref, z_ref)
    for layer, a in ((0, 0), (1, 3)):
        for source, target in ((edge_in, edge_ref), (base_in, base_ref), (half_in, half_ref)):
            target[span_of(a)] = source[span_of(layer)]
        z_ref[a] = z_face[layer]
    join_axial(edge_ref)
    g_ref[:, 0:8, :] = edge_ref[:, 0:8, :]
    g_ref[:, 8:56, :] = inner_ref[...]
    g_ref[:, 56:64, :] = edge_ref[:, 8:16, :]
    for low in (7, 55):
        total = g_ref[:, low, :] + g_ref[:, low + 1, :]
        g_ref[:, low, :] = total
        g_ref[:, low + 1, :] = total
    for n, value in enumerate(join_packed([z_ref[a] + z_in[a] for a in range(4)])):
        z_ref[n] = value


def weight_kernel(weight_ref, out_ref):
    row = row_ids((512, 512))
    source = (row & 63) * 8 + (row >> 6)
    order = jnp.where(lane_ids((512, 512)) == source, 1.0, 0.0).astype(BF16)
    for m in range(8):
        out_ref[:, 128 * m : 128 * m + 128] = dot(order, weight_ref[m]).astype(BF16)


def pick_kernel(cut_ref, pick_ref):
    cut = cut_ref[...]
    a, b, c = cut >> 7, (cut >> 4) & 7, cut & 15
    order = jnp.where(a == 0, 2, jnp.where(a == 3, 3, a - 1))
    inner = 128 * order + 16 * b + c
    ends = 512 + 16 * a + 2 * b + (c >> 3)
    place = jnp.where((c == 0) | (c == 15), ends, inner)
    turned = place.astype(F32).T.astype(jnp.int32)
    lane = lane_ids((128, 640))
    for m in range(8):
        pick_ref[m] = jnp.where(lane == turned[:, m : m + 1], 1.0, 0.0).astype(BF16)


def turn(blocks, table):
    rows = []
    for block in blocks:
        value = block.astype(BF16)
        zero = jnp.zeros_like(value)
        rows.append(jnp.concatenate([value, zero], axis=1))
        rows.append(jnp.concatenate([zero, value], axis=1))
    return lax.dot_general(
        table,
        jnp.concatenate(rows, axis=0),
        (((1,), (1,)), ((), ())),
        preferred_element_type=F32,
    )


PAIRS = ((0, 1), (2, 3), (4, 5), (6, 7))


def term(refs, a, b):
    inner_ref, outer_ref = refs
    at = span_of(a)
    if b in (0, 7):
        return outer_ref[at, 8 * (b // 7) : 8 * (b // 7) + 8, :].reshape(64, 128)
    return inner_ref[at, 8 * b - 8 : 8 * b, :].reshape(64, 128)


def advanced(g_ref, x_ref, packed, bases, halfs, a, pair):
    blocks = []
    for b in pair:
        g = assembled(g_ref, x_ref, packed, 0, a, b)
        blocks.append(term(bases, a, b) - term(halfs, a, b) * g)
    return blocks


def store_elements(element_ref, blocks, table_ref, place):
    turned = turn(blocks, turn_table(table_ref)).astype(BF16)
    for h in range(2):
        for k in range(4):
            element_ref[place + 16 * h : place + 16 * h + 16, 128 * k : 128 * k + 128] = turned[
                16 * k : 16 * k + 16, 128 * h : 128 * h + 128
            ]


def pixel_values(element_ref, weight_ref, m):
    return dot(element_ref[...], weight_ref[:, 256 * m : 256 * m + 256]).astype(BF16)


def layer_elements(layers, g_ref, x_ref, bases, halfs, table_ref, element_ref):
    place = 0
    for a in layers:
        for pair in PAIRS:
            blocks = advanced(g_ref, x_ref, None, bases, halfs, a, pair)
            store_elements(element_ref, blocks, table_ref, place)
            place += 32


def early_kernel(
    g_ref, base_one, half_one, base_two, half_two, table_ref, weight_ref, value_ref, element_ref
):
    bases, halfs = (base_one, base_two), (half_one, half_two)
    layer_elements((1, 2), g_ref, None, bases, halfs, table_ref, element_ref)
    for m in range(4):
        value_ref[:, 256 * m : 256 * m + 256] = pixel_values(element_ref, weight_ref, m)


def middle_kernel(
    g_ref, x_ref, base_one, half_one, base_two, half_two, table_ref, weight_ref, pick_ref,
    early_ref, pixel_ref, element_ref,
):
    bases, halfs = (base_one, base_two), (half_one, half_two)
    layer_elements((0, 3), g_ref, x_ref, bases, halfs, table_ref, element_ref)
    for m in range(4):
        late = pixel_values(element_ref, weight_ref, m)
        both = jnp.concatenate([early_ref[:, 256 * m : 256 * m + 256], late], axis=0)
        for n in range(2):
            pixel_ref[2 * m + n] = dot(
                pick_ref[2 * m + n, :, :512], both[:, 128 * n : 128 * n + 128]
            )


def fill_payload(payload_ref, d, cam_count, pick_ref, value_ref, pixel_ref):
    me = lax.axis_index("cam")
    share = pixel_ref.shape[0] // cam_count
    for n in range(share):
        m = share * (me ^ d) + n
        values = dot(pick_ref[m, :, 512:576], value_ref[m]) + pixel_ref[m]
        payload_ref[n] = values.astype(BF16)


def final_layers(cam_count, g_ref, x_ref, one_ref, two_ref, terms, use):
    base_one, half_one, base_two, half_two = terms
    bases, halfs = (base_one, base_two), (half_one, half_two)
    one, two = one_ref[:32, :].astype(F32), two_ref[:32, :].astype(F32)
    for a in range(4):
        packed = merged(one[8 * a : 8 * a + 8], two[8 * a : 8 * a + 8], cam_count)
        for pair in PAIRS:
            use(a, pair, advanced(g_ref, x_ref, packed, bases, halfs, a, pair))


def render_far_kernel(
    cam_count, g_ref, x_ref, one_ref, two_ref, base_one, half_one, base_two, half_two,
    table_ref, weight_ref, pick_ref, pixel_ref, value_ref, *rest,
):
    payload_refs, end_ref = rest[:-1], rest[-1]

    def use(a, pair, blocks):
        turned = turn(blocks, end_table(table_ref))
        for h, b in enumerate(pair):
            place = 16 * a + 2 * b
            for k in range(4):
                end_ref[place : place + 2, 128 * k : 128 * k + 128] = turned[
                    2 * k : 2 * k + 2, 128 * h : 128 * h + 128
                ]

    terms = (base_one, half_one, base_two, half_two)
    final_layers(cam_count, g_ref, x_ref, one_ref, two_ref, terms, use)
    ends = end_ref[...].astype(BF16)
    for m in range(pixel_ref.shape[0] // 2):
        values = dot(ends, weight_ref[:, 256 * m : 256 * m + 256]).astype(BF16)
        value_ref[2 * m] = values[:, :128]
        value_ref[2 * m + 1] = values[:, 128:]
    for d in range(2, cam_count):
        fill_payload(payload_refs[d - 2], d, cam_count, pick_ref, value_ref, pixel_ref)


def advected_kernel(
    cam_count, g_ref, x_ref, one_ref, two_ref, base_one, half_one, base_two, half_two,
    out_hbm, advected_ref, sems,
):
    copies = []

    def use(a, pair, blocks):
        for h, b in enumerate(pair):
            advected_ref[span_of(a), 8 * b : 8 * b + 8, :] = blocks[h].reshape(8, 8, 128)
        if pair == PAIRS[-1]:
            at = span_of(a)
            copy = pltpu.make_async_copy(advected_ref.at[at], out_hbm.at[at], sems.at[a])
            copy.start()
            copies.append(copy)

    terms = (base_one, half_one, base_two, half_two)
    final_layers(cam_count, g_ref, x_ref, one_ref, two_ref, terms, use)
    for copy in copies:
        copy.wait()


def render_near_kernel(cam_count, d, value_ref, pick_ref, pixel_ref, payload_ref):
    fill_payload(payload_ref, d, cam_count, pick_ref, value_ref, pixel_ref)


def own_image_kernel(
    cam_count, value_ref, pick_ref, pixel_ref, block_ref, first_ref, second_ref,
    image_ref, onehot_ref, payload_ref, id_ref,
):
    me = lax.axis_index("cam")
    share = image_ref.shape[0]
    id_ref[0] = block_ref[...]
    tiles = ((1, first_ref[64:80, :]), (3, second_ref[32:48, :]), (2, second_ref[48:64, :]))
    for d, tile in tiles:
        ids = tile.astype(F32).astype(jnp.int32)
        id_ref[d] = ids[:8] * 32 + ids[8:]
    fill_payload(payload_ref, 0, cam_count, pick_ref, value_ref, pixel_ref)
    for m in range(share):
        ids = [id_ref[d, pl.ds(share * me + m, 1), :] for d in range(4)]
        ids = jnp.concatenate(ids, axis=1)
        for chunk in range(4):
            at = slice(256 * chunk, 256 * chunk + 256)
            row = row_ids((256, ids.shape[1])) + 256 * chunk
            onehot = jnp.where(row == ids, 1.0, 0.0).astype(BF16)
            onehot_ref[m, at, :] = onehot
            image_ref[m, at, :] = dot(onehot[:, :128], payload_ref[m])


def image_kernel(own_ref, onehot_ref, *refs):
    payload_refs, (image_hbm, image_ref, sems) = refs[:-3], refs[-3:]
    copies = []
    for m in range(image_ref.shape[0]):
        values = jnp.concatenate([payload_ref[m] for payload_ref in payload_refs], axis=0)
        for chunk in range(4):
            at = slice(256 * chunk, 256 * chunk + 256)
            image_ref[m, at, :] = own_ref[m, at, :] + dot(onehot_ref[m, at, 128:], values)
            copy = pltpu.make_async_copy(
                image_ref.at[m, at], image_hbm.at[m, at], sems.at[4 * m + chunk]
            )
            copy.start()
            copies.append(copy)
    for copy in copies:
        copy.wait()


def call(kernel, out_shape, flops=10**8, size=10**7, **options):
    return pl.pallas_call(
        kernel,
        out_shape=out_shape,
        compiler_params=pltpu.CompilerParams(vmem_limit_bytes=24 * 2**20),
        cost_estimate=pl.CostEstimate(flops=flops, bytes_accessed=size, transcendentals=0),
        **options,
    )


def shape_of(*shape, dtype=F32):
    return jax.ShapeDtypeStruct(shape, dtype)


def stay(*arrays):
    return [pltpu.with_memory_space_constraint(x, pltpu.HBM) for x in arrays]


def swaps(axis):
    count = lax.axis_size(axis)
    even = [(i, i ^ 1) for i in range(count)]
    odd = [(i, (i + 1) % count if i & 1 else (i - 1) % count) for i in range(count)]
    return even, odd


def swap_axial(x):
    count = lax.axis_size("ex")
    up = [(i, (i + 1) % count) for i in range(count)]
    if count == 2:
        return lax.ppermute(x, "ex", up)
    down = [(j, i) for i, j in up]
    return jnp.stack([lax.ppermute(x[0], "ex", up), lax.ppermute(x[1], "ex", down)])


def swap_both(one, two, axis):
    even, odd = swaps(axis)
    return lax.ppermute(one, axis, even), lax.ppermute(two, axis, odd)


def per_device(scalar, velocity, lumped_mass, pixel_weights, cut_element, pixel_block):
    shape = scalar.shape
    flat = (32, 64, 128)
    inner, outer = (32, 48, 128), (32, 16, 128)
    scalar = scalar.reshape(flat)
    velocity = velocity.reshape((3,) + flat)
    mass = lumped_mass.reshape(flat)
    tables = derivative_tables()
    n_cam = lax.axis_size("cam")
    cameras = pixel_weights.shape[0]
    share = cameras // n_cam
    part = functools.partial

    x, near = call(
        face_kernel,
        (shape_of(2, 2, 64, 128, dtype=BF16), shape_of(*tables.shape, dtype=BF16)),
        in_specs=[HBM] * 4,
        scratch_shapes=[
            pltpu.VMEM((2, 8, 64, 128), F32),
            pltpu.VMEM((2, 3, 64, 128), F32),
            pltpu.VMEM((2, 64, 128), F32),
            pltpu.SemaphoreType.DMA((7,)),
        ],
    )(*stay(scalar, velocity, mass, tables))
    x_got = swap_axial(x)
    s, z = call(first_kernel, (shape_of(64, 64, 128), shape_of(8, 8, 128)))(
        scalar, velocity, mass, near
    )
    weights = call(weight_kernel, shape_of(512, 128 * cameras, dtype=BF16))(pixel_weights)
    picks = call(pick_kernel, shape_of(cameras, 128, 640, dtype=BF16))(cut_element)

    half = functools.partial(shape_of, dtype=BF16)
    *z, x_got = call(
        first_radial_kernel, (half(80, 128), half(64, 128), shape_of(2, 2, 64, 128))
    )(z, x_got, pixel_block)
    z_got = swap_both(*z, "cam")
    z_got, weights, picks = lax.optimization_barrier((z_got, weights, picks))
    ids_got = z_got[0]
    *y, packed = call(
        part(azimuth_kernel, n_cam), (half(224, 128), half(224, 128), shape_of(8, 8, 128))
    )(s, x_got, *z_got, scalar, velocity, mass, near)
    near_swap, wrap_swap = swaps("ey")
    y_got = (lax.ppermute(y[0], "ey", wrap_swap), lax.ppermute(y[1], "ey", near_swap))
    g_inner, *inner_terms, z_inner = call(
        second_inner_kernel, (shape_of(*inner),) * 3 + (shape_of(4, 8, 128),)
    )(s, x_got, packed, scalar, velocity, mass, near)
    args = (s, x_got, packed, *y_got, scalar, velocity, mass, near, g_inner)
    some = (16, 16, 128)
    x, *faces = call(
        second_face_kernel,
        (shape_of(2, 1, 64, 128, dtype=BF16),) + (shape_of(*some),) * 3 + (shape_of(2, 8, 128),),
        scratch_shapes=[pltpu.VMEM(some, F32)],
    )(*args)
    g, *outer_terms, z = call(
        second_outer_kernel,
        (shape_of(*flat), shape_of(*outer), shape_of(*outer), shape_of(4, 8, 128)),
        scratch_shapes=[pltpu.VMEM(outer, F32), pltpu.VMEM(outer, F32)],
    )(*args, z_inner, *faces)

    terms = (*inner_terms, *outer_terms)
    x_got = swap_axial(x)
    early = call(
        early_kernel,
        shape_of(256, 128 * cameras, dtype=BF16),
        scratch_shapes=[pltpu.VMEM((256, 512), BF16)],
    )(g, *terms, near, weights)
    x_got, early = lax.optimization_barrier((x_got, early))
    *z, x_got = call(
        second_radial_kernel, (half(32, 128), half(64, 128), shape_of(2, 1, 64, 128))
    )(z, x_got, pixel_block, ids_got)
    z_got = swap_both(*z, "cam")
    pixels = call(
        middle_kernel,
        shape_of(cameras, 128, 128),
        scratch_shapes=[pltpu.VMEM((256, 512), BF16)],
    )(g, x_got, *terms, near, weights, picks, early)
    z_got, pixels = lax.optimization_barrier((z_got, pixels))
    payload_shape = half(share, 128, 128)
    values, *far = call(
        part(render_far_kernel, n_cam),
        (half(cameras, 64, 128),) + (payload_shape,) * (n_cam - 2),
        scratch_shapes=[pltpu.VMEM((64, 512), F32)],
    )(g, x_got, *z_got, *terms, near, weights, picks, pixels)
    parts = (values, picks, pixels)
    image_shape = shape_of(share, NBLK, 128)
    images, onehot = call(
        part(own_image_kernel, n_cam),
        (image_shape, half(share, NBLK, 128 * n_cam)),
        scratch_shapes=[
            pltpu.VMEM(payload_shape.shape, BF16),
            pltpu.VMEM((n_cam, cameras, 128), jnp.int32),
        ],
    )(*parts, pixel_block, ids_got, z_got[1])
    images, parts = lax.optimization_barrier((images, parts))
    beside = call(part(render_near_kernel, n_cam, 1), payload_shape)(*parts)
    final = (g, x_got, *z_got, *terms)
    final, beside = lax.optimization_barrier((final, beside))
    advected = call(
        part(advected_kernel, n_cam),
        shape_of(*flat),
        out_specs=HBM,
        scratch_shapes=[pltpu.VMEM(flat, F32), pltpu.SemaphoreType.DMA((4,))],
    )(*final)
    images, advected = lax.optimization_barrier((images, advected))
    received = []
    for d, payload in [(1, beside)] + [(n + 2, p) for n, p in enumerate(far)]:
        received.append(lax.ppermute(payload, "cam", [(i, i ^ d) for i in range(n_cam)]))
    images = call(
        image_kernel,
        image_shape,
        out_specs=HBM,
        scratch_shapes=[
            pltpu.VMEM((share, NBLK, 128), F32),
            pltpu.SemaphoreType.DMA((4 * share,)),
        ],
    )(images, onehot, *received)
    return (advected.reshape(shape), images)


def solution(mesh):
    placed = (
        P("ex", None, "ey", None, "cam"),
        P(None, "ex", None, "ey", None, "cam"),
        P("ex", None, "ey", None, "cam"),
        P(),
        P(None, ("cam", "ex", "ey")),
        P(None, ("cam", "ex", "ey")),
    )
    return jax.shard_map(
        per_device,
        mesh=mesh,
        in_specs=placed,
        out_specs=(P("ex", None, "ey", None, "cam"), P("cam", ("ex", "ey"), None)),
        check_vma=False,
    )
```

```python
import functools

import jax
import jax.numpy as jnp
import numpy as np
from jax import lax
from jax.experimental import pallas as pl
from jax.experimental.pallas import tpu as pltpu
from jax.sharding import PartitionSpec as P

NBLK = 1024
F32 = jnp.float32
BF16 = jnp.bfloat16
VMEM = pl.BlockSpec(memory_space=pltpu.VMEM)
HBM = pl.BlockSpec(memory_space=pltpu.HBM)
time_step = 0.01


def legendre_seven(points):
    previous = points * 0.0 + 1.0
    current = points * 1.0
    for order in range(1, 7):
        following = ((2 * order + 1) * points * current - order * previous) / (order + 1)
        previous = current
        current = following
    return current


def gll_derivative():
    degree = 7
    gll_nodes = np.array(
        [
            -1.0,
            -0.8717401485096066,
            -0.5917001814331423,
            -0.2092992179024789,
            0.2092992179024789,
            0.5917001814331423,
            0.8717401485096066,
            1.0,
        ]
    )
    values = legendre_seven(gll_nodes)
    derivative = np.zeros((degree + 1, degree + 1))
    for target in range(degree + 1):
        for source in range(degree + 1):
            if target != source:
                derivative[target, source] = values[target] / (
                    values[source] * (gll_nodes[target] - gll_nodes[source])
                )
    derivative[0, 0] = -degree * (degree + 1) / 4.0
    derivative[degree, degree] = degree * (degree + 1) / 4.0
    return derivative


def split_two(table):
    high = table.astype(np.float32).astype(BF16)
    low = (table - high.astype(np.float64)).astype(np.float32).astype(BF16)
    return high, low


def derivative_tables():
    derivative = gll_derivative()
    eye = np.eye(8)
    rows = np.concatenate([np.kron(derivative, eye), np.kron(eye, derivative)], axis=0)
    high, low = split_two(rows)
    row_table = np.concatenate([high, high, low, np.zeros_like(high)], axis=1)
    high, low = split_two(np.kron(np.eye(16), derivative.T))
    lane_table = np.concatenate(
        [
            np.concatenate([high, low], axis=1),
            np.concatenate([high, np.zeros_like(high)], axis=1),
        ],
        axis=0,
    )
    swap = np.zeros((128, 128))
    for c in range(15):
        swap[8 * c + 7, 8 * c + 8] = 1.0
        swap[8 * c + 8, 8 * c + 7] = 1.0
    join_table = np.concatenate([swap, swap], axis=0).astype(np.float32).astype(BF16)
    spread = np.zeros((128, 128))
    spread[0, 0::2] = 1.0
    spread[127, 1::2] = 1.0
    turn = np.zeros((64, 256))
    for k in range(4):
        for c in range(16):
            turn[16 * k + c, 8 * c + 2 * k] = 1.0
            turn[16 * k + c, 128 + 8 * c + 2 * k + 1] = 1.0
    ends = turn.reshape(4, 16, 256)[:, ::15].reshape(8, 256)
    ends = np.concatenate([ends, np.zeros_like(ends)], axis=0)
    partial = np.zeros((16, 64))
    for i in range(8):
        partial[i, 8 * i + 1 : 8 * i + 8] = derivative[0, 1:]
        partial[8 + i, 8 * i : 8 * i + 7] = derivative[7, :7]
    high, low = split_two(partial)
    partial = np.concatenate([high, high, low, np.zeros_like(high)], axis=1)
    exact = [spread, spread, turn[:, :128], turn[:, 128:], ends[:, :128], ends[:, 128:]]
    exact = np.concatenate(exact, axis=0)
    split = [row_table[:, :128], row_table[:, 128:], lane_table[:, :128], lane_table[:, 128:]]
    split += [join_table, exact.astype(np.float32).astype(BF16)]
    split += [partial[:, :128], partial[:, 128:]]
    return jnp.asarray(np.concatenate(split, axis=0))


def row_table(table_ref, first=0):
    high, low = table_ref[first:128], table_ref[128 + first : 256]
    return jnp.concatenate([high, low[:, :64]], axis=1)


def lane_table(table_ref):
    return jnp.concatenate([table_ref[256:512], table_ref[512:768]], axis=1)


def join_table(table_ref):
    return jnp.concatenate([table_ref[768:1024], table_ref[1024:1280]], axis=1)


def turn_table(table_ref):
    return jnp.concatenate([table_ref[1280:1344], table_ref[1344:1408]], axis=1)


def end_table(table_ref):
    return jnp.concatenate([table_ref[1408:1424], table_ref[1424:1440]], axis=1)


def partial_table(table_ref):
    return jnp.concatenate([table_ref[1440:1456], table_ref[1456:1472][:, :64]], axis=1)


def span_of(a, offset=0):
    if isinstance(a, int):
        return slice(8 * a + offset, 8 * a + offset + 8)
    return pl.ds(pl.multiple_of(a * 8 + offset, 8), 8)


def sweep(body, together):
    if together == 4:
        for a in range(4):
            body(a)
        return

    def step(n, carry):
        for m in range(together):
            body(n * together + m)
        return carry

    lax.fori_loop(0, 4 // together, step, 0)


def lane_ids(shape):
    return lax.broadcasted_iota(jnp.int32, shape, len(shape) - 1)


def row_ids(shape):
    return lax.broadcasted_iota(jnp.int32, shape, len(shape) - 2)


def halves(value):
    high = value.astype(BF16)
    return high, (value - high.astype(F32)).astype(BF16)


def dot(a, b):
    return jnp.dot(a, b, preferred_element_type=F32)


def by_lanes(pairs, table_ref):
    rows = jnp.concatenate([jnp.concatenate(p, axis=1) for p in pairs], axis=0)
    both = dot(rows, lane_table(table_ref))
    return both[:, :128] + both[:, 128:]


def join_lanes(values, table_ref):
    rows = jnp.concatenate([jnp.concatenate(halves(v), axis=1) for v in values], axis=0)
    other = dot(rows, join_table(table_ref))
    joined, spread, at = [], [], 0
    for v in values:
        span = slice(at, at + v.shape[0])
        joined.append(v + other[span, :128])
        spread.append(other[span, 128:])
        at += v.shape[0]
    return joined, spread


def join_rows(value):
    row = row_ids(value.shape)
    last = ((row & 7) == 7) & (row != 63)
    first = ((row & 7) == 0) & (row != 0)
    other = jnp.where(
        last, pltpu.roll(value, 63, 0), jnp.where(first, pltpu.roll(value, 1, 0), 0.0)
    )
    return value + other


def convect_pair(fields, velocities, masses, table_ref):
    pairs = [halves(f) for f in fields]
    high = jnp.concatenate([p[0] for p in pairs], axis=1)
    low = jnp.concatenate([p[1] for p in pairs], axis=1)
    stacked = jnp.concatenate([high, low, high], axis=0)
    rows = dot(row_table(table_ref), stacked)
    radius = by_lanes(pairs, table_ref)
    out = []
    for n in range(2):
        lanes = slice(128 * n, 128 * n + 128)
        v = velocities[n]
        slope = v[0] * rows[:64, lanes] + v[1] * rows[64:, lanes]
        out.append(masses[n] * (slope + v[2] * radius[64 * n : 64 * n + 64]))
    return out


def face_kernel(
    scalar_hbm, velocity_hbm, mass_hbm, table_hbm, x_ref, table_ref, f_ref, v_ref, m_ref, sems,
):
    copies = []

    def start(source, target):
        copy = pltpu.make_async_copy(source, target, sems.at[len(copies)])
        copy.start()
        copies.append(copy)

    last = scalar_hbm.shape[0] - 1
    start(scalar_hbm.at[pl.ds(last - 7, 8)], f_ref.at[0])
    start(scalar_hbm.at[pl.ds(0, 8)], f_ref.at[1])
    start(table_hbm, table_ref)
    start(velocity_hbm.at[:, last], v_ref.at[0])
    start(velocity_hbm.at[:, 0], v_ref.at[1])
    start(mass_hbm.at[last], m_ref.at[0])
    start(mass_hbm.at[0], m_ref.at[1])
    for copy in copies[:3]:
        copy.wait()
    derivative = gll_derivative()
    fields = [f_ref[0, 7], f_ref[1, 0]]
    pairs = [halves(f) for f in fields]
    high = jnp.concatenate([p[0] for p in pairs], axis=1)
    low = jnp.concatenate([p[1] for p in pairs], axis=1)
    azimuth = dot(row_table(table_ref, 64), jnp.concatenate([high, low, high], axis=0))
    radius = by_lanes(pairs, table_ref)
    for copy in copies[3:]:
        copy.wait()
    values = []
    for n, node in enumerate((7, 0)):
        axial = f_ref[n, 0] * float(derivative[node, 0])
        for p in range(1, 8):
            axial = axial + f_ref[n, p] * float(derivative[node, p])
        slope = v_ref[n, 0] * axial + v_ref[n, 1] * azimuth[:, 128 * n : 128 * n + 128]
        values.append(m_ref[n] * (slope + v_ref[n, 2] * radius[64 * n : 64 * n + 64]))
        values.append(m_ref[n])
    for n, value in enumerate(join_lanes(values, table_ref)[0]):
        x_ref[n // 2, n % 2] = join_rows(value).astype(BF16)


def join_block(s_ref):
    for b in range(s_ref.shape[1] // 8 - 1):
        total = s_ref[:, 8 * b + 7, :] + s_ref[:, 8 * b + 8, :]
        s_ref[:, 8 * b + 7, :] = total
        s_ref[:, 8 * b + 8, :] = total
    join_axial(s_ref)


def join_axial(s_ref):
    for f in range(s_ref.shape[0] // 32):
        for a in range(3):
            at = 32 * f + 8 * a + 7
            total = s_ref[at] + s_ref[at + 1]
            s_ref[at] = total
            s_ref[at + 1] = total


def pack_blocks(blocks):
    slot = ((lane_ids((8, 128)) + 1) >> 1) & 63
    parts = [jnp.zeros((8, 128), F32) for _ in range(4)]
    for n, (u, block) in enumerate(blocks):
        if u:
            block = pltpu.roll(block, 2 * u, 1)
        parts[n % 4] = jnp.where(slot == u, block, parts[n % 4])
    return (parts[0] + parts[1]) + (parts[2] + parts[3])


def pick_spread(spreads):
    slot = ((lane_ids((8, 128)) + 1) >> 1) & 63
    parts = [jnp.zeros((8, 128), F32) for _ in range(2)]
    for b, spread in spreads:
        for i in range(8):
            block = spread[8 * i : 8 * i + 8]
            parts[i % 2] = jnp.where(slot == 56 - 8 * i + b, block, parts[i % 2])
    return parts[0] + parts[1]


def join_packed(packed):
    lane, row = lane_ids((8, 128)), row_ids((8, 128))
    slot = ((lane + 1) >> 1) & 63
    b = slot & 7
    rows = []
    for value in packed:
        after = pltpu.roll(pltpu.roll(value, 126, 1), 7, 0)
        before = pltpu.roll(pltpu.roll(value, 2, 1), 1, 0)
        value = value + jnp.where((row == 7) & (b < 7), after, 0.0)
        rows.append(value + jnp.where((row == 0) & (b > 0), before, 0.0))
    out = list(rows)
    for a in range(3):
        out[a] = out[a] + jnp.where(slot < 8, pltpu.roll(rows[a + 1], 16, 1), 0.0)
        out[a + 1] = out[a + 1] + jnp.where(slot >= 56, pltpu.roll(rows[a], 112, 1), 0.0)
    return out


def first_kernel(scalar_ref, velocity_ref, mass_ref, table_ref, s_ref, z_ref):
    def body(a):
        at = span_of(a)
        spreads = [[], []]
        for pair in range(4):
            spans = [slice(16 * pair + 8 * n, 16 * pair + 8 * n + 8) for n in range(2)]
            fields = [scalar_ref[at, s, :].reshape(64, 128) for s in spans]
            velocities = [
                [velocity_ref[d, at, s, :].reshape(64, 128) for d in range(3)] for s in spans
            ]
            masses = [mass_ref[at, s, :].reshape(64, 128) for s in spans]
            values = convect_pair(fields, velocities, masses, table_ref)
            joined, spread = join_lanes(values + masses, table_ref)
            for n, s in enumerate(spans):
                for f in range(2):
                    s_ref[span_of(a, 32 * f), s, :] = joined[n + 2 * f].reshape(8, 8, 128)
                    spreads[f].append((2 * pair + n, spread[n + 2 * f]))
        for f in range(2):
            z_ref[a + 4 * f] = pick_spread(spreads[f])

    sweep(body, 2)
    join_block(s_ref)
    for f in range(2):
        for n, value in enumerate(join_packed([z_ref[4 * f + a] for a in range(4)])):
            z_ref[4 * f + n] = value


def radial_faces(count, z_in, x_in, x_ref):
    x_ref[...] = x_in[...].astype(F32)
    rows = []
    for f in range(count):
        spans = [slice(8 * b, 8 * b + 8) for b in range(8)]
        low = pack_blocks([(56 + b, x_ref[0, f, s, :]) for b, s in enumerate(spans)])
        high = pack_blocks([(b, x_ref[1, f, s, :]) for b, s in enumerate(spans)])
        rows += [z_in[4 * f] + low, z_in[4 * f + 1], z_in[4 * f + 2], z_in[4 * f + 3] + high]
    return jnp.concatenate(rows, axis=0).astype(BF16)


def id_tile(block_ref):
    ids = block_ref[...]
    return jnp.concatenate([ids >> 5, ids & 31], axis=0).astype(F32).astype(BF16)


def first_radial_kernel(z_in, x_in, block_ref, one_ref, two_ref, x_ref):
    faces = radial_faces(2, z_in, x_in, x_ref)
    one_ref[:64, :] = faces
    one_ref[64:, :] = id_tile(block_ref)
    two_ref[...] = faces


def second_radial_kernel(z_in, x_in, block_ref, got_ref, one_ref, two_ref, x_ref):
    faces = radial_faces(1, z_in, x_in, x_ref)
    one_ref[...] = faces
    two_ref[:32, :] = faces
    two_ref[32:48, :] = id_tile(block_ref)
    two_ref[48:, :] = got_ref[64:, :]


def merged(one, two, cam_count):
    me = lax.axis_index("cam")
    even = (me & 1) == 0
    left = jnp.where(even, two, one)
    right = jnp.where(even, one, two)
    left = jnp.where(me == 0, 0.0, left)
    right = jnp.where(me == cam_count - 1, 0.0, right)
    lane = lane_ids((8, 128))
    return jnp.where((lane & 1) == 0, pltpu.roll(left, 1, 1), pltpu.roll(right, 127, 1))


def end_lanes(shape):
    lane = lane_ids(shape)
    return (lane == 0) | (lane == 127)


def azimuth_kernel(
    cam_count, s_ref, x_ref, one_ref, two_ref, scalar_ref, velocity_ref, mass_ref, table_ref,
    even_ref, odd_ref, packed_ref,
):
    ends = end_lanes((8, 128))
    row = row_ids((8, 128))
    even = (lax.axis_index("ey") & 1) == 0
    count = s_ref.shape[0]
    one = one_ref[:count, :].astype(F32)
    two = two_ref[:count, :].astype(F32)
    low, high = [], []
    for q in range(count // 8):
        at = slice(8 * q, 8 * q + 8)
        packed = merged(one[at], two[at], cam_count)
        packed_ref[q] = packed
        f, a = q // 4, q % 4
        for line, shift, faces in ((0, 16, low), (63, 2, high)):
            j = line & 7
            spread = jnp.broadcast_to(packed[j : j + 1, :], (8, 128))
            moved = pltpu.roll(spread, shift, 1, stride=16, stride_axis=0)
            face = s_ref[at, line, :] + jnp.where(ends, moved, 0.0)
            if a == 0:
                face = face + jnp.where(row == 0, x_ref[0, f, line : line + 1, :], 0.0)
            if a == 3:
                face = face + jnp.where(row == 7, x_ref[1, f, line : line + 1, :], 0.0)
            faces.append(face)
    slopes = [[], []]
    for a in range(4):
        pairs = []
        for b in (0, 7):
            g = assembled(s_ref, x_ref, packed_ref[a], 0, a, b)
            m = assembled(s_ref, x_ref, packed_ref[a + 4], 1, a, b)
            scalar = scalar_ref[span_of(a), 8 * b : 8 * b + 8, :].reshape(64, 128)
            pairs.append(halves(scalar - (time_step / m) * g))
        tops = jnp.concatenate([p[0] for p in pairs], axis=1)
        rests = jnp.concatenate([p[1] for p in pairs], axis=1)
        both = dot(partial_table(table_ref), jnp.concatenate([tops, rests, tops], axis=0))
        slopes[0].append(both[:8, :128])
        slopes[1].append(both[8:, 128:])
    messages = []
    for faces, line, slope in ((low, 0, slopes[0]), (high, 63, slopes[1])):
        flow = [mass_ref[:, line, :] * velocity_ref[d, :, line, :] for d in range(3)]
        share = flow[1] * jnp.concatenate(slope, axis=0)
        rows = faces + [share] + flow + [scalar_ref[:, line, :]]
        messages.append(jnp.concatenate(rows, axis=0))
    even_ref[...] = jnp.where(even, messages[1], messages[0]).astype(BF16)
    odd_ref[...] = jnp.where(even, messages[0], messages[1]).astype(BF16)


def unpacked(packed, b):
    ends = end_lanes((8, 128))
    rows = []
    for i in range(8):
        u = 56 - 8 * i + b
        moved = pltpu.roll(packed, (128 - 2 * u) % 128, 1) if u else packed
        rows.append(jnp.where(ends, moved, 0.0))
    return rows


def spread_back(packed, pair, table_ref):
    slot = ((lane_ids((8, 128)) + 1) >> 1) & 63
    high, low = halves(packed)
    high, low = high.astype(F32), low.astype(F32)
    rows = []
    for b in pair:
        for i in range(8):
            here = slot == 56 - 8 * i + b
            both = [jnp.where(here, high, 0.0), jnp.where(here, low, 0.0)]
            rows.append(jnp.concatenate(both, axis=1))
    spread = table_ref[1024:1152]
    return lax.dot_general(
        jnp.concatenate(rows, axis=0).astype(BF16),
        jnp.concatenate([spread, spread], axis=1),
        (((1,), (1,)), ((), ())),
        preferred_element_type=F32,
    )


def assembled(s_ref, x_ref, packed, f, a, b, y_refs=None):
    span = slice(8 * b, 8 * b + 8)
    at = span_of(a, 32 * f)
    block = s_ref[at, span, :]
    if packed is None:
        rows = [jnp.zeros((8, 128), F32) for _ in range(8)]
    else:
        rows = unpacked(packed, b)
    if not isinstance(a, int):
        rows[0] = rows[0] + jnp.where(a == 0, x_ref[0, f, span, :], 0.0)
        rows[7] = rows[7] + jnp.where(a == 3, x_ref[1, f, span, :], 0.0)
    elif a == 0:
        rows[0] = rows[0] + x_ref[0, f, span, :]
    elif a == 3:
        rows[7] = rows[7] + x_ref[1, f, span, :]
    if y_refs is not None:
        one_ref, two_ref = y_refs
        even = (lax.axis_index("ey") & 1) == 0
        at = slice(16 * (a // 2) + 32 * f, 16 * (a // 2) + 32 * f + 16)
        one, two = one_ref[at, :].astype(F32), two_ref[at, :].astype(F32)
        if b == 0:
            line, sublane = jnp.where(even, two, one), 0
        else:
            line, sublane = jnp.where(even, one, two), 7
        line = line[8 * (a % 2) : 8 * (a % 2) + 8]
        node = lax.broadcasted_iota(jnp.int32, (8, 8, 128), 1)
        block = block + jnp.where(node == sublane, line[:, None, :], 0.0)
    return block.reshape(64, 128) + jnp.concatenate(rows, axis=0)


def second_pairs(
    pairs, s_ref, x_ref, packed_ref, y_refs, scalar_ref, velocity_ref,
    mass_ref, table_ref, g_ref, base_ref, half_ref, z_ref, first_ref=None,
):
    def body(a, layer=None):
        at = span_of(a)
        layer = a if layer is None else layer
        to = span_of(layer)
        radial_g = packed_ref[a]
        radial_m = packed_ref[a + 4]
        spreads = []
        for n, pair in enumerate(pairs):
            fields, velocities, masses = [], [], []
            for h, b in enumerate(pair):
                s = slice(8 * b, 8 * b + 8)
                out = slice(16 * n + 8 * h, 16 * n + 8 * h + 8)
                g = assembled(s_ref, x_ref, radial_g, 0, a, b, y_refs)
                m = assembled(s_ref, x_ref, radial_m, 1, a, b, y_refs)
                scale = time_step / m
                scalar = scalar_ref[at, s, :].reshape(64, 128)
                first = scalar - scale * g
                base_ref[to, out, :] = (0.5 * (scalar + first)).reshape(8, 8, 128)
                half_ref[to, out, :] = (0.5 * scale).reshape(8, 8, 128)
                fields.append(first)
                if first_ref is not None:
                    first_ref[to, out, :] = first.reshape(8, 8, 128)
                velocities.append(
                    [velocity_ref[d, at, s, :].reshape(64, 128) for d in range(3)]
                )
                masses.append(mass_ref[at, s, :].reshape(64, 128))
            values = convect_pair(fields, velocities, masses, table_ref)
            joined, spread = join_lanes(values, table_ref)
            for h, b in enumerate(pair):
                out = slice(16 * n + 8 * h, 16 * n + 8 * h + 8)
                g_ref[to, out, :] = joined[h].reshape(8, 8, 128)
                spreads.append((b, spread[h]))
        z_ref[layer] = pick_spread(spreads)

    return body


def second_inner_kernel(
    s_ref, x_ref, packed_ref, scalar_ref, velocity_ref, mass_ref,
    table_ref, g_ref, base_ref, half_ref, z_ref,
):
    body = second_pairs(
        ((1, 2), (3, 4), (5, 6)), s_ref, x_ref, packed_ref, None,
        scalar_ref, velocity_ref, mass_ref, table_ref, g_ref, base_ref, half_ref, z_ref,
    )
    sweep(body, 2)
    join_block(g_ref)


def add_beyond(layers, y_one_ref, y_two_ref, first_ref, scalar_ref, table_ref, g_ref, z_ref):
    even = (lax.axis_index("ey") & 1) == 0
    one, two = y_one_ref[64:, :].astype(F32), y_two_ref[64:, :].astype(F32)
    sides = (jnp.where(even, two, one), jnp.where(even, one, two))
    rows = []
    for h, (line, outer) in enumerate(((0, 0), (15, 63))):
        for a, n in layers:
            change = first_ref[span_of(n), line, :] - scalar_ref[span_of(a), outer, :]
            rows.append(sides[h][128 + 8 * a : 136 + 8 * a] + change)
    count = len(layers)
    field = jnp.concatenate(rows + [jnp.zeros((64 - 16 * count, 128), F32)], axis=0)
    high, low = halves(field)
    axial = dot(row_table(table_ref, 64), jnp.concatenate([high, low, high], axis=0))
    radius = by_lanes([(high, low)], table_ref)
    corner = float(gll_derivative()[7, 7])
    values = []
    for h, sign in ((0, corner), (1, -corner)):
        for k, (a, _) in enumerate(layers):
            at = slice(8 * (count * h + k), 8 * (count * h + k) + 8)
            share, *flow = [sides[h][32 * n + 8 * a : 32 * n + 8 * a + 8] for n in range(4)]
            azimuth = sign * field[at]
            values.append(share + flow[0] * axial[at] + flow[1] * azimuth + flow[2] * radius[at])
    (joined,), (spread,) = join_lanes([jnp.concatenate(values, axis=0)], table_ref)
    slot = ((lane_ids((8, 128)) + 1) >> 1) & 63
    row = row_ids((8, 128))
    for h, line in ((0, 0), (1, 15)):
        for k, (_, n) in enumerate(layers):
            at = slice(8 * (count * h + k), 8 * (count * h + k) + 8)
            g_ref[span_of(n), line, :] = g_ref[span_of(n), line, :] + joined[at]
            mine = jnp.where(slot == 56 - 8 * row + 7 * h, spread[at], 0.0)
            total = jnp.sum(mine, axis=0, keepdims=True)
            z_ref[n] = z_ref[n] + jnp.where(row == 7 * h, total, 0.0)


def second_face_kernel(
    s_ref, x_ref, packed_ref, y_one_ref, y_two_ref, scalar_ref, velocity_ref,
    mass_ref, table_ref, inner_ref, x_out_ref, edge_ref, base_ref, half_ref, z_ref, first_ref,
):
    body = second_pairs(
        ((0, 7),), s_ref, x_ref, packed_ref, (y_one_ref, y_two_ref), scalar_ref, velocity_ref,
        mass_ref, table_ref, edge_ref, base_ref, half_ref, z_ref, first_ref,
    )
    body(0, 0)
    body(3, 1)
    add_beyond(((0, 0), (3, 1)), y_one_ref, y_two_ref, first_ref, scalar_ref, table_ref, edge_ref, z_ref)
    row = row_ids((64, 128))
    for n, (layer, at) in enumerate(((15, 31), (0, 0))):
        face = jnp.concatenate(
            [edge_ref[layer, 0:8, :], inner_ref[at], edge_ref[layer, 8:16, :]], axis=0
        )
        after = jnp.where((row == 7) | (row == 55), pltpu.roll(face, 63, 0), 0.0)
        before = jnp.where((row == 8) | (row == 56), pltpu.roll(face, 1, 0), 0.0)
        x_out_ref[n, 0] = (face + (after + before)).astype(BF16)


def second_outer_kernel(
    s_ref, x_ref, packed_ref, y_one_ref, y_two_ref, scalar_ref, velocity_ref,
    mass_ref, table_ref, inner_ref, z_in, edge_in, base_in, half_in, z_face,
    g_ref, base_ref, half_ref, z_ref, edge_ref, first_ref,
):
    body = second_pairs(
        ((0, 7),), s_ref, x_ref, packed_ref, (y_one_ref, y_two_ref), scalar_ref, velocity_ref,
        mass_ref, table_ref, edge_ref, base_ref, half_ref, z_ref, first_ref,
    )
    body(1)
    body(2)
    add_beyond(((1, 1), (2, 2)), y_one_ref, y_two_ref, first_ref, scalar_ref, table_ref, edge_ref, z_ref)
    for layer, a in ((0, 0), (1, 3)):
        for source, target in ((edge_in, edge_ref), (base_in, base_ref), (half_in, half_ref)):
            target[span_of(a)] = source[span_of(layer)]
        z_ref[a] = z_face[layer]
    join_axial(edge_ref)
    g_ref[:, 0:8, :] = edge_ref[:, 0:8, :]
    g_ref[:, 8:56, :] = inner_ref[...]
    g_ref[:, 56:64, :] = edge_ref[:, 8:16, :]
    for low in (7, 55):
        total = g_ref[:, low, :] + g_ref[:, low + 1, :]
        g_ref[:, low, :] = total
        g_ref[:, low + 1, :] = total
    for n, value in enumerate(join_packed([z_ref[a] + z_in[a] for a in range(4)])):
        z_ref[n] = value


def weight_kernel(weight_ref, out_ref):
    row = row_ids((512, 512))
    source = (row & 63) * 8 + (row >> 6)
    order = jnp.where(lane_ids((512, 512)) == source, 1.0, 0.0).astype(BF16)
    for m in range(8):
        out_ref[:, 128 * m : 128 * m + 128] = dot(order, weight_ref[m]).astype(BF16)


def pick_kernel(cut_ref, pick_ref):
    cut = cut_ref[...]
    a, b, c = cut >> 7, (cut >> 4) & 7, cut & 15
    order = jnp.where(a == 0, 2, jnp.where(a == 3, 3, a - 1))
    inner = 128 * order + 16 * b + c
    ends = 512 + 16 * a + 2 * b + (c >> 3)
    place = jnp.where((c == 0) | (c == 15), ends, inner)
    turned = place.astype(F32).T.astype(jnp.int32)
    lane = lane_ids((128, 640))
    for m in range(8):
        pick_ref[m] = jnp.where(lane == turned[:, m : m + 1], 1.0, 0.0).astype(BF16)


def turn(blocks, table):
    rows = []
    for block in blocks:
        value = block.astype(BF16)
        zero = jnp.zeros_like(value)
        rows.append(jnp.concatenate([value, zero], axis=1))
        rows.append(jnp.concatenate([zero, value], axis=1))
    return lax.dot_general(
        table,
        jnp.concatenate(rows, axis=0),
        (((1,), (1,)), ((), ())),
        preferred_element_type=F32,
    )


PAIRS = ((0, 1), (2, 3), (4, 5), (6, 7))


def term(refs, a, b):
    inner_ref, outer_ref = refs
    at = span_of(a)
    if b in (0, 7):
        return outer_ref[at, 8 * (b // 7) : 8 * (b // 7) + 8, :].reshape(64, 128)
    return inner_ref[at, 8 * b - 8 : 8 * b, :].reshape(64, 128)


def advanced(g_ref, x_ref, packed, bases, halfs, a, pair):
    blocks = []
    for b in pair:
        g = assembled(g_ref, x_ref, packed, 0, a, b)
        blocks.append(term(bases, a, b) - term(halfs, a, b) * g)
    return blocks


def store_elements(element_ref, blocks, table_ref, place):
    turned = turn(blocks, turn_table(table_ref)).astype(BF16)
    for h in range(2):
        for k in range(4):
            element_ref[place + 16 * h : place + 16 * h + 16, 128 * k : 128 * k + 128] = turned[
                16 * k : 16 * k + 16, 128 * h : 128 * h + 128
            ]


def pixel_values(element_ref, weight_ref, m):
    return dot(element_ref[...], weight_ref[:, 256 * m : 256 * m + 256]).astype(BF16)


def layer_elements(layers, g_ref, x_ref, bases, halfs, table_ref, element_ref):
    place = 0
    for a in layers:
        for pair in PAIRS:
            blocks = advanced(g_ref, x_ref, None, bases, halfs, a, pair)
            store_elements(element_ref, blocks, table_ref, place)
            place += 32


def early_kernel(
    g_ref, base_one, half_one, base_two, half_two, table_ref, weight_ref, value_ref, element_ref
):
    bases, halfs = (base_one, base_two), (half_one, half_two)
    layer_elements((1, 2), g_ref, None, bases, halfs, table_ref, element_ref)
    for m in range(4):
        value_ref[:, 256 * m : 256 * m + 256] = pixel_values(element_ref, weight_ref, m)


def middle_kernel(
    g_ref, x_ref, base_one, half_one, base_two, half_two, table_ref, weight_ref, pick_ref,
    early_ref, pixel_ref, element_ref,
):
    bases, halfs = (base_one, base_two), (half_one, half_two)
    layer_elements((0, 3), g_ref, x_ref, bases, halfs, table_ref, element_ref)
    for m in range(4):
        late = pixel_values(element_ref, weight_ref, m)
        both = jnp.concatenate([early_ref[:, 256 * m : 256 * m + 256], late], axis=0)
        for n in range(2):
            pixel_ref[2 * m + n] = dot(
                pick_ref[2 * m + n, :, :512], both[:, 128 * n : 128 * n + 128]
            )


def fill_payload(payload_ref, d, cam_count, pick_ref, value_ref, pixel_ref):
    me = lax.axis_index("cam")
    share = pixel_ref.shape[0] // cam_count
    for n in range(share):
        m = share * (me ^ d) + n
        values = dot(pick_ref[m, :, 512:576], value_ref[m]) + pixel_ref[m]
        payload_ref[n] = values.astype(BF16)


def final_layers(cam_count, g_ref, x_ref, one_ref, two_ref, terms, use, table_ref=None):
    base_one, half_one, base_two, half_two = terms
    bases, halfs = (base_one, base_two), (half_one, half_two)
    one, two = one_ref[:32, :].astype(F32), two_ref[:32, :].astype(F32)
    for a in range(4):
        packed = merged(one[8 * a : 8 * a + 8], two[8 * a : 8 * a + 8], cam_count)
        for pair in PAIRS:
            if table_ref is None:
                use(a, pair, advanced(g_ref, x_ref, packed, bases, halfs, a, pair))
                continue
            ends = spread_back(packed, pair, table_ref)
            blocks = []
            for h, b in enumerate(pair):
                g = assembled(g_ref, x_ref, None, 0, a, b) + ends[64 * h : 64 * h + 64]
                blocks.append(term(bases, a, b) - term(halfs, a, b) * g)
            use(a, pair, blocks)


def render_far_kernel(
    cam_count, g_ref, x_ref, one_ref, two_ref, base_one, half_one, base_two, half_two,
    table_ref, weight_ref, pick_ref, pixel_ref, value_ref, *rest,
):
    payload_refs, end_ref = rest[:-1], rest[-1]

    def use(a, pair, blocks):
        turned = turn(blocks, end_table(table_ref))
        for h, b in enumerate(pair):
            place = 16 * a + 2 * b
            for k in range(4):
                end_ref[place : place + 2, 128 * k : 128 * k + 128] = turned[
                    2 * k : 2 * k + 2, 128 * h : 128 * h + 128
                ]

    terms = (base_one, half_one, base_two, half_two)
    final_layers(cam_count, g_ref, x_ref, one_ref, two_ref, terms, use, table_ref)
    ends = end_ref[...].astype(BF16)
    for m in range(pixel_ref.shape[0] // 2):
        values = dot(ends, weight_ref[:, 256 * m : 256 * m + 256]).astype(BF16)
        value_ref[2 * m] = values[:, :128]
        value_ref[2 * m + 1] = values[:, 128:]
    for d in range(2, cam_count):
        fill_payload(payload_refs[d - 2], d, cam_count, pick_ref, value_ref, pixel_ref)


def advected_kernel(
    cam_count, g_ref, x_ref, one_ref, two_ref, base_one, half_one, base_two, half_two,
    out_hbm, advected_ref, sems,
):
    copies = []

    def use(a, pair, blocks):
        for h, b in enumerate(pair):
            advected_ref[span_of(a), 8 * b : 8 * b + 8, :] = blocks[h].reshape(8, 8, 128)
        if pair == PAIRS[-1]:
            at = span_of(a)
            copy = pltpu.make_async_copy(advected_ref.at[at], out_hbm.at[at], sems.at[a])
            copy.start()
            copies.append(copy)

    terms = (base_one, half_one, base_two, half_two)
    final_layers(cam_count, g_ref, x_ref, one_ref, two_ref, terms, use)
    for copy in copies:
        copy.wait()


def render_near_kernel(cam_count, d, value_ref, pick_ref, pixel_ref, payload_ref):
    fill_payload(payload_ref, d, cam_count, pick_ref, value_ref, pixel_ref)


def own_image_kernel(
    cam_count, value_ref, pick_ref, pixel_ref, block_ref, first_ref, second_ref,
    image_ref, onehot_ref, payload_ref, id_ref,
):
    me = lax.axis_index("cam")
    share = image_ref.shape[0]
    id_ref[0] = block_ref[...]
    tiles = ((1, first_ref[64:80, :]), (3, second_ref[32:48, :]), (2, second_ref[48:64, :]))
    for d, tile in tiles:
        ids = tile.astype(F32).astype(jnp.int32)
        id_ref[d] = ids[:8] * 32 + ids[8:]
    fill_payload(payload_ref, 0, cam_count, pick_ref, value_ref, pixel_ref)
    for m in range(share):
        ids = [id_ref[d, pl.ds(share * me + m, 1), :] for d in range(4)]
        ids = jnp.concatenate(ids, axis=1)
        for chunk in range(4):
            at = slice(256 * chunk, 256 * chunk + 256)
            row = row_ids((256, ids.shape[1])) + 256 * chunk
            onehot = jnp.where(row == ids, 1.0, 0.0).astype(BF16)
            onehot_ref[m, at, :] = onehot
            image_ref[m, at, :] = dot(onehot[:, :128], payload_ref[m])


def image_kernel(own_ref, onehot_ref, *refs):
    payload_refs, (image_hbm, image_ref, sems) = refs[:-3], refs[-3:]
    copies = []
    for m in range(image_ref.shape[0]):
        values = jnp.concatenate([payload_ref[m] for payload_ref in payload_refs], axis=0)
        for chunk in range(4):
            at = slice(256 * chunk, 256 * chunk + 256)
            image_ref[m, at, :] = own_ref[m, at, :] + dot(onehot_ref[m, at, 128:], values)
            copy = pltpu.make_async_copy(
                image_ref.at[m, at], image_hbm.at[m, at], sems.at[4 * m + chunk]
            )
            copy.start()
            copies.append(copy)
    for copy in copies:
        copy.wait()


def call(kernel, out_shape, flops=10**8, size=10**7, **options):
    return pl.pallas_call(
        kernel,
        out_shape=out_shape,
        compiler_params=pltpu.CompilerParams(vmem_limit_bytes=24 * 2**20),
        cost_estimate=pl.CostEstimate(flops=flops, bytes_accessed=size, transcendentals=0),
        **options,
    )


def shape_of(*shape, dtype=F32):
    return jax.ShapeDtypeStruct(shape, dtype)


def stay(*arrays):
    return [pltpu.with_memory_space_constraint(x, pltpu.HBM) for x in arrays]


def swaps(axis):
    count = lax.axis_size(axis)
    even = [(i, i ^ 1) for i in range(count)]
    odd = [(i, (i + 1) % count if i & 1 else (i - 1) % count) for i in range(count)]
    return even, odd


def swap_axial(x):
    count = lax.axis_size("ex")
    up = [(i, (i + 1) % count) for i in range(count)]
    if count == 2:
        return lax.ppermute(x, "ex", up)
    down = [(j, i) for i, j in up]
    return jnp.stack([lax.ppermute(x[0], "ex", up), lax.ppermute(x[1], "ex", down)])


def swap_both(one, two, axis):
    even, odd = swaps(axis)
    return lax.ppermute(one, axis, even), lax.ppermute(two, axis, odd)


def per_device(scalar, velocity, lumped_mass, pixel_weights, cut_element, pixel_block):
    shape = scalar.shape
    flat = (32, 64, 128)
    inner, outer = (32, 48, 128), (32, 16, 128)
    scalar = scalar.reshape(flat)
    velocity = velocity.reshape((3,) + flat)
    mass = lumped_mass.reshape(flat)
    tables = derivative_tables()
    n_cam = lax.axis_size("cam")
    cameras = pixel_weights.shape[0]
    share = cameras // n_cam
    part = functools.partial

    x, near = call(
        face_kernel,
        (shape_of(2, 2, 64, 128, dtype=BF16), shape_of(*tables.shape, dtype=BF16)),
        in_specs=[HBM] * 4,
        scratch_shapes=[
            pltpu.VMEM((2, 8, 64, 128), F32),
            pltpu.VMEM((2, 3, 64, 128), F32),
            pltpu.VMEM((2, 64, 128), F32),
            pltpu.SemaphoreType.DMA((7,)),
        ],
    )(*stay(scalar, velocity, mass, tables))
    x_got = swap_axial(x)
    s, z = call(first_kernel, (shape_of(64, 64, 128), shape_of(8, 8, 128)))(
        scalar, velocity, mass, near
    )
    weights = call(weight_kernel, shape_of(512, 128 * cameras, dtype=BF16))(pixel_weights)
    picks = call(pick_kernel, shape_of(cameras, 128, 640, dtype=BF16))(cut_element)

    half = functools.partial(shape_of, dtype=BF16)
    *z, x_got = call(
        first_radial_kernel, (half(80, 128), half(64, 128), shape_of(2, 2, 64, 128))
    )(z, x_got, pixel_block)
    z_got = swap_both(*z, "cam")
    z_got, weights, picks = lax.optimization_barrier((z_got, weights, picks))
    ids_got = z_got[0]
    *y, packed = call(
        part(azimuth_kernel, n_cam), (half(224, 128), half(224, 128), shape_of(8, 8, 128))
    )(s, x_got, *z_got, scalar, velocity, mass, near)
    y_got = swap_both(*y, "ey")
    g_inner, *inner_terms, z_inner = call(
        second_inner_kernel, (shape_of(*inner),) * 3 + (shape_of(4, 8, 128),)
    )(s, x_got, packed, scalar, velocity, mass, near)
    args = (s, x_got, packed, *y_got, scalar, velocity, mass, near, g_inner)
    some = (16, 16, 128)
    x, *faces = call(
        second_face_kernel,
        (shape_of(2, 1, 64, 128, dtype=BF16),) + (shape_of(*some),) * 3 + (shape_of(2, 8, 128),),
        scratch_shapes=[pltpu.VMEM(some, F32)],
    )(*args)
    g, *outer_terms, z = call(
        second_outer_kernel,
        (shape_of(*flat), shape_of(*outer), shape_of(*outer), shape_of(4, 8, 128)),
        scratch_shapes=[pltpu.VMEM(outer, F32), pltpu.VMEM(outer, F32)],
    )(*args, z_inner, *faces)

    terms = (*inner_terms, *outer_terms)
    x_got = swap_axial(x)
    early = call(
        early_kernel,
        shape_of(256, 128 * cameras, dtype=BF16),
        scratch_shapes=[pltpu.VMEM((256, 512), BF16)],
    )(g, *terms, near, weights)
    x_got, early = lax.optimization_barrier((x_got, early))
    *z, x_got = call(
        second_radial_kernel, (half(32, 128), half(64, 128), shape_of(2, 1, 64, 128))
    )(z, x_got, pixel_block, ids_got)
    z_got = swap_both(*z, "cam")
    pixels = call(
        middle_kernel,
        shape_of(cameras, 128, 128),
        scratch_shapes=[pltpu.VMEM((256, 512), BF16)],
    )(g, x_got, *terms, near, weights, picks, early)
    z_got, pixels = lax.optimization_barrier((z_got, pixels))
    payload_shape = half(share, 128, 128)
    values, *far = call(
        part(render_far_kernel, n_cam),
        (half(cameras, 64, 128),) + (payload_shape,) * (n_cam - 2),
        scratch_shapes=[pltpu.VMEM((64, 512), F32)],
    )(g, x_got, *z_got, *terms, near, weights, picks, pixels)
    parts = (values, picks, pixels)
    image_shape = shape_of(share, NBLK, 128)
    images, onehot = call(
        part(own_image_kernel, n_cam),
        (image_shape, half(share, NBLK, 128 * n_cam)),
        scratch_shapes=[
            pltpu.VMEM(payload_shape.shape, BF16),
            pltpu.VMEM((n_cam, cameras, 128), jnp.int32),
        ],
    )(*parts, pixel_block, ids_got, z_got[1])
    images, parts = lax.optimization_barrier((images, parts))
    beside = call(part(render_near_kernel, n_cam, 1), payload_shape)(*parts)
    final = (g, x_got, *z_got, *terms)
    final, beside = lax.optimization_barrier((final, beside))
    advected = call(
        part(advected_kernel, n_cam),
        shape_of(*flat),
        out_specs=HBM,
        scratch_shapes=[pltpu.VMEM(flat, F32), pltpu.SemaphoreType.DMA((4,))],
    )(*final)
    images, advected = lax.optimization_barrier((images, advected))
    received = []
    for d, payload in [(1, beside)] + [(n + 2, p) for n, p in enumerate(far)]:
        received.append(lax.ppermute(payload, "cam", [(i, i ^ d) for i in range(n_cam)]))
    images = call(
        image_kernel,
        image_shape,
        out_specs=HBM,
        scratch_shapes=[
            pltpu.VMEM((share, NBLK, 128), F32),
            pltpu.SemaphoreType.DMA((4 * share,)),
        ],
    )(images, onehot, *received)
    return (advected.reshape(shape), images)


def solution(mesh):
    placed = (
        P("ex", None, "ey", None, "cam"),
        P(None, "ex", None, "ey", None, "cam"),
        P("ex", None, "ey", None, "cam"),
        P(),
        P(None, ("cam", "ex", "ey")),
        P(None, ("cam", "ex", "ey")),
    )
    return jax.shard_map(
        per_device,
        mesh=mesh,
        in_specs=placed,
        out_specs=(P("ex", None, "ey", None, "cam"), P("cam", ("ex", "ey"), None)),
        check_vma=False,
    )
```

```python
import functools

import jax
import jax.numpy as jnp
import numpy as np
from jax import lax
from jax.experimental import pallas as pl
from jax.experimental.pallas import tpu as pltpu
from jax.sharding import PartitionSpec as P

NBLK = 1024
F32 = jnp.float32
BF16 = jnp.bfloat16
VMEM = pl.BlockSpec(memory_space=pltpu.VMEM)
HBM = pl.BlockSpec(memory_space=pltpu.HBM)
time_step = 0.01


def legendre_seven(points):
    previous = points * 0.0 + 1.0
    current = points * 1.0
    for order in range(1, 7):
        following = ((2 * order + 1) * points * current - order * previous) / (order + 1)
        previous = current
        current = following
    return current


def gll_derivative():
    degree = 7
    gll_nodes = np.array(
        [
            -1.0,
            -0.8717401485096066,
            -0.5917001814331423,
            -0.2092992179024789,
            0.2092992179024789,
            0.5917001814331423,
            0.8717401485096066,
            1.0,
        ]
    )
    values = legendre_seven(gll_nodes)
    derivative = np.zeros((degree + 1, degree + 1))
    for target in range(degree + 1):
        for source in range(degree + 1):
            if target != source:
                derivative[target, source] = values[target] / (
                    values[source] * (gll_nodes[target] - gll_nodes[source])
                )
    derivative[0, 0] = -degree * (degree + 1) / 4.0
    derivative[degree, degree] = degree * (degree + 1) / 4.0
    return derivative


def split_two(table):
    high = table.astype(np.float32).astype(BF16)
    low = (table - high.astype(np.float64)).astype(np.float32).astype(BF16)
    return high, low


def derivative_tables():
    derivative = gll_derivative()
    eye = np.eye(8)
    rows = np.concatenate([np.kron(derivative, eye), np.kron(eye, derivative)], axis=0)
    high, low = split_two(rows)
    row_table = np.concatenate([high, high, low, np.zeros_like(high)], axis=1)
    high, low = split_two(np.kron(np.eye(16), derivative.T))
    lane_table = np.concatenate(
        [
            np.concatenate([high, low], axis=1),
            np.concatenate([high, np.zeros_like(high)], axis=1),
        ],
        axis=0,
    )
    swap = np.zeros((128, 128))
    for c in range(15):
        swap[8 * c + 7, 8 * c + 8] = 1.0
        swap[8 * c + 8, 8 * c + 7] = 1.0
    join_table = np.concatenate([swap, swap], axis=0).astype(np.float32).astype(BF16)
    spread = np.zeros((128, 128))
    spread[0, 0::2] = 1.0
    spread[127, 1::2] = 1.0
    turn = np.zeros((64, 256))
    for k in range(4):
        for c in range(16):
            turn[16 * k + c, 8 * c + 2 * k] = 1.0
            turn[16 * k + c, 128 + 8 * c + 2 * k + 1] = 1.0
    ends = turn.reshape(4, 16, 256)[:, ::15].reshape(8, 256)
    ends = np.concatenate([ends, np.zeros_like(ends)], axis=0)
    partial = np.zeros((16, 64))
    for i in range(8):
        partial[i, 8 * i + 1 : 8 * i + 8] = derivative[0, 1:]
        partial[8 + i, 8 * i : 8 * i + 7] = derivative[7, :7]
    high, low = split_two(partial)
    partial = np.concatenate([high, high, low, np.zeros_like(high)], axis=1)
    exact = [spread, spread, turn[:, :128], turn[:, 128:], ends[:, :128], ends[:, 128:]]
    exact = np.concatenate(exact, axis=0)
    split = [row_table[:, :128], row_table[:, 128:], lane_table[:, :128], lane_table[:, 128:]]
    split += [join_table, exact.astype(np.float32).astype(BF16)]
    split += [partial[:, :128], partial[:, 128:]]
    return jnp.asarray(np.concatenate(split, axis=0))


def row_table(table_ref, first=0):
    high, low = table_ref[first:128], table_ref[128 + first : 256]
    return jnp.concatenate([high, low[:, :64]], axis=1)


def lane_table(table_ref):
    return jnp.concatenate([table_ref[256:512], table_ref[512:768]], axis=1)


def join_table(table_ref):
    return jnp.concatenate([table_ref[768:1024], table_ref[1024:1280]], axis=1)


def turn_table(table_ref):
    return jnp.concatenate([table_ref[1280:1344], table_ref[1344:1408]], axis=1)


def end_table(table_ref):
    return jnp.concatenate([table_ref[1408:1424], table_ref[1424:1440]], axis=1)


def partial_table(table_ref):
    return jnp.concatenate([table_ref[1440:1456], table_ref[1456:1472][:, :64]], axis=1)


def span_of(a, offset=0):
    if isinstance(a, int):
        return slice(8 * a + offset, 8 * a + offset + 8)
    return pl.ds(pl.multiple_of(a * 8 + offset, 8), 8)


def sweep(body, together):
    if together == 4:
        for a in range(4):
            body(a)
        return

    def step(n, carry):
        for m in range(together):
            body(n * together + m)
        return carry

    lax.fori_loop(0, 4 // together, step, 0)


def lane_ids(shape):
    return lax.broadcasted_iota(jnp.int32, shape, len(shape) - 1)


def row_ids(shape):
    return lax.broadcasted_iota(jnp.int32, shape, len(shape) - 2)


def halves(value):
    high = value.astype(BF16)
    return high, (value - high.astype(F32)).astype(BF16)


def dot(a, b):
    return jnp.dot(a, b, preferred_element_type=F32)


def by_lanes(pairs, table_ref):
    rows = jnp.concatenate([jnp.concatenate(p, axis=1) for p in pairs], axis=0)
    both = dot(rows, lane_table(table_ref))
    return both[:, :128] + both[:, 128:]


def join_lanes(values, table_ref):
    rows = jnp.concatenate([jnp.concatenate(halves(v), axis=1) for v in values], axis=0)
    other = dot(rows, join_table(table_ref))
    joined, spread, at = [], [], 0
    for v in values:
        span = slice(at, at + v.shape[0])
        joined.append(v + other[span, :128])
        spread.append(other[span, 128:])
        at += v.shape[0]
    return joined, spread


def join_rows(value):
    row = row_ids(value.shape)
    last = ((row & 7) == 7) & (row != 63)
    first = ((row & 7) == 0) & (row != 0)
    other = jnp.where(
        last, pltpu.roll(value, 63, 0), jnp.where(first, pltpu.roll(value, 1, 0), 0.0)
    )
    return value + other


def convect_pair(fields, velocities, masses, table_ref):
    pairs = [halves(f) for f in fields]
    high = jnp.concatenate([p[0] for p in pairs], axis=1)
    low = jnp.concatenate([p[1] for p in pairs], axis=1)
    stacked = jnp.concatenate([high, low, high], axis=0)
    rows = dot(row_table(table_ref), stacked)
    radius = by_lanes(pairs, table_ref)
    out = []
    for n in range(2):
        lanes = slice(128 * n, 128 * n + 128)
        v = velocities[n]
        slope = v[0] * rows[:64, lanes] + v[1] * rows[64:, lanes]
        out.append(masses[n] * (slope + v[2] * radius[64 * n : 64 * n + 64]))
    return out


def face_kernel(
    scalar_hbm, velocity_hbm, mass_hbm, table_hbm, x_ref, table_ref, f_ref, v_ref, m_ref, sems,
):
    copies = []

    def start(source, target):
        copy = pltpu.make_async_copy(source, target, sems.at[len(copies)])
        copy.start()
        copies.append(copy)

    last = scalar_hbm.shape[0] - 1
    start(scalar_hbm.at[pl.ds(last - 7, 8)], f_ref.at[0])
    start(scalar_hbm.at[pl.ds(0, 8)], f_ref.at[1])
    start(table_hbm, table_ref)
    start(velocity_hbm.at[:, last], v_ref.at[0])
    start(velocity_hbm.at[:, 0], v_ref.at[1])
    start(mass_hbm.at[last], m_ref.at[0])
    start(mass_hbm.at[0], m_ref.at[1])
    for copy in copies[:3]:
        copy.wait()
    derivative = gll_derivative()
    fields = [f_ref[0, 7], f_ref[1, 0]]
    pairs = [halves(f) for f in fields]
    high = jnp.concatenate([p[0] for p in pairs], axis=1)
    low = jnp.concatenate([p[1] for p in pairs], axis=1)
    azimuth = dot(row_table(table_ref, 64), jnp.concatenate([high, low, high], axis=0))
    radius = by_lanes(pairs, table_ref)
    for copy in copies[3:]:
        copy.wait()
    values = []
    for n, node in enumerate((7, 0)):
        axial = f_ref[n, 0] * float(derivative[node, 0])
        for p in range(1, 8):
            axial = axial + f_ref[n, p] * float(derivative[node, p])
        slope = v_ref[n, 0] * axial + v_ref[n, 1] * azimuth[:, 128 * n : 128 * n + 128]
        values.append(m_ref[n] * (slope + v_ref[n, 2] * radius[64 * n : 64 * n + 64]))
        values.append(m_ref[n])
    for n, value in enumerate(join_lanes(values, table_ref)[0]):
        x_ref[n // 2, n % 2] = join_rows(value).astype(BF16)


def join_block(s_ref):
    for b in range(s_ref.shape[1] // 8 - 1):
        total = s_ref[:, 8 * b + 7, :] + s_ref[:, 8 * b + 8, :]
        s_ref[:, 8 * b + 7, :] = total
        s_ref[:, 8 * b + 8, :] = total
    join_axial(s_ref)


def join_axial(s_ref):
    for f in range(s_ref.shape[0] // 32):
        for a in range(3):
            at = 32 * f + 8 * a + 7
            total = s_ref[at] + s_ref[at + 1]
            s_ref[at] = total
            s_ref[at + 1] = total


def pack_blocks(blocks):
    slot = ((lane_ids((8, 128)) + 1) >> 1) & 63
    parts = [jnp.zeros((8, 128), F32) for _ in range(4)]
    for n, (u, block) in enumerate(blocks):
        if u:
            block = pltpu.roll(block, 2 * u, 1)
        parts[n % 4] = jnp.where(slot == u, block, parts[n % 4])
    return (parts[0] + parts[1]) + (parts[2] + parts[3])


def pick_spread(spreads):
    slot = ((lane_ids((8, 128)) + 1) >> 1) & 63
    parts = [jnp.zeros((8, 128), F32) for _ in range(2)]
    for b, spread in spreads:
        for i in range(8):
            block = spread[8 * i : 8 * i + 8]
            parts[i % 2] = jnp.where(slot == 56 - 8 * i + b, block, parts[i % 2])
    return parts[0] + parts[1]


def join_packed(packed):
    lane, row = lane_ids((8, 128)), row_ids((8, 128))
    slot = ((lane + 1) >> 1) & 63
    b = slot & 7
    rows = []
    for value in packed:
        after = pltpu.roll(pltpu.roll(value, 126, 1), 7, 0)
        before = pltpu.roll(pltpu.roll(value, 2, 1), 1, 0)
        value = value + jnp.where((row == 7) & (b < 7), after, 0.0)
        rows.append(value + jnp.where((row == 0) & (b > 0), before, 0.0))
    out = list(rows)
    for a in range(3):
        out[a] = out[a] + jnp.where(slot < 8, pltpu.roll(rows[a + 1], 16, 1), 0.0)
        out[a + 1] = out[a + 1] + jnp.where(slot >= 56, pltpu.roll(rows[a], 112, 1), 0.0)
    return out


def first_kernel(scalar_ref, velocity_ref, mass_ref, table_ref, s_ref, z_ref):
    def body(a):
        at = span_of(a)
        spreads = [[], []]
        for pair in range(4):
            spans = [slice(16 * pair + 8 * n, 16 * pair + 8 * n + 8) for n in range(2)]
            fields = [scalar_ref[at, s, :].reshape(64, 128) for s in spans]
            velocities = [
                [velocity_ref[d, at, s, :].reshape(64, 128) for d in range(3)] for s in spans
            ]
            masses = [mass_ref[at, s, :].reshape(64, 128) for s in spans]
            values = convect_pair(fields, velocities, masses, table_ref)
            joined, spread = join_lanes(values + masses, table_ref)
            for n, s in enumerate(spans):
                for f in range(2):
                    s_ref[span_of(a, 32 * f), s, :] = joined[n + 2 * f].reshape(8, 8, 128)
                    spreads[f].append((2 * pair + n, spread[n + 2 * f]))
        for f in range(2):
            z_ref[a + 4 * f] = pick_spread(spreads[f])

    sweep(body, 2)
    join_block(s_ref)
    for f in range(2):
        for n, value in enumerate(join_packed([z_ref[4 * f + a] for a in range(4)])):
            z_ref[4 * f + n] = value


def radial_faces(count, z_in, x_in, x_ref):
    x_ref[...] = x_in[...].astype(F32)
    rows = []
    for f in range(count):
        spans = [slice(8 * b, 8 * b + 8) for b in range(8)]
        low = pack_blocks([(56 + b, x_ref[0, f, s, :]) for b, s in enumerate(spans)])
        high = pack_blocks([(b, x_ref[1, f, s, :]) for b, s in enumerate(spans)])
        rows += [z_in[4 * f] + low, z_in[4 * f + 1], z_in[4 * f + 2], z_in[4 * f + 3] + high]
    return jnp.concatenate(rows, axis=0).astype(BF16)


def id_tile(block_ref):
    ids = block_ref[...]
    return jnp.concatenate([ids >> 5, ids & 31], axis=0).astype(F32).astype(BF16)


def first_radial_kernel(z_in, x_in, block_ref, one_ref, two_ref, x_ref):
    faces = radial_faces(2, z_in, x_in, x_ref)
    one_ref[:64, :] = faces
    one_ref[64:, :] = id_tile(block_ref)
    two_ref[...] = faces


def second_radial_kernel(z_in, x_in, block_ref, got_ref, one_ref, two_ref, x_ref):
    faces = radial_faces(1, z_in, x_in, x_ref)
    one_ref[...] = faces
    two_ref[:32, :] = faces
    two_ref[32:48, :] = id_tile(block_ref)
    two_ref[48:, :] = got_ref[64:, :]


def merged(one, two, cam_count):
    me = lax.axis_index("cam")
    even = (me & 1) == 0
    left = jnp.where(even, two, one)
    right = jnp.where(even, one, two)
    left = jnp.where(me == 0, 0.0, left)
    right = jnp.where(me == cam_count - 1, 0.0, right)
    lane = lane_ids((8, 128))
    return jnp.where((lane & 1) == 0, pltpu.roll(left, 1, 1), pltpu.roll(right, 127, 1))


def end_lanes(shape):
    lane = lane_ids(shape)
    return (lane == 0) | (lane == 127)


def azimuth_kernel(
    cam_count, s_ref, x_ref, one_ref, two_ref, scalar_ref, velocity_ref, mass_ref, table_ref,
    even_ref, odd_ref, packed_ref,
):
    ends = end_lanes((8, 128))
    row = row_ids((8, 128))
    even = (lax.axis_index("ey") & 1) == 0
    count = s_ref.shape[0]
    one = one_ref[:count, :].astype(F32)
    two = two_ref[:count, :].astype(F32)
    low, high = [], []
    for q in range(count // 8):
        at = slice(8 * q, 8 * q + 8)
        packed = merged(one[at], two[at], cam_count)
        packed_ref[q] = packed
        f, a = q // 4, q % 4
        for line, shift, faces in ((0, 16, low), (63, 2, high)):
            j = line & 7
            spread = jnp.broadcast_to(packed[j : j + 1, :], (8, 128))
            moved = pltpu.roll(spread, shift, 1, stride=16, stride_axis=0)
            face = s_ref[at, line, :] + jnp.where(ends, moved, 0.0)
            if a == 0:
                face = face + jnp.where(row == 0, x_ref[0, f, line : line + 1, :], 0.0)
            if a == 3:
                face = face + jnp.where(row == 7, x_ref[1, f, line : line + 1, :], 0.0)
            faces.append(face)
    slopes = [[], []]
    for a in range(4):
        pairs = []
        for b in (0, 7):
            g = assembled(s_ref, x_ref, packed_ref[a], 0, a, b)
            m = assembled(s_ref, x_ref, packed_ref[a + 4], 1, a, b)
            scalar = scalar_ref[span_of(a), 8 * b : 8 * b + 8, :].reshape(64, 128)
            pairs.append(halves(scalar - (time_step / m) * g))
        tops = jnp.concatenate([p[0] for p in pairs], axis=1)
        rests = jnp.concatenate([p[1] for p in pairs], axis=1)
        both = dot(partial_table(table_ref), jnp.concatenate([tops, rests, tops], axis=0))
        slopes[0].append(both[:8, :128])
        slopes[1].append(both[8:, 128:])
    messages = []
    for faces, line, slope in ((low, 0, slopes[0]), (high, 63, slopes[1])):
        flow = [mass_ref[:, line, :] * velocity_ref[d, :, line, :] for d in range(3)]
        share = flow[1] * jnp.concatenate(slope, axis=0)
        rows = faces + [share] + flow + [scalar_ref[:, line, :]]
        messages.append(jnp.concatenate(rows, axis=0))
    even_ref[...] = jnp.where(even, messages[1], messages[0]).astype(BF16)
    odd_ref[...] = jnp.where(even, messages[0], messages[1]).astype(BF16)


def unpacked(packed, b):
    ends = end_lanes((8, 128))
    rows = []
    for i in range(8):
        u = 56 - 8 * i + b
        moved = pltpu.roll(packed, (128 - 2 * u) % 128, 1) if u else packed
        rows.append(jnp.where(ends, moved, 0.0))
    return rows


def assembled(s_ref, x_ref, packed, f, a, b, y_refs=None):
    span = slice(8 * b, 8 * b + 8)
    at = span_of(a, 32 * f)
    block = s_ref[at, span, :]
    if packed is None:
        rows = [jnp.zeros((8, 128), F32) for _ in range(8)]
    else:
        rows = unpacked(packed, b)
    if not isinstance(a, int):
        rows[0] = rows[0] + jnp.where(a == 0, x_ref[0, f, span, :], 0.0)
        rows[7] = rows[7] + jnp.where(a == 3, x_ref[1, f, span, :], 0.0)
    elif a == 0:
        rows[0] = rows[0] + x_ref[0, f, span, :]
    elif a == 3:
        rows[7] = rows[7] + x_ref[1, f, span, :]
    if y_refs is not None:
        one_ref, two_ref = y_refs
        even = (lax.axis_index("ey") & 1) == 0
        at = slice(16 * (a // 2) + 32 * f, 16 * (a // 2) + 32 * f + 16)
        one, two = one_ref[at, :].astype(F32), two_ref[at, :].astype(F32)
        if b == 0:
            line, sublane = jnp.where(even, two, one), 0
        else:
            line, sublane = jnp.where(even, one, two), 7
        line = line[8 * (a % 2) : 8 * (a % 2) + 8]
        node = lax.broadcasted_iota(jnp.int32, (8, 8, 128), 1)
        block = block + jnp.where(node == sublane, line[:, None, :], 0.0)
    return block.reshape(64, 128) + jnp.concatenate(rows, axis=0)


def second_pairs(
    pairs, s_ref, x_ref, packed_ref, y_refs, scalar_ref, velocity_ref,
    mass_ref, table_ref, g_ref, base_ref, half_ref, z_ref, first_ref=None,
):
    def body(a, layer=None):
        at = span_of(a)
        layer = a if layer is None else layer
        to = span_of(layer)
        radial_g = packed_ref[a]
        radial_m = packed_ref[a + 4]
        spreads = []
        for n, pair in enumerate(pairs):
            fields, velocities, masses = [], [], []
            for h, b in enumerate(pair):
                s = slice(8 * b, 8 * b + 8)
                out = slice(16 * n + 8 * h, 16 * n + 8 * h + 8)
                g = assembled(s_ref, x_ref, radial_g, 0, a, b, y_refs)
                m = assembled(s_ref, x_ref, radial_m, 1, a, b, y_refs)
                scale = time_step / m
                scalar = scalar_ref[at, s, :].reshape(64, 128)
                first = scalar - scale * g
                base_ref[to, out, :] = (0.5 * (scalar + first)).reshape(8, 8, 128)
                half_ref[to, out, :] = (0.5 * scale).reshape(8, 8, 128)
                fields.append(first)
                if first_ref is not None:
                    first_ref[to, out, :] = first.reshape(8, 8, 128)
                velocities.append(
                    [velocity_ref[d, at, s, :].reshape(64, 128) for d in range(3)]
                )
                masses.append(mass_ref[at, s, :].reshape(64, 128))
            values = convect_pair(fields, velocities, masses, table_ref)
            joined, spread = join_lanes(values, table_ref)
            for h, b in enumerate(pair):
                out = slice(16 * n + 8 * h, 16 * n + 8 * h + 8)
                g_ref[to, out, :] = joined[h].reshape(8, 8, 128)
                spreads.append((b, spread[h]))
        z_ref[layer] = pick_spread(spreads)

    return body


def second_inner_kernel(
    s_ref, x_ref, packed_ref, scalar_ref, velocity_ref, mass_ref,
    table_ref, g_ref, base_ref, half_ref, z_ref,
):
    body = second_pairs(
        ((1, 2), (3, 4), (5, 6)), s_ref, x_ref, packed_ref, None,
        scalar_ref, velocity_ref, mass_ref, table_ref, g_ref, base_ref, half_ref, z_ref,
    )
    sweep(body, 2)
    join_block(g_ref)


def add_beyond(layers, y_one_ref, y_two_ref, first_ref, scalar_ref, table_ref, g_ref, z_ref):
    even = (lax.axis_index("ey") & 1) == 0
    one, two = y_one_ref[64:, :].astype(F32), y_two_ref[64:, :].astype(F32)
    sides = (jnp.where(even, two, one), jnp.where(even, one, two))
    rows = []
    for h, (line, outer) in enumerate(((0, 0), (15, 63))):
        for a, n in layers:
            change = first_ref[span_of(n), line, :] - scalar_ref[span_of(a), outer, :]
            rows.append(sides[h][128 + 8 * a : 136 + 8 * a] + change)
    count = len(layers)
    field = jnp.concatenate(rows + [jnp.zeros((64 - 16 * count, 128), F32)], axis=0)
    high, low = halves(field)
    axial = dot(row_table(table_ref, 64), jnp.concatenate([high, low, high], axis=0))
    radius = by_lanes([(high, low)], table_ref)
    corner = float(gll_derivative()[7, 7])
    values = []
    for h, sign in ((0, corner), (1, -corner)):
        for k, (a, _) in enumerate(layers):
            at = slice(8 * (count * h + k), 8 * (count * h + k) + 8)
            share, *flow = [sides[h][32 * n + 8 * a : 32 * n + 8 * a + 8] for n in range(4)]
            azimuth = sign * field[at]
            values.append(share + flow[0] * axial[at] + flow[1] * azimuth + flow[2] * radius[at])
    (joined,), (spread,) = join_lanes([jnp.concatenate(values, axis=0)], table_ref)
    slot = ((lane_ids((8, 128)) + 1) >> 1) & 63
    row = row_ids((8, 128))
    for h, line in ((0, 0), (1, 15)):
        for k, (_, n) in enumerate(layers):
            at = slice(8 * (count * h + k), 8 * (count * h + k) + 8)
            g_ref[span_of(n), line, :] = g_ref[span_of(n), line, :] + joined[at]
            mine = jnp.where(slot == 56 - 8 * row + 7 * h, spread[at], 0.0)
            total = jnp.sum(mine, axis=0, keepdims=True)
            z_ref[n] = z_ref[n] + jnp.where(row == 7 * h, total, 0.0)


def second_face_kernel(
    s_ref, x_ref, packed_ref, y_one_ref, y_two_ref, scalar_ref, velocity_ref,
    mass_ref, table_ref, inner_ref, x_out_ref, edge_ref, base_ref, half_ref, z_ref, first_ref,
):
    body = second_pairs(
        ((0, 7),), s_ref, x_ref, packed_ref, (y_one_ref, y_two_ref), scalar_ref, velocity_ref,
        mass_ref, table_ref, edge_ref, base_ref, half_ref, z_ref, first_ref,
    )
    body(0, 0)
    body(3, 1)
    add_beyond(((0, 0), (3, 1)), y_one_ref, y_two_ref, first_ref, scalar_ref, table_ref, edge_ref, z_ref)
    row = row_ids((64, 128))
    for n, (layer, at) in enumerate(((15, 31), (0, 0))):
        face = jnp.concatenate(
            [edge_ref[layer, 0:8, :], inner_ref[at], edge_ref[layer, 8:16, :]], axis=0
        )
        after = jnp.where((row == 7) | (row == 55), pltpu.roll(face, 63, 0), 0.0)
        before = jnp.where((row == 8) | (row == 56), pltpu.roll(face, 1, 0), 0.0)
        x_out_ref[n, 0] = (face + (after + before)).astype(BF16)


def second_outer_kernel(
    s_ref, x_ref, packed_ref, y_one_ref, y_two_ref, scalar_ref, velocity_ref,
    mass_ref, table_ref, inner_ref, z_in, edge_in, base_in, half_in, z_face,
    g_ref, base_ref, half_ref, z_ref, edge_ref, first_ref,
):
    body = second_pairs(
        ((0, 7),), s_ref, x_ref, packed_ref, (y_one_ref, y_two_ref), scalar_ref, velocity_ref,
        mass_ref, table_ref, edge_ref, base_ref, half_ref, z_ref, first_ref,
    )
    body(1)
    body(2)
    add_beyond(((1, 1), (2, 2)), y_one_ref, y_two_ref, first_ref, scalar_ref, table_ref, edge_ref, z_ref)
    for layer, a in ((0, 0), (1, 3)):
        for source, target in ((edge_in, edge_ref), (base_in, base_ref), (half_in, half_ref)):
            target[span_of(a)] = source[span_of(layer)]
        z_ref[a] = z_face[layer]
    join_axial(edge_ref)
    g_ref[:, 0:8, :] = edge_ref[:, 0:8, :]
    g_ref[:, 8:56, :] = inner_ref[...]
    g_ref[:, 56:64, :] = edge_ref[:, 8:16, :]
    for low in (7, 55):
        total = g_ref[:, low, :] + g_ref[:, low + 1, :]
        g_ref[:, low, :] = total
        g_ref[:, low + 1, :] = total
    for n, value in enumerate(join_packed([z_ref[a] + z_in[a] for a in range(4)])):
        z_ref[n] = value


def weight_kernel(weight_ref, out_ref):
    row = row_ids((512, 512))
    source = (row & 63) * 8 + (row >> 6)
    order = jnp.where(lane_ids((512, 512)) == source, 1.0, 0.0).astype(BF16)
    for m in range(8):
        out_ref[:, 128 * m : 128 * m + 128] = dot(order, weight_ref[m]).astype(BF16)


def pick_kernel(cut_ref, pick_ref):
    cut = cut_ref[...]
    a, b, c = cut >> 7, (cut >> 4) & 7, cut & 15
    order = jnp.where(a == 0, 2, jnp.where(a == 3, 3, a - 1))
    inner = 128 * order + 16 * b + c
    ends = 512 + 16 * a + 2 * b + (c >> 3)
    place = jnp.where((c == 0) | (c == 15), ends, inner)
    turned = place.astype(F32).T.astype(jnp.int32)
    lane = lane_ids((128, 640))
    for m in range(8):
        pick_ref[m] = jnp.where(lane == turned[:, m : m + 1], 1.0, 0.0).astype(BF16)


def turn(blocks, table):
    rows = []
    for block in blocks:
        value = block.astype(BF16)
        zero = jnp.zeros_like(value)
        rows.append(jnp.concatenate([value, zero], axis=1))
        rows.append(jnp.concatenate([zero, value], axis=1))
    return lax.dot_general(
        table,
        jnp.concatenate(rows, axis=0),
        (((1,), (1,)), ((), ())),
        preferred_element_type=F32,
    )


PAIRS = ((0, 1), (2, 3), (4, 5), (6, 7))


def term(refs, a, b):
    inner_ref, outer_ref = refs
    at = span_of(a)
    if b in (0, 7):
        return outer_ref[at, 8 * (b // 7) : 8 * (b // 7) + 8, :].reshape(64, 128)
    return inner_ref[at, 8 * b - 8 : 8 * b, :].reshape(64, 128)


def advanced(g_ref, x_ref, packed, bases, halfs, a, pair):
    blocks = []
    for b in pair:
        g = assembled(g_ref, x_ref, packed, 0, a, b)
        blocks.append(term(bases, a, b) - term(halfs, a, b) * g)
    return blocks


def store_elements(element_ref, blocks, table_ref, place):
    turned = turn(blocks, turn_table(table_ref)).astype(BF16)
    for h in range(2):
        for k in range(4):
            element_ref[place + 16 * h : place + 16 * h + 16, 128 * k : 128 * k + 128] = turned[
                16 * k : 16 * k + 16, 128 * h : 128 * h + 128
            ]


def pixel_values(element_ref, weight_ref, m):
    return dot(element_ref[...], weight_ref[:, 256 * m : 256 * m + 256]).astype(BF16)


def layer_elements(layers, g_ref, x_ref, bases, halfs, table_ref, element_ref):
    place = 0
    for a in layers:
        for pair in PAIRS:
            blocks = advanced(g_ref, x_ref, None, bases, halfs, a, pair)
            store_elements(element_ref, blocks, table_ref, place)
            place += 32


def early_kernel(
    g_ref, base_one, half_one, base_two, half_two, table_ref, weight_ref, value_ref, element_ref
):
    bases, halfs = (base_one, base_two), (half_one, half_two)
    layer_elements((1, 2), g_ref, None, bases, halfs, table_ref, element_ref)
    for m in range(4):
        value_ref[:, 256 * m : 256 * m + 256] = pixel_values(element_ref, weight_ref, m)


def middle_kernel(
    g_ref, x_ref, base_one, half_one, base_two, half_two, table_ref, weight_ref, pick_ref,
    early_ref, pixel_ref, element_ref,
):
    bases, halfs = (base_one, base_two), (half_one, half_two)
    layer_elements((0, 3), g_ref, x_ref, bases, halfs, table_ref, element_ref)
    for m in range(4):
        late = pixel_values(element_ref, weight_ref, m)
        both = jnp.concatenate([early_ref[:, 256 * m : 256 * m + 256], late], axis=0)
        for n in range(2):
            pixel_ref[2 * m + n] = dot(
                pick_ref[2 * m + n, :, :512], both[:, 128 * n : 128 * n + 128]
            )


def fill_payload(payload_ref, d, cam_count, pick_ref, value_ref, pixel_ref):
    me = lax.axis_index("cam")
    share = pixel_ref.shape[0] // cam_count
    for n in range(share):
        m = share * (me ^ d) + n
        values = dot(pick_ref[m, :, 512:576], value_ref[m]) + pixel_ref[m]
        payload_ref[n] = values.astype(BF16)


def final_layers(cam_count, g_ref, x_ref, one_ref, two_ref, terms, use):
    base_one, half_one, base_two, half_two = terms
    bases, halfs = (base_one, base_two), (half_one, half_two)
    one, two = one_ref[:32, :].astype(F32), two_ref[:32, :].astype(F32)
    for a in range(4):
        packed = merged(one[8 * a : 8 * a + 8], two[8 * a : 8 * a + 8], cam_count)
        for pair in PAIRS:
            use(a, pair, advanced(g_ref, x_ref, packed, bases, halfs, a, pair))


def render_far_kernel(
    cam_count, g_ref, x_ref, one_ref, two_ref, base_one, half_one, base_two, half_two,
    table_ref, weight_ref, pick_ref, pixel_ref, value_ref, *rest,
):
    payload_refs, end_ref = rest[:-1], rest[-1]

    def use(a, pair, blocks):
        turned = turn(blocks, end_table(table_ref))
        for h, b in enumerate(pair):
            place = 16 * a + 2 * b
            for k in range(4):
                end_ref[place : place + 2, 128 * k : 128 * k + 128] = turned[
                    2 * k : 2 * k + 2, 128 * h : 128 * h + 128
                ]

    terms = (base_one, half_one, base_two, half_two)
    final_layers(cam_count, g_ref, x_ref, one_ref, two_ref, terms, use)
    ends = end_ref[...].astype(BF16)
    for m in range(pixel_ref.shape[0] // 2):
        values = dot(ends, weight_ref[:, 256 * m : 256 * m + 256]).astype(BF16)
        value_ref[2 * m] = values[:, :128]
        value_ref[2 * m + 1] = values[:, 128:]
    for d in range(2, cam_count):
        fill_payload(payload_refs[d - 2], d, cam_count, pick_ref, value_ref, pixel_ref)


def advected_kernel(
    cam_count, g_ref, x_ref, one_ref, two_ref, base_one, half_one, base_two, half_two,
    out_hbm, advected_ref, sems,
):
    copies = []

    def use(a, pair, blocks):
        for h, b in enumerate(pair):
            advected_ref[span_of(a), 8 * b : 8 * b + 8, :] = blocks[h].reshape(8, 8, 128)
        if pair == PAIRS[-1]:
            at = span_of(a)
            copy = pltpu.make_async_copy(advected_ref.at[at], out_hbm.at[at], sems.at[a])
            copy.start()
            copies.append(copy)

    terms = (base_one, half_one, base_two, half_two)
    final_layers(cam_count, g_ref, x_ref, one_ref, two_ref, terms, use)
    for copy in copies:
        copy.wait()


def render_near_kernel(cam_count, d, value_ref, pick_ref, pixel_ref, payload_ref):
    fill_payload(payload_ref, d, cam_count, pick_ref, value_ref, pixel_ref)


def own_image_kernel(
    cam_count, value_ref, pick_ref, pixel_ref, block_ref, first_ref, second_ref,
    image_ref, onehot_ref, payload_ref, id_ref,
):
    me = lax.axis_index("cam")
    share = image_ref.shape[0]
    id_ref[0] = block_ref[...]
    tiles = ((1, first_ref[64:80, :]), (3, second_ref[32:48, :]), (2, second_ref[48:64, :]))
    for d, tile in tiles:
        ids = tile.astype(F32).astype(jnp.int32)
        id_ref[d] = ids[:8] * 32 + ids[8:]
    fill_payload(payload_ref, 0, cam_count, pick_ref, value_ref, pixel_ref)
    for m in range(share):
        ids = [id_ref[d, pl.ds(share * me + m, 1), :] for d in range(4)]
        ids = jnp.concatenate(ids, axis=1)
        for chunk in range(4):
            at = slice(256 * chunk, 256 * chunk + 256)
            row = row_ids((256, ids.shape[1])) + 256 * chunk
            onehot = jnp.where(row == ids, 1.0, 0.0).astype(BF16)
            onehot_ref[m, at, :] = onehot
            image_ref[m, at, :] = dot(onehot[:, :128], payload_ref[m])


def image_kernel(own_ref, onehot_ref, *refs):
    payload_refs, (image_hbm, image_ref, sems) = refs[:-3], refs[-3:]
    copies = []
    for m in range(image_ref.shape[0]):
        values = jnp.concatenate([payload_ref[m] for payload_ref in payload_refs], axis=0)
        for chunk in range(2):
            at = slice(512 * chunk, 512 * chunk + 512)
            image_ref[m, at, :] = own_ref[m, at, :] + dot(onehot_ref[m, at, 128:], values)
            copy = pltpu.make_async_copy(
                image_ref.at[m, at], image_hbm.at[m, at], sems.at[2 * m + chunk]
            )
            copy.start()
            copies.append(copy)
    for copy in copies:
        copy.wait()


def call(kernel, out_shape, flops=10**8, size=10**7, **options):
    return pl.pallas_call(
        kernel,
        out_shape=out_shape,
        compiler_params=pltpu.CompilerParams(vmem_limit_bytes=24 * 2**20),
        cost_estimate=pl.CostEstimate(flops=flops, bytes_accessed=size, transcendentals=0),
        **options,
    )


def shape_of(*shape, dtype=F32):
    return jax.ShapeDtypeStruct(shape, dtype)


def stay(*arrays):
    return [pltpu.with_memory_space_constraint(x, pltpu.HBM) for x in arrays]


def swaps(axis):
    count = lax.axis_size(axis)
    even = [(i, i ^ 1) for i in range(count)]
    odd = [(i, (i + 1) % count if i & 1 else (i - 1) % count) for i in range(count)]
    return even, odd


def swap_axial(x):
    count = lax.axis_size("ex")
    up = [(i, (i + 1) % count) for i in range(count)]
    if count == 2:
        return lax.ppermute(x, "ex", up)
    down = [(j, i) for i, j in up]
    return jnp.stack([lax.ppermute(x[0], "ex", up), lax.ppermute(x[1], "ex", down)])


def swap_both(one, two, axis):
    even, odd = swaps(axis)
    return lax.ppermute(one, axis, even), lax.ppermute(two, axis, odd)


def per_device(scalar, velocity, lumped_mass, pixel_weights, cut_element, pixel_block):
    shape = scalar.shape
    flat = (32, 64, 128)
    inner, outer = (32, 48, 128), (32, 16, 128)
    scalar = scalar.reshape(flat)
    velocity = velocity.reshape((3,) + flat)
    mass = lumped_mass.reshape(flat)
    tables = derivative_tables()
    n_cam = lax.axis_size("cam")
    cameras = pixel_weights.shape[0]
    share = cameras // n_cam
    part = functools.partial

    x, near = call(
        face_kernel,
        (shape_of(2, 2, 64, 128, dtype=BF16), shape_of(*tables.shape, dtype=BF16)),
        in_specs=[HBM] * 4,
        scratch_shapes=[
            pltpu.VMEM((2, 8, 64, 128), F32),
            pltpu.VMEM((2, 3, 64, 128), F32),
            pltpu.VMEM((2, 64, 128), F32),
            pltpu.SemaphoreType.DMA((7,)),
        ],
    )(*stay(scalar, velocity, mass, tables))
    x_got = swap_axial(x)
    s, z = call(first_kernel, (shape_of(64, 64, 128), shape_of(8, 8, 128)))(
        scalar, velocity, mass, near
    )
    weights = call(weight_kernel, shape_of(512, 128 * cameras, dtype=BF16))(pixel_weights)
    picks = call(pick_kernel, shape_of(cameras, 128, 640, dtype=BF16))(cut_element)

    half = functools.partial(shape_of, dtype=BF16)
    *z, x_got = call(
        first_radial_kernel, (half(80, 128), half(64, 128), shape_of(2, 2, 64, 128))
    )(z, x_got, pixel_block)
    z_got = swap_both(*z, "cam")
    z_got, weights, picks = lax.optimization_barrier((z_got, weights, picks))
    ids_got = z_got[0]
    *y, packed = call(
        part(azimuth_kernel, n_cam), (half(224, 128), half(224, 128), shape_of(8, 8, 128))
    )(s, x_got, *z_got, scalar, velocity, mass, near)
    y_got = swap_both(*y, "ey")
    g_inner, *inner_terms, z_inner = call(
        second_inner_kernel, (shape_of(*inner),) * 3 + (shape_of(4, 8, 128),)
    )(s, x_got, packed, scalar, velocity, mass, near)
    args = (s, x_got, packed, *y_got, scalar, velocity, mass, near, g_inner)
    some = (16, 16, 128)
    x, *faces = call(
        second_face_kernel,
        (shape_of(2, 1, 64, 128, dtype=BF16),) + (shape_of(*some),) * 3 + (shape_of(2, 8, 128),),
        scratch_shapes=[pltpu.VMEM(some, F32)],
    )(*args)
    g, *outer_terms, z = call(
        second_outer_kernel,
        (shape_of(*flat), shape_of(*outer), shape_of(*outer), shape_of(4, 8, 128)),
        scratch_shapes=[pltpu.VMEM(outer, F32), pltpu.VMEM(outer, F32)],
    )(*args, z_inner, *faces)

    terms = (*inner_terms, *outer_terms)
    x_got = swap_axial(x)
    early = call(
        early_kernel,
        shape_of(256, 128 * cameras, dtype=BF16),
        scratch_shapes=[pltpu.VMEM((256, 512), BF16)],
    )(g, *terms, near, weights)
    x_got, early = lax.optimization_barrier((x_got, early))
    *z, x_got = call(
        second_radial_kernel, (half(32, 128), half(64, 128), shape_of(2, 1, 64, 128))
    )(z, x_got, pixel_block, ids_got)
    z_got = swap_both(*z, "cam")
    pixels = call(
        middle_kernel,
        shape_of(cameras, 128, 128),
        scratch_shapes=[pltpu.VMEM((256, 512), BF16)],
    )(g, x_got, *terms, near, weights, picks, early)
    z_got, pixels = lax.optimization_barrier((z_got, pixels))
    payload_shape = half(share, 128, 128)
    values, *far = call(
        part(render_far_kernel, n_cam),
        (half(cameras, 64, 128),) + (payload_shape,) * (n_cam - 2),
        scratch_shapes=[pltpu.VMEM((64, 512), F32)],
    )(g, x_got, *z_got, *terms, near, weights, picks, pixels)
    parts = (values, picks, pixels)
    image_shape = shape_of(share, NBLK, 128)
    images, onehot = call(
        part(own_image_kernel, n_cam),
        (image_shape, half(share, NBLK, 128 * n_cam)),
        scratch_shapes=[
            pltpu.VMEM(payload_shape.shape, BF16),
            pltpu.VMEM((n_cam, cameras, 128), jnp.int32),
        ],
    )(*parts, pixel_block, ids_got, z_got[1])
    images, parts = lax.optimization_barrier((images, parts))
    beside = call(part(render_near_kernel, n_cam, 1), payload_shape)(*parts)
    final = (g, x_got, *z_got, *terms)
    final, beside = lax.optimization_barrier((final, beside))
    advected = call(
        part(advected_kernel, n_cam),
        shape_of(*flat),
        out_specs=HBM,
        scratch_shapes=[pltpu.VMEM(flat, F32), pltpu.SemaphoreType.DMA((4,))],
    )(*final)
    images, advected = lax.optimization_barrier((images, advected))
    received = []
    for d, payload in [(1, beside)] + [(n + 2, p) for n, p in enumerate(far)]:
        received.append(lax.ppermute(payload, "cam", [(i, i ^ d) for i in range(n_cam)]))
    images = call(
        image_kernel,
        image_shape,
        out_specs=HBM,
        scratch_shapes=[
            pltpu.VMEM((share, NBLK, 128), F32),
            pltpu.SemaphoreType.DMA((4 * share,)),
        ],
    )(images, onehot, *received)
    return (advected.reshape(shape), images)


def solution(mesh):
    placed = (
        P("ex", None, "ey", None, "cam"),
        P(None, "ex", None, "ey", None, "cam"),
        P("ex", None, "ey", None, "cam"),
        P(),
        P(None, ("cam", "ex", "ey")),
        P(None, ("cam", "ex", "ey")),
    )
    return jax.shard_map(
        per_device,
        mesh=mesh,
        in_specs=placed,
        out_specs=(P("ex", None, "ey", None, "cam"), P("cam", ("ex", "ey"), None)),
        check_vma=False,
    )
```
